32 devices in a mesh: grp: 2 (over x), tp: 8 (over z, y), rb: 2 (over core).
Axes of the slice: x: 2, y: 2, z: 4, core: 2. Of those that a mesh axis runs over, the one named last changes fastest.
Arguments:
- peram: bfloat16 [2048, 24, 2, 1024], P(('grp', 'tp'), None, None, 'rb'), parts along dimension 0, may hold values from -1 to 1
- src_elems: bfloat16 [14, 2, 256, 256], P('grp'), parts along dimension 0, may hold values from -0.25 to 0.25
- owner_times: int32 [16, 2], P('grp'), parts along dimension 0, may hold values from 0 to 23
- diag_mom: int32 [16, 2, 2], P(('grp', 'tp')), parts along dimension 0, may hold values from 0 to 6
- diag_count: int32 [16], P(('grp', 'tp')), parts along dimension 0, may hold values from 1 to 2, as said below
Outputs:
- corr: float32 [16, 2, 2, 2], P(('grp', 'tp')), parts along dimension 0
The draws below stay inside these ranges and needn't reach their ends.
There are 2 independent parts, one for each index of `grp`. The reference program is written for one: setup_inputs(seed, part) draws one part's arguments, and reference() takes and returns one part's arrays. A program takes and returns all parts, laid end to end along the dimension named above; each array names one. Nothing has to cross between parts.
Inputs may be any that keep to these rules, and one draw needn't show every extreme that they name: `diag_count`: some pair has 2 assignments.
All inputs are finite; a program needn't handle non-finite values.
Results may differ from the reference program's by a relative error of at most 0.0031.
Values may be sent and summed in bfloat16 or wider, within the bound.
No kernel may reach another device: no remote copies, remote signals or barrier semaphores. Data moves between devices by JAX's collectives and lax.ppermute only.
A program may use at most 128 MiB of HBM per device.

```python
import math
from functools import partial
import jax
import jax.numpy as jnp
from jax import lax

NV = 256
NSPIN = 4
NS = 1024
T_SNK = 24
NMOM = 7
MAXD = 2
PAIRS = 8


def draw_peram(key, part):
    key_base, key_col = jax.random.split(jax.random.fold_in(key, 11), 2)
    array_shape = (NS, T_SNK, 2, NS)
    column = jnp.exp(jax.random.uniform(key_col, (NS, T_SNK, 1, 1), jnp.float32) * math.log(10.0))
    noise = jax.random.truncated_normal(key_base, -4.0, 4.0, array_shape, jnp.float32)
    return (noise * column / jnp.sqrt(2.0 * NS * 21.5)).astype(jnp.bfloat16)


def draw_diag_count(key, part):
    key_val, key_pos = jax.random.split(jax.random.fold_in(key, 23))
    counts = jax.random.randint(key_val, (PAIRS,), 1, MAXD + 1, jnp.int32)
    position = jax.random.randint(key_pos, (), 0, PAIRS, jnp.int32)
    return counts.at[position].set(MAXD)


def with_ends(drawn, rng, least, high):
    longest = drawn.shape.index(max(drawn.shape))
    spots = []
    for shift in (0, 1):
        where = [jax.random.randint(jax.random.fold_in(rng, axis), (), 0, length) for axis, length in enumerate(drawn.shape)]
        where[longest] = (where[longest] + shift) % drawn.shape[longest]
        spots.append(tuple(where))
    return drawn.at[spots[0]].set(least).at[spots[1]].set(high)


def scatter_about(stream_key, shape, scale, most, kind=jnp.bfloat16):
    drawn = jax.random.normal(stream_key, shape, jnp.float32) * scale
    return jnp.minimum(jnp.maximum(drawn, -most), most).astype(kind)


def setup_inputs(seed: int = 0, part: int = 0) -> dict:
    streams_of = jax.random.split(jax.random.key(seed), 6)
    own_keys = jax.random.split(jax.random.fold_in(streams_of[5], part), 6)
    peram = draw_peram(jax.random.fold_in(jax.random.fold_in(streams_of[5], part), 71), part)
    src_elems = scatter_about(own_keys[1], (NMOM, 2, NV, NV), (2 * NV) ** -0.5, 0.25)
    owner_times = with_ends(jax.random.randint(own_keys[2], (PAIRS, 2), 0, T_SNK), jax.random.fold_in(own_keys[2], 1), 0, T_SNK - 1).astype(jnp.int32)
    diag_mom = with_ends(jax.random.randint(own_keys[3], (PAIRS, MAXD, 2), 0, NMOM), jax.random.fold_in(own_keys[3], 1), 0, NMOM - 1).astype(jnp.int32)
    diag_count = draw_diag_count(jax.random.fold_in(jax.random.fold_in(streams_of[5], part), 71), part)
    return {"peram": peram, "src_elems": src_elems, "owner_times": owner_times, "diag_mom": diag_mom, "diag_count": diag_count}


def meson_matrix(peram, time_slot):
    factor = lax.dynamic_index_in_dim(peram, time_slot, 1, keepdims=False).astype(jnp.float32)
    swapped = jnp.stack([factor[:, 1], -factor[:, 0]], axis=1)
    flat_rows = factor.reshape(NS, 2 * NS)
    flat_swap = swapped.reshape(NS, 2 * NS)
    real_part = jnp.dot(flat_rows, flat_rows.T, preferred_element_type=jnp.float32, precision=lax.Precision.HIGHEST)
    imag_part = jnp.dot(flat_rows, flat_swap.T, preferred_element_type=jnp.float32, precision=lax.Precision.HIGHEST)
    return jnp.stack([real_part, imag_part], axis=1).astype(jnp.bfloat16)


def spin_trace(element, meson):
    blocks = meson.reshape(NSPIN, NV, 2, NSPIN, NV)
    flipped = jnp.swapaxes(element, 1, 2)
    real_sum = jnp.zeros((), jnp.float32)
    imag_sum = jnp.zeros((), jnp.float32)
    for spin_index in range(NSPIN):
        diag_block = blocks[spin_index, :, :, spin_index, :]
        real_sum = real_sum + jnp.sum(flipped[0] * diag_block[:, 0] - flipped[1] * diag_block[:, 1])
        imag_sum = imag_sum + jnp.sum(flipped[0] * diag_block[:, 1] + flipped[1] * diag_block[:, 0])
    return real_sum, imag_sum


def owner_values(mesons, src_elems, owner_times, diag_mom, diag_count, owner):
    high = lax.Precision.HIGHEST
    meson_a = mesons[owner_times[owner, 0]].astype(jnp.float32)
    meson_b = mesons[owner_times[owner, 1]].astype(jnp.float32)
    rows_b = meson_b.reshape(NS, 2, NSPIN, NV)
    rows_a = meson_a.reshape(NSPIN, NV, 2, NS)
    results = []
    for slot_index in range(MAXD):
        elem_three = src_elems[diag_mom[owner, slot_index, 0]].astype(jnp.float32)
        elem_four = src_elems[diag_mom[owner, slot_index, 1]].astype(jnp.float32)
        left_re = jnp.einsum('jsl,le->jse', rows_b[:, 0], elem_four[0], precision=high) - jnp.einsum('jsl,le->jse', rows_b[:, 1], elem_four[1], precision=high)
        left_im = jnp.einsum('jsl,le->jse', rows_b[:, 0], elem_four[1], precision=high) + jnp.einsum('jsl,le->jse', rows_b[:, 1], elem_four[0], precision=high)
        right_re = jnp.einsum('le,slk->sek', elem_three[0], rows_a[:, :, 0], precision=high) + jnp.einsum('le,slk->sek', elem_three[1], rows_a[:, :, 1], precision=high)
        right_im = jnp.einsum('le,slk->sek', elem_three[1], rows_a[:, :, 0], precision=high) - jnp.einsum('le,slk->sek', elem_three[0], rows_a[:, :, 1], precision=high)
        left_re = left_re.reshape(NS, NS)
        left_im = left_im.reshape(NS, NS)
        right_re = right_re.reshape(NS, NS)
        right_im = right_im.reshape(NS, NS)
        cross_re = jnp.sum(left_re * right_re - left_im * right_im)
        cross_im = jnp.sum(left_re * right_im + left_im * right_re)
        three_re, three_im = spin_trace(elem_three, meson_a)
        four_re, four_im = spin_trace(elem_four, meson_b)
        direct_re = three_re * four_re - three_im * four_im
        direct_im = three_re * four_im + three_im * four_re
        results.append(jnp.stack([jnp.stack([direct_re, direct_im]), jnp.stack([cross_re, cross_im])]))
    stacked = 0.25 * jnp.stack(results)
    keep = (jnp.arange(MAXD, dtype=jnp.int32) < diag_count[owner])[:, None, None]
    return jnp.where(keep, stacked, jnp.zeros_like(stacked))


def reference(peram, src_elems, owner_times, diag_mom, diag_count):
    mesons = lax.map(partial(meson_matrix, peram), jnp.arange(T_SNK, dtype=jnp.int32))
    return lax.map(partial(owner_values, mesons, src_elems, owner_times, diag_mom, diag_count), jnp.arange(PAIRS, dtype=jnp.int32))
```

```python
import functools

import jax
import jax.numpy as jnp
from jax import lax
from jax.experimental import pallas as pl
from jax.experimental.pallas import tpu as pltpu
from jax.sharding import PartitionSpec as P

F32 = jnp.float32
BF16 = jnp.bfloat16
ANY = pl.BlockSpec(memory_space=pl.ANY)
SMEM = pl.BlockSpec(memory_space=pltpu.SMEM)
VMEM = pl.BlockSpec(memory_space=pltpu.VMEM)


def dot(left, right):
    return jnp.dot(left, right, preferred_element_type=F32)


def dot_nt(left, right):
    return lax.dot_general(left, right, (((1,), (1,)), ((), ())), preferred_element_type=F32)


def block_table(spins):
    diag = [(s, s) for s in range(spins)]
    off = [(s, t) for s in range(spins) for t in range(s + 1, spins)]
    return [diag[half::2] + off[half::2] for half in range(2)]


def choose(index, values):
    out = jnp.int32(values[0])
    for n in range(1, len(values)):
        out = jnp.where(index == n, jnp.int32(values[n]), out)
    return out


def gram_kernel(eig, table, rb_count, *refs):
    pieces = refs[:-6]
    keep_ref, send_ref, flat, blocks, in_sem, out_sem = refs[-6:]
    rank = lax.axis_index("rb")
    rows, width = pieces[0].shape[1], pieces[0].shape[2]
    per_spin = eig // rows
    low = lax.axis_index("tp") % per_spin
    depth = rb_count * width
    copies = []
    for n, piece in enumerate(pieces):
        far, side = n // rb_count, n % rb_count
        place = (far // per_spin) * per_spin + lax.bitwise_xor(jnp.int32(far % per_spin), low)
        where = pl.ds(pl.multiple_of(place * rows, rows), rows)
        for part in range(2):
            column = part * depth + side * width
            copy = pltpu.make_async_copy(
                piece.at[part], flat.at[where, pl.ds(column, width)], in_sem.at[2 * n + part]
            )
            copy.start()
            copies.append(copy)
    for copy in copies:
        copy.wait()
    total = len(table[0])

    def step(n, carry):
        own = n // total
        half = lax.bitwise_xor(lax.bitwise_xor(rank, 1), own)
        entry = half * total + n % total
        both = table[0] + table[1]
        top = choose(entry, [block[0] for block in both])
        side = choose(entry, [block[1] for block in both])
        top_rows = pl.ds(pl.multiple_of(top * eig, eig), eig)
        side_rows = pl.ds(pl.multiple_of(side * eig, eig), eig)
        left = flat[top_rows, :]
        right = flat[side_rows, :]
        blocks[n, 0] = dot_nt(left, right).astype(BF16)
        imag = dot_nt(left[:, :depth], right[:, depth:]) - dot_nt(left[:, depth:], right[:, :depth])
        blocks[n, 1] = imag.astype(BF16)
        return carry

    lax.fori_loop(0, 2 * total, step, 0)
    send = pltpu.make_async_copy(blocks.at[pl.ds(0, total)], send_ref, out_sem.at[0])
    keep = pltpu.make_async_copy(blocks.at[pl.ds(total, total)], keep_ref, out_sem.at[1])
    send.start()
    keep.start()
    send.wait()
    keep.wait()


def gram(pieces, spins, eig, rb_count):
    table = block_table(spins)
    total = len(table[0])
    side = jax.ShapeDtypeStruct((total, 2, eig, eig), BF16)
    depth = 2 * rb_count * pieces[0].shape[2]
    return pl.pallas_call(
        functools.partial(gram_kernel, eig, table, rb_count),
        out_shape=(side, side),
        in_specs=[ANY] * len(pieces),
        out_specs=(ANY, ANY),
        scratch_shapes=[
            pltpu.VMEM((spins * eig, depth), BF16),
            pltpu.VMEM((2 * total, 2, eig, eig), BF16),
            pltpu.SemaphoreType.DMA((2 * len(pieces),)),
            pltpu.SemaphoreType.DMA((2,)),
        ],
        compiler_params=pltpu.CompilerParams(vmem_limit_bytes=32 << 20),
        cost_estimate=pl.CostEstimate(
            flops=4 * total * 2 * eig * eig * depth, bytes_accessed=8 << 20, transcendentals=0
        ),
        name="gram",
    )(*pieces)


def factors_kernel(slots, diag_mom, elems, right_ref, left_ref, held, sem):
    rank = lax.axis_index("rb")
    eig = held.shape[-1]
    copies = []
    for time in range(2):
        for slot in range(slots):
            which = diag_mom[0, slot, lax.bitwise_xor(rank, time)]
            copy = pltpu.make_async_copy(elems.at[which], held.at[time, slot], sem.at[time, slot])
            copy.start()
            copies.append(copy)
    for copy in copies:
        copy.wait()
    for time in range(2):
        for slot in range(slots):
            re, im = held[time, slot, 0], held[time, slot, 1]
            at = 2 * slot * eig
            right_ref[time, 0:eig, at : at + eig] = re
            right_ref[time, 0:eig, at + eig : at + 2 * eig] = im
            right_ref[time, eig : 2 * eig, at : at + eig] = -im
            right_ref[time, eig : 2 * eig, at + eig : at + 2 * eig] = re
            re_t = re.astype(F32).T.astype(BF16)
            im_t = im.astype(F32).T.astype(BF16)
            left_ref[time, at : at + eig, 0:eig] = re_t
            left_ref[time, at : at + eig, eig : 2 * eig] = im_t
            left_ref[time, at + eig : at + 2 * eig, 0:eig] = im_t
            left_ref[time, at + eig : at + 2 * eig, eig : 2 * eig] = -re_t


def factors(diag_mom, src_elems):
    slots, eig = diag_mom.shape[1], src_elems.shape[-1]
    return pl.pallas_call(
        functools.partial(factors_kernel, slots),
        out_shape=(
            jax.ShapeDtypeStruct((2, 2 * eig, 2 * slots * eig), BF16),
            jax.ShapeDtypeStruct((2, 2 * slots * eig, 2 * eig), BF16),
        ),
        in_specs=[SMEM, ANY],
        out_specs=(VMEM, VMEM),
        scratch_shapes=[
            pltpu.VMEM((2, slots, 2, eig, eig), BF16),
            pltpu.SemaphoreType.DMA((2, slots)),
        ],
        compiler_params=pltpu.CompilerParams(vmem_limit_bytes=32 << 20),
        cost_estimate=pl.CostEstimate(flops=0, bytes_accessed=16 << 20, transcendentals=0),
        name="factors",
    )(diag_mom, src_elems)


def fold(values):
    rows, columns = values.shape
    return jnp.sum(values.reshape(rows // 8, 8, columns), axis=0)


def spread(scalars):
    row = lax.broadcasted_iota(jnp.int32, (8, 128), 0)
    column = lax.broadcasted_iota(jnp.int32, (8, 128), 1)
    tile = jnp.zeros((8, 128), F32)
    for n, (real, imag) in enumerate(scalars):
        tile = jnp.where((row == n) & (column == 0), real, tile)
        tile = jnp.where((row == n) & (column == 1), imag, tile)
    return tile


def direct_kernel(slots, keep, send, right, out):
    eig = keep.shape[-1]
    mesons = [ref[n, part].astype(F32) for part in range(2) for ref in (keep, send) for n in range(keep.shape[0])]
    count = len(mesons) // 2
    real = functools.reduce(jnp.add, mesons[:count])
    imag = functools.reduce(jnp.add, mesons[count:])
    scalars = []
    for slot in range(slots):
        at = 2 * slot * eig
        elem_re = right[0, 0:eig, at : at + eig].astype(F32)
        elem_im = right[0, 0:eig, at + eig : at + 2 * eig].astype(F32)
        scalars.append(
            (jnp.sum(elem_re * real + elem_im * imag), jnp.sum(elem_im * real - elem_re * imag))
        )
    out[...] = spread(scalars)


def direct_traces(slots, keep, send, right, diagonals):
    eig = keep.shape[-1]
    first = pl.BlockSpec((diagonals, 2, eig, eig), lambda i: (0, 0, 0, 0))
    return pl.pallas_call(
        functools.partial(direct_kernel, slots),
        out_shape=jax.ShapeDtypeStruct((8, 128), F32),
        grid=(1,),
        in_specs=[first, first, pl.BlockSpec((1, eig, right.shape[2]), lambda i: (0, 0, 0))],
        out_specs=pl.BlockSpec((8, 128), lambda i: (0, 0)),
        compiler_params=pltpu.CompilerParams(vmem_limit_bytes=32 << 20),
        cost_estimate=pl.CostEstimate(flops=0, bytes_accessed=4 << 20, transcendentals=0),
        name="direct",
    )(keep, send, right)


def cross_kernel(slots, diagonals, own, other, right, left, direct, out, acc):
    total, eig = own.shape[0], own.shape[-1]
    acc[...] = jnp.zeros_like(acc)

    def add(x, y, from_right, from_left):
        product = dot(jnp.concatenate([x[0], x[1]], axis=1), from_right)
        partner = dot(from_left, y.reshape(2 * eig, eig))
        for slot in range(slots):
            at = 2 * slot * eig
            p_re, p_im = product[:, at : at + eig], product[:, at + eig : at + 2 * eig]
            w_re, w_im = partner[at : at + eig], partner[at + eig : at + 2 * eig]
            acc[slot, 0] += fold(p_re * w_re - p_im * w_im)
            acc[slot, 1] += fold(p_re * w_im + p_im * w_re)

    def plain(n, carry):
        add(other[n], own[n], right[1], left[0])
        return carry

    def swapped(n, carry):
        add(own[n], other[n], right[0], left[1])
        return carry

    lax.fori_loop(0, total, plain, 0)
    lax.fori_loop(diagonals, total, swapped, 0)
    scalars = [(jnp.sum(acc[slot, 0]), jnp.sum(acc[slot, 1])) for slot in range(slots)]
    tile = spread([(0.0, 0.0)] * slots + scalars)
    out[...] = direct[...] + tile


def cross_traces(slots, own, other, right, left, direct, diagonals):
    total, eig = own.shape[0], own.shape[-1]
    return pl.pallas_call(
        functools.partial(cross_kernel, slots, diagonals),
        out_shape=jax.ShapeDtypeStruct((8, 128), F32),
        in_specs=[VMEM] * 5,
        out_specs=VMEM,
        scratch_shapes=[pltpu.VMEM((slots, 2, 8, eig), F32)],
        compiler_params=pltpu.CompilerParams(vmem_limit_bytes=48 << 20),
        cost_estimate=pl.CostEstimate(
            flops=(2 * total - diagonals) * 16 * slots * eig**3, bytes_accessed=8 << 20, transcendentals=0
        ),
        name="cross",
    )(own, other, right, left, direct)


def final_kernel(slots, mine, theirs, count, out):
    first = lax.axis_index("rb") == 0
    for slot in range(slots):
        used = slot < count[0]
        mine_re, mine_im = mine[slot, 0], mine[slot, 1]
        theirs_re, theirs_im = theirs[slot, 0], theirs[slot, 1]
        re = mine_re * theirs_re - mine_im * theirs_im
        im = mine_re * theirs_im + mine_im * theirs_re
        out[0, slot, 0, 0] = jnp.where(used, 0.25 * re, 0.0)
        out[0, slot, 0, 1] = jnp.where(used, 0.25 * im, 0.0)
        for part in range(2):
            crossed = mine[slots + slot, part] + theirs[slots + slot, part]
            out[0, slot, 1, part] = jnp.where(used, 0.25 * crossed, 0.0)


def final(mine, theirs, diag_count, slots):
    return pl.pallas_call(
        functools.partial(final_kernel, slots),
        out_shape=jax.ShapeDtypeStruct((1, slots, 2, 2), F32),
        in_specs=[SMEM] * 3,
        out_specs=SMEM,
        name="final",
    )(mine, theirs, diag_count)


def shards(peram, src_elems, owner_times, diag_mom, diag_count):
    tp_count, rb_count = lax.axis_size("tp"), lax.axis_size("rb")
    tp_rank, rb_rank = lax.axis_index("tp"), lax.axis_index("rb")
    eig = src_elems.shape[-1]
    spins = tp_count * peram.shape[0] // eig
    slots = diag_mom.shape[1]
    diagonals = spins // 2

    pieces = []
    for far in reversed(range(tp_count)):
        for side in reversed(range(rb_count)):
            owner = lax.bitwise_xor(tp_rank, far)
            time = owner_times[owner, lax.bitwise_xor(rb_rank, side)]
            picked = lax.dynamic_index_in_dim(peram, time, 1, keepdims=False)
            piece = jnp.swapaxes(picked, 0, 1)
            if far or side:
                pairs = [
                    (tp * rb_count + rb, (tp ^ far) * rb_count + (rb ^ side))
                    for tp in range(tp_count)
                    for rb in range(rb_count)
                ]
                piece = lax.ppermute(piece, ("tp", "rb"), pairs)
            pieces.append(piece)
    pieces = pieces[::-1]

    right, left = factors(diag_mom, src_elems)
    keep, send = gram(pieces, spins, eig, rb_count)
    swap = [(rb, rb ^ 1) for rb in range(rb_count)]
    other = lax.ppermute(send, "rb", swap)
    direct = direct_traces(slots, keep, send, right, diagonals)
    mine = cross_traces(slots, keep, other, right, left, direct, diagonals)
    theirs = lax.ppermute(mine, "rb", swap)
    return final(mine, theirs, diag_count, slots)


def solution(mesh):
    in_specs = (
        P(("grp", "tp"), None, None, "rb"),
        P("grp", None, None, None),
        P("grp", None),
        P(("grp", "tp"), None, None),
        P(("grp", "tp")),
    )
    out_specs = P(("grp", "tp"), None, None, None)
    return jax.shard_map(shards, mesh=mesh, in_specs=in_specs, out_specs=out_specs, check_vma=False)
```

```python
import functools

import jax
import jax.numpy as jnp
from jax import lax
from jax.experimental import pallas as pl
from jax.experimental.pallas import tpu as pltpu
from jax.sharding import PartitionSpec as P

F32 = jnp.float32
BF16 = jnp.bfloat16
ANY = pl.BlockSpec(memory_space=pl.ANY)
HBM = pl.BlockSpec(memory_space=pltpu.HBM)
SMEM = pl.BlockSpec(memory_space=pltpu.SMEM)
VMEM = pl.BlockSpec(memory_space=pltpu.VMEM)


def dot(left, right):
    return jnp.dot(left, right, preferred_element_type=F32)


def dot_nt(left, right):
    return lax.dot_general(left, right, (((1,), (1,)), ((), ())), preferred_element_type=F32)


def block_table(spins):
    diag = [(s, s) for s in range(spins)]
    off = [(s, t) for s in range(spins) for t in range(s + 1, spins)]
    return [diag[half::2] + off[half::2] for half in range(2)]


def choose(index, values):
    out = jnp.int32(values[0])
    for n in range(1, len(values)):
        out = jnp.where(index == n, jnp.int32(values[n]), out)
    return out


def travel_order(tp_count, rb_count):
    every = [(far, side) for far in range(tp_count) for side in range(rb_count)]
    long = [key for key in every if key[0] >= tp_count // 2]
    short = [key for key in every if key[0] < tp_count // 2 and key != (0, 0)][::-1]
    order = [(0, 0)]
    while long or short:
        order += long[:3] + short[:2]
        long, short = long[3:], short[2:]
    return order


def pick_kernel(order, times, peram, *refs):
    outs, sem = refs[:-1], refs[-1]
    tp_rank, rb_rank = lax.axis_index("tp"), lax.axis_index("rb")
    copies = []
    for n, (far, side) in enumerate(order):
        time = times[lax.bitwise_xor(rb_rank, side), lax.bitwise_xor(tp_rank, far)]
        copy = pltpu.make_async_copy(peram.at[:, time], outs[n], sem.at[n])
        copy.start()
        copies.append(copy)
    for copy in copies:
        copy.wait()


def pick(owner_times, peram, order):
    rows, _, parts, width = peram.shape
    piece = jax.ShapeDtypeStruct((rows, parts, width), BF16)
    return pl.pallas_call(
        functools.partial(pick_kernel, order),
        out_shape=(piece,) * len(order),
        in_specs=[SMEM, HBM],
        out_specs=(ANY,) * len(order),
        scratch_shapes=[pltpu.SemaphoreType.DMA((len(order),))],
        cost_estimate=pl.CostEstimate(flops=0, bytes_accessed=8 << 20, transcendentals=0),
        name="pick",
    )(owner_times.T, peram)


def gram_kernel(eig, table, rb_count, order, *refs):
    pieces = refs[:-6]
    keep_ref, send_ref, flat, blocks, in_sem, out_sem = refs[-6:]
    rank = lax.axis_index("rb")
    rows, width = pieces[0].shape[1], pieces[0].shape[2]
    per_spin = eig // rows
    low = lax.axis_index("tp") % per_spin
    depth = rb_count * width
    copies = []
    for n, ((far, side), piece) in enumerate(zip(order, pieces)):
        place = (far // per_spin) * per_spin + lax.bitwise_xor(jnp.int32(far % per_spin), low)
        where = pl.ds(pl.multiple_of(place * rows, rows), rows)
        for part in range(2):
            column = part * depth + side * width
            copy = pltpu.make_async_copy(
                piece.at[part], flat.at[where, pl.ds(column, width)], in_sem.at[2 * n + part]
            )
            copy.start()
            copies.append(copy)
    for copy in copies:
        copy.wait()
    total = len(table[0])

    def step(n, carry):
        own = n // total
        half = lax.bitwise_xor(lax.bitwise_xor(rank, 1), own)
        entry = half * total + n % total
        both = table[0] + table[1]
        top = choose(entry, [block[0] for block in both])
        side = choose(entry, [block[1] for block in both])
        top_rows = pl.ds(pl.multiple_of(top * eig, eig), eig)
        side_rows = pl.ds(pl.multiple_of(side * eig, eig), eig)
        left = flat[top_rows, :]
        right = flat[side_rows, :]
        blocks[n, 0] = dot_nt(left, right).astype(BF16)
        imag = dot_nt(left[:, :depth], right[:, depth:]) - dot_nt(left[:, depth:], right[:, :depth])
        blocks[n, 1] = imag.astype(BF16)
        return carry

    lax.fori_loop(0, 2 * total, step, 0)
    send = pltpu.make_async_copy(blocks.at[pl.ds(0, total)], send_ref, out_sem.at[0])
    keep = pltpu.make_async_copy(blocks.at[pl.ds(total, total)], keep_ref, out_sem.at[1])
    send.start()
    keep.start()
    send.wait()
    keep.wait()


def gram(order, pieces, spins, eig, rb_count):
    table = block_table(spins)
    total = len(table[0])
    side = jax.ShapeDtypeStruct((total, 2, eig, eig), BF16)
    depth = 2 * rb_count * pieces[0].shape[2]
    return pl.pallas_call(
        functools.partial(gram_kernel, eig, table, rb_count, order),
        out_shape=(side, side),
        in_specs=[ANY] * len(pieces),
        out_specs=(ANY, ANY),
        scratch_shapes=[
            pltpu.VMEM((spins * eig, depth), BF16),
            pltpu.VMEM((2 * total, 2, eig, eig), BF16),
            pltpu.SemaphoreType.DMA((2 * len(pieces),)),
            pltpu.SemaphoreType.DMA((2,)),
        ],
        compiler_params=pltpu.CompilerParams(vmem_limit_bytes=32 << 20),
        cost_estimate=pl.CostEstimate(
            flops=4 * total * 2 * eig * eig * depth, bytes_accessed=8 << 20, transcendentals=0
        ),
        name="gram",
    )(*pieces)


def factors_kernel(slots, diag_mom, elems, right_ref, left_ref, held, sem):
    rank = lax.axis_index("rb")
    eig = held.shape[-1]
    copies = []
    for time in range(2):
        for slot in range(slots):
            which = diag_mom[0, slot, lax.bitwise_xor(rank, time)]
            copy = pltpu.make_async_copy(elems.at[which], held.at[time, slot], sem.at[time, slot])
            copy.start()
            copies.append(copy)
    for copy in copies:
        copy.wait()
    for time in range(2):
        for slot in range(slots):
            re, im = held[time, slot, 0], held[time, slot, 1]
            at = 2 * slot * eig
            right_ref[time, 0:eig, at : at + eig] = re
            right_ref[time, 0:eig, at + eig : at + 2 * eig] = im
            right_ref[time, eig : 2 * eig, at : at + eig] = -im
            right_ref[time, eig : 2 * eig, at + eig : at + 2 * eig] = re
            re_t = re.astype(F32).T.astype(BF16)
            im_t = im.astype(F32).T.astype(BF16)
            left_ref[time, at : at + eig, 0:eig] = re_t
            left_ref[time, at : at + eig, eig : 2 * eig] = im_t
            left_ref[time, at + eig : at + 2 * eig, 0:eig] = im_t
            left_ref[time, at + eig : at + 2 * eig, eig : 2 * eig] = -re_t


def factors(diag_mom, src_elems):
    slots, eig = diag_mom.shape[1], src_elems.shape[-1]
    return pl.pallas_call(
        functools.partial(factors_kernel, slots),
        out_shape=(
            jax.ShapeDtypeStruct((2, 2 * eig, 2 * slots * eig), BF16),
            jax.ShapeDtypeStruct((2, 2 * slots * eig, 2 * eig), BF16),
        ),
        in_specs=[SMEM, ANY],
        out_specs=(VMEM, VMEM),
        scratch_shapes=[
            pltpu.VMEM((2, slots, 2, eig, eig), BF16),
            pltpu.SemaphoreType.DMA((2, slots)),
        ],
        compiler_params=pltpu.CompilerParams(vmem_limit_bytes=32 << 20),
        cost_estimate=pl.CostEstimate(flops=0, bytes_accessed=16 << 20, transcendentals=0),
        name="factors",
    )(diag_mom, src_elems)


def fold(values):
    rows, columns = values.shape
    return jnp.sum(values.reshape(rows // 8, 8, columns), axis=0)


def spread(scalars):
    row = lax.broadcasted_iota(jnp.int32, (8, 128), 0)
    column = lax.broadcasted_iota(jnp.int32, (8, 128), 1)
    tile = jnp.zeros((8, 128), F32)
    for n, (real, imag) in enumerate(scalars):
        tile = jnp.where((row == n) & (column == 0), real, tile)
        tile = jnp.where((row == n) & (column == 1), imag, tile)
    return tile


def direct_kernel(slots, keep, send, right, out):
    eig = keep.shape[-1]
    mesons = [ref[n, part].astype(F32) for part in range(2) for ref in (keep, send) for n in range(keep.shape[0])]
    count = len(mesons) // 2
    real = functools.reduce(jnp.add, mesons[:count])
    imag = functools.reduce(jnp.add, mesons[count:])
    scalars = []
    for slot in range(slots):
        at = 2 * slot * eig
        elem_re = right[0, 0:eig, at : at + eig].astype(F32)
        elem_im = right[0, 0:eig, at + eig : at + 2 * eig].astype(F32)
        scalars.append(
            (jnp.sum(elem_re * real + elem_im * imag), jnp.sum(elem_im * real - elem_re * imag))
        )
    out[...] = spread(scalars)


def direct_traces(slots, keep, send, right, diagonals):
    eig = keep.shape[-1]
    first = pl.BlockSpec((diagonals, 2, eig, eig), lambda i: (0, 0, 0, 0))
    return pl.pallas_call(
        functools.partial(direct_kernel, slots),
        out_shape=jax.ShapeDtypeStruct((8, 128), F32),
        grid=(1,),
        in_specs=[first, first, pl.BlockSpec((1, eig, right.shape[2]), lambda i: (0, 0, 0))],
        out_specs=pl.BlockSpec((8, 128), lambda i: (0, 0)),
        compiler_params=pltpu.CompilerParams(vmem_limit_bytes=32 << 20),
        cost_estimate=pl.CostEstimate(flops=0, bytes_accessed=4 << 20, transcendentals=0),
        name="direct",
    )(keep, send, right)


def cross_kernel(slots, diagonals, own, other, right, left, direct, out, acc):
    total, eig = own.shape[0], own.shape[-1]
    acc[...] = jnp.zeros_like(acc)

    def add(x, y, from_right, from_left):
        product = dot(jnp.concatenate([x[0], x[1]], axis=1), from_right)
        partner = dot(from_left, y.reshape(2 * eig, eig))
        for slot in range(slots):
            at = 2 * slot * eig
            p_re, p_im = product[:, at : at + eig], product[:, at + eig : at + 2 * eig]
            w_re, w_im = partner[at : at + eig], partner[at + eig : at + 2 * eig]
            acc[slot, 0] += fold(p_re * w_re - p_im * w_im)
            acc[slot, 1] += fold(p_re * w_im + p_im * w_re)

    def plain(n, carry):
        add(other[n], own[n], right[1], left[0])
        return carry

    def swapped(n, carry):
        add(own[n], other[n], right[0], left[1])
        return carry

    lax.fori_loop(0, total, plain, 0)
    lax.fori_loop(diagonals, total, swapped, 0)
    scalars = [(jnp.sum(acc[slot, 0]), jnp.sum(acc[slot, 1])) for slot in range(slots)]
    tile = spread([(0.0, 0.0)] * slots + scalars)
    out[...] = direct[...] + tile


def cross_traces(slots, own, other, right, left, direct, diagonals):
    total, eig = own.shape[0], own.shape[-1]
    return pl.pallas_call(
        functools.partial(cross_kernel, slots, diagonals),
        out_shape=jax.ShapeDtypeStruct((8, 128), F32),
        in_specs=[VMEM] * 5,
        out_specs=VMEM,
        scratch_shapes=[pltpu.VMEM((slots, 2, 8, eig), F32)],
        compiler_params=pltpu.CompilerParams(vmem_limit_bytes=48 << 20),
        cost_estimate=pl.CostEstimate(
            flops=(2 * total - diagonals) * 16 * slots * eig**3, bytes_accessed=8 << 20, transcendentals=0
        ),
        name="cross",
    )(own, other, right, left, direct)


def final_kernel(slots, mine, theirs, count, out):
    first = lax.axis_index("rb") == 0
    for slot in range(slots):
        used = slot < count[0]
        mine_re, mine_im = mine[slot, 0], mine[slot, 1]
        theirs_re, theirs_im = theirs[slot, 0], theirs[slot, 1]
        re = mine_re * theirs_re - mine_im * theirs_im
        im = mine_re * theirs_im + mine_im * theirs_re
        out[0, slot, 0, 0] = jnp.where(used, 0.25 * re, 0.0)
        out[0, slot, 0, 1] = jnp.where(used, 0.25 * im, 0.0)
        for part in range(2):
            crossed = mine[slots + slot, part] + theirs[slots + slot, part]
            out[0, slot, 1, part] = jnp.where(used, 0.25 * crossed, 0.0)


def final(mine, theirs, diag_count, slots):
    return pl.pallas_call(
        functools.partial(final_kernel, slots),
        out_shape=jax.ShapeDtypeStruct((1, slots, 2, 2), F32),
        in_specs=[SMEM] * 3,
        out_specs=SMEM,
        name="final",
    )(mine, theirs, diag_count)


def shards(peram, src_elems, owner_times, diag_mom, diag_count):
    tp_count, rb_count = lax.axis_size("tp"), lax.axis_size("rb")
    tp_rank, rb_rank = lax.axis_index("tp"), lax.axis_index("rb")
    eig = src_elems.shape[-1]
    spins = tp_count * peram.shape[0] // eig
    slots = diag_mom.shape[1]
    diagonals = spins // 2

    order = travel_order(tp_count, rb_count)
    raw = pick(owner_times, peram, order)
    arrived = {}
    for (far, side), picked in zip(order, raw):
        piece = jnp.swapaxes(picked, 0, 1)
        if far or side:
            pairs = [
                (tp * rb_count + rb, (tp ^ far) * rb_count + (rb ^ side))
                for tp in range(tp_count)
                for rb in range(rb_count)
            ]
            piece = lax.ppermute(piece, ("tp", "rb"), pairs)
        arrived[far, side] = piece
    right, left = factors(diag_mom, src_elems)
    keep, send = gram(order, [arrived[key] for key in order], spins, eig, rb_count)
    swap = [(rb, rb ^ 1) for rb in range(rb_count)]
    other = lax.ppermute(send, "rb", swap)
    direct = direct_traces(slots, keep, send, right, diagonals)
    mine = cross_traces(slots, keep, other, right, left, direct, diagonals)
    theirs = lax.ppermute(mine, "rb", swap)
    return final(mine, theirs, diag_count, slots)


def solution(mesh):
    in_specs = (
        P(("grp", "tp"), None, None, "rb"),
        P("grp", None, None, None),
        P("grp", None),
        P(("grp", "tp"), None, None),
        P(("grp", "tp")),
    )
    out_specs = P(("grp", "tp"), None, None, None)
    return jax.shard_map(shards, mesh=mesh, in_specs=in_specs, out_specs=out_specs, check_vma=False)
```

```python
import functools

import jax
import jax.numpy as jnp
from jax import lax
from jax.experimental import pallas as pl
from jax.experimental.pallas import tpu as pltpu
from jax.sharding import PartitionSpec as P

F32 = jnp.float32
BF16 = jnp.bfloat16
ANY = pl.BlockSpec(memory_space=pl.ANY)
HBM = pl.BlockSpec(memory_space=pltpu.HBM)
SMEM = pl.BlockSpec(memory_space=pltpu.SMEM)
VMEM = pl.BlockSpec(memory_space=pltpu.VMEM)


def dot(left, right):
    return jnp.dot(left, right, preferred_element_type=F32)


def dot_nt(left, right):
    return lax.dot_general(left, right, (((1,), (1,)), ((), ())), preferred_element_type=F32)


def block_table(spins):
    diag = [(s, s) for s in range(spins)]
    off = [(s, t) for s in range(spins) for t in range(s + 1, spins)]
    return [diag[half::2] + off[half::2] for half in range(2)]


def choose(index, values):
    out = jnp.int32(values[0])
    for n in range(1, len(values)):
        out = jnp.where(index == n, jnp.int32(values[n]), out)
    return out


def travel_order(tp_count, rb_count):
    every = [(far, side) for far in range(tp_count) for side in range(rb_count)]
    long = [key for key in every if key[0] >= tp_count // 2]
    short = [key for key in every if key[0] < tp_count // 2 and key != (0, 0)][::-1]
    order = [(0, 0)]
    while long or short:
        order += long[:3] + short[:2]
        long, short = long[3:], short[2:]
    return order


LANES = 128
STEP = 16


def pick_kernel(order, times, table, *refs):
    outs, (held, wide, sem) = refs[:-3], refs[-3:]
    tp_rank, rb_rank = lax.axis_index("tp"), lax.axis_index("rb")
    rows, _, packed, _ = table.shape

    def fetch(chunk):
        where = pl.ds(pl.multiple_of(chunk * STEP, STEP), STEP)
        return pltpu.make_async_copy(table.at[where], held.at[where], sem.at[chunk])

    for chunk in range(rows // STEP):
        fetch(chunk).start()

    def step(chunk, carry):
        fetch(chunk).wait()
        where = pl.ds(pl.multiple_of(chunk * STEP, STEP), STEP)
        for n, (far, side) in enumerate(order):
            time = times[lax.bitwise_xor(rb_rank, side), lax.bitwise_xor(tp_rank, far)]
            slot = n % wide.shape[0]
            wide[slot] = held[where, time].astype(F32).reshape(STEP * packed, LANES)
            for tile in range(packed // 2):
                for part in range(2):
                    taken = wide[slot, pl.ds(2 * tile + part, STEP, stride=packed), :]
                    outs[n][part, where, tile * LANES : (tile + 1) * LANES] = taken.astype(BF16)
        return carry

    lax.fori_loop(0, rows // STEP, step, 0)


def pick(owner_times, peram, order):
    rows, times, parts, width = peram.shape
    tiles = width // LANES
    table = peram.reshape(rows, times, parts, tiles, LANES).swapaxes(2, 3)
    table = table.reshape(rows, times, tiles * parts, LANES)
    piece = jax.ShapeDtypeStruct((parts, rows, width), BF16)
    return pl.pallas_call(
        functools.partial(pick_kernel, order),
        out_shape=(piece,) * len(order),
        in_specs=[SMEM, ANY],
        out_specs=(VMEM,) * len(order),
        scratch_shapes=[
            pltpu.VMEM(table.shape, BF16),
            pltpu.VMEM((4, STEP * tiles * parts, LANES), F32),
            pltpu.SemaphoreType.DMA((rows // STEP,)),
        ],
        compiler_params=pltpu.CompilerParams(vmem_limit_bytes=32 << 20),
        cost_estimate=pl.CostEstimate(flops=0, bytes_accessed=10 << 20, transcendentals=0),
        name="pick",
    )(owner_times.T, table)


def gram_kernel(eig, table, rb_count, order, *refs):
    pieces = refs[:-6]
    keep_ref, send_ref, flat, blocks, in_sem, out_sem = refs[-6:]
    rank = lax.axis_index("rb")
    rows, width = pieces[0].shape[1], pieces[0].shape[2]
    per_spin = eig // rows
    low = lax.axis_index("tp") % per_spin
    depth = rb_count * width
    copies = []
    for n, ((far, side), piece) in enumerate(zip(order, pieces)):
        place = (far // per_spin) * per_spin + lax.bitwise_xor(jnp.int32(far % per_spin), low)
        where = pl.ds(pl.multiple_of(place * rows, rows), rows)
        for part in range(2):
            column = part * depth + side * width
            copy = pltpu.make_async_copy(
                piece.at[part], flat.at[where, pl.ds(column, width)], in_sem.at[2 * n + part]
            )
            copy.start()
            copies.append(copy)
    for copy in copies:
        copy.wait()
    total = len(table[0])

    def step(n, carry):
        own = n // total
        half = lax.bitwise_xor(lax.bitwise_xor(rank, 1), own)
        entry = half * total + n % total
        both = table[0] + table[1]
        top = choose(entry, [block[0] for block in both])
        side = choose(entry, [block[1] for block in both])
        top_rows = pl.ds(pl.multiple_of(top * eig, eig), eig)
        side_rows = pl.ds(pl.multiple_of(side * eig, eig), eig)
        left = flat[top_rows, :]
        right = flat[side_rows, :]
        blocks[n, 0] = dot_nt(left, right).astype(BF16)
        imag = dot_nt(left[:, :depth], right[:, depth:]) - dot_nt(left[:, depth:], right[:, :depth])
        blocks[n, 1] = imag.astype(BF16)
        return carry

    lax.fori_loop(0, 2 * total, step, 0)
    send = pltpu.make_async_copy(blocks.at[pl.ds(0, total)], send_ref, out_sem.at[0])
    keep = pltpu.make_async_copy(blocks.at[pl.ds(total, total)], keep_ref, out_sem.at[1])
    send.start()
    keep.start()
    send.wait()
    keep.wait()


def gram(order, pieces, spins, eig, rb_count):
    table = block_table(spins)
    total = len(table[0])
    side = jax.ShapeDtypeStruct((total, 2, eig, eig), BF16)
    depth = 2 * rb_count * pieces[0].shape[2]
    return pl.pallas_call(
        functools.partial(gram_kernel, eig, table, rb_count, order),
        out_shape=(side, side),
        in_specs=[ANY] * len(pieces),
        out_specs=(ANY, ANY),
        scratch_shapes=[
            pltpu.VMEM((spins * eig, depth), BF16),
            pltpu.VMEM((2 * total, 2, eig, eig), BF16),
            pltpu.SemaphoreType.DMA((2 * len(pieces),)),
            pltpu.SemaphoreType.DMA((2,)),
        ],
        compiler_params=pltpu.CompilerParams(vmem_limit_bytes=32 << 20),
        cost_estimate=pl.CostEstimate(
            flops=4 * total * 2 * eig * eig * depth, bytes_accessed=8 << 20, transcendentals=0
        ),
        name="gram",
    )(*pieces)


def factors_kernel(slots, diag_mom, elems, right_ref, left_ref, held, sem):
    rank = lax.axis_index("rb")
    eig = held.shape[-1]
    copies = []
    for time in range(2):
        for slot in range(slots):
            which = diag_mom[0, slot, lax.bitwise_xor(rank, time)]
            copy = pltpu.make_async_copy(elems.at[which], held.at[time, slot], sem.at[time, slot])
            copy.start()
            copies.append(copy)
    for copy in copies:
        copy.wait()
    for time in range(2):
        for slot in range(slots):
            re, im = held[time, slot, 0], held[time, slot, 1]
            at = 2 * slot * eig
            right_ref[time, 0:eig, at : at + eig] = re
            right_ref[time, 0:eig, at + eig : at + 2 * eig] = im
            right_ref[time, eig : 2 * eig, at : at + eig] = -im
            right_ref[time, eig : 2 * eig, at + eig : at + 2 * eig] = re
            re_t = re.astype(F32).T.astype(BF16)
            im_t = im.astype(F32).T.astype(BF16)
            left_ref[time, at : at + eig, 0:eig] = re_t
            left_ref[time, at : at + eig, eig : 2 * eig] = im_t
            left_ref[time, at + eig : at + 2 * eig, 0:eig] = im_t
            left_ref[time, at + eig : at + 2 * eig, eig : 2 * eig] = -re_t


def factors(diag_mom, src_elems):
    slots, eig = diag_mom.shape[1], src_elems.shape[-1]
    return pl.pallas_call(
        functools.partial(factors_kernel, slots),
        out_shape=(
            jax.ShapeDtypeStruct((2, 2 * eig, 2 * slots * eig), BF16),
            jax.ShapeDtypeStruct((2, 2 * slots * eig, 2 * eig), BF16),
        ),
        in_specs=[SMEM, ANY],
        out_specs=(VMEM, VMEM),
        scratch_shapes=[
            pltpu.VMEM((2, slots, 2, eig, eig), BF16),
            pltpu.SemaphoreType.DMA((2, slots)),
        ],
        compiler_params=pltpu.CompilerParams(vmem_limit_bytes=32 << 20),
        cost_estimate=pl.CostEstimate(flops=0, bytes_accessed=16 << 20, transcendentals=0),
        name="factors",
    )(diag_mom, src_elems)


def fold(values):
    rows, columns = values.shape
    return jnp.sum(values.reshape(rows // 8, 8, columns), axis=0)


def spread(scalars):
    row = lax.broadcasted_iota(jnp.int32, (8, 128), 0)
    column = lax.broadcasted_iota(jnp.int32, (8, 128), 1)
    tile = jnp.zeros((8, 128), F32)
    for n, (real, imag) in enumerate(scalars):
        tile = jnp.where((row == n) & (column == 0), real, tile)
        tile = jnp.where((row == n) & (column == 1), imag, tile)
    return tile


def direct_kernel(slots, keep, send, right, out):
    eig = keep.shape[-1]
    mesons = [ref[n, part].astype(F32) for part in range(2) for ref in (keep, send) for n in range(keep.shape[0])]
    count = len(mesons) // 2
    real = functools.reduce(jnp.add, mesons[:count])
    imag = functools.reduce(jnp.add, mesons[count:])
    scalars = []
    for slot in range(slots):
        at = 2 * slot * eig
        elem_re = right[0, 0:eig, at : at + eig].astype(F32)
        elem_im = right[0, 0:eig, at + eig : at + 2 * eig].astype(F32)
        scalars.append(
            (jnp.sum(elem_re * real + elem_im * imag), jnp.sum(elem_im * real - elem_re * imag))
        )
    out[...] = spread(scalars)


def direct_traces(slots, keep, send, right, diagonals):
    eig = keep.shape[-1]
    first = pl.BlockSpec((diagonals, 2, eig, eig), lambda i: (0, 0, 0, 0))
    return pl.pallas_call(
        functools.partial(direct_kernel, slots),
        out_shape=jax.ShapeDtypeStruct((8, 128), F32),
        grid=(1,),
        in_specs=[first, first, pl.BlockSpec((1, eig, right.shape[2]), lambda i: (0, 0, 0))],
        out_specs=pl.BlockSpec((8, 128), lambda i: (0, 0)),
        compiler_params=pltpu.CompilerParams(vmem_limit_bytes=32 << 20),
        cost_estimate=pl.CostEstimate(flops=0, bytes_accessed=4 << 20, transcendentals=0),
        name="direct",
    )(keep, send, right)


def cross_kernel(slots, diagonals, own, other, right, left, direct, out, acc):
    total, eig = own.shape[0], own.shape[-1]
    acc[...] = jnp.zeros_like(acc)

    def add(x, y, from_right, from_left):
        product = dot(jnp.concatenate([x[0], x[1]], axis=1), from_right)
        partner = dot(from_left, y.reshape(2 * eig, eig))
        for slot in range(slots):
            at = 2 * slot * eig
            p_re, p_im = product[:, at : at + eig], product[:, at + eig : at + 2 * eig]
            w_re, w_im = partner[at : at + eig], partner[at + eig : at + 2 * eig]
            acc[slot, 0] += fold(p_re * w_re - p_im * w_im)
            acc[slot, 1] += fold(p_re * w_im + p_im * w_re)

    def plain(n, carry):
        add(other[n], own[n], right[1], left[0])
        return carry

    def swapped(n, carry):
        add(own[n], other[n], right[0], left[1])
        return carry

    lax.fori_loop(0, total, plain, 0)
    lax.fori_loop(diagonals, total, swapped, 0)
    scalars = [(jnp.sum(acc[slot, 0]), jnp.sum(acc[slot, 1])) for slot in range(slots)]
    tile = spread([(0.0, 0.0)] * slots + scalars)
    out[...] = direct[...] + tile


def cross_traces(slots, own, other, right, left, direct, diagonals):
    total, eig = own.shape[0], own.shape[-1]
    return pl.pallas_call(
        functools.partial(cross_kernel, slots, diagonals),
        out_shape=jax.ShapeDtypeStruct((8, 128), F32),
        in_specs=[VMEM] * 5,
        out_specs=VMEM,
        scratch_shapes=[pltpu.VMEM((slots, 2, 8, eig), F32)],
        compiler_params=pltpu.CompilerParams(vmem_limit_bytes=48 << 20),
        cost_estimate=pl.CostEstimate(
            flops=(2 * total - diagonals) * 16 * slots * eig**3, bytes_accessed=8 << 20, transcendentals=0
        ),
        name="cross",
    )(own, other, right, left, direct)


def final_kernel(slots, mine, theirs, count, out):
    first = lax.axis_index("rb") == 0
    for slot in range(slots):
        used = slot < count[0]
        mine_re, mine_im = mine[slot, 0], mine[slot, 1]
        theirs_re, theirs_im = theirs[slot, 0], theirs[slot, 1]
        re = mine_re * theirs_re - mine_im * theirs_im
        im = mine_re * theirs_im + mine_im * theirs_re
        out[0, slot, 0, 0] = jnp.where(used, 0.25 * re, 0.0)
        out[0, slot, 0, 1] = jnp.where(used, 0.25 * im, 0.0)
        for part in range(2):
            crossed = mine[slots + slot, part] + theirs[slots + slot, part]
            out[0, slot, 1, part] = jnp.where(used, 0.25 * crossed, 0.0)


def final(mine, theirs, diag_count, slots):
    return pl.pallas_call(
        functools.partial(final_kernel, slots),
        out_shape=jax.ShapeDtypeStruct((1, slots, 2, 2), F32),
        in_specs=[SMEM] * 3,
        out_specs=SMEM,
        name="final",
    )(mine, theirs, diag_count)


def shards(peram, src_elems, owner_times, diag_mom, diag_count):
    tp_count, rb_count = lax.axis_size("tp"), lax.axis_size("rb")
    tp_rank, rb_rank = lax.axis_index("tp"), lax.axis_index("rb")
    eig = src_elems.shape[-1]
    spins = tp_count * peram.shape[0] // eig
    slots = diag_mom.shape[1]
    diagonals = spins // 2

    order = travel_order(tp_count, rb_count)
    raw = pick(owner_times, peram, order)
    arrived = {}
    for (far, side), picked in zip(order, raw):
        piece = picked
        if far or side:
            pairs = [
                (tp * rb_count + rb, (tp ^ far) * rb_count + (rb ^ side))
                for tp in range(tp_count)
                for rb in range(rb_count)
            ]
            piece = lax.ppermute(piece, ("tp", "rb"), pairs)
        arrived[far, side] = piece
    right, left = factors(diag_mom, src_elems)
    keep, send = gram(order, [arrived[key] for key in order], spins, eig, rb_count)
    swap = [(rb, rb ^ 1) for rb in range(rb_count)]
    other = lax.ppermute(send, "rb", swap)
    direct = direct_traces(slots, keep, send, right, diagonals)
    mine = cross_traces(slots, keep, other, right, left, direct, diagonals)
    theirs = lax.ppermute(mine, "rb", swap)
    return final(mine, theirs, diag_count, slots)


def solution(mesh):
    in_specs = (
        P(("grp", "tp"), None, None, "rb"),
        P("grp", None, None, None),
        P("grp", None),
        P(("grp", "tp"), None, None),
        P(("grp", "tp")),
    )
    out_specs = P(("grp", "tp"), None, None, None)
    return jax.shard_map(shards, mesh=mesh, in_specs=in_specs, out_specs=out_specs, check_vma=False)
```

```python
import functools

import jax
import jax.numpy as jnp
from jax import lax
from jax.experimental import pallas as pl
from jax.experimental.pallas import tpu as pltpu
from jax.sharding import PartitionSpec as P

F32 = jnp.float32
BF16 = jnp.bfloat16
ANY = pl.BlockSpec(memory_space=pl.ANY)
HBM = pl.BlockSpec(memory_space=pltpu.HBM)
SMEM = pl.BlockSpec(memory_space=pltpu.SMEM)
VMEM = pl.BlockSpec(memory_space=pltpu.VMEM)


def dot(left, right):
    return jnp.dot(left, right, preferred_element_type=F32)


def dot_nt(left, right):
    return lax.dot_general(left, right, (((1,), (1,)), ((), ())), preferred_element_type=F32)


def block_table(spins):
    diag = [(s, s) for s in range(spins)]
    off = [(s, t) for s in range(spins) for t in range(s + 1, spins)]
    return [diag[half::2] + off[half::2] for half in range(2)]


def choose(index, values):
    out = jnp.int32(values[0])
    for n in range(1, len(values)):
        out = jnp.where(index == n, jnp.int32(values[n]), out)
    return out


def travel_order(tp_count, rb_count):
    half, quarter = tp_count // 2, tp_count // 4
    long = [(far, side) for far in range(half, tp_count) for side in range(rb_count)]
    near = [(far, side) for far in reversed(range(quarter, half)) for side in range(rb_count)]
    rest = [(far, side) for far in range(1, quarter) for side in range(rb_count)]
    third, last = 3 * len(long) // 8, 7 * len(long) // 8
    order = [(0, 0)] + long[:third] + near[: len(near) // 2]
    order += long[third : 2 * third] + near[len(near) // 2 :]
    order += long[2 * third : last] + rest + long[last:]
    return order + [(0, side) for side in range(1, rb_count)]


LANES = 128
STEP = 16


def pick_kernel(order, times, table, *refs):
    outs, (held, wide, sem) = refs[:-3], refs[-3:]
    tp_rank, rb_rank = lax.axis_index("tp"), lax.axis_index("rb")
    rows, _, packed, _ = table.shape

    def fetch(chunk):
        where = pl.ds(pl.multiple_of(chunk * STEP, STEP), STEP)
        return pltpu.make_async_copy(table.at[where], held.at[where], sem.at[chunk])

    for chunk in range(rows // STEP):
        fetch(chunk).start()

    def step(chunk, carry):
        fetch(chunk).wait()
        where = pl.ds(pl.multiple_of(chunk * STEP, STEP), STEP)
        for n, (far, side) in enumerate(order):
            time = times[lax.bitwise_xor(rb_rank, side), lax.bitwise_xor(tp_rank, far)]
            slot = n % wide.shape[0]
            wide[slot] = held[where, time].astype(F32).reshape(STEP * packed, LANES)
            for tile in range(packed // 2):
                for part in range(2):
                    taken = wide[slot, pl.ds(2 * tile + part, STEP, stride=packed), :]
                    outs[n][part, where, tile * LANES : (tile + 1) * LANES] = taken.astype(BF16)
        return carry

    lax.fori_loop(0, rows // STEP, step, 0)


def pick(owner_times, peram, order):
    rows, times, parts, width = peram.shape
    tiles = width // LANES
    table = peram.reshape(rows, times, parts, tiles, LANES).swapaxes(2, 3)
    table = table.reshape(rows, times, tiles * parts, LANES)
    piece = jax.ShapeDtypeStruct((parts, rows, width), BF16)
    return pl.pallas_call(
        functools.partial(pick_kernel, order),
        out_shape=(piece,) * len(order),
        in_specs=[SMEM, ANY],
        out_specs=(VMEM,) * len(order),
        scratch_shapes=[
            pltpu.VMEM(table.shape, BF16),
            pltpu.VMEM((4, STEP * tiles * parts, LANES), F32),
            pltpu.SemaphoreType.DMA((rows // STEP,)),
        ],
        compiler_params=pltpu.CompilerParams(vmem_limit_bytes=32 << 20),
        cost_estimate=pl.CostEstimate(flops=0, bytes_accessed=10 << 20, transcendentals=0),
        name="pick",
    )(owner_times.T, table)


def gram_kernel(eig, table, rb_count, order, *refs):
    pieces = refs[:-6]
    keep_ref, send_ref, flat, blocks, in_sem, out_sem = refs[-6:]
    rank = lax.axis_index("rb")
    rows, width = pieces[0].shape[1], pieces[0].shape[2]
    per_spin = eig // rows
    low = lax.axis_index("tp") % per_spin
    depth = rb_count * width
    copies = []
    for n, ((far, side), piece) in enumerate(zip(order, pieces)):
        place = (far // per_spin) * per_spin + lax.bitwise_xor(jnp.int32(far % per_spin), low)
        where = pl.ds(pl.multiple_of(place * rows, rows), rows)
        for part in range(2):
            column = part * depth + side * width
            copy = pltpu.make_async_copy(
                piece.at[part], flat.at[where, pl.ds(column, width)], in_sem.at[2 * n + part]
            )
            copy.start()
            copies.append(copy)
    for copy in copies:
        copy.wait()
    total = len(table[0])

    def step(n, carry):
        own = n // total
        half = lax.bitwise_xor(lax.bitwise_xor(rank, 1), own)
        entry = half * total + n % total
        both = table[0] + table[1]
        top = choose(entry, [block[0] for block in both])
        side = choose(entry, [block[1] for block in both])
        top_rows = pl.ds(pl.multiple_of(top * eig, eig), eig)
        side_rows = pl.ds(pl.multiple_of(side * eig, eig), eig)
        left = flat[top_rows, :]
        right = flat[side_rows, :]
        blocks[n, 0] = dot_nt(left, right).astype(BF16)
        imag = dot_nt(left[:, :depth], right[:, depth:]) - dot_nt(left[:, depth:], right[:, :depth])
        blocks[n, 1] = imag.astype(BF16)
        return carry

    lax.fori_loop(0, 2 * total, step, 0)
    send = pltpu.make_async_copy(blocks.at[pl.ds(0, total)], send_ref, out_sem.at[0])
    keep = pltpu.make_async_copy(blocks.at[pl.ds(total, total)], keep_ref, out_sem.at[1])
    send.start()
    keep.start()
    send.wait()
    keep.wait()


def gram(order, pieces, spins, eig, rb_count):
    table = block_table(spins)
    total = len(table[0])
    side = jax.ShapeDtypeStruct((total, 2, eig, eig), BF16)
    depth = 2 * rb_count * pieces[0].shape[2]
    return pl.pallas_call(
        functools.partial(gram_kernel, eig, table, rb_count, order),
        out_shape=(side, side),
        in_specs=[ANY] * len(pieces),
        out_specs=(ANY, ANY),
        scratch_shapes=[
            pltpu.VMEM((spins * eig, depth), BF16),
            pltpu.VMEM((2 * total, 2, eig, eig), BF16),
            pltpu.SemaphoreType.DMA((2 * len(pieces),)),
            pltpu.SemaphoreType.DMA((2,)),
        ],
        compiler_params=pltpu.CompilerParams(vmem_limit_bytes=32 << 20),
        cost_estimate=pl.CostEstimate(
            flops=4 * total * 2 * eig * eig * depth, bytes_accessed=8 << 20, transcendentals=0
        ),
        name="gram",
    )(*pieces)


def factors_kernel(slots, diag_mom, elems, right_ref, left_ref, held, sem):
    rank = lax.axis_index("rb")
    eig = held.shape[-1]
    copies = []
    for time in range(2):
        for slot in range(slots):
            which = diag_mom[0, slot, lax.bitwise_xor(rank, time)]
            copy = pltpu.make_async_copy(elems.at[which], held.at[time, slot], sem.at[time, slot])
            copy.start()
            copies.append(copy)
    for copy in copies:
        copy.wait()
    for time in range(2):
        for slot in range(slots):
            re, im = held[time, slot, 0], held[time, slot, 1]
            at = 2 * slot * eig
            right_ref[time, 0:eig, at : at + eig] = re
            right_ref[time, 0:eig, at + eig : at + 2 * eig] = im
            right_ref[time, eig : 2 * eig, at : at + eig] = -im
            right_ref[time, eig : 2 * eig, at + eig : at + 2 * eig] = re
            re_t = re.astype(F32).T.astype(BF16)
            im_t = im.astype(F32).T.astype(BF16)
            left_ref[time, at : at + eig, 0:eig] = re_t
            left_ref[time, at : at + eig, eig : 2 * eig] = im_t
            left_ref[time, at + eig : at + 2 * eig, 0:eig] = im_t
            left_ref[time, at + eig : at + 2 * eig, eig : 2 * eig] = -re_t


def factors(diag_mom, src_elems):
    slots, eig = diag_mom.shape[1], src_elems.shape[-1]
    return pl.pallas_call(
        functools.partial(factors_kernel, slots),
        out_shape=(
            jax.ShapeDtypeStruct((2, 2 * eig, 2 * slots * eig), BF16),
            jax.ShapeDtypeStruct((2, 2 * slots * eig, 2 * eig), BF16),
        ),
        in_specs=[SMEM, ANY],
        out_specs=(VMEM, VMEM),
        scratch_shapes=[
            pltpu.VMEM((2, slots, 2, eig, eig), BF16),
            pltpu.SemaphoreType.DMA((2, slots)),
        ],
        compiler_params=pltpu.CompilerParams(vmem_limit_bytes=32 << 20),
        cost_estimate=pl.CostEstimate(flops=0, bytes_accessed=16 << 20, transcendentals=0),
        name="factors",
    )(diag_mom, src_elems)


def fold(values):
    rows, columns = values.shape
    return jnp.sum(values.reshape(rows // 8, 8, columns), axis=0)


def spread(scalars):
    row = lax.broadcasted_iota(jnp.int32, (8, 128), 0)
    column = lax.broadcasted_iota(jnp.int32, (8, 128), 1)
    tile = jnp.zeros((8, 128), F32)
    for n, (real, imag) in enumerate(scalars):
        tile = jnp.where((row == n) & (column == 0), real, tile)
        tile = jnp.where((row == n) & (column == 1), imag, tile)
    return tile


def direct_kernel(slots, keep, send, right, out):
    eig = keep.shape[-1]
    mesons = [ref[n, part].astype(F32) for part in range(2) for ref in (keep, send) for n in range(keep.shape[0])]
    count = len(mesons) // 2
    real = functools.reduce(jnp.add, mesons[:count])
    imag = functools.reduce(jnp.add, mesons[count:])
    scalars = []
    for slot in range(slots):
        at = 2 * slot * eig
        elem_re = right[0, 0:eig, at : at + eig].astype(F32)
        elem_im = right[0, 0:eig, at + eig : at + 2 * eig].astype(F32)
        scalars.append(
            (jnp.sum(elem_re * real + elem_im * imag), jnp.sum(elem_im * real - elem_re * imag))
        )
    out[...] = spread(scalars)


def direct_traces(slots, keep, send, right, diagonals):
    eig = keep.shape[-1]
    first = pl.BlockSpec((diagonals, 2, eig, eig), lambda i: (0, 0, 0, 0))
    return pl.pallas_call(
        functools.partial(direct_kernel, slots),
        out_shape=jax.ShapeDtypeStruct((8, 128), F32),
        grid=(1,),
        in_specs=[first, first, pl.BlockSpec((1, eig, right.shape[2]), lambda i: (0, 0, 0))],
        out_specs=pl.BlockSpec((8, 128), lambda i: (0, 0)),
        compiler_params=pltpu.CompilerParams(vmem_limit_bytes=32 << 20),
        cost_estimate=pl.CostEstimate(flops=0, bytes_accessed=4 << 20, transcendentals=0),
        name="direct",
    )(keep, send, right)


def cross_kernel(slots, diagonals, own, other, right, left, direct, out, acc):
    total, eig = own.shape[0], own.shape[-1]
    acc[...] = jnp.zeros_like(acc)

    def add(x, y, from_right, from_left):
        product = dot(jnp.concatenate([x[0], x[1]], axis=1), from_right)
        partner = dot(from_left, y.reshape(2 * eig, eig))
        for slot in range(slots):
            at = 2 * slot * eig
            p_re, p_im = product[:, at : at + eig], product[:, at + eig : at + 2 * eig]
            w_re, w_im = partner[at : at + eig], partner[at + eig : at + 2 * eig]
            acc[slot, 0] += fold(p_re * w_re - p_im * w_im)
            acc[slot, 1] += fold(p_re * w_im + p_im * w_re)

    def plain(n, carry):
        add(other[n], own[n], right[1], left[0])
        return carry

    def swapped(n, carry):
        add(own[n], other[n], right[0], left[1])
        return carry

    lax.fori_loop(0, total, plain, 0)
    lax.fori_loop(diagonals, total, swapped, 0)
    scalars = [(jnp.sum(acc[slot, 0]), jnp.sum(acc[slot, 1])) for slot in range(slots)]
    tile = spread([(0.0, 0.0)] * slots + scalars)
    out[...] = direct[...] + tile


def cross_traces(slots, own, other, right, left, direct, diagonals):
    total, eig = own.shape[0], own.shape[-1]
    return pl.pallas_call(
        functools.partial(cross_kernel, slots, diagonals),
        out_shape=jax.ShapeDtypeStruct((8, 128), F32),
        in_specs=[VMEM] * 5,
        out_specs=VMEM,
        scratch_shapes=[pltpu.VMEM((slots, 2, 8, eig), F32)],
        compiler_params=pltpu.CompilerParams(vmem_limit_bytes=48 << 20),
        cost_estimate=pl.CostEstimate(
            flops=(2 * total - diagonals) * 16 * slots * eig**3, bytes_accessed=8 << 20, transcendentals=0
        ),
        name="cross",
    )(own, other, right, left, direct)


def final_kernel(slots, mine, theirs, count, out):
    first = lax.axis_index("rb") == 0
    for slot in range(slots):
        used = slot < count[0]
        mine_re, mine_im = mine[slot, 0], mine[slot, 1]
        theirs_re, theirs_im = theirs[slot, 0], theirs[slot, 1]
        re = mine_re * theirs_re - mine_im * theirs_im
        im = mine_re * theirs_im + mine_im * theirs_re
        out[0, slot, 0, 0] = jnp.where(used, 0.25 * re, 0.0)
        out[0, slot, 0, 1] = jnp.where(used, 0.25 * im, 0.0)
        for part in range(2):
            crossed = mine[slots + slot, part] + theirs[slots + slot, part]
            out[0, slot, 1, part] = jnp.where(used, 0.25 * crossed, 0.0)


def final(mine, theirs, diag_count, slots):
    return pl.pallas_call(
        functools.partial(final_kernel, slots),
        out_shape=jax.ShapeDtypeStruct((1, slots, 2, 2), F32),
        in_specs=[SMEM] * 3,
        out_specs=SMEM,
        name="final",
    )(mine, theirs, diag_count)


def shards(peram, src_elems, owner_times, diag_mom, diag_count):
    tp_count, rb_count = lax.axis_size("tp"), lax.axis_size("rb")
    tp_rank, rb_rank = lax.axis_index("tp"), lax.axis_index("rb")
    eig = src_elems.shape[-1]
    spins = tp_count * peram.shape[0] // eig
    slots = diag_mom.shape[1]
    diagonals = spins // 2

    order = travel_order(tp_count, rb_count)
    raw = pick(owner_times, peram, order)
    arrived = {}
    for (far, side), picked in zip(order, raw):
        piece = picked
        if far or side:
            pairs = [
                (tp * rb_count + rb, (tp ^ far) * rb_count + (rb ^ side))
                for tp in range(tp_count)
                for rb in range(rb_count)
            ]
            piece = lax.ppermute(piece, ("tp", "rb"), pairs)
        arrived[far, side] = piece
    right, left = factors(diag_mom, src_elems)
    keep, send = gram(order, [arrived[key] for key in order], spins, eig, rb_count)
    swap = [(rb, rb ^ 1) for rb in range(rb_count)]
    other = lax.ppermute(send, "rb", swap)
    direct = direct_traces(slots, keep, send, right, diagonals)
    mine = cross_traces(slots, keep, other, right, left, direct, diagonals)
    theirs = lax.ppermute(mine, "rb", swap)
    return final(mine, theirs, diag_count, slots)


def solution(mesh):
    in_specs = (
        P(("grp", "tp"), None, None, "rb"),
        P("grp", None, None, None),
        P("grp", None),
        P(("grp", "tp"), None, None),
        P(("grp", "tp")),
    )
    out_specs = P(("grp", "tp"), None, None, None)
    return jax.shard_map(shards, mesh=mesh, in_specs=in_specs, out_specs=out_specs, check_vma=False)
```

```python
import functools

import jax
import jax.numpy as jnp
from jax import lax
from jax.experimental import pallas as pl
from jax.experimental.pallas import tpu as pltpu
from jax.sharding import PartitionSpec as P

F32 = jnp.float32
BF16 = jnp.bfloat16
ANY = pl.BlockSpec(memory_space=pl.ANY)
SMEM = pl.BlockSpec(memory_space=pltpu.SMEM)
VMEM = pl.BlockSpec(memory_space=pltpu.VMEM)
TILE = (8, 128)
LANES = 128
STEP = 16
MIB = 1 << 20
LITTLE = pl.CostEstimate(flops=1000, bytes_accessed=1000, transcendentals=0)
LONG = pl.CostEstimate(flops=5 * 10**10, bytes_accessed=1000, transcendentals=0)


def params(mib):
    return pltpu.CompilerParams(vmem_limit_bytes=mib * MIB)


def dot(left, right):
    return jnp.dot(left, right, preferred_element_type=F32)


def dot_nt(left, right):
    return lax.dot_general(left, right, (((1,), (1,)), ((), ())), preferred_element_type=F32)


def choose(index, values):
    out = jnp.int32(values[0])
    for n in range(1, len(values)):
        out = jnp.where(index == n, jnp.int32(values[n]), out)
    return out


def aligned(start, size):
    return pl.ds(pl.multiple_of(start, size), size)


def travel_order(tp_count, rb_count):
    half, quarter = tp_count // 2, tp_count // 4

    def both(distances):
        return [(far, side) for far in distances for side in range(rb_count)]

    long, late = both(range(half, half + quarter)), both(range(half + quarter, tp_count))
    near, rest = both(reversed(range(quarter, half))), both(range(1, quarter))
    cut, part = 3 * len(long) // 4, len(near) // 2
    early = long[:cut] + near[:part] + long[cut:] + near[part:] + rest
    early += [(0, side) for side in range(1, rb_count)]
    return early, late, [(0, 0)]


def pick_kernel(keys, times, table, *refs):
    outs, (held, wide, sem) = refs[:-3], refs[-3:]
    tp_rank, rb_rank = lax.axis_index("tp"), lax.axis_index("rb")
    rows, _, packed, _ = table.shape

    def fetch(chunk):
        where = aligned(chunk * STEP, STEP)
        return pltpu.make_async_copy(table.at[where], held.at[where], sem.at[chunk])

    for chunk in range(rows // STEP):
        fetch(chunk).start()

    def step(chunk, carry):
        fetch(chunk).wait()
        where = aligned(chunk * STEP, STEP)
        for n, (far, side) in enumerate(keys):
            time = times[lax.bitwise_xor(rb_rank, side), lax.bitwise_xor(tp_rank, far)]
            slot = n % wide.shape[0]
            wide[slot] = held[where, time].astype(F32).reshape(STEP * packed, LANES)
            for tile in range(packed // 2):
                for part in range(2):
                    taken = wide[slot, pl.ds(2 * tile + part, STEP, stride=packed), :]
                    outs[n][part, where, tile * LANES : (tile + 1) * LANES] = taken.astype(BF16)
        return carry

    lax.fori_loop(0, rows // STEP, step, 0)


def pick(owner_times, peram, keys):
    rows, times, parts, width = peram.shape
    tiles = width // LANES
    table = peram.reshape(rows, times, parts, tiles, LANES).swapaxes(2, 3)
    table = table.reshape(rows, times, tiles * parts, LANES)
    picked = pl.pallas_call(
        functools.partial(pick_kernel, keys),
        out_shape=[jax.ShapeDtypeStruct((parts, rows, width), BF16)] * len(keys),
        in_specs=[SMEM, ANY],
        out_specs=[VMEM] * len(keys),
        scratch_shapes=[
            pltpu.VMEM(table.shape, BF16),
            pltpu.VMEM((4, STEP * tiles * parts, LANES), F32),
            pltpu.SemaphoreType.DMA((rows // STEP,)),
        ],
        compiler_params=params(32),
        cost_estimate=LITTLE,
        name="pick",
    )(owner_times.T, table)
    return dict(zip(keys, picked))


def place(far, per_spin):
    low = lax.axis_index("tp") % per_spin
    return (far // per_spin) * per_spin + lax.bitwise_xor(jnp.int32(far % per_spin), low)


def gram_block(left, right):
    depth = left.shape[1] // 2
    real = dot_nt(left, right)
    imag = dot_nt(left[:, :depth], right[:, depth:]) - dot_nt(left[:, depth:], right[:, :depth])
    return real.astype(BF16), imag.astype(BF16)


def fold(values):
    rows, columns = values.shape
    return jnp.sum(values.reshape(rows // 8, 8, columns), axis=0)


def down(values):
    row = lax.broadcasted_iota(jnp.int32, TILE, 0)
    tile = jnp.zeros(TILE, F32)
    for n, value in values:
        tile = jnp.where(row == n, jnp.sum(value, keepdims=True), tile)
    return tile


def direct_sums(diagonal, own):
    real = functools.reduce(jnp.add, [block[0].astype(F32) for block in diagonal])
    imag = functools.reduce(jnp.add, [block[1].astype(F32) for block in diagonal])
    sums = []
    for slot in range(own.shape[0]):
        elem_re, elem_im = own[slot, 0].astype(F32), own[slot, 1].astype(F32)
        sums.append((2 * slot, fold(elem_re * real + elem_im * imag)))
        sums.append((2 * slot + 1, fold(elem_im * real - elem_re * imag)))
    return sums


def early_blocks(spins):
    off = [(s, t) for s in range(spins - 1) for t in range(s + 1, spins - 1)]
    return off + [(s, s) for s in range(spins - 1)]


def early_kernel(eig, keys, rb_count, blocks, *refs):
    pieces, (own, flat, out, traces, sem) = refs[:-5], refs[-5:]
    rows, width = pieces[0].shape[1:]
    depth = rb_count * width
    copies = []
    for n, ((far, side), piece) in enumerate(zip(keys, pieces)):
        where = aligned(place(far, eig // rows) * rows, rows)
        for part in range(2):
            columns = pl.ds(part * depth + side * width, width)
            copies.append(pltpu.make_async_copy(piece.at[part], flat.at[where, columns], sem.at[2 * n + part]))
    for copy in copies:
        copy.start()
    for copy in copies:
        copy.wait()

    def step(n, carry):
        top, side = choose(n, [b[0] for b in blocks]), choose(n, [b[1] for b in blocks])
        out[n, 0], out[n, 1] = gram_block(flat[aligned(top * eig, eig), :], flat[aligned(side * eig, eig), :])
        return carry

    lax.fori_loop(0, len(blocks), step, 0)
    diagonal = [out.at[n] for n, block in enumerate(blocks) if block[0] == block[1]]
    traces[...] = down(direct_sums(diagonal, own))


def early_gram(keys, pieces, own_elems, spins, eig, rb_count):
    blocks = early_blocks(spins)
    depth = 2 * rb_count * pieces[0].shape[2]
    return pl.pallas_call(
        functools.partial(early_kernel, eig, keys, rb_count, blocks),
        out_shape=(
            jax.ShapeDtypeStruct(((spins - 1) * eig, depth), BF16),
            jax.ShapeDtypeStruct((len(blocks), 2, eig, eig), BF16),
            jax.ShapeDtypeStruct(TILE, F32),
        ),
        in_specs=[ANY] * len(pieces) + [VMEM],
        out_specs=(VMEM, VMEM, VMEM),
        scratch_shapes=[pltpu.SemaphoreType.DMA((2 * len(pieces),))],
        compiler_params=params(32),
        cost_estimate=LONG,
        name="early_gram",
    )(*pieces, own_elems)


def late_kernel(eig, keys, rb_count, flat, *refs):
    pieces, (out, last) = refs[:-2], refs[-2:]
    rows, width = pieces[0].shape[1:]
    depth = rb_count * width
    others = flat.shape[0] // eig
    for (far, side), piece in zip(keys, pieces):
        where = aligned((place(far, eig // rows) - others * (eig // rows)) * rows, rows)
        for part in range(2):
            column = part * depth + side * width
            last[where, column : column + width] = piece[part]

    def step(n, carry):
        out[n, 0], out[n, 1] = gram_block(flat[aligned(n * eig, eig), :], last[...])
        return carry

    lax.fori_loop(0, others, step, 0)
    out[others, 0], out[others, 1] = gram_block(last[...], last[...])


def late_gram(keys, flat, pieces, spins, eig, rb_count):
    return pl.pallas_call(
        functools.partial(late_kernel, eig, keys, rb_count),
        out_shape=jax.ShapeDtypeStruct((spins, 2, eig, eig), BF16),
        in_specs=[VMEM] * (1 + len(pieces)),
        out_specs=VMEM,
        scratch_shapes=[pltpu.VMEM((eig, flat.shape[1]), BF16)],
        compiler_params=params(32),
        cost_estimate=LONG,
        name="late_gram",
    )(flat, *pieces)


def factors_kernel(diag_mom, elems, right_ref, left_ref, own_ref, held, sem):
    rank = lax.axis_index("rb")
    eig = held.shape[-1]
    copies = []
    for time in range(2):
        which = diag_mom[0, rank, lax.bitwise_xor(rank, time)]
        copies.append(pltpu.make_async_copy(elems.at[which], held.at[time], sem.at[time]))
    for slot in range(own_ref.shape[0]):
        copies.append(pltpu.make_async_copy(elems.at[diag_mom[0, slot, rank]], own_ref.at[slot], sem.at[2 + slot]))
    for copy in copies:
        copy.start()
    for copy in copies:
        copy.wait()
    for time in range(2):
        re, im = held[time, 0], held[time, 1]
        right_ref[time, :eig, :eig] = re
        right_ref[time, :eig, eig:] = im
        right_ref[time, eig:, :eig] = -im
        right_ref[time, eig:, eig:] = re
        re_t = re.astype(F32).T.astype(BF16)
        im_t = im.astype(F32).T.astype(BF16)
        left_ref[time, :eig, :eig] = re_t
        left_ref[time, :eig, eig:] = im_t
        left_ref[time, eig:, :eig] = im_t
        left_ref[time, eig:, eig:] = -re_t


def factors(diag_mom, src_elems):
    slots, eig = diag_mom.shape[1], src_elems.shape[-1]
    form = jax.ShapeDtypeStruct((2, 2 * eig, 2 * eig), BF16)
    return pl.pallas_call(
        factors_kernel,
        out_shape=(form, form, jax.ShapeDtypeStruct((slots, 2, eig, eig), BF16)),
        in_specs=[SMEM, ANY],
        out_specs=(VMEM, VMEM, VMEM),
        scratch_shapes=[pltpu.VMEM((2, 2, eig, eig), BF16), pltpu.SemaphoreType.DMA((2 + slots,))],
        compiler_params=params(32),
        cost_estimate=LITTLE,
        name="factors",
    )(diag_mom, src_elems)


def cross_kernel(offs, at, own, other, right, left, *refs):
    carried, (out, acc) = refs[:-2], refs[-2:]
    elems, carried = (carried[0], carried[1:]) if carried else (None, [])
    eig = own.shape[-1]
    acc[...] = jnp.zeros_like(acc)

    def add(x, y, from_right, from_left):
        product = dot(jnp.concatenate([x[0], x[1]], axis=1), from_right)
        partner = dot(from_left, y.reshape(2 * eig, eig))
        p_re, p_im = product[:, :eig], product[:, eig:]
        w_re, w_im = partner[:eig], partner[eig:]
        acc[0] += fold(p_re * w_re - p_im * w_im)
        acc[1] += fold(p_re * w_im + p_im * w_re)

    def both(n, carry):
        add(other[n], own[n], right[1], left[0])
        add(own[n], other[n], right[0], left[1])
        return carry

    def once(n, carry):
        add(other[n], own[n], right[1], left[0])
        return carry

    lax.fori_loop(0, offs, both, 0)
    lax.fori_loop(offs, own.shape[0], once, 0)
    sums = [(at, acc[0]), (at + 1, acc[1])]
    if elems is not None:
        sums += direct_sums([own.at[n] for n in range(offs, own.shape[0])], elems)
    tile = down(sums)
    out[...] = functools.reduce(jnp.add, [ref[...] for ref in carried], tile)


def cross_traces(offs, at, own, other, right, left, carried, name):
    eig = own.shape[-1]
    return pl.pallas_call(
        functools.partial(cross_kernel, offs, at),
        out_shape=jax.ShapeDtypeStruct(TILE, F32),
        in_specs=[VMEM] * (4 + len(carried)),
        out_specs=VMEM,
        scratch_shapes=[pltpu.VMEM((2, 8, eig), F32)],
        compiler_params=params(32),
        cost_estimate=LITTLE,
        name=name,
    )(own, other, right, left, *carried)


def final_kernel(slots, mine, theirs, count, out):
    rank = lax.axis_index("rb")
    lane = lax.broadcasted_iota(jnp.int32, (1, LANES), 1)

    def row(ref, n):
        return ref[n : n + 1, :]

    def put(slot, kind, re, im):
        value = jnp.where(lane == 0, re, im) * 0.25
        out[0, slot, kind : kind + 1, :] = jnp.where(slot < count[0], value, 0.0)[:, :2]

    for slot in range(slots):
        m_re, m_im = row(mine, 2 * slot), row(mine, 2 * slot + 1)
        t_re, t_im = row(theirs, 2 * slot), row(theirs, 2 * slot + 1)
        put(slot, 0, m_re * t_re - m_im * t_im, m_re * t_im + m_im * t_re)
        here = rank == slot
        re = jnp.where(here, row(mine, 2 * slots), row(theirs, 2 * slots))
        im = jnp.where(here, row(mine, 2 * slots + 1), row(theirs, 2 * slots + 1))
        put(slot, 1, re, im)


def final(mine, theirs, diag_count, slots):
    return pl.pallas_call(
        functools.partial(final_kernel, slots),
        out_shape=jax.ShapeDtypeStruct((1, slots, 2, 2), F32),
        in_specs=[VMEM, VMEM, SMEM],
        out_specs=VMEM,
        name="final",
    )(mine, theirs, diag_count)


def shards(peram, src_elems, owner_times, diag_mom, diag_count):
    tp_count, rb_count = lax.axis_size("tp"), lax.axis_size("rb")
    eig = src_elems.shape[-1]
    spins = tp_count * peram.shape[0] // eig
    slots = diag_mom.shape[1]

    early_keys, late, own = travel_order(tp_count, rb_count)
    picked = pick(owner_times, peram, own + early_keys + late)

    def send(key):
        far, side = key
        pairs = [
            (tp * rb_count + rb, (tp ^ far) * rb_count + (rb ^ side))
            for tp in range(tp_count)
            for rb in range(rb_count)
        ]
        return lax.ppermute(picked[key], ("tp", "rb"), pairs)

    swap = [(rb, rb ^ 1) for rb in range(rb_count)]
    right, left, own_elems = factors(diag_mom, src_elems)
    arrived = [picked[key] for key in own] + [send(key) for key in early_keys]
    flat, early, direct = early_gram(own + early_keys, arrived, own_elems, spins, eig, rb_count)
    early_other = lax.ppermute(early, "rb", swap)
    offs = early.shape[0] - (spins - 1)
    begun = cross_traces(offs, 2 * slots, early, early_other, right, left, [], "early_cross")

    last = late_gram(late, flat, [send(key) for key in late], spins, eig, rb_count)
    last_other = lax.ppermute(last, "rb", swap)
    carried = [own_elems, direct, begun]
    mine = cross_traces(spins - 1, 2 * slots, last, last_other, right, left, carried, "late_cross")
    theirs = lax.ppermute(mine, "rb", swap)
    return final(mine, theirs, diag_count, slots)


def solution(mesh):
    in_specs = (
        P(("grp", "tp"), None, None, "rb"),
        P("grp", None, None, None),
        P("grp", None),
        P(("grp", "tp"), None, None),
        P(("grp", "tp")),
    )
    out_specs = P(("grp", "tp"), None, None, None)
    return jax.shard_map(shards, mesh=mesh, in_specs=in_specs, out_specs=out_specs, check_vma=False)
```

```python
import functools

import jax
import jax.numpy as jnp
from jax import lax
from jax.experimental import pallas as pl
from jax.experimental.pallas import tpu as pltpu
from jax.sharding import PartitionSpec as P

F32 = jnp.float32
BF16 = jnp.bfloat16
ANY = pl.BlockSpec(memory_space=pl.ANY)
SMEM = pl.BlockSpec(memory_space=pltpu.SMEM)
VMEM = pl.BlockSpec(memory_space=pltpu.VMEM)
TILE = (8, 128)
LANES = 128
STEP = 16
MIB = 1 << 20
LITTLE = pl.CostEstimate(flops=1000, bytes_accessed=1000, transcendentals=0)
LONG = pl.CostEstimate(flops=5 * 10**10, bytes_accessed=1000, transcendentals=0)


def in_hbm(array):
    return pltpu.with_memory_space_constraint(array, pltpu.HBM)


def params(mib):
    return pltpu.CompilerParams(vmem_limit_bytes=mib * MIB)


def dot(left, right):
    return jnp.dot(left, right, preferred_element_type=F32)


def dot_nt(left, right):
    return lax.dot_general(left, right, (((1,), (1,)), ((), ())), preferred_element_type=F32)


def choose(index, values):
    out = jnp.int32(values[0])
    for n in range(1, len(values)):
        out = jnp.where(index == n, jnp.int32(values[n]), out)
    return out


def aligned(start, size):
    return pl.ds(pl.multiple_of(start, size), size)


def travel_order(tp_count, rb_count):
    half, quarter = tp_count // 2, tp_count // 4

    def both(distances):
        return [(far, side) for far in distances for side in range(rb_count)]

    long, late = both(range(half, half + quarter)), both(range(half + quarter, tp_count))
    near, rest = both(reversed(range(quarter, half))), both(range(1, quarter))
    cut, part = 3 * len(long) // 4, len(near) // 2
    early = long[:cut] + near[:part] + long[cut:] + near[part:] + rest
    early += [(0, side) for side in range(1, rb_count)]
    return early, late, [(0, 0)]


def pick_kernel(keys, times, table, *refs):
    outs, (held, wide, taken_times, sem, times_sem) = refs[:-5], refs[-5:]
    tp_rank, rb_rank = lax.axis_index("tp"), lax.axis_index("rb")
    rows, _, packed, _ = table.shape

    def fetch(chunk):
        where = aligned(chunk * STEP, STEP)
        return pltpu.make_async_copy(table.at[where], held.at[where], sem.at[chunk])

    copy = pltpu.make_async_copy(times, taken_times, times_sem)
    copy.start()
    for chunk in range(rows // STEP):
        fetch(chunk).start()
    copy.wait()

    def step(chunk, carry):
        fetch(chunk).wait()
        where = aligned(chunk * STEP, STEP)
        for n, (far, side) in enumerate(keys):
            time = taken_times[lax.bitwise_xor(rb_rank, side), lax.bitwise_xor(tp_rank, far)]
            slot = n % wide.shape[0]
            wide[slot] = held[where, time].astype(F32).reshape(STEP * packed, LANES)
            for tile in range(packed // 2):
                for part in range(2):
                    taken = wide[slot, pl.ds(2 * tile + part, STEP, stride=packed), :]
                    outs[n][part, where, tile * LANES : (tile + 1) * LANES] = taken.astype(BF16)
        return carry

    lax.fori_loop(0, rows // STEP, step, 0)


def pick(owner_times, peram, keys):
    rows, times, parts, width = peram.shape
    tiles = width // LANES
    table = peram.reshape(rows, times, parts, tiles, LANES).swapaxes(2, 3)
    table = table.reshape(rows, times, tiles * parts, LANES)
    picked = pl.pallas_call(
        functools.partial(pick_kernel, keys),
        out_shape=[jax.ShapeDtypeStruct((parts, rows, width), BF16)] * len(keys),
        in_specs=[ANY, ANY],
        out_specs=[VMEM] * len(keys),
        scratch_shapes=[
            pltpu.VMEM(table.shape, BF16),
            pltpu.VMEM((4, STEP * tiles * parts, LANES), F32),
            pltpu.SMEM(owner_times.shape[::-1], jnp.int32),
            pltpu.SemaphoreType.DMA((rows // STEP,)),
            pltpu.SemaphoreType.DMA,
        ],
        compiler_params=params(32),
        cost_estimate=LITTLE,
        name="pick",
    )(in_hbm(owner_times.T), in_hbm(table))
    return dict(zip(keys, picked))


def place(far, per_spin):
    low = lax.axis_index("tp") % per_spin
    return (far // per_spin) * per_spin + lax.bitwise_xor(jnp.int32(far % per_spin), low)


def gram_block(left, right):
    depth = left.shape[1] // 2
    real = dot_nt(left, right)
    imag = dot_nt(left[:, :depth], right[:, depth:]) - dot_nt(left[:, depth:], right[:, :depth])
    return real.astype(BF16), imag.astype(BF16)


def fold(values):
    rows, columns = values.shape
    return jnp.sum(values.reshape(rows // 8, 8, columns), axis=0)


def down(values):
    row = lax.broadcasted_iota(jnp.int32, TILE, 0)
    tile = jnp.zeros(TILE, F32)
    for n, value in values:
        tile = jnp.where(row == n, jnp.sum(value, keepdims=True), tile)
    return tile


def direct_sums(diagonal, own):
    real = functools.reduce(jnp.add, [block[0].astype(F32) for block in diagonal])
    imag = functools.reduce(jnp.add, [block[1].astype(F32) for block in diagonal])
    sums = []
    for slot in range(own.shape[0]):
        elem_re, elem_im = own[slot, 0].astype(F32), own[slot, 1].astype(F32)
        sums.append((2 * slot, fold(elem_re * real + elem_im * imag)))
        sums.append((2 * slot + 1, fold(elem_im * real - elem_re * imag)))
    return sums


def early_blocks(spins):
    off = [(s, t) for s in range(spins - 1) for t in range(s + 1, spins - 1)]
    return off + [(s, s) for s in range(spins - 1)]


def early_kernel(eig, keys, rb_count, blocks, *refs):
    pieces, (own, flat, out, traces, sem) = refs[:-5], refs[-5:]
    rows, width = pieces[0].shape[1:]
    depth = rb_count * width
    copies = []
    for n, ((far, side), piece) in enumerate(zip(keys, pieces)):
        where = aligned(place(far, eig // rows) * rows, rows)
        for part in range(2):
            columns = pl.ds(part * depth + side * width, width)
            copies.append(pltpu.make_async_copy(piece.at[part], flat.at[where, columns], sem.at[2 * n + part]))
    for copy in copies:
        copy.start()
    for copy in copies:
        copy.wait()

    def step(n, carry):
        top, side = choose(n, [b[0] for b in blocks]), choose(n, [b[1] for b in blocks])
        out[n, 0], out[n, 1] = gram_block(flat[aligned(top * eig, eig), :], flat[aligned(side * eig, eig), :])
        return carry

    lax.fori_loop(0, len(blocks), step, 0)
    diagonal = [out.at[n] for n, block in enumerate(blocks) if block[0] == block[1]]
    traces[...] = down(direct_sums(diagonal, own))


def early_gram(keys, pieces, own_elems, spins, eig, rb_count):
    blocks = early_blocks(spins)
    depth = 2 * rb_count * pieces[0].shape[2]
    return pl.pallas_call(
        functools.partial(early_kernel, eig, keys, rb_count, blocks),
        out_shape=(
            jax.ShapeDtypeStruct(((spins - 1) * eig, depth), BF16),
            jax.ShapeDtypeStruct((len(blocks), 2, eig, eig), BF16),
            jax.ShapeDtypeStruct(TILE, F32),
        ),
        in_specs=[ANY] * len(pieces) + [VMEM],
        out_specs=(VMEM, VMEM, VMEM),
        scratch_shapes=[pltpu.SemaphoreType.DMA((2 * len(pieces),))],
        compiler_params=params(32),
        cost_estimate=LONG,
        name="early_gram",
    )(*pieces, own_elems)


def late_kernel(eig, keys, rb_count, flat, begun, *refs):
    pieces, (out, last) = refs[:-2], refs[-2:]
    rows, width = pieces[0].shape[1:]
    depth = rb_count * width
    others = flat.shape[0] // eig
    for (far, side), piece in zip(keys, pieces):
        where = aligned((place(far, eig // rows) - others * (eig // rows)) * rows, rows)
        for part in range(2):
            column = part * depth + side * width
            last[where, column : column + width] = piece[part]

    def step(n, carry):
        out[n, 0], out[n, 1] = gram_block(flat[aligned(n * eig, eig), :], last[...])
        return carry

    lax.fori_loop(0, others, step, 0, unroll=True)
    out[others, 0], out[others, 1] = gram_block(last[...], last[...])


def late_gram(keys, flat, begun, pieces, spins, eig, rb_count):
    return pl.pallas_call(
        functools.partial(late_kernel, eig, keys, rb_count),
        out_shape=jax.ShapeDtypeStruct((spins, 2, eig, eig), BF16),
        in_specs=[VMEM, ANY] + [VMEM] * len(pieces),
        out_specs=VMEM,
        scratch_shapes=[pltpu.VMEM((eig, flat.shape[1]), BF16)],
        compiler_params=params(32),
        cost_estimate=LONG,
        name="late_gram",
    )(flat, begun, *pieces)


def factors_kernel(diag_mom, elems, right_ref, left_ref, own_ref, held, sem):
    rank = lax.axis_index("rb")
    eig = held.shape[-1]
    copies = []
    for time in range(2):
        which = diag_mom[0, rank, lax.bitwise_xor(rank, time)]
        copies.append(pltpu.make_async_copy(elems.at[which], held.at[time], sem.at[time]))
    for slot in range(own_ref.shape[0]):
        copies.append(pltpu.make_async_copy(elems.at[diag_mom[0, slot, rank]], own_ref.at[slot], sem.at[2 + slot]))
    for copy in copies:
        copy.start()
    for copy in copies:
        copy.wait()
    for time in range(2):
        re, im = held[time, 0], held[time, 1]
        right_ref[time, :eig, :eig] = re
        right_ref[time, :eig, eig:] = im
        right_ref[time, eig:, :eig] = -im
        right_ref[time, eig:, eig:] = re
        re_t = re.astype(F32).T.astype(BF16)
        im_t = im.astype(F32).T.astype(BF16)
        left_ref[time, :eig, :eig] = re_t
        left_ref[time, :eig, eig:] = im_t
        left_ref[time, eig:, :eig] = im_t
        left_ref[time, eig:, eig:] = -re_t


def factors(diag_mom, src_elems):
    slots, eig = diag_mom.shape[1], src_elems.shape[-1]
    form = jax.ShapeDtypeStruct((2, 2 * eig, 2 * eig), BF16)
    return pl.pallas_call(
        factors_kernel,
        out_shape=(form, form, jax.ShapeDtypeStruct((slots, 2, eig, eig), BF16)),
        in_specs=[SMEM, ANY],
        out_specs=(VMEM, VMEM, VMEM),
        scratch_shapes=[pltpu.VMEM((2, 2, eig, eig), BF16), pltpu.SemaphoreType.DMA((2 + slots,))],
        compiler_params=params(32),
        cost_estimate=LITTLE,
        name="factors",
    )(diag_mom, src_elems)


def cross_kernel(offs, at, own, other, right, left, *refs):
    carried, (out, acc) = refs[:-2], refs[-2:]
    elems, carried = (carried[0], carried[1:]) if carried else (None, [])
    eig = own.shape[-1]
    if len(other.shape) > len(own.shape):
        other = other.at[1 - lax.axis_index("rb")]
    acc[...] = jnp.zeros_like(acc)

    def add(x, y, from_right, from_left):
        product = dot(jnp.concatenate([x[0], x[1]], axis=1), from_right)
        partner = dot(from_left, y.reshape(2 * eig, eig))
        p_re, p_im = product[:, :eig], product[:, eig:]
        w_re, w_im = partner[:eig], partner[eig:]
        acc[0] += fold(p_re * w_re - p_im * w_im)
        acc[1] += fold(p_re * w_im + p_im * w_re)

    def both(n, carry):
        add(other[n], own[n], right[1], left[0])
        add(own[n], other[n], right[0], left[1])
        return carry

    def once(n, carry):
        add(other[n], own[n], right[1], left[0])
        return carry

    lax.fori_loop(0, offs, both, 0, unroll=True)
    lax.fori_loop(offs, own.shape[0], once, 0, unroll=True)
    sums = [(at, acc[0]), (at + 1, acc[1])]
    if elems is not None:
        sums += direct_sums([own.at[n] for n in range(offs, own.shape[0])], elems)
    tile = down(sums)
    out[...] = functools.reduce(jnp.add, [ref[...] for ref in carried], tile)


def cross_traces(offs, at, own, other, right, left, carried, name):
    eig = own.shape[-1]
    return pl.pallas_call(
        functools.partial(cross_kernel, offs, at),
        out_shape=jax.ShapeDtypeStruct(TILE, F32),
        in_specs=[VMEM] * (4 + len(carried)),
        out_specs=VMEM,
        scratch_shapes=[pltpu.VMEM((2, 8, eig), F32)],
        compiler_params=params(32),
        cost_estimate=LITTLE,
        name=name,
    )(own, other, right, left, *carried)


def final_kernel(slots, mine, theirs, count, out):
    rank = lax.axis_index("rb")
    lane = lax.broadcasted_iota(jnp.int32, (1, LANES), 1)

    def row(ref, n):
        return ref[n : n + 1, :]

    def put(slot, kind, re, im):
        value = jnp.where(lane == 0, re, im) * 0.25
        out[0, slot, kind : kind + 1, :] = jnp.where(slot < count[0], value, 0.0)[:, :2]

    for slot in range(slots):
        m_re, m_im = row(mine, 2 * slot), row(mine, 2 * slot + 1)
        t_re, t_im = row(theirs, 2 * slot), row(theirs, 2 * slot + 1)
        put(slot, 0, m_re * t_re - m_im * t_im, m_re * t_im + m_im * t_re)
        here = rank == slot
        re = jnp.where(here, row(mine, 2 * slots), row(theirs, 2 * slots))
        im = jnp.where(here, row(mine, 2 * slots + 1), row(theirs, 2 * slots + 1))
        put(slot, 1, re, im)


def final(mine, theirs, diag_count, slots):
    return pl.pallas_call(
        functools.partial(final_kernel, slots),
        out_shape=jax.ShapeDtypeStruct((1, slots, 2, 2), F32),
        in_specs=[VMEM, VMEM, SMEM],
        out_specs=VMEM,
        compiler_params=params(32),
        name="final",
    )(mine, theirs, diag_count)


def shards(peram, src_elems, owner_times, diag_mom, diag_count):
    tp_count, rb_count = lax.axis_size("tp"), lax.axis_size("rb")
    eig = src_elems.shape[-1]
    spins = tp_count * peram.shape[0] // eig
    slots = diag_mom.shape[1]

    early_keys, late, own = travel_order(tp_count, rb_count)
    picked = pick(owner_times, peram, early_keys + late + own)

    def send(key):
        far, side = key
        pairs = [
            (tp * rb_count + rb, (tp ^ far) * rb_count + (rb ^ side))
            for tp in range(tp_count)
            for rb in range(rb_count)
        ]
        return lax.ppermute(picked[key], ("tp", "rb"), pairs)

    swap = [(rb, rb ^ 1) for rb in range(rb_count)]
    right, left, own_elems = factors(diag_mom, src_elems)
    arrived = [send(key) for key in early_keys] + [picked[key] for key in own]
    flat, early, direct = early_gram(early_keys + own, arrived, own_elems, spins, eig, rb_count)
    early_both = lax.all_to_all(jnp.stack([early] * rb_count), "rb", 0, 0)
    offs = early.shape[0] - (spins - 1)
    begun = cross_traces(offs, 2 * slots, early, early_both, right, left, [], "early_cross")

    last = late_gram(late, flat, begun, [send(key) for key in late], spins, eig, rb_count)
    last_other = lax.ppermute(last, "rb", swap)
    carried = [own_elems, direct, begun]
    mine = cross_traces(spins - 1, 2 * slots, last, last_other, right, left, carried, "late_cross")
    theirs = lax.ppermute(mine, "rb", swap)
    return final(mine, theirs, diag_count, slots)


def solution(mesh):
    in_specs = (
        P(("grp", "tp"), None, None, "rb"),
        P("grp", None, None, None),
        P("grp", None),
        P(("grp", "tp"), None, None),
        P(("grp", "tp")),
    )
    out_specs = P(("grp", "tp"), None, None, None)
    return jax.shard_map(shards, mesh=mesh, in_specs=in_specs, out_specs=out_specs, check_vma=False)
```

```python
import functools

import jax
import jax.numpy as jnp
from jax import lax
from jax.experimental import pallas as pl
from jax.experimental.pallas import tpu as pltpu
from jax.sharding import PartitionSpec as P

F32 = jnp.float32
BF16 = jnp.bfloat16
ANY = pl.BlockSpec(memory_space=pl.ANY)
SMEM = pl.BlockSpec(memory_space=pltpu.SMEM)
VMEM = pl.BlockSpec(memory_space=pltpu.VMEM)
TILE = (8, 128)
LANES = 128
STEP = 16
MIB = 1 << 20
LITTLE = pl.CostEstimate(flops=1000, bytes_accessed=1000, transcendentals=0)
LONG = pl.CostEstimate(flops=5 * 10**10, bytes_accessed=1000, transcendentals=0)


def in_hbm(array):
    return pltpu.with_memory_space_constraint(array, pltpu.HBM)


def params(mib):
    return pltpu.CompilerParams(vmem_limit_bytes=mib * MIB)


def dot(left, right):
    return jnp.dot(left, right, preferred_element_type=F32)


def dot_nt(left, right):
    return lax.dot_general(left, right, (((1,), (1,)), ((), ())), preferred_element_type=F32)


def choose(index, values):
    out = jnp.int32(values[0])
    for n in range(1, len(values)):
        out = jnp.where(index == n, jnp.int32(values[n]), out)
    return out


def aligned(start, size):
    return pl.ds(pl.multiple_of(start, size), size)


def travel_order(tp_count, rb_count):
    half, quarter = tp_count // 2, tp_count // 4

    def both(distances):
        return [(far, side) for far in distances for side in range(rb_count)]

    long, late = both(range(half, half + quarter)), both(range(half + quarter, tp_count))
    near, rest = both(reversed(range(quarter, half))), both(range(1, quarter))
    cut, part = 3 * len(long) // 4, len(near) // 2
    early = long[:cut] + near[:part] + long[cut:] + near[part:] + rest
    early += [(0, side) for side in range(1, rb_count)]
    return early, late, [(0, 0)]


def pick_kernel(keys, times, table, *refs):
    outs, (held, wide, taken_times, sem, times_sem) = refs[:-5], refs[-5:]
    tp_rank, rb_rank = lax.axis_index("tp"), lax.axis_index("rb")
    rows, _, packed, _ = table.shape

    def fetch(chunk):
        where = aligned(chunk * STEP, STEP)
        return pltpu.make_async_copy(table.at[where], held.at[where], sem.at[chunk])

    copy = pltpu.make_async_copy(times, taken_times, times_sem)
    copy.start()
    for chunk in range(rows // STEP):
        fetch(chunk).start()
    copy.wait()

    def step(chunk, carry):
        fetch(chunk).wait()
        where = aligned(chunk * STEP, STEP)
        for n, (far, side) in enumerate(keys):
            time = taken_times[lax.bitwise_xor(rb_rank, side), lax.bitwise_xor(tp_rank, far)]
            slot = n % wide.shape[0]
            wide[slot] = held[where, time].astype(F32).reshape(STEP * packed, LANES)
            for tile in range(packed // 2):
                for part in range(2):
                    taken = wide[slot, pl.ds(2 * tile + part, STEP, stride=packed), :]
                    outs[n][part, where, tile * LANES : (tile + 1) * LANES] = taken.astype(BF16)
        return carry

    lax.fori_loop(0, rows // STEP, step, 0)


def pick(owner_times, peram, keys, name, spare):
    rows, times, parts, width = peram.shape
    tiles = width // LANES
    table = peram.reshape(rows, times, parts, tiles, LANES).swapaxes(2, 3)
    table = table.reshape(rows, times, tiles * parts, LANES)
    picked = pl.pallas_call(
        functools.partial(pick_kernel, keys),
        out_shape=[jax.ShapeDtypeStruct((parts, rows, width), BF16)] * len(keys) + spare,
        in_specs=[ANY, ANY],
        out_specs=[VMEM] * len(keys) + [ANY] * len(spare),
        scratch_shapes=[
            pltpu.VMEM(table.shape, BF16),
            pltpu.VMEM((4, STEP * tiles * parts, LANES), F32),
            pltpu.SMEM(owner_times.shape[::-1], jnp.int32),
            pltpu.SemaphoreType.DMA((rows // STEP,)),
            pltpu.SemaphoreType.DMA,
        ],
        compiler_params=params(32),
        cost_estimate=LITTLE,
        name=name,
    )(in_hbm(owner_times.T), in_hbm(table))
    return dict(zip(keys, picked))


def place(far, per_spin):
    low = lax.axis_index("tp") % per_spin
    return (far // per_spin) * per_spin + lax.bitwise_xor(jnp.int32(far % per_spin), low)


def gram_block(left, right):
    depth = left.shape[1] // 2
    real = dot_nt(left, right)
    imag = dot_nt(left[:, :depth], right[:, depth:]) - dot_nt(left[:, depth:], right[:, :depth])
    return real.astype(BF16), imag.astype(BF16)


def fold(values):
    rows, columns = values.shape
    return jnp.sum(values.reshape(rows // 8, 8, columns), axis=0)


def down(values):
    row = lax.broadcasted_iota(jnp.int32, TILE, 0)
    tile = jnp.zeros(TILE, F32)
    for n, value in values:
        tile = jnp.where(row == n, jnp.sum(value, keepdims=True), tile)
    return tile


def direct_sums(diagonal, own):
    real = functools.reduce(jnp.add, [block[0].astype(F32) for block in diagonal])
    imag = functools.reduce(jnp.add, [block[1].astype(F32) for block in diagonal])
    sums = []
    for slot in range(own.shape[0]):
        elem_re, elem_im = own[slot, 0].astype(F32), own[slot, 1].astype(F32)
        sums.append((2 * slot, fold(elem_re * real + elem_im * imag)))
        sums.append((2 * slot + 1, fold(elem_im * real - elem_re * imag)))
    return sums


def early_blocks(spins):
    off = [(s, t) for s in range(spins - 1) for t in range(s + 1, spins - 1)]
    return off + [(s, s) for s in range(spins - 1)]


def early_kernel(eig, keys, rb_count, blocks, *refs):
    pieces, (own, flat, out, traces, sem) = refs[:-5], refs[-5:]
    rows, width = pieces[0].shape[1:]
    depth = rb_count * width
    copies = []
    for n, ((far, side), piece) in enumerate(zip(keys, pieces)):
        where = aligned(place(far, eig // rows) * rows, rows)
        for part in range(2):
            columns = pl.ds(part * depth + side * width, width)
            copies.append(pltpu.make_async_copy(piece.at[part], flat.at[where, columns], sem.at[2 * n + part]))
    for copy in copies:
        copy.start()
    for copy in copies:
        copy.wait()

    def step(n, carry):
        top, side = choose(n, [b[0] for b in blocks]), choose(n, [b[1] for b in blocks])
        out[n, 0], out[n, 1] = gram_block(flat[aligned(top * eig, eig), :], flat[aligned(side * eig, eig), :])
        return carry

    lax.fori_loop(0, len(blocks), step, 0)
    diagonal = [out.at[n] for n, block in enumerate(blocks) if block[0] == block[1]]
    traces[...] = down(direct_sums(diagonal, own))


def early_gram(keys, pieces, own_elems, spins, eig, rb_count):
    blocks = early_blocks(spins)
    depth = 2 * rb_count * pieces[0].shape[2]
    return pl.pallas_call(
        functools.partial(early_kernel, eig, keys, rb_count, blocks),
        out_shape=(
            jax.ShapeDtypeStruct(((spins - 1) * eig, depth), BF16),
            jax.ShapeDtypeStruct((len(blocks), 2, eig, eig), BF16),
            jax.ShapeDtypeStruct(TILE, F32),
        ),
        in_specs=[ANY] * len(pieces) + [VMEM],
        out_specs=(VMEM, VMEM, VMEM),
        scratch_shapes=[pltpu.SemaphoreType.DMA((2 * len(pieces),))],
        compiler_params=params(32),
        cost_estimate=LONG,
        name="early_gram",
    )(*pieces, own_elems)


def late_rows_kernel(eig, keys, rb_count, flat, begun, *refs):
    pieces, (out, last) = refs[:-2], refs[-2:]
    rows, width = pieces[0].shape[1:]
    depth = rb_count * width
    others = flat.shape[0] // eig
    for (far, side), piece in zip(keys, pieces):
        where = aligned((place(far, eig // rows) - others * (eig // rows)) * rows, rows)
        for part in range(2):
            column = part * depth + side * width
            last[where, column : column + width] = piece[part]
    for n in range(out.shape[0]):
        out[n, 0], out[n, 1] = gram_block(flat[n * eig : (n + 1) * eig, :], last[...])


def late_rest_kernel(eig, flat, last, out):
    count = out.shape[0] - 1
    first = flat.shape[0] // eig - count
    for n in range(count):
        out[n, 0], out[n, 1] = gram_block(flat[(first + n) * eig : (first + n + 1) * eig, :], last[...])
    out[count, 0], out[count, 1] = gram_block(last[...], last[...])


def late_rows(keys, flat, begun, pieces, spins, eig, rb_count):
    return pl.pallas_call(
        functools.partial(late_rows_kernel, eig, keys, rb_count),
        out_shape=(
            jax.ShapeDtypeStruct((spins // 2, 2, eig, eig), BF16),
            jax.ShapeDtypeStruct((eig, flat.shape[1]), BF16),
        ),
        in_specs=[VMEM, ANY] + [VMEM] * len(pieces),
        out_specs=(VMEM, VMEM),
        compiler_params=params(32),
        cost_estimate=LONG,
        name="late_rows",
    )(flat, begun, *pieces)


def late_rest(flat, last, spins, eig):
    return pl.pallas_call(
        functools.partial(late_rest_kernel, eig),
        out_shape=jax.ShapeDtypeStruct((spins - spins // 2, 2, eig, eig), BF16),
        in_specs=[VMEM, VMEM],
        out_specs=VMEM,
        compiler_params=params(32),
        cost_estimate=LITTLE,
        name="late_rest",
    )(flat, last)


def factors_kernel(diag_mom, elems, right_ref, left_ref, own_ref, held, sem):
    rank = lax.axis_index("rb")
    eig = held.shape[-1]
    copies = []
    for time in range(2):
        which = diag_mom[0, rank, lax.bitwise_xor(rank, time)]
        copies.append(pltpu.make_async_copy(elems.at[which], held.at[time], sem.at[time]))
    for slot in range(own_ref.shape[0]):
        copies.append(pltpu.make_async_copy(elems.at[diag_mom[0, slot, rank]], own_ref.at[slot], sem.at[2 + slot]))
    for copy in copies:
        copy.start()
    for copy in copies:
        copy.wait()
    for time in range(2):
        re, im = held[time, 0], held[time, 1]
        right_ref[time, :eig, :eig] = re
        right_ref[time, :eig, eig:] = im
        right_ref[time, eig:, :eig] = -im
        right_ref[time, eig:, eig:] = re
        re_t = re.astype(F32).T.astype(BF16)
        im_t = im.astype(F32).T.astype(BF16)
        left_ref[time, :eig, :eig] = re_t
        left_ref[time, :eig, eig:] = im_t
        left_ref[time, eig:, :eig] = im_t
        left_ref[time, eig:, eig:] = -re_t


def factors(diag_mom, src_elems):
    slots, eig = diag_mom.shape[1], src_elems.shape[-1]
    form = jax.ShapeDtypeStruct((2, 2 * eig, 2 * eig), BF16)
    return pl.pallas_call(
        factors_kernel,
        out_shape=(form, form, jax.ShapeDtypeStruct((slots, 2, eig, eig), BF16)),
        in_specs=[SMEM, ANY],
        out_specs=(VMEM, VMEM, VMEM),
        scratch_shapes=[pltpu.VMEM((2, 2, eig, eig), BF16), pltpu.SemaphoreType.DMA((2 + slots,))],
        compiler_params=params(32),
        cost_estimate=LITTLE,
        name="factors",
    )(diag_mom, src_elems)


def cross_kernel(offs, at, own, other, right, left, *refs):
    carried, (out, acc) = refs[:-2], refs[-2:]
    elems, carried = (carried[0], carried[1:]) if carried else (None, [])
    eig = own.shape[-1]
    if len(other.shape) > len(own.shape):
        other = other.at[1 - lax.axis_index("rb")]
    acc[...] = jnp.zeros_like(acc)

    def add(x, y, from_right, from_left):
        product = dot(jnp.concatenate([x[0], x[1]], axis=1), from_right)
        partner = dot(from_left, y.reshape(2 * eig, eig))
        p_re, p_im = product[:, :eig], product[:, eig:]
        w_re, w_im = partner[:eig], partner[eig:]
        acc[0] += fold(p_re * w_re - p_im * w_im)
        acc[1] += fold(p_re * w_im + p_im * w_re)

    def both(n, carry):
        add(other[n], own[n], right[1], left[0])
        add(own[n], other[n], right[0], left[1])
        return carry

    def once(n, carry):
        add(other[n], own[n], right[1], left[0])
        return carry

    lax.fori_loop(0, offs, both, 0, unroll=True)
    lax.fori_loop(offs, own.shape[0], once, 0, unroll=True)
    sums = [(at, acc[0]), (at + 1, acc[1])]
    if elems is not None and offs < own.shape[0]:
        sums += direct_sums([own.at[n] for n in range(offs, own.shape[0])], elems)
    tile = down(sums)
    out[...] = functools.reduce(jnp.add, [ref[...] for ref in carried], tile)


def cross_traces(offs, at, own, other, right, left, carried, name):
    eig = own.shape[-1]
    return pl.pallas_call(
        functools.partial(cross_kernel, offs, at),
        out_shape=jax.ShapeDtypeStruct(TILE, F32),
        in_specs=[VMEM] * (4 + len(carried)),
        out_specs=VMEM,
        scratch_shapes=[pltpu.VMEM((2, 8, eig), F32)],
        compiler_params=params(32),
        cost_estimate=LITTLE,
        name=name,
    )(own, other, right, left, *carried)


def final_kernel(slots, mine, theirs, count, out):
    rank = lax.axis_index("rb")
    lane = lax.broadcasted_iota(jnp.int32, (1, LANES), 1)

    def row(ref, n):
        return ref[n : n + 1, :]

    def put(slot, kind, re, im):
        value = jnp.where(lane == 0, re, im) * 0.25
        out[0, slot, kind : kind + 1, :] = jnp.where(slot < count[0], value, 0.0)[:, :2]

    for slot in range(slots):
        m_re, m_im = row(mine, 2 * slot), row(mine, 2 * slot + 1)
        t_re, t_im = row(theirs, 2 * slot), row(theirs, 2 * slot + 1)
        put(slot, 0, m_re * t_re - m_im * t_im, m_re * t_im + m_im * t_re)
        here = rank == slot
        re = jnp.where(here, row(mine, 2 * slots), row(theirs, 2 * slots))
        im = jnp.where(here, row(mine, 2 * slots + 1), row(theirs, 2 * slots + 1))
        put(slot, 1, re, im)


def final(mine, theirs, diag_count, slots):
    return pl.pallas_call(
        functools.partial(final_kernel, slots),
        out_shape=jax.ShapeDtypeStruct((1, slots, 2, 2), F32),
        in_specs=[VMEM, VMEM, SMEM],
        out_specs=VMEM,
        compiler_params=params(32),
        name="final",
    )(mine, theirs, diag_count)


def shards(peram, src_elems, owner_times, diag_mom, diag_count):
    tp_count, rb_count = lax.axis_size("tp"), lax.axis_size("rb")
    eig = src_elems.shape[-1]
    spins = tp_count * peram.shape[0] // eig
    slots = diag_mom.shape[1]

    early_keys, late, own = travel_order(tp_count, rb_count)
    head = early_keys[: 3 * tp_count * rb_count // 16]
    tail = [key for key in early_keys if key not in head]
    picked = pick(owner_times, peram, head, "pick_head", [jax.ShapeDtypeStruct((4, *peram.shape), BF16)])
    picked.update(pick(owner_times, peram, tail + late + own, "pick_tail", []))

    def send(key):
        far, side = key
        pairs = [
            (tp * rb_count + rb, (tp ^ far) * rb_count + (rb ^ side))
            for tp in range(tp_count)
            for rb in range(rb_count)
        ]
        return lax.ppermute(picked[key], ("tp", "rb"), pairs)

    swap = [(rb, rb ^ 1) for rb in range(rb_count)]
    right, left, own_elems = factors(diag_mom, src_elems)
    arrived = [send(key) for key in early_keys] + [picked[key] for key in own]
    flat, early, direct = early_gram(early_keys + own, arrived, own_elems, spins, eig, rb_count)
    early_both = lax.all_to_all(jnp.stack([early] * rb_count), "rb", 0, 0)
    offs = early.shape[0] - (spins - 1)
    begun = cross_traces(offs, 2 * slots, early, early_both, right, left, [], "early_cross")

    blocks, last = late_rows(late, flat, begun, [send(key) for key in late], spins, eig, rb_count)
    swapped = lax.ppermute(blocks, "rb", swap)
    rest = late_rest(flat, last, spins, eig)
    rest_swapped = lax.ppermute(rest, "rb", swap)
    count = blocks.shape[0]
    partial = cross_traces(count, 2 * slots, blocks, swapped, right, left, [own_elems, direct, begun], "late_cross")
    count = rest.shape[0] - 1
    mine = cross_traces(count, 2 * slots, rest, rest_swapped, right, left, [own_elems, partial], "last_cross")
    theirs = lax.ppermute(mine, "rb", swap)
    return final(mine, theirs, diag_count, slots)


def solution(mesh):
    in_specs = (
        P(("grp", "tp"), None, None, "rb"),
        P("grp", None, None, None),
        P("grp", None),
        P(("grp", "tp"), None, None),
        P(("grp", "tp")),
    )
    out_specs = P(("grp", "tp"), None, None, None)
    return jax.shard_map(shards, mesh=mesh, in_specs=in_specs, out_specs=out_specs, check_vma=False)
```

```python
import functools

import jax
import jax.numpy as jnp
from jax import lax
from jax.experimental import pallas as pl
from jax.experimental.pallas import tpu as pltpu
from jax.sharding import PartitionSpec as P

F32 = jnp.float32
BF16 = jnp.bfloat16
ANY = pl.BlockSpec(memory_space=pl.ANY)
SMEM = pl.BlockSpec(memory_space=pltpu.SMEM)
VMEM = pl.BlockSpec(memory_space=pltpu.VMEM)
TILE = (8, 128)
LANES = 128
STEP = 16
MIB = 1 << 20
LITTLE = pl.CostEstimate(flops=1000, bytes_accessed=1000, transcendentals=0)
LONG = pl.CostEstimate(flops=5 * 10**10, bytes_accessed=1000, transcendentals=0)


def in_hbm(array):
    return pltpu.with_memory_space_constraint(array, pltpu.HBM)


def params(mib):
    return pltpu.CompilerParams(vmem_limit_bytes=mib * MIB)


def dot(left, right):
    return jnp.dot(left, right, preferred_element_type=F32)


def dot_nt(left, right):
    return lax.dot_general(left, right, (((1,), (1,)), ((), ())), preferred_element_type=F32)


def choose(index, values):
    out = jnp.int32(values[0])
    for n in range(1, len(values)):
        out = jnp.where(index == n, jnp.int32(values[n]), out)
    return out


def aligned(start, size):
    return pl.ds(pl.multiple_of(start, size), size)


def travel_order(tp_count, rb_count):
    half, quarter = tp_count // 2, tp_count // 4

    def both(distances):
        return [(far, side) for far in distances for side in range(rb_count)]

    long, late = both(range(half, half + quarter)), both(range(half + quarter, tp_count))
    near, rest = both(reversed(range(quarter, half))), both(range(1, quarter))
    own, other = (0, 0), [(0, side) for side in range(1, rb_count)]
    step, part = len(long) // 4, len(rest) // 2
    head = long[: 2 * step] + near[: 2 * step] + long[2 * step : 3 * step]
    tail = rest[:part] + other + near[2 * step : 3 * step] + long[3 * step :] + near[3 * step :] + rest[part:]
    return head, tail, late, [own]


def pick_kernel(keys, times, table, *refs):
    outs, (held, wide, taken_times, sem, times_sem) = refs[:-5], refs[-5:]
    tp_rank, rb_rank = lax.axis_index("tp"), lax.axis_index("rb")
    rows, _, packed, _ = table.shape

    def fetch(chunk):
        where = aligned(chunk * STEP, STEP)
        return pltpu.make_async_copy(table.at[where], held.at[where], sem.at[chunk])

    copy = pltpu.make_async_copy(times, taken_times, times_sem)
    copy.start()
    for chunk in range(rows // STEP):
        fetch(chunk).start()
    copy.wait()

    def step(chunk, carry):
        fetch(chunk).wait()
        where = aligned(chunk * STEP, STEP)
        for n, (far, side) in enumerate(keys):
            time = taken_times[lax.bitwise_xor(rb_rank, side), lax.bitwise_xor(tp_rank, far)]
            slot = n % wide.shape[0]
            wide[slot] = held[where, time].astype(F32).reshape(STEP * packed, LANES)
            for tile in range(packed // 2):
                for part in range(2):
                    taken = wide[slot, pl.ds(2 * tile + part, STEP, stride=packed), :]
                    outs[n][part, where, tile * LANES : (tile + 1) * LANES] = taken.astype(BF16)
        return carry

    lax.fori_loop(0, rows // STEP, step, 0)


def pick(owner_times, peram, keys, name, spare):
    rows, times, parts, width = peram.shape
    tiles = width // LANES
    table = peram.reshape(rows, times, parts, tiles, LANES).swapaxes(2, 3)
    table = table.reshape(rows, times, tiles * parts, LANES)
    picked = pl.pallas_call(
        functools.partial(pick_kernel, keys),
        out_shape=[jax.ShapeDtypeStruct((parts, rows, width), BF16)] * len(keys) + spare,
        in_specs=[ANY, ANY],
        out_specs=[VMEM] * len(keys) + [ANY] * len(spare),
        scratch_shapes=[
            pltpu.VMEM(table.shape, BF16),
            pltpu.VMEM((4, STEP * tiles * parts, LANES), F32),
            pltpu.SMEM(owner_times.shape[::-1], jnp.int32),
            pltpu.SemaphoreType.DMA((rows // STEP,)),
            pltpu.SemaphoreType.DMA,
        ],
        compiler_params=params(32),
        cost_estimate=LITTLE,
        name=name,
    )(in_hbm(owner_times.T), in_hbm(table))
    return dict(zip(keys, picked))


def place(far, per_spin):
    low = lax.axis_index("tp") % per_spin
    return (far // per_spin) * per_spin + lax.bitwise_xor(jnp.int32(far % per_spin), low)


def gram_block(left, right):
    depth = left.shape[1] // 2
    real = dot_nt(left, right)
    imag = dot_nt(left[:, :depth], right[:, depth:]) - dot_nt(left[:, depth:], right[:, :depth])
    return real.astype(BF16), imag.astype(BF16)


def fold(values):
    rows, columns = values.shape
    return jnp.sum(values.reshape(rows // 8, 8, columns), axis=0)


def down(values):
    row = lax.broadcasted_iota(jnp.int32, TILE, 0)
    tile = jnp.zeros(TILE, F32)
    for n, value in values:
        tile = jnp.where(row == n, jnp.sum(value, keepdims=True), tile)
    return tile


def direct_sums(diagonal, own):
    real = functools.reduce(jnp.add, [block[0].astype(F32) for block in diagonal])
    imag = functools.reduce(jnp.add, [block[1].astype(F32) for block in diagonal])
    sums = []
    for slot in range(own.shape[0]):
        elem_re, elem_im = own[slot, 0].astype(F32), own[slot, 1].astype(F32)
        sums.append((2 * slot, fold(elem_re * real + elem_im * imag)))
        sums.append((2 * slot + 1, fold(elem_im * real - elem_re * imag)))
    return sums


def early_blocks(spins):
    off = [(s, t) for s in range(spins - 1) for t in range(s + 1, spins - 1)]
    return off + [(s, s) for s in range(spins - 1)]


def early_kernel(eig, keys, rb_count, blocks, *refs):
    pieces, (own, flat, out, traces, sem) = refs[:-5], refs[-5:]
    rows, width = pieces[0].shape[1:]
    depth = rb_count * width
    copies = []
    for n, ((far, side), piece) in enumerate(zip(keys, pieces)):
        where = aligned(place(far, eig // rows) * rows, rows)
        for part in range(2):
            columns = pl.ds(part * depth + side * width, width)
            copies.append(pltpu.make_async_copy(piece.at[part], flat.at[where, columns], sem.at[2 * n + part]))
    for copy in copies:
        copy.start()
    for copy in copies:
        copy.wait()

    def step(n, carry):
        top, side = choose(n, [b[0] for b in blocks]), choose(n, [b[1] for b in blocks])
        out[n, 0], out[n, 1] = gram_block(flat[aligned(top * eig, eig), :], flat[aligned(side * eig, eig), :])
        return carry

    lax.fori_loop(0, len(blocks), step, 0)
    diagonal = [out.at[n] for n, block in enumerate(blocks) if block[0] == block[1]]
    traces[...] = down(direct_sums(diagonal, own))


def early_gram(keys, pieces, own_elems, spins, eig, rb_count):
    blocks = early_blocks(spins)
    depth = 2 * rb_count * pieces[0].shape[2]
    return pl.pallas_call(
        functools.partial(early_kernel, eig, keys, rb_count, blocks),
        out_shape=(
            jax.ShapeDtypeStruct(((spins - 1) * eig, depth), BF16),
            jax.ShapeDtypeStruct((len(blocks), 2, eig, eig), BF16),
            jax.ShapeDtypeStruct(TILE, F32),
        ),
        in_specs=[ANY] * len(pieces) + [VMEM],
        out_specs=(VMEM, VMEM, VMEM),
        scratch_shapes=[pltpu.SemaphoreType.DMA((2 * len(pieces),))],
        compiler_params=params(32),
        cost_estimate=LONG,
        name="early_gram",
    )(*pieces, own_elems)


def late_rows_kernel(eig, keys, rb_count, flat, begun, *refs):
    pieces, (out, last) = refs[:-2], refs[-2:]
    rows, width = pieces[0].shape[1:]
    depth = rb_count * width
    others = flat.shape[0] // eig
    for (far, side), piece in zip(keys, pieces):
        where = aligned((place(far, eig // rows) - others * (eig // rows)) * rows, rows)
        for part in range(2):
            column = part * depth + side * width
            last[where, column : column + width] = piece[part]
    for n in range(out.shape[0]):
        out[n, 0], out[n, 1] = gram_block(flat[n * eig : (n + 1) * eig, :], last[...])


def late_rest_kernel(eig, flat, last, out):
    count = out.shape[0] - 1
    first = flat.shape[0] // eig - count
    for n in range(count):
        out[n, 0], out[n, 1] = gram_block(flat[(first + n) * eig : (first + n + 1) * eig, :], last[...])
    out[count, 0], out[count, 1] = gram_block(last[...], last[...])


def late_rows(keys, flat, begun, pieces, spins, eig, rb_count):
    return pl.pallas_call(
        functools.partial(late_rows_kernel, eig, keys, rb_count),
        out_shape=(
            jax.ShapeDtypeStruct((spins // 2, 2, eig, eig), BF16),
            jax.ShapeDtypeStruct((eig, flat.shape[1]), BF16),
        ),
        in_specs=[VMEM, ANY] + [VMEM] * len(pieces),
        out_specs=(VMEM, VMEM),
        compiler_params=params(32),
        cost_estimate=LONG,
        name="late_rows",
    )(flat, begun, *pieces)


def late_rest(flat, last, spins, eig):
    return pl.pallas_call(
        functools.partial(late_rest_kernel, eig),
        out_shape=jax.ShapeDtypeStruct((spins - spins // 2, 2, eig, eig), BF16),
        in_specs=[VMEM, VMEM],
        out_specs=VMEM,
        compiler_params=params(32),
        cost_estimate=LITTLE,
        name="late_rest",
    )(flat, last)


def factors_kernel(diag_mom, elems, right_ref, left_ref, own_ref, held, sem):
    rank = lax.axis_index("rb")
    eig = held.shape[-1]
    copies = []
    for time in range(2):
        which = diag_mom[0, rank, lax.bitwise_xor(rank, time)]
        copies.append(pltpu.make_async_copy(elems.at[which], held.at[time], sem.at[time]))
    for slot in range(own_ref.shape[0]):
        copies.append(pltpu.make_async_copy(elems.at[diag_mom[0, slot, rank]], own_ref.at[slot], sem.at[2 + slot]))
    for copy in copies:
        copy.start()
    for copy in copies:
        copy.wait()
    for time in range(2):
        re, im = held[time, 0], held[time, 1]
        right_ref[time, :eig, :eig] = re
        right_ref[time, :eig, eig:] = im
        right_ref[time, eig:, :eig] = -im
        right_ref[time, eig:, eig:] = re
        re_t = re.astype(F32).T.astype(BF16)
        im_t = im.astype(F32).T.astype(BF16)
        left_ref[time, :eig, :eig] = re_t
        left_ref[time, :eig, eig:] = im_t
        left_ref[time, eig:, :eig] = im_t
        left_ref[time, eig:, eig:] = -re_t


def factors(diag_mom, src_elems):
    slots, eig = diag_mom.shape[1], src_elems.shape[-1]
    form = jax.ShapeDtypeStruct((2, 2 * eig, 2 * eig), BF16)
    return pl.pallas_call(
        factors_kernel,
        out_shape=(form, form, jax.ShapeDtypeStruct((slots, 2, eig, eig), BF16)),
        in_specs=[SMEM, ANY],
        out_specs=(VMEM, VMEM, VMEM),
        scratch_shapes=[pltpu.VMEM((2, 2, eig, eig), BF16), pltpu.SemaphoreType.DMA((2 + slots,))],
        compiler_params=params(32),
        cost_estimate=LITTLE,
        name="factors",
    )(diag_mom, src_elems)


def cross_kernel(offs, at, own, other, right, left, *refs):
    carried, (out, acc) = refs[:-2], refs[-2:]
    elems, carried = (carried[0], carried[1:]) if carried else (None, [])
    eig = own.shape[-1]
    if len(other.shape) > len(own.shape):
        other = other.at[1 - lax.axis_index("rb")]
    acc[...] = jnp.zeros_like(acc)

    def add(x, y, from_right, from_left):
        product = dot(jnp.concatenate([x[0], x[1]], axis=1), from_right)
        partner = dot(from_left, y.reshape(2 * eig, eig))
        p_re, p_im = product[:, :eig], product[:, eig:]
        w_re, w_im = partner[:eig], partner[eig:]
        acc[0] += fold(p_re * w_re - p_im * w_im)
        acc[1] += fold(p_re * w_im + p_im * w_re)

    def both(n, carry):
        add(other[n], own[n], right[1], left[0])
        add(own[n], other[n], right[0], left[1])
        return carry

    def once(n, carry):
        add(other[n], own[n], right[1], left[0])
        return carry

    lax.fori_loop(0, offs, both, 0, unroll=True)
    lax.fori_loop(offs, own.shape[0], once, 0, unroll=True)
    sums = [(at, acc[0]), (at + 1, acc[1])]
    if elems is not None and offs < own.shape[0]:
        sums += direct_sums([own.at[n] for n in range(offs, own.shape[0])], elems)
    tile = down(sums)
    out[...] = functools.reduce(jnp.add, [ref[...] for ref in carried], tile)


def cross_traces(offs, at, own, other, right, left, carried, name):
    eig = own.shape[-1]
    return pl.pallas_call(
        functools.partial(cross_kernel, offs, at),
        out_shape=jax.ShapeDtypeStruct(TILE, F32),
        in_specs=[VMEM] * (4 + len(carried)),
        out_specs=VMEM,
        scratch_shapes=[pltpu.VMEM((2, 8, eig), F32)],
        compiler_params=params(32),
        cost_estimate=LITTLE,
        name=name,
    )(own, other, right, left, *carried)


def final_kernel(slots, mine, theirs, count, out):
    rank = lax.axis_index("rb")
    lane = lax.broadcasted_iota(jnp.int32, (1, LANES), 1)

    def row(ref, n):
        return ref[n : n + 1, :]

    def put(slot, kind, re, im):
        value = jnp.where(lane == 0, re, im) * 0.25
        out[0, slot, kind : kind + 1, :] = jnp.where(slot < count[0], value, 0.0)[:, :2]

    for slot in range(slots):
        m_re, m_im = row(mine, 2 * slot), row(mine, 2 * slot + 1)
        t_re, t_im = row(theirs, 2 * slot), row(theirs, 2 * slot + 1)
        put(slot, 0, m_re * t_re - m_im * t_im, m_re * t_im + m_im * t_re)
        here = rank == slot
        re = jnp.where(here, row(mine, 2 * slots), row(theirs, 2 * slots))
        im = jnp.where(here, row(mine, 2 * slots + 1), row(theirs, 2 * slots + 1))
        put(slot, 1, re, im)


def final(mine, theirs, diag_count, slots):
    return pl.pallas_call(
        functools.partial(final_kernel, slots),
        out_shape=jax.ShapeDtypeStruct((1, slots, 2, 2), F32),
        in_specs=[VMEM, VMEM, SMEM],
        out_specs=VMEM,
        compiler_params=params(32),
        name="final",
    )(mine, theirs, diag_count)


def shards(peram, src_elems, owner_times, diag_mom, diag_count):
    tp_count, rb_count = lax.axis_size("tp"), lax.axis_size("rb")
    eig = src_elems.shape[-1]
    spins = tp_count * peram.shape[0] // eig
    slots = diag_mom.shape[1]

    head, tail, late, own = travel_order(tp_count, rb_count)
    early_keys = head + tail
    picked = pick(owner_times, peram, head, "pick_head", [jax.ShapeDtypeStruct((4, *peram.shape), BF16)])
    picked.update(pick(owner_times, peram, tail + late + own, "pick_tail", []))

    def send(key):
        far, side = key
        pairs = [
            (tp * rb_count + rb, (tp ^ far) * rb_count + (rb ^ side))
            for tp in range(tp_count)
            for rb in range(rb_count)
        ]
        return lax.ppermute(picked[key], ("tp", "rb"), pairs)

    swap = [(rb, rb ^ 1) for rb in range(rb_count)]
    right, left, own_elems = factors(diag_mom, src_elems)
    arrived = [send(key) for key in early_keys] + [picked[key] for key in own]
    flat, early, direct = early_gram(early_keys + own, arrived, own_elems, spins, eig, rb_count)
    early_both = lax.all_to_all(jnp.stack([early] * rb_count), "rb", 0, 0)
    offs = early.shape[0] - (spins - 1)
    begun = cross_traces(offs, 2 * slots, early, early_both, right, left, [], "early_cross")

    blocks, last = late_rows(late, flat, begun, [send(key) for key in late], spins, eig, rb_count)
    swapped = lax.ppermute(blocks, "rb", swap)
    rest = late_rest(flat, last, spins, eig)
    rest_swapped = lax.ppermute(rest, "rb", swap)
    count = blocks.shape[0]
    partial = cross_traces(count, 2 * slots, blocks, swapped, right, left, [own_elems, direct, begun], "late_cross")
    count = rest.shape[0] - 1
    mine = cross_traces(count, 2 * slots, rest, rest_swapped, right, left, [own_elems, partial], "last_cross")
    theirs = lax.ppermute(mine, "rb", swap)
    return final(mine, theirs, diag_count, slots)


def solution(mesh):
    in_specs = (
        P(("grp", "tp"), None, None, "rb"),
        P("grp", None, None, None),
        P("grp", None),
        P(("grp", "tp"), None, None),
        P(("grp", "tp")),
    )
    out_specs = P(("grp", "tp"), None, None, None)
    return jax.shard_map(shards, mesh=mesh, in_specs=in_specs, out_specs=out_specs, check_vma=False)
```

```python
import functools

import jax
import jax.numpy as jnp
from jax import lax
from jax.experimental import pallas as pl
from jax.experimental.pallas import tpu as pltpu
from jax.sharding import PartitionSpec as P

F32 = jnp.float32
BF16 = jnp.bfloat16
ANY = pl.BlockSpec(memory_space=pl.ANY)
SMEM = pl.BlockSpec(memory_space=pltpu.SMEM)
VMEM = pl.BlockSpec(memory_space=pltpu.VMEM)
TILE = (8, 128)
LANES = 128
STEP = 16
MIB = 1 << 20
LITTLE = pl.CostEstimate(flops=1000, bytes_accessed=1000, transcendentals=0)
LONG = pl.CostEstimate(flops=5 * 10**10, bytes_accessed=1000, transcendentals=0)


def in_hbm(array):
    return pltpu.with_memory_space_constraint(array, pltpu.HBM)


def params(mib):
    return pltpu.CompilerParams(vmem_limit_bytes=mib * MIB)


def dot(left, right):
    return jnp.dot(left, right, preferred_element_type=F32)


def dot_nt(left, right):
    return lax.dot_general(left, right, (((1,), (1,)), ((), ())), preferred_element_type=F32)


def choose(index, values):
    out = jnp.int32(values[0])
    for n in range(1, len(values)):
        out = jnp.where(index == n, jnp.int32(values[n]), out)
    return out


def aligned(start, size):
    return pl.ds(pl.multiple_of(start, size), size)


def travel_order(tp_count, rb_count):
    half, quarter = tp_count // 2, tp_count // 4

    def both(distances):
        return [(far, side) for far in distances for side in range(rb_count)]

    long, late = both(range(half, half + quarter)), both(range(half + quarter, tp_count))
    near, rest = both(reversed(range(quarter, half))), both(range(1, quarter))
    own, other = (0, 0), [(0, side) for side in range(1, rb_count)]
    step, part = len(long) // 4, len(rest) // 2
    head = long[: 2 * step] + near[: 2 * step] + long[2 * step : 3 * step]
    tail = rest[:part] + other + near[2 * step : 3 * step] + long[3 * step :] + near[3 * step :] + rest[part:]
    return head, tail, late, [own]


def pick_kernel(keys, times, table, *refs):
    outs, (held, wide, taken_times, sem, times_sem) = refs[:-5], refs[-5:]
    tp_rank, rb_rank = lax.axis_index("tp"), lax.axis_index("rb")
    rows, _, packed, _ = table.shape

    def fetch(chunk):
        where = aligned(chunk * STEP, STEP)
        return pltpu.make_async_copy(table.at[where], held.at[where], sem.at[chunk])

    copy = pltpu.make_async_copy(times, taken_times, times_sem)
    copy.start()
    for chunk in range(rows // STEP):
        fetch(chunk).start()
    copy.wait()

    def step(chunk, carry):
        fetch(chunk).wait()
        where = aligned(chunk * STEP, STEP)
        for n, (far, side) in enumerate(keys):
            time = taken_times[lax.bitwise_xor(rb_rank, side), lax.bitwise_xor(tp_rank, far)]
            slot = n % wide.shape[0]
            wide[slot] = held[where, time].astype(F32).reshape(STEP * packed, LANES)
            for tile in range(packed // 2):
                for part in range(2):
                    taken = wide[slot, pl.ds(2 * tile + part, STEP, stride=packed), :]
                    outs[n][part, where, tile * LANES : (tile + 1) * LANES] = taken.astype(BF16)
        return carry

    lax.fori_loop(0, rows // STEP, step, 0)


def pick(owner_times, peram, keys, name, spare):
    rows, times, parts, width = peram.shape
    tiles = width // LANES
    table = peram.reshape(rows, times, parts, tiles, LANES).swapaxes(2, 3)
    table = table.reshape(rows, times, tiles * parts, LANES)
    picked = pl.pallas_call(
        functools.partial(pick_kernel, keys),
        out_shape=[jax.ShapeDtypeStruct((parts, rows, width), BF16)] * len(keys) + spare,
        in_specs=[ANY, ANY],
        out_specs=[VMEM] * len(keys) + [ANY] * len(spare),
        scratch_shapes=[
            pltpu.VMEM(table.shape, BF16),
            pltpu.VMEM((4, STEP * tiles * parts, LANES), F32),
            pltpu.SMEM(owner_times.shape[::-1], jnp.int32),
            pltpu.SemaphoreType.DMA((rows // STEP,)),
            pltpu.SemaphoreType.DMA,
        ],
        compiler_params=params(32),
        cost_estimate=LITTLE,
        name=name,
    )(in_hbm(owner_times.T), in_hbm(table))
    return dict(zip(keys, picked))


def place(far, per_spin):
    low = lax.axis_index("tp") % per_spin
    return (far // per_spin) * per_spin + lax.bitwise_xor(jnp.int32(far % per_spin), low)


def gram_block(left, right):
    depth = left.shape[1] // 2
    real = dot_nt(left, right)
    imag = dot_nt(left[:, :depth], right[:, depth:]) - dot_nt(left[:, depth:], right[:, :depth])
    return real.astype(BF16), imag.astype(BF16)


def fold(values):
    rows, columns = values.shape
    return jnp.sum(values.reshape(rows // 8, 8, columns), axis=0)


def down(values):
    row = lax.broadcasted_iota(jnp.int32, TILE, 0)
    tile = jnp.zeros(TILE, F32)
    for n, value in values:
        tile = jnp.where(row == n, jnp.sum(value, keepdims=True), tile)
    return tile


def direct_sums(diagonal, own):
    real = functools.reduce(jnp.add, [block[0].astype(F32) for block in diagonal])
    imag = functools.reduce(jnp.add, [block[1].astype(F32) for block in diagonal])
    sums = []
    for slot in range(own.shape[0]):
        elem_re, elem_im = own[slot, 0].astype(F32), own[slot, 1].astype(F32)
        sums.append((2 * slot, fold(elem_re * real + elem_im * imag)))
        sums.append((2 * slot + 1, fold(elem_im * real - elem_re * imag)))
    return sums


def early_blocks(spins):
    off = [(s, t) for s in range(spins - 1) for t in range(s + 1, spins - 1)]
    return off + [(s, s) for s in range(spins - 1)]


def early_kernel(eig, keys, rb_count, blocks, *refs):
    pieces, (own, flat, out, traces, sem) = refs[:-5], refs[-5:]
    rows, width = pieces[0].shape[1:]
    depth = rb_count * width
    copies = []
    for n, ((far, side), piece) in enumerate(zip(keys, pieces)):
        where = aligned(place(far, eig // rows) * rows, rows)
        for part in range(2):
            columns = pl.ds(part * depth + side * width, width)
            copies.append(pltpu.make_async_copy(piece.at[part], flat.at[where, columns], sem.at[2 * n + part]))
    for copy in copies:
        copy.start()
    for copy in copies:
        copy.wait()

    def step(n, carry):
        top, side = choose(n, [b[0] for b in blocks]), choose(n, [b[1] for b in blocks])
        out[n, 0], out[n, 1] = gram_block(flat[aligned(top * eig, eig), :], flat[aligned(side * eig, eig), :])
        return carry

    lax.fori_loop(0, len(blocks), step, 0)
    diagonal = [out.at[n] for n, block in enumerate(blocks) if block[0] == block[1]]
    traces[...] = down(direct_sums(diagonal, own))


def early_gram(keys, pieces, own_elems, spins, eig, rb_count):
    blocks = early_blocks(spins)
    depth = 2 * rb_count * pieces[0].shape[2]
    return pl.pallas_call(
        functools.partial(early_kernel, eig, keys, rb_count, blocks),
        out_shape=(
            jax.ShapeDtypeStruct(((spins - 1) * eig, depth), BF16),
            jax.ShapeDtypeStruct((len(blocks), 2, eig, eig), BF16),
            jax.ShapeDtypeStruct(TILE, F32),
        ),
        in_specs=[ANY] * len(pieces) + [VMEM],
        out_specs=(VMEM, VMEM, VMEM),
        scratch_shapes=[pltpu.SemaphoreType.DMA((2 * len(pieces),))],
        compiler_params=params(32),
        cost_estimate=LONG,
        name="early_gram",
    )(*pieces, own_elems)


def side_columns(ref, rows, side, width, rb_count):
    return [ref[rows, (part * rb_count + side) * width : (part * rb_count + side + 1) * width] for part in range(2)]


def half_products(left, right):
    real = dot_nt(left[0], right[0]) + dot_nt(left[1], right[1])
    imag = dot_nt(left[0], right[1]) - dot_nt(left[1], right[0])
    return real, imag


def gather_last(eig, keys, others, pieces, last):
    rows, width = pieces[0].shape[1:]
    for (far, _), piece in zip(keys, pieces):
        where = aligned((place(far, eig // rows) - others * (eig // rows)) * rows, rows)
        for part in range(2):
            last[where, part * width : (part + 1) * width] = piece[part]


def late_begin_kernel(eig, keys, rb_count, flat, begun, *refs):
    pieces, (out, last) = refs[:-2], refs[-2:]
    side, width, others = keys[0][1], pieces[0].shape[2], flat.shape[0] // eig
    gather_last(eig, keys, others, pieces, last)
    right = [last[:, :width], last[:, width:]]
    for n in range(others):
        left = side_columns(flat, slice(n * eig, (n + 1) * eig), side, width, rb_count)
        out[n, 0], out[n, 1] = half_products(left, right)
    out[others, 0], out[others, 1] = half_products(right, right)


def late_begin(keys, flat, begun, pieces, spins, eig, rb_count):
    return pl.pallas_call(
        functools.partial(late_begin_kernel, eig, keys, rb_count),
        out_shape=jax.ShapeDtypeStruct((spins, 2, eig, eig), F32),
        in_specs=[VMEM, ANY] + [VMEM] * len(pieces),
        out_specs=VMEM,
        scratch_shapes=[pltpu.VMEM((eig, 2 * pieces[0].shape[2]), BF16)],
        compiler_params=params(32),
        cost_estimate=LITTLE,
        name="late_begin",
    )(flat, begun, *pieces)


def late_rows_kernel(eig, keys, rb_count, flat, partial, *refs):
    pieces, (out, last) = refs[:-2], refs[-2:]
    side, width = keys[0][1], pieces[0].shape[2]
    gather_last(eig, keys, flat.shape[0] // eig, pieces, last)
    right = [last[:, :width], last[:, width:]]
    for n in range(out.shape[0]):
        left = side_columns(flat, slice(n * eig, (n + 1) * eig), side, width, rb_count)
        real, imag = half_products(left, right)
        out[n, 0], out[n, 1] = (partial[n, 0] + real).astype(BF16), (partial[n, 1] + imag).astype(BF16)


def late_rest_kernel(eig, side, rb_count, flat, partial, last, out):
    count, width = out.shape[0] - 1, last.shape[1] // 2
    others = flat.shape[0] // eig
    right = [last[:, :width], last[:, width:]]
    for n in range(count + 1):
        spin = others - count + n
        left = right
        if n < count:
            left = side_columns(flat, slice(spin * eig, (spin + 1) * eig), side, width, rb_count)
        real, imag = half_products(left, right)
        out[n, 0], out[n, 1] = (partial[spin, 0] + real).astype(BF16), (partial[spin, 1] + imag).astype(BF16)


def late_rows(keys, flat, partial, pieces, spins, eig, rb_count):
    return pl.pallas_call(
        functools.partial(late_rows_kernel, eig, keys, rb_count),
        out_shape=(
            jax.ShapeDtypeStruct((spins // 2, 2, eig, eig), BF16),
            jax.ShapeDtypeStruct((eig, 2 * pieces[0].shape[2]), BF16),
        ),
        in_specs=[VMEM] * (2 + len(pieces)),
        out_specs=(VMEM, VMEM),
        compiler_params=params(32),
        cost_estimate=LONG,
        name="late_rows",
    )(flat, partial, *pieces)


def late_rest(side, flat, partial, last, spins, eig, rb_count):
    return pl.pallas_call(
        functools.partial(late_rest_kernel, eig, side, rb_count),
        out_shape=jax.ShapeDtypeStruct((spins - spins // 2, 2, eig, eig), BF16),
        in_specs=[VMEM] * 3,
        out_specs=VMEM,
        compiler_params=params(32),
        cost_estimate=LITTLE,
        name="late_rest",
    )(flat, partial, last)


def factors_kernel(diag_mom, elems, right_ref, left_ref, own_ref, held, sem):
    rank = lax.axis_index("rb")
    eig = held.shape[-1]
    copies = []
    for time in range(2):
        which = diag_mom[0, rank, lax.bitwise_xor(rank, time)]
        copies.append(pltpu.make_async_copy(elems.at[which], held.at[time], sem.at[time]))
    for slot in range(own_ref.shape[0]):
        copies.append(pltpu.make_async_copy(elems.at[diag_mom[0, slot, rank]], own_ref.at[slot], sem.at[2 + slot]))
    for copy in copies:
        copy.start()
    for copy in copies:
        copy.wait()
    for time in range(2):
        re, im = held[time, 0], held[time, 1]
        right_ref[time, :eig, :eig] = re
        right_ref[time, :eig, eig:] = im
        right_ref[time, eig:, :eig] = -im
        right_ref[time, eig:, eig:] = re
        re_t = re.astype(F32).T.astype(BF16)
        im_t = im.astype(F32).T.astype(BF16)
        left_ref[time, :eig, :eig] = re_t
        left_ref[time, :eig, eig:] = im_t
        left_ref[time, eig:, :eig] = im_t
        left_ref[time, eig:, eig:] = -re_t


def factors(diag_mom, src_elems):
    slots, eig = diag_mom.shape[1], src_elems.shape[-1]
    form = jax.ShapeDtypeStruct((2, 2 * eig, 2 * eig), BF16)
    return pl.pallas_call(
        factors_kernel,
        out_shape=(form, form, jax.ShapeDtypeStruct((slots, 2, eig, eig), BF16)),
        in_specs=[SMEM, ANY],
        out_specs=(VMEM, VMEM, VMEM),
        scratch_shapes=[pltpu.VMEM((2, 2, eig, eig), BF16), pltpu.SemaphoreType.DMA((2 + slots,))],
        compiler_params=params(32),
        cost_estimate=LITTLE,
        name="factors",
    )(diag_mom, src_elems)


def cross_kernel(offs, at, own, other, right, left, *refs):
    carried, (out, acc) = refs[:-2], refs[-2:]
    elems, carried = (carried[0], carried[1:]) if carried else (None, [])
    eig = own.shape[-1]
    if len(other.shape) > len(own.shape):
        other = other.at[1 - lax.axis_index("rb")]
    acc[...] = jnp.zeros_like(acc)

    def add(x, y, from_right, from_left):
        product = dot(jnp.concatenate([x[0], x[1]], axis=1), from_right)
        partner = dot(from_left, y.reshape(2 * eig, eig))
        p_re, p_im = product[:, :eig], product[:, eig:]
        w_re, w_im = partner[:eig], partner[eig:]
        acc[0] += fold(p_re * w_re - p_im * w_im)
        acc[1] += fold(p_re * w_im + p_im * w_re)

    def both(n, carry):
        add(other[n], own[n], right[1], left[0])
        add(own[n], other[n], right[0], left[1])
        return carry

    def once(n, carry):
        add(other[n], own[n], right[1], left[0])
        return carry

    lax.fori_loop(0, offs, both, 0, unroll=True)
    lax.fori_loop(offs, own.shape[0], once, 0, unroll=True)
    sums = [(at, acc[0]), (at + 1, acc[1])]
    if elems is not None and offs < own.shape[0]:
        sums += direct_sums([own.at[n] for n in range(offs, own.shape[0])], elems)
    tile = down(sums)
    out[...] = functools.reduce(jnp.add, [ref[...] for ref in carried], tile)


def cross_traces(offs, at, own, other, right, left, carried, name):
    eig = own.shape[-1]
    return pl.pallas_call(
        functools.partial(cross_kernel, offs, at),
        out_shape=jax.ShapeDtypeStruct(TILE, F32),
        in_specs=[VMEM] * (4 + len(carried)),
        out_specs=VMEM,
        scratch_shapes=[pltpu.VMEM((2, 8, eig), F32)],
        compiler_params=params(32),
        cost_estimate=LITTLE,
        name=name,
    )(own, other, right, left, *carried)


def final_kernel(slots, mine, theirs, count, out):
    rank = lax.axis_index("rb")
    lane = lax.broadcasted_iota(jnp.int32, (1, LANES), 1)

    def row(ref, n):
        return ref[n : n + 1, :]

    def put(slot, kind, re, im):
        value = jnp.where(lane == 0, re, im) * 0.25
        out[0, slot, kind : kind + 1, :] = jnp.where(slot < count[0], value, 0.0)[:, :2]

    for slot in range(slots):
        m_re, m_im = row(mine, 2 * slot), row(mine, 2 * slot + 1)
        t_re, t_im = row(theirs, 2 * slot), row(theirs, 2 * slot + 1)
        put(slot, 0, m_re * t_re - m_im * t_im, m_re * t_im + m_im * t_re)
        here = rank == slot
        re = jnp.where(here, row(mine, 2 * slots), row(theirs, 2 * slots))
        im = jnp.where(here, row(mine, 2 * slots + 1), row(theirs, 2 * slots + 1))
        put(slot, 1, re, im)


def final(mine, theirs, diag_count, slots):
    return pl.pallas_call(
        functools.partial(final_kernel, slots),
        out_shape=jax.ShapeDtypeStruct((1, slots, 2, 2), F32),
        in_specs=[VMEM, VMEM, SMEM],
        out_specs=VMEM,
        compiler_params=params(32),
        name="final",
    )(mine, theirs, diag_count)


def shards(peram, src_elems, owner_times, diag_mom, diag_count):
    tp_count, rb_count = lax.axis_size("tp"), lax.axis_size("rb")
    eig = src_elems.shape[-1]
    spins = tp_count * peram.shape[0] // eig
    slots = diag_mom.shape[1]

    head, tail, late, own = travel_order(tp_count, rb_count)
    early_keys = head + tail
    picked = pick(owner_times, peram, head, "pick_head", [jax.ShapeDtypeStruct((4, *peram.shape), BF16)])
    picked.update(pick(owner_times, peram, tail + late + own, "pick_tail", []))

    def send(key):
        far, side = key
        pairs = [
            (tp * rb_count + rb, (tp ^ far) * rb_count + (rb ^ side))
            for tp in range(tp_count)
            for rb in range(rb_count)
        ]
        return lax.ppermute(picked[key], ("tp", "rb"), pairs)

    swap = [(rb, rb ^ 1) for rb in range(rb_count)]
    right, left, own_elems = factors(diag_mom, src_elems)
    arrived = [send(key) for key in early_keys] + [picked[key] for key in own]
    flat, early, direct = early_gram(early_keys + own, arrived, own_elems, spins, eig, rb_count)
    early_both = lax.all_to_all(jnp.stack([early] * rb_count), "rb", 0, 0)
    offs = early.shape[0] - (spins - 1)
    begun = cross_traces(offs, 2 * slots, early, early_both, right, left, [], "early_cross")

    halves = [[key for key in late if key[1] == side] for side in range(rb_count)]
    sent = [[send(key) for key in keys] for keys in halves]
    half = late_begin(halves[0], flat, begun, sent[0], spins, eig, rb_count)
    blocks, last = late_rows(halves[1], flat, half, sent[1], spins, eig, rb_count)
    swapped = lax.ppermute(blocks, "rb", swap)
    rest = late_rest(1, flat, half, last, spins, eig, rb_count)
    rest_swapped = lax.ppermute(rest, "rb", swap)
    count = blocks.shape[0]
    partial = cross_traces(count, 2 * slots, blocks, swapped, right, left, [own_elems, direct, begun], "late_cross")
    count = rest.shape[0] - 1
    mine = cross_traces(count, 2 * slots, rest, rest_swapped, right, left, [own_elems, partial], "last_cross")
    theirs = lax.ppermute(mine, "rb", swap)
    return final(mine, theirs, diag_count, slots)


def solution(mesh):
    in_specs = (
        P(("grp", "tp"), None, None, "rb"),
        P("grp", None, None, None),
        P("grp", None),
        P(("grp", "tp"), None, None),
        P(("grp", "tp")),
    )
    out_specs = P(("grp", "tp"), None, None, None)
    return jax.shard_map(shards, mesh=mesh, in_specs=in_specs, out_specs=out_specs, check_vma=False)
```

```python
import functools

import jax
import jax.numpy as jnp
from jax import lax
from jax.experimental import pallas as pl
from jax.experimental.pallas import tpu as pltpu
from jax.sharding import PartitionSpec as P

F32 = jnp.float32
BF16 = jnp.bfloat16
ANY = pl.BlockSpec(memory_space=pl.ANY)
SMEM = pl.BlockSpec(memory_space=pltpu.SMEM)
VMEM = pl.BlockSpec(memory_space=pltpu.VMEM)
TILE = (8, 128)
LANES = 128
STEP = 16
MIB = 1 << 20
LITTLE = pl.CostEstimate(flops=1000, bytes_accessed=1000, transcendentals=0)
LONG = pl.CostEstimate(flops=5 * 10**10, bytes_accessed=1000, transcendentals=0)


def in_hbm(array):
    return pltpu.with_memory_space_constraint(array, pltpu.HBM)


def params(mib):
    return pltpu.CompilerParams(vmem_limit_bytes=mib * MIB)


def dot(left, right):
    return jnp.dot(left, right, preferred_element_type=F32)


def dot_nt(left, right):
    return lax.dot_general(left, right, (((1,), (1,)), ((), ())), preferred_element_type=F32)


def choose(index, values):
    out = jnp.int32(values[0])
    for n in range(1, len(values)):
        out = jnp.where(index == n, jnp.int32(values[n]), out)
    return out


def aligned(start, size):
    return pl.ds(pl.multiple_of(start, size), size)


def travel_order(tp_count, rb_count):
    half, quarter = tp_count // 2, tp_count // 4

    def both(distances):
        return [(far, side) for far in distances for side in range(rb_count)]

    long, late = both(range(half, half + quarter)), both(range(half + quarter, tp_count))
    near, rest = both(reversed(range(quarter, half))), both(range(1, quarter))
    own, other = (0, 0), [(0, side) for side in range(1, rb_count)]
    step, part = len(long) // 4, len(rest) // 2
    head = long[: 2 * step] + near[: 2 * step] + long[2 * step : 3 * step]
    tail = rest[:part] + other + near[2 * step : 3 * step] + long[3 * step :] + near[3 * step :] + rest[part:]
    return head, tail, late, [own]


def pick_kernel(keys, times, table, *refs):
    outs, (held, wide, taken_times, sem, times_sem) = refs[:-5], refs[-5:]
    tp_rank, rb_rank = lax.axis_index("tp"), lax.axis_index("rb")
    rows, _, packed, _ = table.shape

    def fetch(chunk):
        where = aligned(chunk * STEP, STEP)
        return pltpu.make_async_copy(table.at[where], held.at[where], sem.at[chunk])

    copy = pltpu.make_async_copy(times, taken_times, times_sem)
    copy.start()
    for chunk in range(rows // STEP):
        fetch(chunk).start()
    copy.wait()

    def step(chunk, carry):
        fetch(chunk).wait()
        where = aligned(chunk * STEP, STEP)
        for n, (far, side) in enumerate(keys):
            time = taken_times[lax.bitwise_xor(rb_rank, side), lax.bitwise_xor(tp_rank, far)]
            slot = n % wide.shape[0]
            wide[slot] = held[where, time].astype(F32).reshape(STEP * packed, LANES)
            for tile in range(packed // 2):
                for part in range(2):
                    taken = wide[slot, pl.ds(2 * tile + part, STEP, stride=packed), :]
                    outs[n][part, where, tile * LANES : (tile + 1) * LANES] = taken.astype(BF16)
        return carry

    lax.fori_loop(0, rows // STEP, step, 0)


def pick(owner_times, peram, keys, name, spare):
    rows, times, parts, width = peram.shape
    tiles = width // LANES
    table = peram.reshape(rows, times, parts, tiles, LANES).swapaxes(2, 3)
    table = table.reshape(rows, times, tiles * parts, LANES)
    picked = pl.pallas_call(
        functools.partial(pick_kernel, keys),
        out_shape=[jax.ShapeDtypeStruct((parts, rows, width), BF16)] * len(keys) + spare,
        in_specs=[ANY, ANY],
        out_specs=[VMEM] * len(keys) + [ANY] * len(spare),
        scratch_shapes=[
            pltpu.VMEM(table.shape, BF16),
            pltpu.VMEM((4, STEP * tiles * parts, LANES), F32),
            pltpu.SMEM(owner_times.shape[::-1], jnp.int32),
            pltpu.SemaphoreType.DMA((rows // STEP,)),
            pltpu.SemaphoreType.DMA,
        ],
        compiler_params=params(32),
        cost_estimate=LITTLE,
        name=name,
    )(in_hbm(owner_times.T), in_hbm(table))
    return dict(zip(keys, picked))


def place(far, per_spin):
    low = lax.axis_index("tp") % per_spin
    return (far // per_spin) * per_spin + lax.bitwise_xor(jnp.int32(far % per_spin), low)


def gram_block(left, right):
    depth = left.shape[1] // 2
    real = dot_nt(left, right)
    imag = dot_nt(left[:, :depth], right[:, depth:]) - dot_nt(left[:, depth:], right[:, :depth])
    return real.astype(BF16), imag.astype(BF16)


def fold(values):
    rows, columns = values.shape
    return jnp.sum(values.reshape(rows // 8, 8, columns), axis=0)


def down(values):
    row = lax.broadcasted_iota(jnp.int32, TILE, 0)
    tile = jnp.zeros(TILE, F32)
    for n, value in values:
        tile = jnp.where(row == n, jnp.sum(value, keepdims=True), tile)
    return tile


def direct_sums(diagonal, own):
    real = functools.reduce(jnp.add, [block[0].astype(F32) for block in diagonal])
    imag = functools.reduce(jnp.add, [block[1].astype(F32) for block in diagonal])
    sums = []
    for slot in range(own.shape[0]):
        elem_re, elem_im = own[slot, 0].astype(F32), own[slot, 1].astype(F32)
        sums.append((2 * slot, fold(elem_re * real + elem_im * imag)))
        sums.append((2 * slot + 1, fold(elem_im * real - elem_re * imag)))
    return sums


def early_blocks(spins):
    off = [(s, t) for s in range(spins - 1) for t in range(s + 1, spins - 1)]
    return off + [(s, s) for s in range(spins - 1)]


def early_kernel(eig, keys, rb_count, blocks, *refs):
    pieces, (own, flat, out, traces, sem) = refs[:-5], refs[-5:]
    rows, width = pieces[0].shape[1:]
    depth = rb_count * width
    copies = []
    for n, ((far, side), piece) in enumerate(zip(keys, pieces)):
        where = aligned(place(far, eig // rows) * rows, rows)
        for part in range(2):
            columns = pl.ds(part * depth + side * width, width)
            copies.append(pltpu.make_async_copy(piece.at[part], flat.at[where, columns], sem.at[2 * n + part]))
    for copy in copies:
        copy.start()
    for copy in copies:
        copy.wait()

    def step(n, carry):
        top, side = choose(n, [b[0] for b in blocks]), choose(n, [b[1] for b in blocks])
        out[n, 0], out[n, 1] = gram_block(flat[aligned(top * eig, eig), :], flat[aligned(side * eig, eig), :])
        return carry

    lax.fori_loop(0, len(blocks), step, 0)
    diagonal = [out.at[n] for n, block in enumerate(blocks) if block[0] == block[1]]
    traces[...] = down(direct_sums(diagonal, own))


def early_gram(keys, pieces, own_elems, spins, eig, rb_count):
    blocks = early_blocks(spins)
    depth = 2 * rb_count * pieces[0].shape[2]
    return pl.pallas_call(
        functools.partial(early_kernel, eig, keys, rb_count, blocks),
        out_shape=(
            jax.ShapeDtypeStruct(((spins - 1) * eig, depth), BF16),
            jax.ShapeDtypeStruct((len(blocks), 2, eig, eig), BF16),
            jax.ShapeDtypeStruct(TILE, F32),
        ),
        in_specs=[ANY] * len(pieces) + [VMEM],
        out_specs=(VMEM, VMEM, VMEM),
        scratch_shapes=[pltpu.SemaphoreType.DMA((2 * len(pieces),))],
        compiler_params=params(32),
        cost_estimate=LONG,
        name="early_gram",
    )(*pieces, own_elems)


def side_columns(ref, rows, side, width, rb_count):
    return [ref[rows, (part * rb_count + side) * width : (part * rb_count + side + 1) * width] for part in range(2)]


def half_products(left, right):
    real = dot_nt(left[0], right[0]) + dot_nt(left[1], right[1])
    imag = dot_nt(left[0], right[1]) - dot_nt(left[1], right[0])
    return real, imag


def gather_last(eig, keys, others, pieces, last):
    rows, width = pieces[0].shape[1:]
    for (far, _), piece in zip(keys, pieces):
        where = aligned((place(far, eig // rows) - others * (eig // rows)) * rows, rows)
        for part in range(2):
            last[where, part * width : (part + 1) * width] = piece[part]


def late_begin_kernel(eig, keys, rb_count, flat, begun, *refs):
    pieces, (out, last) = refs[:-2], refs[-2:]
    side, width, others = keys[0][1], pieces[0].shape[2], flat.shape[0] // eig
    gather_last(eig, keys, others, pieces, last)
    right = [last[:, :width], last[:, width:]]
    for n in range(others):
        left = side_columns(flat, slice(n * eig, (n + 1) * eig), side, width, rb_count)
        out[n, 0], out[n, 1] = half_products(left, right)
    out[others, 0], out[others, 1] = half_products(right, right)


def late_begin(keys, flat, begun, pieces, spins, eig, rb_count):
    return pl.pallas_call(
        functools.partial(late_begin_kernel, eig, keys, rb_count),
        out_shape=jax.ShapeDtypeStruct((spins, 2, eig, eig), F32),
        in_specs=[VMEM, ANY] + [VMEM] * len(pieces),
        out_specs=VMEM,
        scratch_shapes=[pltpu.VMEM((eig, 2 * pieces[0].shape[2]), BF16)],
        compiler_params=params(32),
        cost_estimate=LITTLE,
        name="late_begin",
    )(flat, begun, *pieces)


def late_rows_kernel(eig, keys, rb_count, flat, partial, *refs):
    pieces, (out, last) = refs[:-2], refs[-2:]
    side, width = keys[0][1], pieces[0].shape[2]
    gather_last(eig, keys, flat.shape[0] // eig, pieces, last)
    right = [last[:, :width], last[:, width:]]
    for n in range(out.shape[0]):
        left = side_columns(flat, slice(n * eig, (n + 1) * eig), side, width, rb_count)
        real, imag = half_products(left, right)
        out[n, 0], out[n, 1] = (partial[n, 0] + real).astype(BF16), (partial[n, 1] + imag).astype(BF16)


def late_rest_kernel(eig, side, rb_count, flat, partial, last, out):
    count, width = out.shape[0] - 1, last.shape[1] // 2
    others = flat.shape[0] // eig
    right = [last[:, :width], last[:, width:]]
    for n in range(count + 1):
        spin = others - count + n
        left = right
        if n < count:
            left = side_columns(flat, slice(spin * eig, (spin + 1) * eig), side, width, rb_count)
        real, imag = half_products(left, right)
        out[n, 0], out[n, 1] = (partial[spin, 0] + real).astype(BF16), (partial[spin, 1] + imag).astype(BF16)


def late_rows(keys, flat, partial, pieces, spins, eig, rb_count):
    return pl.pallas_call(
        functools.partial(late_rows_kernel, eig, keys, rb_count),
        out_shape=(
            jax.ShapeDtypeStruct((spins // 2, 2, eig, eig), BF16),
            jax.ShapeDtypeStruct((eig, 2 * pieces[0].shape[2]), BF16),
        ),
        in_specs=[VMEM] * (2 + len(pieces)),
        out_specs=(VMEM, VMEM),
        compiler_params=params(32),
        cost_estimate=LONG,
        name="late_rows",
    )(flat, partial, *pieces)


def late_rest(side, flat, partial, last, spins, eig, rb_count):
    return pl.pallas_call(
        functools.partial(late_rest_kernel, eig, side, rb_count),
        out_shape=jax.ShapeDtypeStruct((spins - spins // 2, 2, eig, eig), BF16),
        in_specs=[VMEM] * 3,
        out_specs=VMEM,
        compiler_params=params(32),
        cost_estimate=LITTLE,
        name="late_rest",
    )(flat, partial, last)


def factors_kernel(diag_mom, elems, right_ref, left_ref, own_ref, held, sem):
    rank = lax.axis_index("rb")
    eig = held.shape[-1]
    copies = []
    for time in range(2):
        which = diag_mom[0, rank, lax.bitwise_xor(rank, time)]
        copies.append(pltpu.make_async_copy(elems.at[which], held.at[time], sem.at[time]))
    for slot in range(own_ref.shape[0]):
        copies.append(pltpu.make_async_copy(elems.at[diag_mom[0, slot, rank]], own_ref.at[slot], sem.at[2 + slot]))
    for copy in copies:
        copy.start()
    for copy in copies:
        copy.wait()
    for time in range(2):
        re, im = held[time, 0], held[time, 1]
        right_ref[time, :eig, :eig] = re
        right_ref[time, :eig, eig:] = im
        right_ref[time, eig:, :eig] = -im
        right_ref[time, eig:, eig:] = re
        re_t = re.astype(F32).T.astype(BF16)
        im_t = im.astype(F32).T.astype(BF16)
        left_ref[time, :eig, :eig] = re_t
        left_ref[time, :eig, eig:] = im_t
        left_ref[time, eig:, :eig] = im_t
        left_ref[time, eig:, eig:] = -re_t


def factors(diag_mom, src_elems):
    slots, eig = diag_mom.shape[1], src_elems.shape[-1]
    form = jax.ShapeDtypeStruct((2, 2 * eig, 2 * eig), BF16)
    return pl.pallas_call(
        factors_kernel,
        out_shape=(form, form, jax.ShapeDtypeStruct((slots, 2, eig, eig), BF16)),
        in_specs=[SMEM, ANY],
        out_specs=(VMEM, VMEM, VMEM),
        scratch_shapes=[pltpu.VMEM((2, 2, eig, eig), BF16), pltpu.SemaphoreType.DMA((2 + slots,))],
        compiler_params=params(32),
        cost_estimate=LITTLE,
        name="factors",
    )(diag_mom, src_elems)


def cross_kernel(offs, at, own, other, right, left, *refs):
    carried, (out, acc) = refs[:-2], refs[-2:]
    elems, carried = (carried[0], carried[1:]) if carried else (None, [])
    eig = own.shape[-1]
    if len(other.shape) > len(own.shape):
        other = other.at[1 - lax.axis_index("rb")]
    acc[...] = jnp.zeros_like(acc)

    def add(x, y, count, from_right, from_left):
        rows = [jnp.concatenate([x[n, 0], x[n, 1]], axis=1) for n in range(count)]
        product = dot(jnp.concatenate(rows, axis=0), from_right)
        for n in range(count):
            partner = dot(from_left, y[n].reshape(2 * eig, eig))
            mine = product[n * eig : (n + 1) * eig]
            p_re, p_im = mine[:, :eig], mine[:, eig:]
            w_re, w_im = partner[:eig], partner[eig:]
            acc[0] += fold(p_re * w_re - p_im * w_im)
            acc[1] += fold(p_re * w_im + p_im * w_re)

    add(other, own, own.shape[0], right[1], left[0])
    add(own, other, offs, right[0], left[1])
    sums = [(at, acc[0]), (at + 1, acc[1])]
    if elems is not None and offs < own.shape[0]:
        sums += direct_sums([own.at[n] for n in range(offs, own.shape[0])], elems)
    tile = down(sums)
    out[...] = functools.reduce(jnp.add, [ref[...] for ref in carried], tile)


def cross_traces(offs, at, own, other, right, left, carried, name):
    eig = own.shape[-1]
    return pl.pallas_call(
        functools.partial(cross_kernel, offs, at),
        out_shape=jax.ShapeDtypeStruct(TILE, F32),
        in_specs=[VMEM] * (4 + len(carried)),
        out_specs=VMEM,
        scratch_shapes=[pltpu.VMEM((2, 8, eig), F32)],
        compiler_params=params(32),
        cost_estimate=LITTLE,
        name=name,
    )(own, other, right, left, *carried)


def final_kernel(slots, mine, theirs, count, out):
    rank = lax.axis_index("rb")
    lane = lax.broadcasted_iota(jnp.int32, (1, LANES), 1)

    def row(ref, n):
        return ref[n : n + 1, :]

    def put(slot, kind, re, im):
        value = jnp.where(lane == 0, re, im) * 0.25
        out[0, slot, kind : kind + 1, :] = jnp.where(slot < count[0], value, 0.0)[:, :2]

    for slot in range(slots):
        m_re, m_im = row(mine, 2 * slot), row(mine, 2 * slot + 1)
        t_re, t_im = row(theirs, 2 * slot), row(theirs, 2 * slot + 1)
        put(slot, 0, m_re * t_re - m_im * t_im, m_re * t_im + m_im * t_re)
        here = rank == slot
        re = jnp.where(here, row(mine, 2 * slots), row(theirs, 2 * slots))
        im = jnp.where(here, row(mine, 2 * slots + 1), row(theirs, 2 * slots + 1))
        put(slot, 1, re, im)


def final(mine, theirs, diag_count, slots):
    return pl.pallas_call(
        functools.partial(final_kernel, slots),
        out_shape=jax.ShapeDtypeStruct((1, slots, 2, 2), F32),
        in_specs=[VMEM, VMEM, SMEM],
        out_specs=VMEM,
        compiler_params=params(32),
        name="final",
    )(mine, theirs, diag_count)


def shards(peram, src_elems, owner_times, diag_mom, diag_count):
    tp_count, rb_count = lax.axis_size("tp"), lax.axis_size("rb")
    eig = src_elems.shape[-1]
    spins = tp_count * peram.shape[0] // eig
    slots = diag_mom.shape[1]

    head, tail, late, own = travel_order(tp_count, rb_count)
    early_keys = head + tail
    picked = pick(owner_times, peram, head, "pick_head", [jax.ShapeDtypeStruct((4, *peram.shape), BF16)])
    picked.update(pick(owner_times, peram, tail + late + own, "pick_tail", []))

    def send(key):
        far, side = key
        pairs = [
            (tp * rb_count + rb, (tp ^ far) * rb_count + (rb ^ side))
            for tp in range(tp_count)
            for rb in range(rb_count)
        ]
        return lax.ppermute(picked[key], ("tp", "rb"), pairs)

    swap = [(rb, rb ^ 1) for rb in range(rb_count)]
    right, left, own_elems = factors(diag_mom, src_elems)
    arrived = [send(key) for key in early_keys] + [picked[key] for key in own]
    flat, early, direct = early_gram(early_keys + own, arrived, own_elems, spins, eig, rb_count)
    early_both = lax.all_to_all(jnp.stack([early] * rb_count), "rb", 0, 0)
    offs = early.shape[0] - (spins - 1)
    begun = cross_traces(offs, 2 * slots, early, early_both, right, left, [], "early_cross")

    halves = [[key for key in late if key[1] == side] for side in range(rb_count)]
    sent = [[send(key) for key in keys] for keys in halves]
    half = late_begin(halves[0], flat, begun, sent[0], spins, eig, rb_count)
    blocks, last = late_rows(halves[1], flat, half, sent[1], spins, eig, rb_count)
    swapped = lax.ppermute(blocks, "rb", swap)
    rest = late_rest(1, flat, half, last, spins, eig, rb_count)
    rest_swapped = lax.ppermute(rest, "rb", swap)
    count = blocks.shape[0]
    partial = cross_traces(count, 2 * slots, blocks, swapped, right, left, [own_elems, direct, begun], "late_cross")
    count = rest.shape[0] - 1
    mine = cross_traces(count, 2 * slots, rest, rest_swapped, right, left, [own_elems, partial], "last_cross")
    theirs = lax.ppermute(mine, "rb", swap)
    return final(mine, theirs, diag_count, slots)


def solution(mesh):
    in_specs = (
        P(("grp", "tp"), None, None, "rb"),
        P("grp", None, None, None),
        P("grp", None),
        P(("grp", "tp"), None, None),
        P(("grp", "tp")),
    )
    out_specs = P(("grp", "tp"), None, None, None)
    return jax.shard_map(shards, mesh=mesh, in_specs=in_specs, out_specs=out_specs, check_vma=False)
```

```python
import functools

import jax
import jax.numpy as jnp
from jax import lax
from jax.experimental import pallas as pl
from jax.experimental.pallas import tpu as pltpu
from jax.sharding import PartitionSpec as P

F32 = jnp.float32
BF16 = jnp.bfloat16
ANY = pl.BlockSpec(memory_space=pl.ANY)
SMEM = pl.BlockSpec(memory_space=pltpu.SMEM)
VMEM = pl.BlockSpec(memory_space=pltpu.VMEM)
SUBLANES = 8
LANES = 128
STEP = 16
MIB = 1 << 20
LITTLE = pl.CostEstimate(flops=1000, bytes_accessed=1000, transcendentals=0)
LONG = pl.CostEstimate(flops=5 * 10**10, bytes_accessed=1000, transcendentals=0)


def in_hbm(array):
    return pltpu.with_memory_space_constraint(array, pltpu.HBM)


def params(mib):
    return pltpu.CompilerParams(vmem_limit_bytes=mib * MIB)


def dot(left, right):
    return jnp.dot(left, right, preferred_element_type=F32)


def dot_nt(left, right):
    return lax.dot_general(left, right, (((1,), (1,)), ((), ())), preferred_element_type=F32)


def choose(index, values):
    out = jnp.int32(values[0])
    for n in range(1, len(values)):
        out = jnp.where(index == n, jnp.int32(values[n]), out)
    return out


def aligned(start, size):
    return pl.ds(pl.multiple_of(start, size), size)


def travel_order(tp_count, rb_count):
    half, quarter = tp_count // 2, tp_count // 4

    def both(distances):
        return [(far, side) for far in distances for side in range(rb_count)]

    long, late = both(range(half, half + quarter)), both(range(half + quarter, tp_count))
    near, rest = both(reversed(range(quarter, half))), both(range(1, quarter))
    own, other = (0, 0), [(0, side) for side in range(1, rb_count)]
    step, part = len(long) // 4, len(rest) // 2
    head = long[: 2 * step] + near[: 2 * step] + long[2 * step : 3 * step]
    tail = rest[:part] + other + near[2 * step : 3 * step] + long[3 * step :] + near[3 * step :] + rest[part:]
    return head, tail, late, [own]


def pick_kernel(keys, times, table, *refs):
    outs, (held, wide, taken_times, sem, times_sem) = refs[:-5], refs[-5:]
    tp_rank, rb_rank = lax.axis_index("tp"), lax.axis_index("rb")
    rows, _, packed, _ = table.shape

    def fetch(chunk):
        where = aligned(chunk * STEP, STEP)
        return pltpu.make_async_copy(table.at[where], held.at[where], sem.at[chunk])

    copy = pltpu.make_async_copy(times, taken_times, times_sem)
    copy.start()
    for chunk in range(rows // STEP):
        fetch(chunk).start()
    copy.wait()

    def step(chunk, carry):
        fetch(chunk).wait()
        where = aligned(chunk * STEP, STEP)
        for n, (far, side) in enumerate(keys):
            time = taken_times[lax.bitwise_xor(rb_rank, side), lax.bitwise_xor(tp_rank, far)]
            slot = n % wide.shape[0]
            wide[slot] = held[where, time].astype(F32).reshape(STEP * packed, LANES)
            for tile in range(packed // 2):
                for part in range(2):
                    taken = wide[slot, pl.ds(2 * tile + part, STEP, stride=packed), :]
                    outs[n][part, where, tile * LANES : (tile + 1) * LANES] = taken.astype(BF16)
        return carry

    lax.fori_loop(0, rows // STEP, step, 0)


def pick(owner_times, peram, keys, name, spare):
    rows, times, parts, width = peram.shape
    tiles = width // LANES
    table = peram.reshape(rows, times, parts, tiles, LANES).swapaxes(2, 3)
    table = table.reshape(rows, times, tiles * parts, LANES)
    picked = pl.pallas_call(
        functools.partial(pick_kernel, keys),
        out_shape=[jax.ShapeDtypeStruct((parts, rows, width), BF16)] * len(keys) + spare,
        in_specs=[ANY, ANY],
        out_specs=[VMEM] * len(keys) + [ANY] * len(spare),
        scratch_shapes=[
            pltpu.VMEM(table.shape, BF16),
            pltpu.VMEM((4, STEP * tiles * parts, LANES), F32),
            pltpu.SMEM(owner_times.shape[::-1], jnp.int32),
            pltpu.SemaphoreType.DMA((rows // STEP,)),
            pltpu.SemaphoreType.DMA,
        ],
        compiler_params=params(32),
        cost_estimate=LITTLE,
        name=name,
    )(in_hbm(owner_times.T), in_hbm(table))
    return dict(zip(keys, picked))


def place(far, per_spin):
    low = lax.axis_index("tp") % per_spin
    return (far // per_spin) * per_spin + lax.bitwise_xor(jnp.int32(far % per_spin), low)


def gram_block(left, right):
    depth = left.shape[1] // 2
    real = dot_nt(left, right)
    imag = dot_nt(left[:, :depth], right[:, depth:]) - dot_nt(left[:, depth:], right[:, :depth])
    return real.astype(BF16), imag.astype(BF16)


def fold(values):
    rows, columns = values.shape
    folded = jnp.sum(values.reshape(rows // SUBLANES, SUBLANES, columns), axis=0)
    return functools.reduce(jnp.add, [folded[:, n : n + LANES] for n in range(0, columns, LANES)])


def direct_sums(diagonal, own, out, carried=None):
    real = functools.reduce(jnp.add, [block[0].astype(F32) for block in diagonal])
    imag = functools.reduce(jnp.add, [block[1].astype(F32) for block in diagonal])
    for slot in range(own.shape[0]):
        elem_re, elem_im = own[slot, 0].astype(F32), own[slot, 1].astype(F32)
        sums = [fold(elem_re * real + elem_im * imag), fold(elem_im * real - elem_re * imag)]
        for part in range(2):
            n = 2 * slot + part
            out[n] = sums[part] if carried is None else sums[part] + carried[n]


def sums_shape(count):
    return jax.ShapeDtypeStruct((count, SUBLANES, LANES), F32)


def early_blocks(spins):
    off = [(s, t) for s in range(spins - 1) for t in range(s + 1, spins - 1)]
    return off + [(s, s) for s in range(spins - 1)]


def early_kernel(eig, keys, rb_count, blocks, *refs):
    pieces, (own, flat, out, traces, sem) = refs[:-5], refs[-5:]
    rows, width = pieces[0].shape[1:]
    depth = rb_count * width
    copies = []
    for n, ((far, side), piece) in enumerate(zip(keys, pieces)):
        where = aligned(place(far, eig // rows) * rows, rows)
        for part in range(2):
            columns = pl.ds(part * depth + side * width, width)
            copies.append(pltpu.make_async_copy(piece.at[part], flat.at[where, columns], sem.at[2 * n + part]))
    for copy in copies:
        copy.start()
    for copy in copies:
        copy.wait()

    def step(n, carry):
        top, side = choose(n, [b[0] for b in blocks]), choose(n, [b[1] for b in blocks])
        out[n, 0], out[n, 1] = gram_block(flat[aligned(top * eig, eig), :], flat[aligned(side * eig, eig), :])
        return carry

    lax.fori_loop(0, len(blocks), step, 0)
    diagonal = [out.at[n] for n, block in enumerate(blocks) if block[0] == block[1]]
    direct_sums(diagonal, own, traces)


def early_gram(keys, pieces, own_elems, spins, eig, rb_count):
    blocks = early_blocks(spins)
    depth = 2 * rb_count * pieces[0].shape[2]
    return pl.pallas_call(
        functools.partial(early_kernel, eig, keys, rb_count, blocks),
        out_shape=(
            jax.ShapeDtypeStruct(((spins - 1) * eig, depth), BF16),
            jax.ShapeDtypeStruct((len(blocks), 2, eig, eig), BF16),
            sums_shape(2 * own_elems.shape[0]),
        ),
        in_specs=[ANY] * len(pieces) + [VMEM],
        out_specs=(VMEM, VMEM, VMEM),
        scratch_shapes=[pltpu.SemaphoreType.DMA((2 * len(pieces),))],
        compiler_params=params(32),
        cost_estimate=LONG,
        name="early_gram",
    )(*pieces, own_elems)


def side_columns(ref, rows, side, width, rb_count):
    return [ref[rows, (part * rb_count + side) * width : (part * rb_count + side + 1) * width] for part in range(2)]


def half_products(left, right):
    real = dot_nt(left[0], right[0]) + dot_nt(left[1], right[1])
    imag = dot_nt(left[0], right[1]) - dot_nt(left[1], right[0])
    return real, imag


def gather_last(eig, keys, others, pieces, last):
    rows, width = pieces[0].shape[1:]
    for (far, _), piece in zip(keys, pieces):
        where = aligned((place(far, eig // rows) - others * (eig // rows)) * rows, rows)
        for part in range(2):
            last[where, part * width : (part + 1) * width] = piece[part]


def late_begin_kernel(eig, keys, rb_count, flat, begun, *refs):
    pieces, (out, last) = refs[:-2], refs[-2:]
    side, width, others = keys[0][1], pieces[0].shape[2], flat.shape[0] // eig
    gather_last(eig, keys, others, pieces, last)
    right = [last[:, :width], last[:, width:]]
    for n in range(others):
        left = side_columns(flat, slice(n * eig, (n + 1) * eig), side, width, rb_count)
        out[n, 0], out[n, 1] = half_products(left, right)
    out[others, 0], out[others, 1] = half_products(right, right)


def late_begin(keys, flat, begun, pieces, spins, eig, rb_count):
    return pl.pallas_call(
        functools.partial(late_begin_kernel, eig, keys, rb_count),
        out_shape=jax.ShapeDtypeStruct((spins, 2, eig, eig), F32),
        in_specs=[VMEM, ANY] + [VMEM] * len(pieces),
        out_specs=VMEM,
        scratch_shapes=[pltpu.VMEM((eig, 2 * pieces[0].shape[2]), BF16)],
        compiler_params=params(32),
        cost_estimate=LITTLE,
        name="late_begin",
    )(flat, begun, *pieces)


def late_rows_kernel(eig, keys, rb_count, flat, partial, *refs):
    pieces, (out, last) = refs[:-2], refs[-2:]
    side, width = keys[0][1], pieces[0].shape[2]
    gather_last(eig, keys, flat.shape[0] // eig, pieces, last)
    right = [last[:, :width], last[:, width:]]
    for n in range(out.shape[0]):
        left = side_columns(flat, slice(n * eig, (n + 1) * eig), side, width, rb_count)
        real, imag = half_products(left, right)
        out[n, 0], out[n, 1] = (partial[n, 0] + real).astype(BF16), (partial[n, 1] + imag).astype(BF16)


def late_rest_kernel(eig, side, rb_count, flat, partial, last, out):
    count, width = out.shape[0] - 1, last.shape[1] // 2
    others = flat.shape[0] // eig
    right = [last[:, :width], last[:, width:]]
    for n in range(count + 1):
        spin = others - count + n
        left = right
        if n < count:
            left = side_columns(flat, slice(spin * eig, (spin + 1) * eig), side, width, rb_count)
        real, imag = half_products(left, right)
        out[n, 0], out[n, 1] = (partial[spin, 0] + real).astype(BF16), (partial[spin, 1] + imag).astype(BF16)


def late_rows(keys, flat, partial, pieces, spins, eig, rb_count):
    return pl.pallas_call(
        functools.partial(late_rows_kernel, eig, keys, rb_count),
        out_shape=(
            jax.ShapeDtypeStruct((spins // 2, 2, eig, eig), BF16),
            jax.ShapeDtypeStruct((eig, 2 * pieces[0].shape[2]), BF16),
        ),
        in_specs=[VMEM] * (2 + len(pieces)),
        out_specs=(VMEM, VMEM),
        compiler_params=params(32),
        cost_estimate=LONG,
        name="late_rows",
    )(flat, partial, *pieces)


def late_rest(side, flat, partial, last, spins, eig, rb_count):
    return pl.pallas_call(
        functools.partial(late_rest_kernel, eig, side, rb_count),
        out_shape=jax.ShapeDtypeStruct((spins - spins // 2, 2, eig, eig), BF16),
        in_specs=[VMEM] * 3,
        out_specs=VMEM,
        compiler_params=params(32),
        cost_estimate=LITTLE,
        name="late_rest",
    )(flat, partial, last)


def factors_kernel(diag_mom, elems, right_ref, left_ref, own_ref, held, sem):
    rank = lax.axis_index("rb")
    eig = held.shape[-1]
    copies = []
    for time in range(2):
        which = diag_mom[0, rank, lax.bitwise_xor(rank, time)]
        copies.append(pltpu.make_async_copy(elems.at[which], held.at[time], sem.at[time]))
    for slot in range(own_ref.shape[0]):
        copies.append(pltpu.make_async_copy(elems.at[diag_mom[0, slot, rank]], own_ref.at[slot], sem.at[2 + slot]))
    for copy in copies:
        copy.start()
    for copy in copies:
        copy.wait()
    for time in range(2):
        re, im = held[time, 0], held[time, 1]
        right_ref[time, :eig, :eig] = re
        right_ref[time, :eig, eig:] = im
        right_ref[time, eig:, :eig] = -im
        right_ref[time, eig:, eig:] = re
        re_t = re.astype(F32).T.astype(BF16)
        im_t = im.astype(F32).T.astype(BF16)
        left_ref[time, :eig, :eig] = re_t
        left_ref[time, :eig, eig:] = im_t
        left_ref[time, eig:, :eig] = im_t
        left_ref[time, eig:, eig:] = -re_t


def factors(diag_mom, src_elems):
    slots, eig = diag_mom.shape[1], src_elems.shape[-1]
    form = jax.ShapeDtypeStruct((2, 2 * eig, 2 * eig), BF16)
    return pl.pallas_call(
        factors_kernel,
        out_shape=(form, form, jax.ShapeDtypeStruct((slots, 2, eig, eig), BF16)),
        in_specs=[SMEM, ANY],
        out_specs=(VMEM, VMEM, VMEM),
        scratch_shapes=[pltpu.VMEM((2, 2, eig, eig), BF16), pltpu.SemaphoreType.DMA((2 + slots,))],
        compiler_params=params(32),
        cost_estimate=LITTLE,
        name="factors",
    )(diag_mom, src_elems)


def late_direct_kernel(rest, own, carried, out):
    direct_sums([rest.at[rest.shape[0] - 1]], own, out, carried)


def late_direct(rest, own, carried):
    return pl.pallas_call(
        late_direct_kernel,
        out_shape=sums_shape(carried.shape[0]),
        in_specs=[VMEM] * 3,
        out_specs=VMEM,
        compiler_params=params(32),
        cost_estimate=LITTLE,
        name="late_direct",
    )(rest, own, carried)


def cross_kernel(offs, own, other, right, left, *refs):
    carried, out = refs[:-1], refs[-1]
    eig = own.shape[-1]
    if len(other.shape) > len(own.shape):
        other = other.at[1 - lax.axis_index("rb")]
    real, imag = [], []

    def add(x, y, count, from_right, from_left):
        rows = [jnp.concatenate([x[n, 0], x[n, 1]], axis=1) for n in range(count)]
        product = dot(jnp.concatenate(rows, axis=0), from_right)
        for n in range(count):
            partner = dot(from_left, y[n].reshape(2 * eig, eig))
            mine = product[n * eig : (n + 1) * eig]
            p_re, p_im = mine[:, :eig], mine[:, eig:]
            w_re, w_im = partner[:eig], partner[eig:]
            real.append(fold(p_re * w_re - p_im * w_im))
            imag.append(fold(p_re * w_im + p_im * w_re))

    add(other, own, own.shape[0], right[1], left[0])
    add(own, other, offs, right[0], left[1])
    out[0] = functools.reduce(jnp.add, real + [ref[0] for ref in carried])
    out[1] = functools.reduce(jnp.add, imag + [ref[1] for ref in carried])


def cross_traces(offs, own, other, right, left, carried, name):
    return pl.pallas_call(
        functools.partial(cross_kernel, offs),
        out_shape=sums_shape(2),
        in_specs=[VMEM] * (4 + len(carried)),
        out_specs=VMEM,
        compiler_params=params(32),
        cost_estimate=LITTLE,
        name=name,
    )(own, other, right, left, *carried)


def last_cross_kernel(offs, own, other, right, left, direct, carried, out):
    count = direct.shape[0]
    for n in range(count):
        out[n] = direct[n]
    cross_kernel(offs, own, other, right, left, carried, out.at[pl.ds(count, 2)])


def last_cross(offs, own, other, right, left, direct, carried):
    return pl.pallas_call(
        functools.partial(last_cross_kernel, offs),
        out_shape=sums_shape(direct.shape[0] + 2),
        in_specs=[VMEM] * 6,
        out_specs=VMEM,
        compiler_params=params(32),
        cost_estimate=LITTLE,
        name="last_cross",
    )(own, other, right, left, direct, carried)


def final_kernel(slots, mine, theirs, count, out):
    rank = lax.axis_index("rb")
    lane = lax.broadcasted_iota(jnp.int32, (1, LANES), 1)

    def totals(ref):
        rows = jnp.concatenate([jnp.sum(ref[n], axis=0, keepdims=True) for n in range(ref.shape[0])], axis=0)
        sums = jnp.broadcast_to(jnp.sum(rows, axis=1, keepdims=True), rows.shape)
        return [sums[n : n + 1] for n in range(ref.shape[0])]

    def put(slot, kind, re, im):
        value = jnp.where(lane == 0, re, im) * 0.25
        out[0, slot, kind : kind + 1, :] = jnp.where(slot < count[0], value, 0.0)[:, :2]

    m, t = totals(mine), totals(theirs)
    for slot in range(slots):
        m_re, m_im, t_re, t_im = m[2 * slot], m[2 * slot + 1], t[2 * slot], t[2 * slot + 1]
        put(slot, 0, m_re * t_re - m_im * t_im, m_re * t_im + m_im * t_re)
        here = rank == slot
        put(slot, 1, jnp.where(here, m[2 * slots], t[2 * slots]), jnp.where(here, m[2 * slots + 1], t[2 * slots + 1]))


def final(mine, theirs, diag_count, slots):
    return pl.pallas_call(
        functools.partial(final_kernel, slots),
        out_shape=jax.ShapeDtypeStruct((1, slots, 2, 2), F32),
        in_specs=[VMEM, VMEM, SMEM],
        out_specs=VMEM,
        compiler_params=params(32),
        name="final",
    )(mine, theirs, diag_count)


def shards(peram, src_elems, owner_times, diag_mom, diag_count):
    tp_count, rb_count = lax.axis_size("tp"), lax.axis_size("rb")
    eig = src_elems.shape[-1]
    spins = tp_count * peram.shape[0] // eig
    slots = diag_mom.shape[1]

    head, tail, late, own = travel_order(tp_count, rb_count)
    early_keys = head + tail
    picked = pick(owner_times, peram, head, "pick_head", [jax.ShapeDtypeStruct((4, *peram.shape), BF16)])
    picked.update(pick(owner_times, peram, tail + late + own, "pick_tail", []))

    def send(key):
        far, side = key
        pairs = [
            (tp * rb_count + rb, (tp ^ far) * rb_count + (rb ^ side))
            for tp in range(tp_count)
            for rb in range(rb_count)
        ]
        return lax.ppermute(picked[key], ("tp", "rb"), pairs)

    swap = [(rb, rb ^ 1) for rb in range(rb_count)]
    right, left, own_elems = factors(diag_mom, src_elems)
    arrived = [send(key) for key in early_keys] + [picked[key] for key in own]
    flat, early, direct = early_gram(early_keys + own, arrived, own_elems, spins, eig, rb_count)
    early_both = lax.all_to_all(jnp.stack([early] * rb_count), "rb", 0, 0)
    offs = early.shape[0] - (spins - 1)
    begun = cross_traces(offs, early, early_both, right, left, [], "early_cross")

    halves = [[key for key in late if key[1] == side] for side in range(rb_count)]
    sent = [[send(key) for key in keys] for keys in halves]
    half = late_begin(halves[0], flat, begun, sent[0], spins, eig, rb_count)
    blocks, last = late_rows(halves[1], flat, half, sent[1], spins, eig, rb_count)
    swapped = lax.ppermute(blocks, "rb", swap)
    rest = late_rest(1, flat, half, last, spins, eig, rb_count)
    rest_swapped = lax.ppermute(rest, "rb", swap)
    traces = late_direct(rest, own_elems, direct)
    partial = cross_traces(blocks.shape[0], blocks, swapped, right, left, [begun], "late_cross")
    mine = last_cross(rest.shape[0] - 1, rest, rest_swapped, right, left, traces, partial)
    theirs = lax.ppermute(mine, "rb", swap)
    return final(mine, theirs, diag_count, slots)


def solution(mesh):
    in_specs = (
        P(("grp", "tp"), None, None, "rb"),
        P("grp", None, None, None),
        P("grp", None),
        P(("grp", "tp"), None, None),
        P(("grp", "tp")),
    )
    out_specs = P(("grp", "tp"), None, None, None)
    return jax.shard_map(shards, mesh=mesh, in_specs=in_specs, out_specs=out_specs, check_vma=False)
```

```python
import functools

import jax
import jax.numpy as jnp
from jax import lax
from jax.experimental import pallas as pl
from jax.experimental.pallas import tpu as pltpu
from jax.sharding import PartitionSpec as P

F32 = jnp.float32
BF16 = jnp.bfloat16
ANY = pl.BlockSpec(memory_space=pl.ANY)
SMEM = pl.BlockSpec(memory_space=pltpu.SMEM)
VMEM = pl.BlockSpec(memory_space=pltpu.VMEM)
SUBLANES = 8
LANES = 128
STEP = 16
MIB = 1 << 20
LITTLE = pl.CostEstimate(flops=1000, bytes_accessed=1000, transcendentals=0)
LONG = pl.CostEstimate(flops=5 * 10**10, bytes_accessed=1000, transcendentals=0)


def in_hbm(array):
    return pltpu.with_memory_space_constraint(array, pltpu.HBM)


def params(mib):
    return pltpu.CompilerParams(vmem_limit_bytes=mib * MIB)


def dot(left, right):
    return jnp.dot(left, right, preferred_element_type=F32)


def dot_nt(left, right):
    return lax.dot_general(left, right, (((1,), (1,)), ((), ())), preferred_element_type=F32)


def choose(index, values):
    out = jnp.int32(values[0])
    for n in range(1, len(values)):
        out = jnp.where(index == n, jnp.int32(values[n]), out)
    return out


def aligned(start, size):
    return pl.ds(pl.multiple_of(start, size), size)


def travel_order(tp_count, rb_count, rows):
    half, quarter = tp_count // 2, tp_count // 4
    cut = rows // 2 if rows % (2 * STEP) == 0 else rows

    def both(distances):
        return [(far, side, 0, rows) for far in distances for side in range(rb_count)]

    long, late = both(range(half, half + quarter)), both(range(half + quarter, tp_count))
    near, rest = both(reversed(range(quarter, half))), both(range(1, quarter))
    own, other = (0, 0, 0, rows), [(0, side, 0, rows) for side in range(1, rb_count)]
    step, part = len(long) // 4, len(rest) // 2
    first = long[: 2 * step]
    head = [(far, side, 0, cut) for far, side, _, _ in first]
    tail = [(far, side, cut, rows - cut) for far, side, _, _ in first if cut < rows]
    tail += near[: 2 * step] + long[2 * step : 3 * step]
    tail += rest[:part] + other + near[2 * step : 3 * step] + long[3 * step :] + near[3 * step :] + rest[part:]
    return head, tail, late, [own]


def pick_kernel(keys, times, table, *refs):
    outs, (held, wide, taken_times, sem, times_sem) = refs[:-5], refs[-5:]
    tp_rank, rb_rank = lax.axis_index("tp"), lax.axis_index("rb")
    packed = table.shape[2]
    ends = sorted({end for _, _, start, size in keys for end in (start, start + size)})

    def fetch(chunk):
        where = aligned(chunk * STEP, STEP)
        return pltpu.make_async_copy(table.at[where], held.at[where], sem.at[chunk])

    copy = pltpu.make_async_copy(times, taken_times, times_sem)
    copy.start()
    for chunk in range(ends[0] // STEP, ends[-1] // STEP):
        fetch(chunk).start()
    copy.wait()

    def step(covered, chunk, carry):
        fetch(chunk).wait()
        for n, (key, out) in enumerate(covered):
            far, side, start, _ = key
            time = taken_times[lax.bitwise_xor(rb_rank, side), lax.bitwise_xor(tp_rank, far)]
            slot = n % wide.shape[0]
            wide[slot] = held[aligned(chunk * STEP, STEP), time].astype(F32).reshape(STEP * packed, LANES)
            where = aligned(chunk * STEP - start, STEP)
            for tile in range(packed // 2):
                for part in range(2):
                    taken = wide[slot, pl.ds(2 * tile + part, STEP, stride=packed), :]
                    out[part, where, tile * LANES : (tile + 1) * LANES] = taken.astype(BF16)
        return carry

    for low, high in zip(ends, ends[1:]):
        covered = [(key, out) for key, out in zip(keys, outs) if key[2] <= low and high <= key[2] + key[3]]
        lax.fori_loop(low // STEP, high // STEP, functools.partial(step, covered), 0)


def pick(owner_times, peram, keys, name, spare):
    rows, times, parts, width = peram.shape
    tiles = width // LANES
    table = peram.reshape(rows, times, parts, tiles, LANES).swapaxes(2, 3)
    table = table.reshape(rows, times, tiles * parts, LANES)
    picked = pl.pallas_call(
        functools.partial(pick_kernel, keys),
        out_shape=[jax.ShapeDtypeStruct((parts, size, width), BF16) for _, _, _, size in keys] + spare,
        in_specs=[ANY, ANY],
        out_specs=[VMEM] * len(keys) + [ANY] * len(spare),
        scratch_shapes=[
            pltpu.VMEM(table.shape, BF16),
            pltpu.VMEM((4, STEP * tiles * parts, LANES), F32),
            pltpu.SMEM(owner_times.shape[::-1], jnp.int32),
            pltpu.SemaphoreType.DMA((rows // STEP,)),
            pltpu.SemaphoreType.DMA,
        ],
        compiler_params=params(32),
        cost_estimate=LITTLE,
        name=name,
    )(in_hbm(owner_times.T), in_hbm(table))
    return dict(zip(keys, picked))


def place(far, per_spin):
    low = lax.axis_index("tp") % per_spin
    return (far // per_spin) * per_spin + lax.bitwise_xor(jnp.int32(far % per_spin), low)


def gram_block(left, right):
    depth = left.shape[1] // 2
    real = dot_nt(left, right)
    imag = dot_nt(left[:, :depth], right[:, depth:]) - dot_nt(left[:, depth:], right[:, :depth])
    return real.astype(BF16), imag.astype(BF16)


def fold(values):
    rows, columns = values.shape
    folded = jnp.sum(values.reshape(rows // SUBLANES, SUBLANES, columns), axis=0)
    return functools.reduce(jnp.add, [folded[:, n : n + LANES] for n in range(0, columns, LANES)])


def direct_sums(diagonal, own, out, carried=None):
    real = functools.reduce(jnp.add, [block[0].astype(F32) for block in diagonal])
    imag = functools.reduce(jnp.add, [block[1].astype(F32) for block in diagonal])
    for slot in range(own.shape[0]):
        elem_re, elem_im = own[slot, 0].astype(F32), own[slot, 1].astype(F32)
        sums = [fold(elem_re * real + elem_im * imag), fold(elem_im * real - elem_re * imag)]
        for part in range(2):
            n = 2 * slot + part
            out[n] = sums[part] if carried is None else sums[part] + carried[n]


def sums_shape(count):
    return jax.ShapeDtypeStruct((count, SUBLANES, LANES), F32)


def early_blocks(spins):
    off = [(s, t) for s in range(spins - 1) for t in range(s + 1, spins - 1)]
    return off + [(s, s) for s in range(spins - 1)]


def early_kernel(eig, keys, rb_count, rows, blocks, *refs):
    pieces, (own, flat, out, traces, sem) = refs[:-5], refs[-5:]
    width = pieces[0].shape[2]
    depth = rb_count * width
    copies = []
    for n, ((far, side, start, size), piece) in enumerate(zip(keys, pieces)):
        where = aligned(place(far, eig // rows) * rows + start, size)
        for part in range(2):
            columns = pl.ds(part * depth + side * width, width)
            copies.append(pltpu.make_async_copy(piece.at[part], flat.at[where, columns], sem.at[2 * n + part]))
    for copy in copies:
        copy.start()
    for copy in copies:
        copy.wait()

    def step(n, carry):
        top, side = choose(n, [b[0] for b in blocks]), choose(n, [b[1] for b in blocks])
        out[n, 0], out[n, 1] = gram_block(flat[aligned(top * eig, eig), :], flat[aligned(side * eig, eig), :])
        return carry

    lax.fori_loop(0, len(blocks), step, 0)
    diagonal = [out.at[n] for n, block in enumerate(blocks) if block[0] == block[1]]
    direct_sums(diagonal, own, traces)


def early_gram(keys, pieces, own_elems, spins, eig, rb_count, rows):
    blocks = early_blocks(spins)
    depth = 2 * rb_count * pieces[0].shape[2]
    return pl.pallas_call(
        functools.partial(early_kernel, eig, keys, rb_count, rows, blocks),
        out_shape=(
            jax.ShapeDtypeStruct(((spins - 1) * eig, depth), BF16),
            jax.ShapeDtypeStruct((len(blocks), 2, eig, eig), BF16),
            sums_shape(2 * own_elems.shape[0]),
        ),
        in_specs=[ANY] * len(pieces) + [VMEM],
        out_specs=(VMEM, VMEM, VMEM),
        scratch_shapes=[pltpu.SemaphoreType.DMA((2 * len(pieces),))],
        compiler_params=params(32),
        cost_estimate=LONG,
        name="early_gram",
    )(*pieces, own_elems)


def side_columns(ref, rows, side, width, rb_count):
    return [ref[rows, (part * rb_count + side) * width : (part * rb_count + side + 1) * width] for part in range(2)]


def half_products(left, right):
    real = dot_nt(left[0], right[0]) + dot_nt(left[1], right[1])
    imag = dot_nt(left[0], right[1]) - dot_nt(left[1], right[0])
    return real, imag


def gather_last(eig, keys, others, pieces, last):
    rows, width = pieces[0].shape[1:]
    for (far, _, _, _), piece in zip(keys, pieces):
        where = aligned((place(far, eig // rows) - others * (eig // rows)) * rows, rows)
        for part in range(2):
            last[where, part * width : (part + 1) * width] = piece[part]


def late_begin_kernel(eig, keys, rb_count, flat, begun, *refs):
    pieces, (out, last) = refs[:-2], refs[-2:]
    side, width, others = keys[0][1], pieces[0].shape[2], flat.shape[0] // eig
    gather_last(eig, keys, others, pieces, last)
    right = [last[:, :width], last[:, width:]]
    for n in range(others):
        left = side_columns(flat, slice(n * eig, (n + 1) * eig), side, width, rb_count)
        out[n, 0], out[n, 1] = half_products(left, right)
    out[others, 0], out[others, 1] = half_products(right, right)


def late_begin(keys, flat, begun, pieces, spins, eig, rb_count):
    return pl.pallas_call(
        functools.partial(late_begin_kernel, eig, keys, rb_count),
        out_shape=jax.ShapeDtypeStruct((spins, 2, eig, eig), F32),
        in_specs=[VMEM, ANY] + [VMEM] * len(pieces),
        out_specs=VMEM,
        scratch_shapes=[pltpu.VMEM((eig, 2 * pieces[0].shape[2]), BF16)],
        compiler_params=params(32),
        cost_estimate=LITTLE,
        name="late_begin",
    )(flat, begun, *pieces)


def late_rows_kernel(eig, keys, rb_count, flat, partial, *refs):
    pieces, (out, last) = refs[:-2], refs[-2:]
    side, width = keys[0][1], pieces[0].shape[2]
    gather_last(eig, keys, flat.shape[0] // eig, pieces, last)
    right = [last[:, :width], last[:, width:]]
    for n in range(out.shape[0]):
        left = side_columns(flat, slice(n * eig, (n + 1) * eig), side, width, rb_count)
        real, imag = half_products(left, right)
        out[n, 0], out[n, 1] = (partial[n, 0] + real).astype(BF16), (partial[n, 1] + imag).astype(BF16)


def late_rest_kernel(eig, side, rb_count, flat, partial, last, out):
    count, width = out.shape[0] - 1, last.shape[1] // 2
    others = flat.shape[0] // eig
    right = [last[:, :width], last[:, width:]]
    for n in range(count + 1):
        spin = others - count + n
        left = right
        if n < count:
            left = side_columns(flat, slice(spin * eig, (spin + 1) * eig), side, width, rb_count)
        real, imag = half_products(left, right)
        out[n, 0], out[n, 1] = (partial[spin, 0] + real).astype(BF16), (partial[spin, 1] + imag).astype(BF16)


def late_rows(keys, flat, partial, pieces, spins, eig, rb_count):
    return pl.pallas_call(
        functools.partial(late_rows_kernel, eig, keys, rb_count),
        out_shape=(
            jax.ShapeDtypeStruct((spins // 2, 2, eig, eig), BF16),
            jax.ShapeDtypeStruct((eig, 2 * pieces[0].shape[2]), BF16),
        ),
        in_specs=[VMEM] * (2 + len(pieces)),
        out_specs=(VMEM, VMEM),
        compiler_params=params(32),
        cost_estimate=LONG,
        name="late_rows",
    )(flat, partial, *pieces)


def late_rest(side, flat, partial, last, spins, eig, rb_count):
    return pl.pallas_call(
        functools.partial(late_rest_kernel, eig, side, rb_count),
        out_shape=jax.ShapeDtypeStruct((spins - spins // 2, 2, eig, eig), BF16),
        in_specs=[VMEM] * 3,
        out_specs=VMEM,
        compiler_params=params(32),
        cost_estimate=LITTLE,
        name="late_rest",
    )(flat, partial, last)


def factors_kernel(diag_mom, elems, right_ref, left_ref, own_ref, held, sem):
    rank = lax.axis_index("rb")
    eig = held.shape[-1]
    copies = []
    for time in range(2):
        which = diag_mom[0, rank, lax.bitwise_xor(rank, time)]
        copies.append(pltpu.make_async_copy(elems.at[which], held.at[time], sem.at[time]))
    for slot in range(own_ref.shape[0]):
        copies.append(pltpu.make_async_copy(elems.at[diag_mom[0, slot, rank]], own_ref.at[slot], sem.at[2 + slot]))
    for copy in copies:
        copy.start()
    for copy in copies:
        copy.wait()
    for time in range(2):
        re, im = held[time, 0], held[time, 1]
        right_ref[time, :eig, :eig] = re
        right_ref[time, :eig, eig:] = im
        right_ref[time, eig:, :eig] = -im
        right_ref[time, eig:, eig:] = re
        re_t = re.astype(F32).T.astype(BF16)
        im_t = im.astype(F32).T.astype(BF16)
        left_ref[time, :eig, :eig] = re_t
        left_ref[time, :eig, eig:] = im_t
        left_ref[time, eig:, :eig] = im_t
        left_ref[time, eig:, eig:] = -re_t


def factors(diag_mom, src_elems):
    slots, eig = diag_mom.shape[1], src_elems.shape[-1]
    form = jax.ShapeDtypeStruct((2, 2 * eig, 2 * eig), BF16)
    return pl.pallas_call(
        factors_kernel,
        out_shape=(form, form, jax.ShapeDtypeStruct((slots, 2, eig, eig), BF16)),
        in_specs=[SMEM, ANY],
        out_specs=(VMEM, VMEM, VMEM),
        scratch_shapes=[pltpu.VMEM((2, 2, eig, eig), BF16), pltpu.SemaphoreType.DMA((2 + slots,))],
        compiler_params=params(32),
        cost_estimate=LITTLE,
        name="factors",
    )(diag_mom, src_elems)


def late_direct_kernel(rest, own, carried, out):
    direct_sums([rest.at[rest.shape[0] - 1]], own, out, carried)


def late_direct(rest, own, carried):
    return pl.pallas_call(
        late_direct_kernel,
        out_shape=sums_shape(carried.shape[0]),
        in_specs=[VMEM] * 3,
        out_specs=VMEM,
        compiler_params=params(32),
        cost_estimate=LITTLE,
        name="late_direct",
    )(rest, own, carried)


def cross_kernel(offs, own, other, right, left, *refs):
    carried, out = refs[:-1], refs[-1]
    eig = own.shape[-1]
    if len(other.shape) > len(own.shape):
        other = other.at[1 - lax.axis_index("rb")]
    real, imag = [], []

    def add(x, y, count, from_right, from_left):
        rows = [jnp.concatenate([x[n, 0], x[n, 1]], axis=1) for n in range(count)]
        product = dot(jnp.concatenate(rows, axis=0), from_right)
        for n in range(count):
            partner = dot(from_left, y[n].reshape(2 * eig, eig))
            mine = product[n * eig : (n + 1) * eig]
            p_re, p_im = mine[:, :eig], mine[:, eig:]
            w_re, w_im = partner[:eig], partner[eig:]
            real.append(fold(p_re * w_re - p_im * w_im))
            imag.append(fold(p_re * w_im + p_im * w_re))

    add(other, own, own.shape[0], right[1], left[0])
    add(own, other, offs, right[0], left[1])
    out[0] = functools.reduce(jnp.add, real + [ref[0] for ref in carried])
    out[1] = functools.reduce(jnp.add, imag + [ref[1] for ref in carried])


def cross_traces(offs, own, other, right, left, carried, name):
    return pl.pallas_call(
        functools.partial(cross_kernel, offs),
        out_shape=sums_shape(2),
        in_specs=[VMEM] * (4 + len(carried)),
        out_specs=VMEM,
        compiler_params=params(32),
        cost_estimate=LITTLE,
        name=name,
    )(own, other, right, left, *carried)


def last_cross_kernel(offs, own, other, right, left, direct, carried, out):
    count = direct.shape[0]
    for n in range(count):
        out[n] = direct[n]
    cross_kernel(offs, own, other, right, left, carried, out.at[pl.ds(count, 2)])


def last_cross(offs, own, other, right, left, direct, carried):
    return pl.pallas_call(
        functools.partial(last_cross_kernel, offs),
        out_shape=sums_shape(direct.shape[0] + 2),
        in_specs=[VMEM] * 6,
        out_specs=VMEM,
        compiler_params=params(32),
        cost_estimate=LITTLE,
        name="last_cross",
    )(own, other, right, left, direct, carried)


def final_kernel(slots, mine, theirs, count, out):
    rank = lax.axis_index("rb")
    lane = lax.broadcasted_iota(jnp.int32, (1, LANES), 1)

    def totals(ref):
        rows = jnp.concatenate([jnp.sum(ref[n], axis=0, keepdims=True) for n in range(ref.shape[0])], axis=0)
        sums = jnp.broadcast_to(jnp.sum(rows, axis=1, keepdims=True), rows.shape)
        return [sums[n : n + 1] for n in range(ref.shape[0])]

    def put(slot, kind, re, im):
        value = jnp.where(lane == 0, re, im) * 0.25
        out[0, slot, kind : kind + 1, :] = jnp.where(slot < count[0], value, 0.0)[:, :2]

    m, t = totals(mine), totals(theirs)
    for slot in range(slots):
        m_re, m_im, t_re, t_im = m[2 * slot], m[2 * slot + 1], t[2 * slot], t[2 * slot + 1]
        put(slot, 0, m_re * t_re - m_im * t_im, m_re * t_im + m_im * t_re)
        here = rank == slot
        put(slot, 1, jnp.where(here, m[2 * slots], t[2 * slots]), jnp.where(here, m[2 * slots + 1], t[2 * slots + 1]))


def final(mine, theirs, diag_count, slots):
    return pl.pallas_call(
        functools.partial(final_kernel, slots),
        out_shape=jax.ShapeDtypeStruct((1, slots, 2, 2), F32),
        in_specs=[VMEM, VMEM, SMEM],
        out_specs=VMEM,
        compiler_params=params(32),
        name="final",
    )(mine, theirs, diag_count)


def shards(peram, src_elems, owner_times, diag_mom, diag_count):
    tp_count, rb_count = lax.axis_size("tp"), lax.axis_size("rb")
    eig = src_elems.shape[-1]
    spins = tp_count * peram.shape[0] // eig
    slots = diag_mom.shape[1]

    rows = peram.shape[0]
    head, tail, late, own = travel_order(tp_count, rb_count, rows)
    early_keys = head + tail
    picked = pick(owner_times, peram, head, "pick_head", [jax.ShapeDtypeStruct((4, *peram.shape), BF16)])
    picked.update(pick(owner_times, peram, tail + late + own, "pick_tail", []))

    def send(key):
        far, side, _, _ = key
        pairs = [
            (tp * rb_count + rb, (tp ^ far) * rb_count + (rb ^ side))
            for tp in range(tp_count)
            for rb in range(rb_count)
        ]
        return lax.ppermute(picked[key], ("tp", "rb"), pairs)

    swap = [(rb, rb ^ 1) for rb in range(rb_count)]
    right, left, own_elems = factors(diag_mom, src_elems)
    arrived = [send(key) for key in early_keys] + [picked[key] for key in own]
    flat, early, direct = early_gram(early_keys + own, arrived, own_elems, spins, eig, rb_count, rows)
    early_both = lax.all_to_all(jnp.stack([early] * rb_count), "rb", 0, 0)
    offs = early.shape[0] - (spins - 1)
    begun = cross_traces(offs, early, early_both, right, left, [], "early_cross")

    halves = [[key for key in late if key[1] == side] for side in range(rb_count)]
    sent = [[send(key) for key in keys] for keys in halves]
    half = late_begin(halves[0], flat, begun, sent[0], spins, eig, rb_count)
    blocks, last = late_rows(halves[1], flat, half, sent[1], spins, eig, rb_count)
    swapped = lax.ppermute(blocks, "rb", swap)
    rest = late_rest(1, flat, half, last, spins, eig, rb_count)
    rest_swapped = lax.ppermute(rest, "rb", swap)
    traces = late_direct(rest, own_elems, direct)
    partial = cross_traces(blocks.shape[0], blocks, swapped, right, left, [begun], "late_cross")
    mine = last_cross(rest.shape[0] - 1, rest, rest_swapped, right, left, traces, partial)
    theirs = lax.ppermute(mine, "rb", swap)
    return final(mine, theirs, diag_count, slots)


def solution(mesh):
    in_specs = (
        P(("grp", "tp"), None, None, "rb"),
        P("grp", None, None, None),
        P("grp", None),
        P(("grp", "tp"), None, None),
        P(("grp", "tp")),
    )
    out_specs = P(("grp", "tp"), None, None, None)
    return jax.shard_map(shards, mesh=mesh, in_specs=in_specs, out_specs=out_specs, check_vma=False)
```

```python
import functools

import jax
import jax.numpy as jnp
from jax import lax
from jax.experimental import pallas as pl
from jax.experimental.pallas import tpu as pltpu
from jax.sharding import PartitionSpec as P

F32 = jnp.float32
BF16 = jnp.bfloat16
ANY = pl.BlockSpec(memory_space=pl.ANY)
SMEM = pl.BlockSpec(memory_space=pltpu.SMEM)
VMEM = pl.BlockSpec(memory_space=pltpu.VMEM)
SUBLANES = 8
LANES = 128
STEP = 16
MIB = 1 << 20
LITTLE = pl.CostEstimate(flops=1000, bytes_accessed=1000, transcendentals=0)
LONG = pl.CostEstimate(flops=5 * 10**10, bytes_accessed=1000, transcendentals=0)


def in_hbm(array):
    return pltpu.with_memory_space_constraint(array, pltpu.HBM)


def params(mib):
    return pltpu.CompilerParams(vmem_limit_bytes=mib * MIB)


def dot(left, right):
    return jnp.dot(left, right, preferred_element_type=F32)


def dot_nt(left, right):
    return lax.dot_general(left, right, (((1,), (1,)), ((), ())), preferred_element_type=F32)


def choose(index, values):
    out = jnp.int32(values[0])
    for n in range(1, len(values)):
        out = jnp.where(index == n, jnp.int32(values[n]), out)
    return out


def aligned(start, size):
    return pl.ds(pl.multiple_of(start, size), size)


def travel_order(tp_count, rb_count, rows):
    half, quarter = tp_count // 2, tp_count // 4
    cut = rows // 2 if rows % (2 * STEP) == 0 else rows

    def both(distances):
        return [(far, side, 0, rows) for far in distances for side in range(rb_count)]

    long, late = both(range(half, half + quarter)), both(range(half + quarter, tp_count))
    near, rest = both(reversed(range(quarter, half))), both(range(1, quarter))
    own, other = (0, 0, 0, rows), [(0, side, 0, rows) for side in range(1, rb_count)]
    step, part = len(long) // 4, len(rest) // 2
    first = long[:step]
    head = [(far, side, 0, cut) for far, side, _, _ in first]
    tail = [(far, side, cut, rows - cut) for far, side, _, _ in first if cut < rows]
    tail += long[step : 2 * step] + near[: 2 * step] + long[2 * step : 3 * step]
    tail += rest[:part] + other + near[2 * step : 3 * step] + long[3 * step :] + near[3 * step :] + rest[part:]
    return head, tail, late, [own]


def pick_kernel(keys, times, table, *refs):
    outs, (held, wide, taken_times, sem, times_sem) = refs[:-5], refs[-5:]
    tp_rank, rb_rank = lax.axis_index("tp"), lax.axis_index("rb")
    packed = table.shape[2]
    ends = sorted({end for _, _, start, size in keys for end in (start, start + size)})

    def fetch(chunk):
        where = aligned(chunk * STEP, STEP)
        return pltpu.make_async_copy(table.at[where], held.at[where], sem.at[chunk])

    copy = pltpu.make_async_copy(times, taken_times, times_sem)
    copy.start()
    for chunk in range(ends[0] // STEP, ends[-1] // STEP):
        fetch(chunk).start()
    copy.wait()

    def step(covered, chunk, carry):
        fetch(chunk).wait()
        for n, (key, out) in enumerate(covered):
            far, side, start, _ = key
            time = taken_times[lax.bitwise_xor(rb_rank, side), lax.bitwise_xor(tp_rank, far)]
            slot = n % wide.shape[0]
            wide[slot] = held[aligned(chunk * STEP, STEP), time].astype(F32).reshape(STEP * packed, LANES)
            where = aligned(chunk * STEP - start, STEP)
            for tile in range(packed // 2):
                for part in range(2):
                    taken = wide[slot, pl.ds(2 * tile + part, STEP, stride=packed), :]
                    out[part, where, tile * LANES : (tile + 1) * LANES] = taken.astype(BF16)
        return carry

    for low, high in zip(ends, ends[1:]):
        covered = [(key, out) for key, out in zip(keys, outs) if key[2] <= low and high <= key[2] + key[3]]
        lax.fori_loop(low // STEP, high // STEP, functools.partial(step, covered), 0)


def pick(owner_times, peram, keys, name, spare):
    rows, times, parts, width = peram.shape
    tiles = width // LANES
    table = peram.reshape(rows, times, parts, tiles, LANES).swapaxes(2, 3)
    table = table.reshape(rows, times, tiles * parts, LANES)
    picked = pl.pallas_call(
        functools.partial(pick_kernel, keys),
        out_shape=[jax.ShapeDtypeStruct((parts, size, width), BF16) for _, _, _, size in keys] + spare,
        in_specs=[ANY, ANY],
        out_specs=[VMEM] * len(keys) + [ANY] * len(spare),
        scratch_shapes=[
            pltpu.VMEM(table.shape, BF16),
            pltpu.VMEM((4, STEP * tiles * parts, LANES), F32),
            pltpu.SMEM(owner_times.shape[::-1], jnp.int32),
            pltpu.SemaphoreType.DMA((rows // STEP,)),
            pltpu.SemaphoreType.DMA,
        ],
        compiler_params=params(32),
        cost_estimate=LITTLE,
        name=name,
    )(in_hbm(owner_times.T), in_hbm(table))
    return dict(zip(keys, picked))


def place(far, per_spin):
    low = lax.axis_index("tp") % per_spin
    return (far // per_spin) * per_spin + lax.bitwise_xor(jnp.int32(far % per_spin), low)


def gram_block(left, right):
    depth = left.shape[1] // 2
    real = dot_nt(left, right)
    imag = dot_nt(left[:, :depth], right[:, depth:]) - dot_nt(left[:, depth:], right[:, :depth])
    return real.astype(BF16), imag.astype(BF16)


def fold(values):
    rows, columns = values.shape
    folded = jnp.sum(values.reshape(rows // SUBLANES, SUBLANES, columns), axis=0)
    return functools.reduce(jnp.add, [folded[:, n : n + LANES] for n in range(0, columns, LANES)])


def direct_sums(diagonal, own, out, carried=None):
    real = functools.reduce(jnp.add, [block[0].astype(F32) for block in diagonal])
    imag = functools.reduce(jnp.add, [block[1].astype(F32) for block in diagonal])
    for slot in range(own.shape[0]):
        elem_re, elem_im = own[slot, 0].astype(F32), own[slot, 1].astype(F32)
        sums = [fold(elem_re * real + elem_im * imag), fold(elem_im * real - elem_re * imag)]
        for part in range(2):
            n = 2 * slot + part
            out[n] = sums[part] if carried is None else sums[part] + carried[n]


def sums_shape(count):
    return jax.ShapeDtypeStruct((count, SUBLANES, LANES), F32)


def early_blocks(spins):
    off = [(s, t) for s in range(spins - 1) for t in range(s + 1, spins - 1)]
    return off + [(s, s) for s in range(spins - 1)]


def early_kernel(eig, keys, rb_count, rows, blocks, *refs):
    pieces, (own, flat, out, traces, sem) = refs[:-5], refs[-5:]
    width = pieces[0].shape[2]
    depth = rb_count * width
    copies = []
    for n, ((far, side, start, size), piece) in enumerate(zip(keys, pieces)):
        where = aligned(place(far, eig // rows) * rows + start, size)
        for part in range(2):
            columns = pl.ds(part * depth + side * width, width)
            copies.append(pltpu.make_async_copy(piece.at[part], flat.at[where, columns], sem.at[2 * n + part]))
    for copy in copies:
        copy.start()
    for copy in copies:
        copy.wait()

    def step(n, carry):
        top, side = choose(n, [b[0] for b in blocks]), choose(n, [b[1] for b in blocks])
        out[n, 0], out[n, 1] = gram_block(flat[aligned(top * eig, eig), :], flat[aligned(side * eig, eig), :])
        return carry

    lax.fori_loop(0, len(blocks), step, 0)
    diagonal = [out.at[n] for n, block in enumerate(blocks) if block[0] == block[1]]
    direct_sums(diagonal, own, traces)


def early_gram(keys, pieces, own_elems, spins, eig, rb_count, rows):
    blocks = early_blocks(spins)
    depth = 2 * rb_count * pieces[0].shape[2]
    return pl.pallas_call(
        functools.partial(early_kernel, eig, keys, rb_count, rows, blocks),
        out_shape=(
            jax.ShapeDtypeStruct(((spins - 1) * eig, depth), BF16),
            jax.ShapeDtypeStruct((len(blocks), 2, eig, eig), BF16),
            sums_shape(2 * own_elems.shape[0]),
        ),
        in_specs=[ANY] * len(pieces) + [VMEM],
        out_specs=(VMEM, VMEM, VMEM),
        scratch_shapes=[pltpu.SemaphoreType.DMA((2 * len(pieces),))],
        compiler_params=params(32),
        cost_estimate=LONG,
        name="early_gram",
    )(*pieces, own_elems)


def side_columns(ref, rows, side, width, rb_count):
    return [ref[rows, (part * rb_count + side) * width : (part * rb_count + side + 1) * width] for part in range(2)]


def half_products(left, right):
    real = dot_nt(left[0], right[0]) + dot_nt(left[1], right[1])
    imag = dot_nt(left[0], right[1]) - dot_nt(left[1], right[0])
    return real, imag


def gather_last(eig, keys, others, pieces, last):
    rows, width = pieces[0].shape[1:]
    for (far, _, _, _), piece in zip(keys, pieces):
        where = aligned((place(far, eig // rows) - others * (eig // rows)) * rows, rows)
        for part in range(2):
            last[where, part * width : (part + 1) * width] = piece[part]


def late_begin_kernel(eig, keys, rb_count, flat, begun, *refs):
    pieces, (out, last) = refs[:-2], refs[-2:]
    side, width, others = keys[0][1], pieces[0].shape[2], flat.shape[0] // eig
    gather_last(eig, keys, others, pieces, last)
    right = [last[:, :width], last[:, width:]]
    for n in range(others):
        left = side_columns(flat, slice(n * eig, (n + 1) * eig), side, width, rb_count)
        out[n, 0], out[n, 1] = half_products(left, right)
    out[others, 0], out[others, 1] = half_products(right, right)


def late_begin(keys, flat, begun, pieces, spins, eig, rb_count):
    return pl.pallas_call(
        functools.partial(late_begin_kernel, eig, keys, rb_count),
        out_shape=jax.ShapeDtypeStruct((spins, 2, eig, eig), F32),
        in_specs=[VMEM, ANY] + [VMEM] * len(pieces),
        out_specs=VMEM,
        scratch_shapes=[pltpu.VMEM((eig, 2 * pieces[0].shape[2]), BF16)],
        compiler_params=params(32),
        cost_estimate=LITTLE,
        name="late_begin",
    )(flat, begun, *pieces)


def late_rows_kernel(eig, keys, rb_count, flat, partial, *refs):
    pieces, (out, last) = refs[:-2], refs[-2:]
    side, width = keys[0][1], pieces[0].shape[2]
    gather_last(eig, keys, flat.shape[0] // eig, pieces, last)
    right = [last[:, :width], last[:, width:]]
    for n in range(out.shape[0]):
        left = side_columns(flat, slice(n * eig, (n + 1) * eig), side, width, rb_count)
        real, imag = half_products(left, right)
        out[n, 0], out[n, 1] = (partial[n, 0] + real).astype(BF16), (partial[n, 1] + imag).astype(BF16)


def late_rest_kernel(eig, side, rb_count, flat, partial, last, out):
    count, width = out.shape[0] - 1, last.shape[1] // 2
    others = flat.shape[0] // eig
    right = [last[:, :width], last[:, width:]]
    for n in range(count + 1):
        spin = others - count + n
        left = right
        if n < count:
            left = side_columns(flat, slice(spin * eig, (spin + 1) * eig), side, width, rb_count)
        real, imag = half_products(left, right)
        out[n, 0], out[n, 1] = (partial[spin, 0] + real).astype(BF16), (partial[spin, 1] + imag).astype(BF16)


def late_rows(keys, flat, partial, pieces, spins, eig, rb_count):
    return pl.pallas_call(
        functools.partial(late_rows_kernel, eig, keys, rb_count),
        out_shape=(
            jax.ShapeDtypeStruct((spins // 2, 2, eig, eig), BF16),
            jax.ShapeDtypeStruct((eig, 2 * pieces[0].shape[2]), BF16),
        ),
        in_specs=[VMEM] * (2 + len(pieces)),
        out_specs=(VMEM, VMEM),
        compiler_params=params(32),
        cost_estimate=LONG,
        name="late_rows",
    )(flat, partial, *pieces)


def late_rest(side, flat, partial, last, spins, eig, rb_count):
    return pl.pallas_call(
        functools.partial(late_rest_kernel, eig, side, rb_count),
        out_shape=jax.ShapeDtypeStruct((spins - spins // 2, 2, eig, eig), BF16),
        in_specs=[VMEM] * 3,
        out_specs=VMEM,
        compiler_params=params(32),
        cost_estimate=LITTLE,
        name="late_rest",
    )(flat, partial, last)


def factors_kernel(diag_mom, elems, right_ref, left_ref, own_ref, held, sem):
    rank = lax.axis_index("rb")
    eig = held.shape[-1]
    copies = []
    for time in range(2):
        which = diag_mom[0, rank, lax.bitwise_xor(rank, time)]
        copies.append(pltpu.make_async_copy(elems.at[which], held.at[time], sem.at[time]))
    for slot in range(own_ref.shape[0]):
        copies.append(pltpu.make_async_copy(elems.at[diag_mom[0, slot, rank]], own_ref.at[slot], sem.at[2 + slot]))
    for copy in copies:
        copy.start()
    for copy in copies:
        copy.wait()
    for time in range(2):
        re, im = held[time, 0], held[time, 1]
        right_ref[time, :eig, :eig] = re
        right_ref[time, :eig, eig:] = im
        right_ref[time, eig:, :eig] = -im
        right_ref[time, eig:, eig:] = re
        re_t = re.astype(F32).T.astype(BF16)
        im_t = im.astype(F32).T.astype(BF16)
        left_ref[time, :eig, :eig] = re_t
        left_ref[time, :eig, eig:] = im_t
        left_ref[time, eig:, :eig] = im_t
        left_ref[time, eig:, eig:] = -re_t


def factors(diag_mom, src_elems):
    slots, eig = diag_mom.shape[1], src_elems.shape[-1]
    form = jax.ShapeDtypeStruct((2, 2 * eig, 2 * eig), BF16)
    return pl.pallas_call(
        factors_kernel,
        out_shape=(form, form, jax.ShapeDtypeStruct((slots, 2, eig, eig), BF16)),
        in_specs=[SMEM, ANY],
        out_specs=(VMEM, VMEM, VMEM),
        scratch_shapes=[pltpu.VMEM((2, 2, eig, eig), BF16), pltpu.SemaphoreType.DMA((2 + slots,))],
        compiler_params=params(32),
        cost_estimate=LITTLE,
        name="factors",
    )(diag_mom, src_elems)


def late_direct_kernel(rest, own, carried, out):
    direct_sums([rest.at[rest.shape[0] - 1]], own, out, carried)


def late_direct(rest, own, carried):
    return pl.pallas_call(
        late_direct_kernel,
        out_shape=sums_shape(carried.shape[0]),
        in_specs=[VMEM] * 3,
        out_specs=VMEM,
        compiler_params=params(32),
        cost_estimate=LITTLE,
        name="late_direct",
    )(rest, own, carried)


def cross_kernel(offs, own, other, right, left, *refs):
    carried, out = refs[:-1], refs[-1]
    eig = own.shape[-1]
    if len(other.shape) > len(own.shape):
        other = other.at[1 - lax.axis_index("rb")]
    real, imag = [], []

    def add(x, y, count, from_right, from_left):
        rows = [jnp.concatenate([x[n, 0], x[n, 1]], axis=1) for n in range(count)]
        product = dot(jnp.concatenate(rows, axis=0), from_right)
        for n in range(count):
            partner = dot(from_left, y[n].reshape(2 * eig, eig))
            mine = product[n * eig : (n + 1) * eig]
            p_re, p_im = mine[:, :eig], mine[:, eig:]
            w_re, w_im = partner[:eig], partner[eig:]
            real.append(fold(p_re * w_re - p_im * w_im))
            imag.append(fold(p_re * w_im + p_im * w_re))

    add(other, own, own.shape[0], right[1], left[0])
    add(own, other, offs, right[0], left[1])
    out[0] = functools.reduce(jnp.add, real + [ref[0] for ref in carried])
    out[1] = functools.reduce(jnp.add, imag + [ref[1] for ref in carried])


def cross_traces(offs, own, other, right, left, carried, name):
    return pl.pallas_call(
        functools.partial(cross_kernel, offs),
        out_shape=sums_shape(2),
        in_specs=[VMEM] * (4 + len(carried)),
        out_specs=VMEM,
        compiler_params=params(32),
        cost_estimate=LITTLE,
        name=name,
    )(own, other, right, left, *carried)


def last_cross_kernel(offs, own, other, right, left, direct, carried, out):
    count = direct.shape[0]
    for n in range(count):
        out[n] = direct[n]
    cross_kernel(offs, own, other, right, left, carried, out.at[pl.ds(count, 2)])


def last_cross(offs, own, other, right, left, direct, carried):
    return pl.pallas_call(
        functools.partial(last_cross_kernel, offs),
        out_shape=sums_shape(direct.shape[0] + 2),
        in_specs=[VMEM] * 6,
        out_specs=VMEM,
        compiler_params=params(32),
        cost_estimate=LITTLE,
        name="last_cross",
    )(own, other, right, left, direct, carried)


def final_kernel(slots, mine, theirs, count, out):
    rank = lax.axis_index("rb")
    lane = lax.broadcasted_iota(jnp.int32, (1, LANES), 1)

    def totals(ref):
        rows = jnp.concatenate([jnp.sum(ref[n], axis=0, keepdims=True) for n in range(ref.shape[0])], axis=0)
        sums = jnp.broadcast_to(jnp.sum(rows, axis=1, keepdims=True), rows.shape)
        return [sums[n : n + 1] for n in range(ref.shape[0])]

    def put(slot, kind, re, im):
        value = jnp.where(lane == 0, re, im) * 0.25
        out[0, slot, kind : kind + 1, :] = jnp.where(slot < count[0], value, 0.0)[:, :2]

    m, t = totals(mine), totals(theirs)
    for slot in range(slots):
        m_re, m_im, t_re, t_im = m[2 * slot], m[2 * slot + 1], t[2 * slot], t[2 * slot + 1]
        put(slot, 0, m_re * t_re - m_im * t_im, m_re * t_im + m_im * t_re)
        here = rank == slot
        put(slot, 1, jnp.where(here, m[2 * slots], t[2 * slots]), jnp.where(here, m[2 * slots + 1], t[2 * slots + 1]))


def final(mine, theirs, diag_count, slots):
    return pl.pallas_call(
        functools.partial(final_kernel, slots),
        out_shape=jax.ShapeDtypeStruct((1, slots, 2, 2), F32),
        in_specs=[VMEM, VMEM, SMEM],
        out_specs=VMEM,
        compiler_params=params(32),
        name="final",
    )(mine, theirs, diag_count)


def shards(peram, src_elems, owner_times, diag_mom, diag_count):
    tp_count, rb_count = lax.axis_size("tp"), lax.axis_size("rb")
    eig = src_elems.shape[-1]
    spins = tp_count * peram.shape[0] // eig
    slots = diag_mom.shape[1]

    rows = peram.shape[0]
    head, tail, late, own = travel_order(tp_count, rb_count, rows)
    early_keys = head + tail
    picked = pick(owner_times, peram, head, "pick_head", [jax.ShapeDtypeStruct((4, *peram.shape), BF16)])
    picked.update(pick(owner_times, peram, tail + late + own, "pick_tail", []))

    def send(key):
        far, side, _, _ = key
        pairs = [
            (tp * rb_count + rb, (tp ^ far) * rb_count + (rb ^ side))
            for tp in range(tp_count)
            for rb in range(rb_count)
        ]
        return lax.ppermute(picked[key], ("tp", "rb"), pairs)

    swap = [(rb, rb ^ 1) for rb in range(rb_count)]
    right, left, own_elems = factors(diag_mom, src_elems)
    arrived = [send(key) for key in early_keys] + [picked[key] for key in own]
    flat, early, direct = early_gram(early_keys + own, arrived, own_elems, spins, eig, rb_count, rows)
    early_both = lax.all_to_all(jnp.stack([early] * rb_count), "rb", 0, 0)
    offs = early.shape[0] - (spins - 1)
    begun = cross_traces(offs, early, early_both, right, left, [], "early_cross")

    halves = [[key for key in late if key[1] == side] for side in range(rb_count)]
    sent = [[send(key) for key in keys] for keys in halves]
    half = late_begin(halves[0], flat, begun, sent[0], spins, eig, rb_count)
    blocks, last = late_rows(halves[1], flat, half, sent[1], spins, eig, rb_count)
    swapped = lax.ppermute(blocks, "rb", swap)
    rest = late_rest(1, flat, half, last, spins, eig, rb_count)
    rest_swapped = lax.ppermute(rest, "rb", swap)
    traces = late_direct(rest, own_elems, direct)
    partial = cross_traces(blocks.shape[0], blocks, swapped, right, left, [begun], "late_cross")
    mine = last_cross(rest.shape[0] - 1, rest, rest_swapped, right, left, traces, partial)
    theirs = lax.ppermute(mine, "rb", swap)
    return final(mine, theirs, diag_count, slots)


def solution(mesh):
    in_specs = (
        P(("grp", "tp"), None, None, "rb"),
        P("grp", None, None, None),
        P("grp", None),
        P(("grp", "tp"), None, None),
        P(("grp", "tp")),
    )
    out_specs = P(("grp", "tp"), None, None, None)
    return jax.shard_map(shards, mesh=mesh, in_specs=in_specs, out_specs=out_specs, check_vma=False)
```

```python
import functools

import jax
import jax.numpy as jnp
from jax import lax
from jax.experimental import pallas as pl
from jax.experimental.pallas import tpu as pltpu
from jax.sharding import PartitionSpec as P

F32 = jnp.float32
BF16 = jnp.bfloat16
ANY = pl.BlockSpec(memory_space=pl.ANY)
SMEM = pl.BlockSpec(memory_space=pltpu.SMEM)
VMEM = pl.BlockSpec(memory_space=pltpu.VMEM)
SUBLANES = 8
LANES = 128
STEP = 16
MIB = 1 << 20
LITTLE = pl.CostEstimate(flops=1000, bytes_accessed=1000, transcendentals=0)
LONG = pl.CostEstimate(flops=5 * 10**10, bytes_accessed=1000, transcendentals=0)


def in_hbm(array):
    return pltpu.with_memory_space_constraint(array, pltpu.HBM)


def params(mib):
    return pltpu.CompilerParams(vmem_limit_bytes=mib * MIB)


def dot(left, right):
    return jnp.dot(left, right, preferred_element_type=F32)


def dot_nt(left, right):
    return lax.dot_general(left, right, (((1,), (1,)), ((), ())), preferred_element_type=F32)


def choose(index, values):
    out = jnp.int32(values[0])
    for n in range(1, len(values)):
        out = jnp.where(index == n, jnp.int32(values[n]), out)
    return out


def aligned(start, size):
    return pl.ds(pl.multiple_of(start, size), size)


def travel_order(tp_count, rb_count):
    half, quarter = tp_count // 2, tp_count // 4

    def both(distances):
        return [(far, side) for far in distances for side in range(rb_count)]

    late, long = both(range(half, half + quarter)), both(range(half + quarter, tp_count))
    near, rest = both(reversed(range(quarter, half))), both(range(1, quarter))
    own, other = (0, 0), [(0, side) for side in range(1, rb_count)]
    step, part = len(long) // 4, len(rest) // 2
    head = long[: 2 * step] + near[: 2 * step] + long[2 * step : 3 * step]
    tail = rest[:part] + other + near[2 * step : 3 * step] + long[3 * step :] + near[3 * step :] + rest[part:]
    return head, tail, late, [own]


def pick_kernel(keys, times, table, *refs):
    outs, (held, wide, taken_times, sem, times_sem) = refs[:-5], refs[-5:]
    tp_rank, rb_rank = lax.axis_index("tp"), lax.axis_index("rb")
    rows, _, packed, _ = table.shape

    def fetch(chunk):
        where = aligned(chunk * STEP, STEP)
        return pltpu.make_async_copy(table.at[where], held.at[where], sem.at[chunk])

    copy = pltpu.make_async_copy(times, taken_times, times_sem)
    copy.start()
    for chunk in range(rows // STEP):
        fetch(chunk).start()
    copy.wait()

    def step(chunk, carry):
        fetch(chunk).wait()
        where = aligned(chunk * STEP, STEP)
        for n, (far, side) in enumerate(keys):
            time = taken_times[lax.bitwise_xor(rb_rank, side), lax.bitwise_xor(tp_rank, far)]
            slot = n % wide.shape[0]
            wide[slot] = held[where, time].astype(F32).reshape(STEP * packed, LANES)
            for tile in range(packed // 2):
                for part in range(2):
                    taken = wide[slot, pl.ds(2 * tile + part, STEP, stride=packed), :]
                    outs[n][part, where, tile * LANES : (tile + 1) * LANES] = taken.astype(BF16)
        return carry

    lax.fori_loop(0, rows // STEP, step, 0)


def pick(owner_times, peram, keys, name, spare):
    rows, times, parts, width = peram.shape
    tiles = width // LANES
    table = peram.reshape(rows, times, parts, tiles, LANES).swapaxes(2, 3)
    table = table.reshape(rows, times, tiles * parts, LANES)
    picked = pl.pallas_call(
        functools.partial(pick_kernel, keys),
        out_shape=[jax.ShapeDtypeStruct((parts, rows, width), BF16)] * len(keys) + spare,
        in_specs=[ANY, ANY],
        out_specs=[VMEM] * len(keys) + [ANY] * len(spare),
        scratch_shapes=[
            pltpu.VMEM(table.shape, BF16),
            pltpu.VMEM((4, STEP * tiles * parts, LANES), F32),
            pltpu.SMEM(owner_times.shape[::-1], jnp.int32),
            pltpu.SemaphoreType.DMA((rows // STEP,)),
            pltpu.SemaphoreType.DMA,
        ],
        compiler_params=params(32),
        cost_estimate=LITTLE,
        name=name,
    )(in_hbm(owner_times.T), in_hbm(table))
    return dict(zip(keys, picked))


def place(far, per_spin):
    low = lax.axis_index("tp") % per_spin
    if far >= 2 * per_spin:
        far ^= per_spin
    return (far // per_spin) * per_spin + lax.bitwise_xor(jnp.int32(far % per_spin), low)


def gram_block(left, right):
    depth = left.shape[1] // 2
    real = dot_nt(left, right)
    imag = dot_nt(left[:, :depth], right[:, depth:]) - dot_nt(left[:, depth:], right[:, :depth])
    return real.astype(BF16), imag.astype(BF16)


def fold(values):
    rows, columns = values.shape
    folded = jnp.sum(values.reshape(rows // SUBLANES, SUBLANES, columns), axis=0)
    return functools.reduce(jnp.add, [folded[:, n : n + LANES] for n in range(0, columns, LANES)])


def direct_sums(diagonal, own, out, carried=None):
    real = functools.reduce(jnp.add, [block[0].astype(F32) for block in diagonal])
    imag = functools.reduce(jnp.add, [block[1].astype(F32) for block in diagonal])
    for slot in range(own.shape[0]):
        elem_re, elem_im = own[slot, 0].astype(F32), own[slot, 1].astype(F32)
        sums = [fold(elem_re * real + elem_im * imag), fold(elem_im * real - elem_re * imag)]
        for part in range(2):
            n = 2 * slot + part
            out[n] = sums[part] if carried is None else sums[part] + carried[n]


def sums_shape(count):
    return jax.ShapeDtypeStruct((count, SUBLANES, LANES), F32)


def early_blocks(spins):
    off = [(s, t) for s in range(spins - 1) for t in range(s + 1, spins - 1)]
    return off + [(s, s) for s in range(spins - 1)]


def early_kernel(eig, keys, rb_count, blocks, *refs):
    pieces, (own, flat, out, traces, sem) = refs[:-5], refs[-5:]
    rows, width = pieces[0].shape[1:]
    depth = rb_count * width
    copies = []
    for n, ((far, side), piece) in enumerate(zip(keys, pieces)):
        where = aligned(place(far, eig // rows) * rows, rows)
        for part in range(2):
            columns = pl.ds(part * depth + side * width, width)
            copies.append(pltpu.make_async_copy(piece.at[part], flat.at[where, columns], sem.at[2 * n + part]))
    for copy in copies:
        copy.start()
    for copy in copies:
        copy.wait()

    def step(n, carry):
        top, side = choose(n, [b[0] for b in blocks]), choose(n, [b[1] for b in blocks])
        out[n, 0], out[n, 1] = gram_block(flat[aligned(top * eig, eig), :], flat[aligned(side * eig, eig), :])
        return carry

    lax.fori_loop(0, len(blocks), step, 0)
    diagonal = [out.at[n] for n, block in enumerate(blocks) if block[0] == block[1]]
    direct_sums(diagonal, own, traces)


def early_gram(keys, pieces, own_elems, spins, eig, rb_count):
    blocks = early_blocks(spins)
    depth = 2 * rb_count * pieces[0].shape[2]
    return pl.pallas_call(
        functools.partial(early_kernel, eig, keys, rb_count, blocks),
        out_shape=(
            jax.ShapeDtypeStruct(((spins - 1) * eig, depth), BF16),
            jax.ShapeDtypeStruct((len(blocks), 2, eig, eig), BF16),
            sums_shape(2 * own_elems.shape[0]),
        ),
        in_specs=[ANY] * len(pieces) + [VMEM],
        out_specs=(VMEM, VMEM, VMEM),
        scratch_shapes=[pltpu.SemaphoreType.DMA((2 * len(pieces),))],
        compiler_params=params(32),
        cost_estimate=LONG,
        name="early_gram",
    )(*pieces, own_elems)


def side_columns(ref, rows, side, width, rb_count):
    return [ref[rows, (part * rb_count + side) * width : (part * rb_count + side + 1) * width] for part in range(2)]


def half_products(left, right):
    real = dot_nt(left[0], right[0]) + dot_nt(left[1], right[1])
    imag = dot_nt(left[0], right[1]) - dot_nt(left[1], right[0])
    return real, imag


def gather_last(eig, keys, others, pieces, last):
    rows, width = pieces[0].shape[1:]
    for (far, _), piece in zip(keys, pieces):
        where = aligned((place(far, eig // rows) - others * (eig // rows)) * rows, rows)
        for part in range(2):
            last[where, part * width : (part + 1) * width] = piece[part]


def late_begin_kernel(eig, keys, rb_count, flat, begun, *refs):
    pieces, (out, last) = refs[:-2], refs[-2:]
    side, width, others = keys[0][1], pieces[0].shape[2], flat.shape[0] // eig
    gather_last(eig, keys, others, pieces, last)
    right = [last[:, :width], last[:, width:]]
    for n in range(others):
        left = side_columns(flat, slice(n * eig, (n + 1) * eig), side, width, rb_count)
        out[n, 0], out[n, 1] = half_products(left, right)
    out[others, 0], out[others, 1] = half_products(right, right)


def late_begin(keys, flat, begun, pieces, spins, eig, rb_count):
    return pl.pallas_call(
        functools.partial(late_begin_kernel, eig, keys, rb_count),
        out_shape=jax.ShapeDtypeStruct((spins, 2, eig, eig), F32),
        in_specs=[VMEM, ANY] + [VMEM] * len(pieces),
        out_specs=VMEM,
        scratch_shapes=[pltpu.VMEM((eig, 2 * pieces[0].shape[2]), BF16)],
        compiler_params=params(32),
        cost_estimate=LITTLE,
        name="late_begin",
    )(flat, begun, *pieces)


def late_rows_kernel(eig, keys, rb_count, flat, partial, *refs):
    pieces, (out, last) = refs[:-2], refs[-2:]
    side, width = keys[0][1], pieces[0].shape[2]
    gather_last(eig, keys, flat.shape[0] // eig, pieces, last)
    right = [last[:, :width], last[:, width:]]
    for n in range(out.shape[0]):
        left = side_columns(flat, slice(n * eig, (n + 1) * eig), side, width, rb_count)
        real, imag = half_products(left, right)
        out[n, 0], out[n, 1] = (partial[n, 0] + real).astype(BF16), (partial[n, 1] + imag).astype(BF16)


def late_rest_kernel(eig, side, rb_count, flat, partial, last, out):
    count, width = out.shape[0] - 1, last.shape[1] // 2
    others = flat.shape[0] // eig
    right = [last[:, :width], last[:, width:]]
    for n in range(count + 1):
        spin = others - count + n
        left = right
        if n < count:
            left = side_columns(flat, slice(spin * eig, (spin + 1) * eig), side, width, rb_count)
        real, imag = half_products(left, right)
        out[n, 0], out[n, 1] = (partial[spin, 0] + real).astype(BF16), (partial[spin, 1] + imag).astype(BF16)


def late_rows(keys, flat, partial, pieces, spins, eig, rb_count):
    return pl.pallas_call(
        functools.partial(late_rows_kernel, eig, keys, rb_count),
        out_shape=(
            jax.ShapeDtypeStruct((spins // 2, 2, eig, eig), BF16),
            jax.ShapeDtypeStruct((eig, 2 * pieces[0].shape[2]), BF16),
        ),
        in_specs=[VMEM] * (2 + len(pieces)),
        out_specs=(VMEM, VMEM),
        compiler_params=params(32),
        cost_estimate=LONG,
        name="late_rows",
    )(flat, partial, *pieces)


def late_rest(side, flat, partial, last, spins, eig, rb_count):
    return pl.pallas_call(
        functools.partial(late_rest_kernel, eig, side, rb_count),
        out_shape=jax.ShapeDtypeStruct((spins - spins // 2, 2, eig, eig), BF16),
        in_specs=[VMEM] * 3,
        out_specs=VMEM,
        compiler_params=params(32),
        cost_estimate=LITTLE,
        name="late_rest",
    )(flat, partial, last)


def factors_kernel(diag_mom, elems, right_ref, left_ref, own_ref, held, sem):
    rank = lax.axis_index("rb")
    eig = held.shape[-1]
    copies = []
    for time in range(2):
        which = diag_mom[0, rank, lax.bitwise_xor(rank, time)]
        copies.append(pltpu.make_async_copy(elems.at[which], held.at[time], sem.at[time]))
    for slot in range(own_ref.shape[0]):
        copies.append(pltpu.make_async_copy(elems.at[diag_mom[0, slot, rank]], own_ref.at[slot], sem.at[2 + slot]))
    for copy in copies:
        copy.start()
    for copy in copies:
        copy.wait()
    for time in range(2):
        re, im = held[time, 0], held[time, 1]
        right_ref[time, :eig, :eig] = re
        right_ref[time, :eig, eig:] = im
        right_ref[time, eig:, :eig] = -im
        right_ref[time, eig:, eig:] = re
        re_t = re.astype(F32).T.astype(BF16)
        im_t = im.astype(F32).T.astype(BF16)
        left_ref[time, :eig, :eig] = re_t
        left_ref[time, :eig, eig:] = im_t
        left_ref[time, eig:, :eig] = im_t
        left_ref[time, eig:, eig:] = -re_t


def factors(diag_mom, src_elems):
    slots, eig = diag_mom.shape[1], src_elems.shape[-1]
    form = jax.ShapeDtypeStruct((2, 2 * eig, 2 * eig), BF16)
    return pl.pallas_call(
        factors_kernel,
        out_shape=(form, form, jax.ShapeDtypeStruct((slots, 2, eig, eig), BF16)),
        in_specs=[SMEM, ANY],
        out_specs=(VMEM, VMEM, VMEM),
        scratch_shapes=[pltpu.VMEM((2, 2, eig, eig), BF16), pltpu.SemaphoreType.DMA((2 + slots,))],
        compiler_params=params(32),
        cost_estimate=LITTLE,
        name="factors",
    )(diag_mom, src_elems)


def late_direct_kernel(rest, own, carried, out):
    direct_sums([rest.at[rest.shape[0] - 1]], own, out, carried)


def late_direct(rest, own, carried):
    return pl.pallas_call(
        late_direct_kernel,
        out_shape=sums_shape(carried.shape[0]),
        in_specs=[VMEM] * 3,
        out_specs=VMEM,
        compiler_params=params(32),
        cost_estimate=LITTLE,
        name="late_direct",
    )(rest, own, carried)


def cross_kernel(offs, own, other, right, left, *refs):
    carried, out = refs[:-1], refs[-1]
    eig = own.shape[-1]
    if len(other.shape) > len(own.shape):
        other = other.at[1 - lax.axis_index("rb")]
    real, imag = [], []

    def add(x, y, count, from_right, from_left):
        rows = [jnp.concatenate([x[n, 0], x[n, 1]], axis=1) for n in range(count)]
        product = dot(jnp.concatenate(rows, axis=0), from_right)
        for n in range(count):
            partner = dot(from_left, y[n].reshape(2 * eig, eig))
            mine = product[n * eig : (n + 1) * eig]
            p_re, p_im = mine[:, :eig], mine[:, eig:]
            w_re, w_im = partner[:eig], partner[eig:]
            real.append(fold(p_re * w_re - p_im * w_im))
            imag.append(fold(p_re * w_im + p_im * w_re))

    add(other, own, own.shape[0], right[1], left[0])
    add(own, other, offs, right[0], left[1])
    out[0] = functools.reduce(jnp.add, real + [ref[0] for ref in carried])
    out[1] = functools.reduce(jnp.add, imag + [ref[1] for ref in carried])


def cross_traces(offs, own, other, right, left, carried, name):
    return pl.pallas_call(
        functools.partial(cross_kernel, offs),
        out_shape=sums_shape(2),
        in_specs=[VMEM] * (4 + len(carried)),
        out_specs=VMEM,
        compiler_params=params(32),
        cost_estimate=LITTLE,
        name=name,
    )(own, other, right, left, *carried)


def last_cross_kernel(offs, own, other, right, left, direct, carried, out):
    count = direct.shape[0]
    for n in range(count):
        out[n] = direct[n]
    cross_kernel(offs, own, other, right, left, carried, out.at[pl.ds(count, 2)])


def last_cross(offs, own, other, right, left, direct, carried):
    return pl.pallas_call(
        functools.partial(last_cross_kernel, offs),
        out_shape=sums_shape(direct.shape[0] + 2),
        in_specs=[VMEM] * 6,
        out_specs=VMEM,
        compiler_params=params(32),
        cost_estimate=LITTLE,
        name="last_cross",
    )(own, other, right, left, direct, carried)


def final_kernel(slots, mine, theirs, count, out):
    rank = lax.axis_index("rb")
    lane = lax.broadcasted_iota(jnp.int32, (1, LANES), 1)

    def totals(ref):
        rows = jnp.concatenate([jnp.sum(ref[n], axis=0, keepdims=True) for n in range(ref.shape[0])], axis=0)
        sums = jnp.broadcast_to(jnp.sum(rows, axis=1, keepdims=True), rows.shape)
        return [sums[n : n + 1] for n in range(ref.shape[0])]

    def put(slot, kind, re, im):
        value = jnp.where(lane == 0, re, im) * 0.25
        out[0, slot, kind : kind + 1, :] = jnp.where(slot < count[0], value, 0.0)[:, :2]

    m, t = totals(mine), totals(theirs)
    for slot in range(slots):
        m_re, m_im, t_re, t_im = m[2 * slot], m[2 * slot + 1], t[2 * slot], t[2 * slot + 1]
        put(slot, 0, m_re * t_re - m_im * t_im, m_re * t_im + m_im * t_re)
        here = rank == slot
        put(slot, 1, jnp.where(here, m[2 * slots], t[2 * slots]), jnp.where(here, m[2 * slots + 1], t[2 * slots + 1]))


def final(mine, theirs, diag_count, slots):
    return pl.pallas_call(
        functools.partial(final_kernel, slots),
        out_shape=jax.ShapeDtypeStruct((1, slots, 2, 2), F32),
        in_specs=[VMEM, VMEM, SMEM],
        out_specs=VMEM,
        compiler_params=params(32),
        name="final",
    )(mine, theirs, diag_count)


def shards(peram, src_elems, owner_times, diag_mom, diag_count):
    tp_count, rb_count = lax.axis_size("tp"), lax.axis_size("rb")
    eig = src_elems.shape[-1]
    spins = tp_count * peram.shape[0] // eig
    slots = diag_mom.shape[1]

    head, tail, late, own = travel_order(tp_count, rb_count)
    early_keys = head + tail
    picked = pick(owner_times, peram, head, "pick_head", [jax.ShapeDtypeStruct((4, *peram.shape), BF16)])
    picked.update(pick(owner_times, peram, tail + late + own, "pick_tail", []))

    def send(key):
        far, side = key
        pairs = [
            (tp * rb_count + rb, (tp ^ far) * rb_count + (rb ^ side))
            for tp in range(tp_count)
            for rb in range(rb_count)
        ]
        return lax.ppermute(picked[key], ("tp", "rb"), pairs)

    swap = [(rb, rb ^ 1) for rb in range(rb_count)]
    right, left, own_elems = factors(diag_mom, src_elems)
    arrived = [send(key) for key in early_keys] + [picked[key] for key in own]
    flat, early, direct = early_gram(early_keys + own, arrived, own_elems, spins, eig, rb_count)
    early_both = lax.all_to_all(jnp.stack([early] * rb_count), "rb", 0, 0)
    offs = early.shape[0] - (spins - 1)
    begun = cross_traces(offs, early, early_both, right, left, [], "early_cross")

    halves = [[key for key in late if key[1] == side] for side in range(rb_count)]
    sent = [[send(key) for key in keys] for keys in halves]
    half = late_begin(halves[0], flat, begun, sent[0], spins, eig, rb_count)
    blocks, last = late_rows(halves[1], flat, half, sent[1], spins, eig, rb_count)
    swapped = lax.ppermute(blocks, "rb", swap)
    rest = late_rest(1, flat, half, last, spins, eig, rb_count)
    rest_swapped = lax.ppermute(rest, "rb", swap)
    traces = late_direct(rest, own_elems, direct)
    partial = cross_traces(blocks.shape[0], blocks, swapped, right, left, [begun], "late_cross")
    mine = last_cross(rest.shape[0] - 1, rest, rest_swapped, right, left, traces, partial)
    theirs = lax.ppermute(mine, "rb", swap)
    return final(mine, theirs, diag_count, slots)


def solution(mesh):
    in_specs = (
        P(("grp", "tp"), None, None, "rb"),
        P("grp", None, None, None),
        P("grp", None),
        P(("grp", "tp"), None, None),
        P(("grp", "tp")),
    )
    out_specs = P(("grp", "tp"), None, None, None)
    return jax.shard_map(shards, mesh=mesh, in_specs=in_specs, out_specs=out_specs, check_vma=False)
```

```python
import functools

import jax
import jax.numpy as jnp
from jax import lax
from jax.experimental import pallas as pl
from jax.experimental.pallas import tpu as pltpu
from jax.sharding import PartitionSpec as P

F32 = jnp.float32
BF16 = jnp.bfloat16
ANY = pl.BlockSpec(memory_space=pl.ANY)
SMEM = pl.BlockSpec(memory_space=pltpu.SMEM)
VMEM = pl.BlockSpec(memory_space=pltpu.VMEM)
SUBLANES = 8
LANES = 128
STEP = 16
MIB = 1 << 20
LITTLE = pl.CostEstimate(flops=1000, bytes_accessed=1000, transcendentals=0)
LONG = pl.CostEstimate(flops=5 * 10**10, bytes_accessed=1000, transcendentals=0)


def in_hbm(array):
    return pltpu.with_memory_space_constraint(array, pltpu.HBM)


def params(mib):
    return pltpu.CompilerParams(vmem_limit_bytes=mib * MIB)


def dot(left, right):
    return jnp.dot(left, right, preferred_element_type=F32)


def dot_nt(left, right):
    return lax.dot_general(left, right, (((1,), (1,)), ((), ())), preferred_element_type=F32)


def choose(index, values):
    out = jnp.int32(values[0])
    for n in range(1, len(values)):
        out = jnp.where(index == n, jnp.int32(values[n]), out)
    return out


def aligned(start, size):
    return pl.ds(pl.multiple_of(start, size), size)


def travel_order(tp_count, rb_count):
    half, quarter = tp_count // 2, tp_count // 4

    def both(distances):
        return [(far, side) for far in distances for side in range(rb_count)]

    long, late = both(range(half, half + quarter)), both(range(half + quarter, tp_count))
    near, rest = both(reversed(range(quarter, half))), both(range(1, quarter))
    own, other = (0, 0), [(0, side) for side in range(1, rb_count)]
    step, part = len(long) // 4, len(rest) // 2
    head = long[: 2 * step] + near[: 2 * step] + long[2 * step : 3 * step]
    tail = rest[:part] + other + near[2 * step : 3 * step] + long[3 * step :] + near[3 * step :] + rest[part:]
    return head, tail, late, [own]


def distance(far, tp_rank, tp_count):
    if far < tp_count // 2:
        return far
    return lax.bitwise_xor(jnp.int32(far), jnp.where(tp_rank < tp_count // 2, jnp.int32(tp_count // 4), jnp.int32(0)))


def pick_kernel(keys, times, table, *refs):
    outs, (held, wide, taken_times, sem, times_sem) = refs[:-5], refs[-5:]
    tp_rank, rb_rank = lax.axis_index("tp"), lax.axis_index("rb")
    rows, _, packed, _ = table.shape

    def fetch(chunk):
        where = aligned(chunk * STEP, STEP)
        return pltpu.make_async_copy(table.at[where], held.at[where], sem.at[chunk])

    copy = pltpu.make_async_copy(times, taken_times, times_sem)
    copy.start()
    for chunk in range(rows // STEP):
        fetch(chunk).start()
    copy.wait()

    def step(chunk, carry):
        fetch(chunk).wait()
        where = aligned(chunk * STEP, STEP)
        for n, (far, side) in enumerate(keys):
            owner = lax.bitwise_xor(tp_rank, distance(far, tp_rank, taken_times.shape[1]))
            time = taken_times[lax.bitwise_xor(rb_rank, side), owner]
            slot = n % wide.shape[0]
            wide[slot] = held[where, time].astype(F32).reshape(STEP * packed, LANES)
            for tile in range(packed // 2):
                for part in range(2):
                    taken = wide[slot, pl.ds(2 * tile + part, STEP, stride=packed), :]
                    outs[n][part, where, tile * LANES : (tile + 1) * LANES] = taken.astype(BF16)
        return carry

    lax.fori_loop(0, rows // STEP, step, 0)


def pick(owner_times, peram, keys, name, spare):
    rows, times, parts, width = peram.shape
    tiles = width // LANES
    table = peram.reshape(rows, times, parts, tiles, LANES).swapaxes(2, 3)
    table = table.reshape(rows, times, tiles * parts, LANES)
    picked = pl.pallas_call(
        functools.partial(pick_kernel, keys),
        out_shape=[jax.ShapeDtypeStruct((parts, rows, width), BF16)] * len(keys) + spare,
        in_specs=[ANY, ANY],
        out_specs=[VMEM] * len(keys) + [ANY] * len(spare),
        scratch_shapes=[
            pltpu.VMEM(table.shape, BF16),
            pltpu.VMEM((4, STEP * tiles * parts, LANES), F32),
            pltpu.SMEM(owner_times.shape[::-1], jnp.int32),
            pltpu.SemaphoreType.DMA((rows // STEP,)),
            pltpu.SemaphoreType.DMA,
        ],
        compiler_params=params(32),
        cost_estimate=LITTLE,
        name=name,
    )(in_hbm(owner_times.T), in_hbm(table))
    return dict(zip(keys, picked))


def place(far, per_spin):
    low = lax.axis_index("tp") % per_spin
    return (far // per_spin) * per_spin + lax.bitwise_xor(jnp.int32(far % per_spin), low)


def gram_block(left, right):
    depth = left.shape[1] // 2
    real = dot_nt(left, right)
    imag = dot_nt(left[:, :depth], right[:, depth:]) - dot_nt(left[:, depth:], right[:, :depth])
    return real.astype(BF16), imag.astype(BF16)


def fold(values):
    rows, columns = values.shape
    folded = jnp.sum(values.reshape(rows // SUBLANES, SUBLANES, columns), axis=0)
    return functools.reduce(jnp.add, [folded[:, n : n + LANES] for n in range(0, columns, LANES)])


def direct_sums(diagonal, own, out, carried=None):
    real = functools.reduce(jnp.add, [block[0].astype(F32) for block in diagonal])
    imag = functools.reduce(jnp.add, [block[1].astype(F32) for block in diagonal])
    for slot in range(own.shape[0]):
        elem_re, elem_im = own[slot, 0].astype(F32), own[slot, 1].astype(F32)
        sums = [fold(elem_re * real + elem_im * imag), fold(elem_im * real - elem_re * imag)]
        for part in range(2):
            n = 2 * slot + part
            out[n] = sums[part] if carried is None else sums[part] + carried[n]


def sums_shape(count):
    return jax.ShapeDtypeStruct((count, SUBLANES, LANES), F32)


def early_blocks(spins):
    off = [(s, t) for s in range(spins - 1) for t in range(s + 1, spins - 1)]
    return off + [(s, s) for s in range(spins - 1)]


def early_kernel(eig, keys, rb_count, blocks, *refs):
    pieces, (own, flat, out, traces, sem) = refs[:-5], refs[-5:]
    rows, width = pieces[0].shape[1:]
    depth = rb_count * width
    copies = []
    for n, ((far, side), piece) in enumerate(zip(keys, pieces)):
        where = aligned(place(far, eig // rows) * rows, rows)
        for part in range(2):
            columns = pl.ds(part * depth + side * width, width)
            copies.append(pltpu.make_async_copy(piece.at[part], flat.at[where, columns], sem.at[2 * n + part]))
    for copy in copies:
        copy.start()
    for copy in copies:
        copy.wait()

    def step(n, carry):
        top, side = choose(n, [b[0] for b in blocks]), choose(n, [b[1] for b in blocks])
        out[n, 0], out[n, 1] = gram_block(flat[aligned(top * eig, eig), :], flat[aligned(side * eig, eig), :])
        return carry

    lax.fori_loop(0, len(blocks), step, 0)
    diagonal = [out.at[n] for n, block in enumerate(blocks) if block[0] == block[1]]
    direct_sums(diagonal, own, traces)


def early_gram(keys, pieces, own_elems, spins, eig, rb_count):
    blocks = early_blocks(spins)
    depth = 2 * rb_count * pieces[0].shape[2]
    return pl.pallas_call(
        functools.partial(early_kernel, eig, keys, rb_count, blocks),
        out_shape=(
            jax.ShapeDtypeStruct(((spins - 1) * eig, depth), BF16),
            jax.ShapeDtypeStruct((len(blocks), 2, eig, eig), BF16),
            sums_shape(2 * own_elems.shape[0]),
        ),
        in_specs=[ANY] * len(pieces) + [VMEM],
        out_specs=(VMEM, VMEM, VMEM),
        scratch_shapes=[pltpu.SemaphoreType.DMA((2 * len(pieces),))],
        compiler_params=params(32),
        cost_estimate=LONG,
        name="early_gram",
    )(*pieces, own_elems)


def side_columns(ref, rows, side, width, rb_count):
    return [ref[rows, (part * rb_count + side) * width : (part * rb_count + side + 1) * width] for part in range(2)]


def half_products(left, right):
    real = dot_nt(left[0], right[0]) + dot_nt(left[1], right[1])
    imag = dot_nt(left[0], right[1]) - dot_nt(left[1], right[0])
    return real, imag


def gather_last(eig, keys, others, pieces, last):
    rows, width = pieces[0].shape[1:]
    for (far, _), piece in zip(keys, pieces):
        where = aligned((place(far, eig // rows) - others * (eig // rows)) * rows, rows)
        for part in range(2):
            last[where, part * width : (part + 1) * width] = piece[part]


def late_begin_kernel(eig, keys, rb_count, flat, begun, *refs):
    pieces, (out, last) = refs[:-2], refs[-2:]
    side, width, others = keys[0][1], pieces[0].shape[2], flat.shape[0] // eig
    gather_last(eig, keys, others, pieces, last)
    right = [last[:, :width], last[:, width:]]
    for n in range(others):
        left = side_columns(flat, slice(n * eig, (n + 1) * eig), side, width, rb_count)
        out[n, 0], out[n, 1] = half_products(left, right)
    out[others, 0], out[others, 1] = half_products(right, right)


def late_begin(keys, flat, begun, pieces, spins, eig, rb_count):
    return pl.pallas_call(
        functools.partial(late_begin_kernel, eig, keys, rb_count),
        out_shape=jax.ShapeDtypeStruct((spins, 2, eig, eig), F32),
        in_specs=[VMEM, ANY] + [VMEM] * len(pieces),
        out_specs=VMEM,
        scratch_shapes=[pltpu.VMEM((eig, 2 * pieces[0].shape[2]), BF16)],
        compiler_params=params(32),
        cost_estimate=LITTLE,
        name="late_begin",
    )(flat, begun, *pieces)


def late_rows_kernel(eig, keys, rb_count, flat, partial, *refs):
    pieces, (out, last) = refs[:-2], refs[-2:]
    side, width = keys[0][1], pieces[0].shape[2]
    gather_last(eig, keys, flat.shape[0] // eig, pieces, last)
    right = [last[:, :width], last[:, width:]]
    for n in range(out.shape[0]):
        left = side_columns(flat, slice(n * eig, (n + 1) * eig), side, width, rb_count)
        real, imag = half_products(left, right)
        out[n, 0], out[n, 1] = (partial[n, 0] + real).astype(BF16), (partial[n, 1] + imag).astype(BF16)


def late_rest_kernel(eig, side, rb_count, flat, partial, last, out):
    count, width = out.shape[0] - 1, last.shape[1] // 2
    others = flat.shape[0] // eig
    right = [last[:, :width], last[:, width:]]
    for n in range(count + 1):
        spin = others - count + n
        left = right
        if n < count:
            left = side_columns(flat, slice(spin * eig, (spin + 1) * eig), side, width, rb_count)
        real, imag = half_products(left, right)
        out[n, 0], out[n, 1] = (partial[spin, 0] + real).astype(BF16), (partial[spin, 1] + imag).astype(BF16)


def late_rows(keys, flat, partial, pieces, spins, eig, rb_count):
    return pl.pallas_call(
        functools.partial(late_rows_kernel, eig, keys, rb_count),
        out_shape=(
            jax.ShapeDtypeStruct((spins // 2, 2, eig, eig), BF16),
            jax.ShapeDtypeStruct((eig, 2 * pieces[0].shape[2]), BF16),
        ),
        in_specs=[VMEM] * (2 + len(pieces)),
        out_specs=(VMEM, VMEM),
        compiler_params=params(32),
        cost_estimate=LONG,
        name="late_rows",
    )(flat, partial, *pieces)


def late_rest(side, flat, partial, last, spins, eig, rb_count):
    return pl.pallas_call(
        functools.partial(late_rest_kernel, eig, side, rb_count),
        out_shape=jax.ShapeDtypeStruct((spins - spins // 2, 2, eig, eig), BF16),
        in_specs=[VMEM] * 3,
        out_specs=VMEM,
        compiler_params=params(32),
        cost_estimate=LITTLE,
        name="late_rest",
    )(flat, partial, last)


def factors_kernel(diag_mom, elems, right_ref, left_ref, own_ref, held, sem):
    rank = lax.axis_index("rb")
    eig = held.shape[-1]
    copies = []
    for time in range(2):
        which = diag_mom[0, rank, lax.bitwise_xor(rank, time)]
        copies.append(pltpu.make_async_copy(elems.at[which], held.at[time], sem.at[time]))
    for slot in range(own_ref.shape[0]):
        copies.append(pltpu.make_async_copy(elems.at[diag_mom[0, slot, rank]], own_ref.at[slot], sem.at[2 + slot]))
    for copy in copies:
        copy.start()
    for copy in copies:
        copy.wait()
    for time in range(2):
        re, im = held[time, 0], held[time, 1]
        right_ref[time, :eig, :eig] = re
        right_ref[time, :eig, eig:] = im
        right_ref[time, eig:, :eig] = -im
        right_ref[time, eig:, eig:] = re
        re_t = re.astype(F32).T.astype(BF16)
        im_t = im.astype(F32).T.astype(BF16)
        left_ref[time, :eig, :eig] = re_t
        left_ref[time, :eig, eig:] = im_t
        left_ref[time, eig:, :eig] = im_t
        left_ref[time, eig:, eig:] = -re_t


def factors(diag_mom, src_elems):
    slots, eig = diag_mom.shape[1], src_elems.shape[-1]
    form = jax.ShapeDtypeStruct((2, 2 * eig, 2 * eig), BF16)
    return pl.pallas_call(
        factors_kernel,
        out_shape=(form, form, jax.ShapeDtypeStruct((slots, 2, eig, eig), BF16)),
        in_specs=[SMEM, ANY],
        out_specs=(VMEM, VMEM, VMEM),
        scratch_shapes=[pltpu.VMEM((2, 2, eig, eig), BF16), pltpu.SemaphoreType.DMA((2 + slots,))],
        compiler_params=params(32),
        cost_estimate=LITTLE,
        name="factors",
    )(diag_mom, src_elems)


def late_direct_kernel(rest, own, carried, out):
    direct_sums([rest.at[rest.shape[0] - 1]], own, out, carried)


def late_direct(rest, own, carried):
    return pl.pallas_call(
        late_direct_kernel,
        out_shape=sums_shape(carried.shape[0]),
        in_specs=[VMEM] * 3,
        out_specs=VMEM,
        compiler_params=params(32),
        cost_estimate=LITTLE,
        name="late_direct",
    )(rest, own, carried)


def cross_kernel(offs, own, other, right, left, *refs):
    carried, out = refs[:-1], refs[-1]
    eig = own.shape[-1]
    if len(other.shape) > len(own.shape):
        other = other.at[1 - lax.axis_index("rb")]
    real, imag = [], []

    def add(x, y, count, from_right, from_left):
        rows = [jnp.concatenate([x[n, 0], x[n, 1]], axis=1) for n in range(count)]
        product = dot(jnp.concatenate(rows, axis=0), from_right)
        for n in range(count):
            partner = dot(from_left, y[n].reshape(2 * eig, eig))
            mine = product[n * eig : (n + 1) * eig]
            p_re, p_im = mine[:, :eig], mine[:, eig:]
            w_re, w_im = partner[:eig], partner[eig:]
            real.append(fold(p_re * w_re - p_im * w_im))
            imag.append(fold(p_re * w_im + p_im * w_re))

    add(other, own, own.shape[0], right[1], left[0])
    add(own, other, offs, right[0], left[1])
    out[0] = functools.reduce(jnp.add, real + [ref[0] for ref in carried])
    out[1] = functools.reduce(jnp.add, imag + [ref[1] for ref in carried])


def cross_traces(offs, own, other, right, left, carried, name):
    return pl.pallas_call(
        functools.partial(cross_kernel, offs),
        out_shape=sums_shape(2),
        in_specs=[VMEM] * (4 + len(carried)),
        out_specs=VMEM,
        compiler_params=params(32),
        cost_estimate=LITTLE,
        name=name,
    )(own, other, right, left, *carried)


def last_cross_kernel(offs, own, other, right, left, direct, carried, out):
    count = direct.shape[0]
    for n in range(count):
        out[n] = direct[n]
    cross_kernel(offs, own, other, right, left, carried, out.at[pl.ds(count, 2)])


def last_cross(offs, own, other, right, left, direct, carried):
    return pl.pallas_call(
        functools.partial(last_cross_kernel, offs),
        out_shape=sums_shape(direct.shape[0] + 2),
        in_specs=[VMEM] * 6,
        out_specs=VMEM,
        compiler_params=params(32),
        cost_estimate=LITTLE,
        name="last_cross",
    )(own, other, right, left, direct, carried)


def final_kernel(slots, mine, theirs, count, out):
    rank = lax.axis_index("rb")
    lane = lax.broadcasted_iota(jnp.int32, (1, LANES), 1)

    def totals(ref):
        rows = jnp.concatenate([jnp.sum(ref[n], axis=0, keepdims=True) for n in range(ref.shape[0])], axis=0)
        sums = jnp.broadcast_to(jnp.sum(rows, axis=1, keepdims=True), rows.shape)
        return [sums[n : n + 1] for n in range(ref.shape[0])]

    def put(slot, kind, re, im):
        value = jnp.where(lane == 0, re, im) * 0.25
        out[0, slot, kind : kind + 1, :] = jnp.where(slot < count[0], value, 0.0)[:, :2]

    m, t = totals(mine), totals(theirs)
    for slot in range(slots):
        m_re, m_im, t_re, t_im = m[2 * slot], m[2 * slot + 1], t[2 * slot], t[2 * slot + 1]
        put(slot, 0, m_re * t_re - m_im * t_im, m_re * t_im + m_im * t_re)
        here = rank == slot
        put(slot, 1, jnp.where(here, m[2 * slots], t[2 * slots]), jnp.where(here, m[2 * slots + 1], t[2 * slots + 1]))


def final(mine, theirs, diag_count, slots):
    return pl.pallas_call(
        functools.partial(final_kernel, slots),
        out_shape=jax.ShapeDtypeStruct((1, slots, 2, 2), F32),
        in_specs=[VMEM, VMEM, SMEM],
        out_specs=VMEM,
        compiler_params=params(32),
        name="final",
    )(mine, theirs, diag_count)


def shards(peram, src_elems, owner_times, diag_mom, diag_count):
    tp_count, rb_count = lax.axis_size("tp"), lax.axis_size("rb")
    eig = src_elems.shape[-1]
    spins = tp_count * peram.shape[0] // eig
    slots = diag_mom.shape[1]

    head, tail, late, own = travel_order(tp_count, rb_count)
    early_keys = head + tail
    picked = pick(owner_times, peram, head, "pick_head", [jax.ShapeDtypeStruct((4, *peram.shape), BF16)])
    picked.update(pick(owner_times, peram, tail + late + own, "pick_tail", []))

    def send(key):
        far, side = key
        swapped = tp_count // 4 if far >= tp_count // 2 else 0
        pairs = [
            (tp * rb_count + rb, (tp ^ far ^ (swapped if tp < tp_count // 2 else 0)) * rb_count + (rb ^ side))
            for tp in range(tp_count)
            for rb in range(rb_count)
        ]
        return lax.ppermute(picked[key], ("tp", "rb"), pairs)

    swap = [(rb, rb ^ 1) for rb in range(rb_count)]
    right, left, own_elems = factors(diag_mom, src_elems)
    arrived = [send(key) for key in early_keys] + [picked[key] for key in own]
    flat, early, direct = early_gram(early_keys + own, arrived, own_elems, spins, eig, rb_count)
    early_both = lax.all_to_all(jnp.stack([early] * rb_count), "rb", 0, 0)
    offs = early.shape[0] - (spins - 1)
    begun = cross_traces(offs, early, early_both, right, left, [], "early_cross")

    halves = [[key for key in late if key[1] == side] for side in range(rb_count)]
    sent = [[send(key) for key in keys] for keys in halves]
    half = late_begin(halves[0], flat, begun, sent[0], spins, eig, rb_count)
    blocks, last = late_rows(halves[1], flat, half, sent[1], spins, eig, rb_count)
    swapped = lax.ppermute(blocks, "rb", swap)
    rest = late_rest(1, flat, half, last, spins, eig, rb_count)
    rest_swapped = lax.ppermute(rest, "rb", swap)
    traces = late_direct(rest, own_elems, direct)
    partial = cross_traces(blocks.shape[0], blocks, swapped, right, left, [begun], "late_cross")
    mine = last_cross(rest.shape[0] - 1, rest, rest_swapped, right, left, traces, partial)
    theirs = lax.ppermute(mine, "rb", swap)
    return final(mine, theirs, diag_count, slots)


def solution(mesh):
    in_specs = (
        P(("grp", "tp"), None, None, "rb"),
        P("grp", None, None, None),
        P("grp", None),
        P(("grp", "tp"), None, None),
        P(("grp", "tp")),
    )
    out_specs = P(("grp", "tp"), None, None, None)
    return jax.shard_map(shards, mesh=mesh, in_specs=in_specs, out_specs=out_specs, check_vma=False)
```

```python
import functools

import jax
import jax.numpy as jnp
from jax import lax
from jax.experimental import pallas as pl
from jax.experimental.pallas import tpu as pltpu
from jax.sharding import PartitionSpec as P

F32 = jnp.float32
BF16 = jnp.bfloat16
ANY = pl.BlockSpec(memory_space=pl.ANY)
SMEM = pl.BlockSpec(memory_space=pltpu.SMEM)
VMEM = pl.BlockSpec(memory_space=pltpu.VMEM)
SUBLANES = 8
LANES = 128
STEP = 16
MIB = 1 << 20
LITTLE = pl.CostEstimate(flops=1000, bytes_accessed=1000, transcendentals=0)
LONG = pl.CostEstimate(flops=5 * 10**10, bytes_accessed=1000, transcendentals=0)


def in_hbm(array):
    return pltpu.with_memory_space_constraint(array, pltpu.HBM)


def params(mib):
    return pltpu.CompilerParams(vmem_limit_bytes=mib * MIB)


def dot(left, right):
    return jnp.dot(left, right, preferred_element_type=F32)


def dot_nt(left, right):
    return lax.dot_general(left, right, (((1,), (1,)), ((), ())), preferred_element_type=F32)


def choose(index, values):
    out = jnp.int32(values[0])
    for n in range(1, len(values)):
        out = jnp.where(index == n, jnp.int32(values[n]), out)
    return out


def aligned(start, size):
    return pl.ds(pl.multiple_of(start, size), size)


def travel_order(tp_count, rb_count, rows):
    half, quarter = tp_count // 2, tp_count // 4
    cut = rows // 2 if rows % (2 * STEP) == 0 else rows

    def both(distances):
        return [(far, side, 0, rows) for far in distances for side in range(rb_count)]

    long, late = both(range(half, half + quarter)), both(range(half + quarter, tp_count))
    near, rest = both(reversed(range(quarter, half))), both(range(1, quarter))
    own, other = (0, 0, 0, rows), [(0, side, 0, rows) for side in range(1, rb_count)]
    step, part = len(long) // 4, len(rest) // 2
    first = long[: 2 * step]
    head = [(far, side, 0, cut) for far, side, _, _ in first]
    rests = [(far, side, cut, rows - cut) for far, side, _, _ in first if cut < rows]
    tail = rests[:step] + near[:step] + rests[step:] + long[2 * step : 3 * step] + rest[:part] + near[step : 2 * step]
    tail += other + long[3 * step :] + near[2 * step :] + rest[part:]
    return head, tail, late, [own]


def distance(far, tp_rank, tp_count):
    if far < tp_count // 2:
        return far
    return lax.bitwise_xor(jnp.int32(far), jnp.where(tp_rank < tp_count // 2, jnp.int32(tp_count // 4), jnp.int32(0)))


def pick_kernel(keys, times, table, *refs):
    outs, (held, wide, taken_times, sem, times_sem) = refs[:-5], refs[-5:]
    tp_rank, rb_rank = lax.axis_index("tp"), lax.axis_index("rb")
    packed = table.shape[2]
    ends = sorted({end for _, _, start, size in keys for end in (start, start + size)})

    def fetch(chunk):
        where = aligned(chunk * STEP, STEP)
        return pltpu.make_async_copy(table.at[where], held.at[where], sem.at[chunk])

    copy = pltpu.make_async_copy(times, taken_times, times_sem)
    copy.start()
    for chunk in range(ends[0] // STEP, ends[-1] // STEP):
        fetch(chunk).start()
    copy.wait()

    def step(covered, chunk, carry):
        fetch(chunk).wait()
        for n, (key, out) in enumerate(covered):
            far, side, start, _ = key
            owner = lax.bitwise_xor(tp_rank, distance(far, tp_rank, taken_times.shape[1]))
            time = taken_times[lax.bitwise_xor(rb_rank, side), owner]
            slot = n % wide.shape[0]
            wide[slot] = held[aligned(chunk * STEP, STEP), time].astype(F32).reshape(STEP * packed, LANES)
            where = aligned(chunk * STEP - start, STEP)
            for tile in range(packed // 2):
                for part in range(2):
                    taken = wide[slot, pl.ds(2 * tile + part, STEP, stride=packed), :]
                    out[part, where, tile * LANES : (tile + 1) * LANES] = taken.astype(BF16)
        return carry

    for low, high in zip(ends, ends[1:]):
        covered = [(key, out) for key, out in zip(keys, outs) if key[2] <= low and high <= key[2] + key[3]]
        lax.fori_loop(low // STEP, high // STEP, functools.partial(step, covered), 0)


def pick(owner_times, peram, keys, name, spare):
    rows, times, parts, width = peram.shape
    tiles = width // LANES
    table = peram.reshape(rows, times, parts, tiles, LANES).swapaxes(2, 3)
    table = table.reshape(rows, times, tiles * parts, LANES)
    picked = pl.pallas_call(
        functools.partial(pick_kernel, keys),
        out_shape=[jax.ShapeDtypeStruct((parts, size, width), BF16) for _, _, _, size in keys] + spare,
        in_specs=[ANY, ANY],
        out_specs=[VMEM] * len(keys) + [ANY] * len(spare),
        scratch_shapes=[
            pltpu.VMEM(table.shape, BF16),
            pltpu.VMEM((4, STEP * tiles * parts, LANES), F32),
            pltpu.SMEM(owner_times.shape[::-1], jnp.int32),
            pltpu.SemaphoreType.DMA((rows // STEP,)),
            pltpu.SemaphoreType.DMA,
        ],
        compiler_params=params(32),
        cost_estimate=LITTLE,
        name=name,
    )(in_hbm(owner_times.T), in_hbm(table))
    return dict(zip(keys, picked))


def place(far, per_spin):
    low = lax.axis_index("tp") % per_spin
    return (far // per_spin) * per_spin + lax.bitwise_xor(jnp.int32(far % per_spin), low)


def gram_block(left, right):
    depth = left.shape[1] // 2
    real = dot_nt(left, right)
    imag = dot_nt(left[:, :depth], right[:, depth:]) - dot_nt(left[:, depth:], right[:, :depth])
    return real.astype(BF16), imag.astype(BF16)


def fold(values):
    rows, columns = values.shape
    folded = jnp.sum(values.reshape(rows // SUBLANES, SUBLANES, columns), axis=0)
    return functools.reduce(jnp.add, [folded[:, n : n + LANES] for n in range(0, columns, LANES)])


def direct_sums(diagonal, own, out, carried=None):
    real = functools.reduce(jnp.add, [block[0].astype(F32) for block in diagonal])
    imag = functools.reduce(jnp.add, [block[1].astype(F32) for block in diagonal])
    for slot in range(own.shape[0]):
        elem_re, elem_im = own[slot, 0].astype(F32), own[slot, 1].astype(F32)
        sums = [fold(elem_re * real + elem_im * imag), fold(elem_im * real - elem_re * imag)]
        for part in range(2):
            n = 2 * slot + part
            out[n] = sums[part] if carried is None else sums[part] + carried[n]


def sums_shape(count):
    return jax.ShapeDtypeStruct((count, SUBLANES, LANES), F32)


def early_blocks(spins):
    off = [(s, t) for s in range(spins - 1) for t in range(s + 1, spins - 1)]
    return off + [(s, s) for s in range(spins - 1)]


def early_kernel(eig, keys, rb_count, rows, blocks, *refs):
    pieces, (own, flat, out, traces, sem) = refs[:-5], refs[-5:]
    width = pieces[0].shape[2]
    depth = rb_count * width
    copies = []
    for n, ((far, side, start, size), piece) in enumerate(zip(keys, pieces)):
        where = aligned(place(far, eig // rows) * rows + start, size)
        for part in range(2):
            columns = pl.ds(part * depth + side * width, width)
            copies.append(pltpu.make_async_copy(piece.at[part], flat.at[where, columns], sem.at[2 * n + part]))
    for copy in copies:
        copy.start()
    for copy in copies:
        copy.wait()

    def step(n, carry):
        top, side = choose(n, [b[0] for b in blocks]), choose(n, [b[1] for b in blocks])
        out[n, 0], out[n, 1] = gram_block(flat[aligned(top * eig, eig), :], flat[aligned(side * eig, eig), :])
        return carry

    lax.fori_loop(0, len(blocks), step, 0)
    diagonal = [out.at[n] for n, block in enumerate(blocks) if block[0] == block[1]]
    direct_sums(diagonal, own, traces)


def early_gram(keys, pieces, own_elems, spins, eig, rb_count, rows):
    blocks = early_blocks(spins)
    depth = 2 * rb_count * pieces[0].shape[2]
    return pl.pallas_call(
        functools.partial(early_kernel, eig, keys, rb_count, rows, blocks),
        out_shape=(
            jax.ShapeDtypeStruct(((spins - 1) * eig, depth), BF16),
            jax.ShapeDtypeStruct((len(blocks), 2, eig, eig), BF16),
            sums_shape(2 * own_elems.shape[0]),
        ),
        in_specs=[ANY] * len(pieces) + [VMEM],
        out_specs=(VMEM, VMEM, VMEM),
        scratch_shapes=[pltpu.SemaphoreType.DMA((2 * len(pieces),))],
        compiler_params=params(32),
        cost_estimate=LONG,
        name="early_gram",
    )(*pieces, own_elems)


def side_columns(ref, rows, side, width, rb_count):
    return [ref[rows, (part * rb_count + side) * width : (part * rb_count + side + 1) * width] for part in range(2)]


def half_products(left, right):
    real = dot_nt(left[0], right[0]) + dot_nt(left[1], right[1])
    imag = dot_nt(left[0], right[1]) - dot_nt(left[1], right[0])
    return real, imag


def gather_last(eig, keys, others, pieces, last):
    rows, width = pieces[0].shape[1:]
    for (far, _, _, _), piece in zip(keys, pieces):
        where = aligned((place(far, eig // rows) - others * (eig // rows)) * rows, rows)
        for part in range(2):
            last[where, part * width : (part + 1) * width] = piece[part]


def late_begin_kernel(eig, keys, rb_count, flat, begun, *refs):
    pieces, (out, last) = refs[:-2], refs[-2:]
    side, width, others = keys[0][1], pieces[0].shape[2], flat.shape[0] // eig
    gather_last(eig, keys, others, pieces, last)
    right = [last[:, :width], last[:, width:]]
    for n in range(others):
        left = side_columns(flat, slice(n * eig, (n + 1) * eig), side, width, rb_count)
        out[n, 0], out[n, 1] = half_products(left, right)
    out[others, 0], out[others, 1] = half_products(right, right)


def late_begin(keys, flat, begun, pieces, spins, eig, rb_count):
    return pl.pallas_call(
        functools.partial(late_begin_kernel, eig, keys, rb_count),
        out_shape=jax.ShapeDtypeStruct((spins, 2, eig, eig), F32),
        in_specs=[VMEM, ANY] + [VMEM] * len(pieces),
        out_specs=VMEM,
        scratch_shapes=[pltpu.VMEM((eig, 2 * pieces[0].shape[2]), BF16)],
        compiler_params=params(32),
        cost_estimate=LITTLE,
        name="late_begin",
    )(flat, begun, *pieces)


def late_rows_kernel(eig, keys, rb_count, flat, partial, *refs):
    pieces, (out, last) = refs[:-2], refs[-2:]
    side, width = keys[0][1], pieces[0].shape[2]
    gather_last(eig, keys, flat.shape[0] // eig, pieces, last)
    right = [last[:, :width], last[:, width:]]
    for n in range(out.shape[0]):
        left = side_columns(flat, slice(n * eig, (n + 1) * eig), side, width, rb_count)
        real, imag = half_products(left, right)
        out[n, 0], out[n, 1] = (partial[n, 0] + real).astype(BF16), (partial[n, 1] + imag).astype(BF16)


def late_rest_kernel(eig, side, rb_count, flat, partial, last, out):
    count, width = out.shape[0] - 1, last.shape[1] // 2
    others = flat.shape[0] // eig
    right = [last[:, :width], last[:, width:]]
    for n in range(count + 1):
        spin = others - count + n
        left = right
        if n < count:
            left = side_columns(flat, slice(spin * eig, (spin + 1) * eig), side, width, rb_count)
        real, imag = half_products(left, right)
        out[n, 0], out[n, 1] = (partial[spin, 0] + real).astype(BF16), (partial[spin, 1] + imag).astype(BF16)


def late_rows(keys, flat, partial, pieces, spins, eig, rb_count):
    return pl.pallas_call(
        functools.partial(late_rows_kernel, eig, keys, rb_count),
        out_shape=(
            jax.ShapeDtypeStruct((spins // 2, 2, eig, eig), BF16),
            jax.ShapeDtypeStruct((eig, 2 * pieces[0].shape[2]), BF16),
        ),
        in_specs=[VMEM] * (2 + len(pieces)),
        out_specs=(VMEM, VMEM),
        compiler_params=params(32),
        cost_estimate=LONG,
        name="late_rows",
    )(flat, partial, *pieces)


def late_rest(side, flat, partial, last, spins, eig, rb_count):
    return pl.pallas_call(
        functools.partial(late_rest_kernel, eig, side, rb_count),
        out_shape=jax.ShapeDtypeStruct((spins - spins // 2, 2, eig, eig), BF16),
        in_specs=[VMEM] * 3,
        out_specs=VMEM,
        compiler_params=params(32),
        cost_estimate=LITTLE,
        name="late_rest",
    )(flat, partial, last)


def factors_kernel(diag_mom, elems, right_ref, left_ref, own_ref, held, sem):
    rank = lax.axis_index("rb")
    eig = held.shape[-1]
    copies = []
    for time in range(2):
        which = diag_mom[0, rank, lax.bitwise_xor(rank, time)]
        copies.append(pltpu.make_async_copy(elems.at[which], held.at[time], sem.at[time]))
    for slot in range(own_ref.shape[0]):
        copies.append(pltpu.make_async_copy(elems.at[diag_mom[0, slot, rank]], own_ref.at[slot], sem.at[2 + slot]))
    for copy in copies:
        copy.start()
    for copy in copies:
        copy.wait()
    for time in range(2):
        re, im = held[time, 0], held[time, 1]
        right_ref[time, :eig, :eig] = re
        right_ref[time, :eig, eig:] = im
        right_ref[time, eig:, :eig] = -im
        right_ref[time, eig:, eig:] = re
        re_t = re.astype(F32).T.astype(BF16)
        im_t = im.astype(F32).T.astype(BF16)
        left_ref[time, :eig, :eig] = re_t
        left_ref[time, :eig, eig:] = im_t
        left_ref[time, eig:, :eig] = im_t
        left_ref[time, eig:, eig:] = -re_t


def factors(diag_mom, src_elems):
    slots, eig = diag_mom.shape[1], src_elems.shape[-1]
    form = jax.ShapeDtypeStruct((2, 2 * eig, 2 * eig), BF16)
    return pl.pallas_call(
        factors_kernel,
        out_shape=(form, form, jax.ShapeDtypeStruct((slots, 2, eig, eig), BF16)),
        in_specs=[SMEM, ANY],
        out_specs=(VMEM, VMEM, VMEM),
        scratch_shapes=[pltpu.VMEM((2, 2, eig, eig), BF16), pltpu.SemaphoreType.DMA((2 + slots,))],
        compiler_params=params(32),
        cost_estimate=LITTLE,
        name="factors",
    )(diag_mom, src_elems)


def late_direct_kernel(rest, own, carried, out):
    direct_sums([rest.at[rest.shape[0] - 1]], own, out, carried)


def late_direct(rest, own, carried):
    return pl.pallas_call(
        late_direct_kernel,
        out_shape=sums_shape(carried.shape[0]),
        in_specs=[VMEM] * 3,
        out_specs=VMEM,
        compiler_params=params(32),
        cost_estimate=LITTLE,
        name="late_direct",
    )(rest, own, carried)


def cross_kernel(offs, own, other, right, left, *refs):
    carried, out = refs[:-1], refs[-1]
    eig = own.shape[-1]
    if len(other.shape) > len(own.shape):
        other = other.at[1 - lax.axis_index("rb")]
    real, imag = [], []

    def add(x, y, count, from_right, from_left):
        rows = [jnp.concatenate([x[n, 0], x[n, 1]], axis=1) for n in range(count)]
        product = dot(jnp.concatenate(rows, axis=0), from_right)
        for n in range(count):
            partner = dot(from_left, y[n].reshape(2 * eig, eig))
            mine = product[n * eig : (n + 1) * eig]
            p_re, p_im = mine[:, :eig], mine[:, eig:]
            w_re, w_im = partner[:eig], partner[eig:]
            real.append(fold(p_re * w_re - p_im * w_im))
            imag.append(fold(p_re * w_im + p_im * w_re))

    add(other, own, own.shape[0], right[1], left[0])
    add(own, other, offs, right[0], left[1])
    out[0] = functools.reduce(jnp.add, real + [ref[0] for ref in carried])
    out[1] = functools.reduce(jnp.add, imag + [ref[1] for ref in carried])


def cross_traces(offs, own, other, right, left, carried, name):
    return pl.pallas_call(
        functools.partial(cross_kernel, offs),
        out_shape=sums_shape(2),
        in_specs=[VMEM] * (4 + len(carried)),
        out_specs=VMEM,
        compiler_params=params(32),
        cost_estimate=LITTLE,
        name=name,
    )(own, other, right, left, *carried)


def last_cross_kernel(offs, own, other, right, left, direct, carried, out):
    count = direct.shape[0]
    for n in range(count):
        out[n] = direct[n]
    cross_kernel(offs, own, other, right, left, carried, out.at[pl.ds(count, 2)])


def last_cross(offs, own, other, right, left, direct, carried):
    return pl.pallas_call(
        functools.partial(last_cross_kernel, offs),
        out_shape=sums_shape(direct.shape[0] + 2),
        in_specs=[VMEM] * 6,
        out_specs=VMEM,
        compiler_params=params(32),
        cost_estimate=LITTLE,
        name="last_cross",
    )(own, other, right, left, direct, carried)


def final_kernel(slots, mine, theirs, count, out):
    rank = lax.axis_index("rb")
    lane = lax.broadcasted_iota(jnp.int32, (1, LANES), 1)

    def totals(ref):
        rows = jnp.concatenate([jnp.sum(ref[n], axis=0, keepdims=True) for n in range(ref.shape[0])], axis=0)
        sums = jnp.broadcast_to(jnp.sum(rows, axis=1, keepdims=True), rows.shape)
        return [sums[n : n + 1] for n in range(ref.shape[0])]

    def put(slot, kind, re, im):
        value = jnp.where(lane == 0, re, im) * 0.25
        out[0, slot, kind : kind + 1, :] = jnp.where(slot < count[0], value, 0.0)[:, :2]

    m, t = totals(mine), totals(theirs)
    for slot in range(slots):
        m_re, m_im, t_re, t_im = m[2 * slot], m[2 * slot + 1], t[2 * slot], t[2 * slot + 1]
        put(slot, 0, m_re * t_re - m_im * t_im, m_re * t_im + m_im * t_re)
        here = rank == slot
        put(slot, 1, jnp.where(here, m[2 * slots], t[2 * slots]), jnp.where(here, m[2 * slots + 1], t[2 * slots + 1]))


def final(mine, theirs, diag_count, slots):
    return pl.pallas_call(
        functools.partial(final_kernel, slots),
        out_shape=jax.ShapeDtypeStruct((1, slots, 2, 2), F32),
        in_specs=[VMEM, VMEM, SMEM],
        out_specs=VMEM,
        compiler_params=params(32),
        name="final",
    )(mine, theirs, diag_count)


def shards(peram, src_elems, owner_times, diag_mom, diag_count):
    tp_count, rb_count = lax.axis_size("tp"), lax.axis_size("rb")
    eig = src_elems.shape[-1]
    spins = tp_count * peram.shape[0] // eig
    slots = diag_mom.shape[1]

    rows = peram.shape[0]
    head, tail, late, own = travel_order(tp_count, rb_count, rows)
    early_keys = head + tail
    picked = pick(owner_times, peram, head, "pick_head", [jax.ShapeDtypeStruct((4, *peram.shape), BF16)])
    picked.update(pick(owner_times, peram, tail + late + own, "pick_tail", []))

    def send(key):
        far, side, _, _ = key
        swapped = tp_count // 4 if far >= tp_count // 2 else 0
        pairs = [
            (tp * rb_count + rb, (tp ^ far ^ (swapped if tp < tp_count // 2 else 0)) * rb_count + (rb ^ side))
            for tp in range(tp_count)
            for rb in range(rb_count)
        ]
        return lax.ppermute(picked[key], ("tp", "rb"), pairs)

    swap = [(rb, rb ^ 1) for rb in range(rb_count)]
    right, left, own_elems = factors(diag_mom, src_elems)
    arrived = [send(key) for key in early_keys] + [picked[key] for key in own]
    flat, early, direct = early_gram(early_keys + own, arrived, own_elems, spins, eig, rb_count, rows)
    early_both = lax.all_to_all(jnp.stack([early] * rb_count), "rb", 0, 0)
    offs = early.shape[0] - (spins - 1)
    begun = cross_traces(offs, early, early_both, right, left, [], "early_cross")

    halves = [[key for key in late if key[1] == side] for side in range(rb_count)]
    sent = [[send(key) for key in keys] for keys in halves]
    half = late_begin(halves[0], flat, begun, sent[0], spins, eig, rb_count)
    blocks, last = late_rows(halves[1], flat, half, sent[1], spins, eig, rb_count)
    swapped = lax.ppermute(blocks, "rb", swap)
    rest = late_rest(1, flat, half, last, spins, eig, rb_count)
    rest_swapped = lax.ppermute(rest, "rb", swap)
    traces = late_direct(rest, own_elems, direct)
    partial = cross_traces(blocks.shape[0], blocks, swapped, right, left, [begun], "late_cross")
    mine = last_cross(rest.shape[0] - 1, rest, rest_swapped, right, left, traces, partial)
    theirs = lax.ppermute(mine, "rb", swap)
    return final(mine, theirs, diag_count, slots)


def solution(mesh):
    in_specs = (
        P(("grp", "tp"), None, None, "rb"),
        P("grp", None, None, None),
        P("grp", None),
        P(("grp", "tp"), None, None),
        P(("grp", "tp")),
    )
    out_specs = P(("grp", "tp"), None, None, None)
    return jax.shard_map(shards, mesh=mesh, in_specs=in_specs, out_specs=out_specs, check_vma=False)
```

```python
import functools

import jax
import jax.numpy as jnp
from jax import lax
from jax.experimental import pallas as pl
from jax.experimental.pallas import tpu as pltpu
from jax.sharding import PartitionSpec as P

F32 = jnp.float32
BF16 = jnp.bfloat16
ANY = pl.BlockSpec(memory_space=pl.ANY)
SMEM = pl.BlockSpec(memory_space=pltpu.SMEM)
VMEM = pl.BlockSpec(memory_space=pltpu.VMEM)
SUBLANES = 8
LANES = 128
STEP = 16
MIB = 1 << 20
LITTLE = pl.CostEstimate(flops=1000, bytes_accessed=1000, transcendentals=0)
LONG = pl.CostEstimate(flops=5 * 10**10, bytes_accessed=1000, transcendentals=0)


def in_hbm(array):
    return pltpu.with_memory_space_constraint(array, pltpu.HBM)


def params(mib):
    return pltpu.CompilerParams(vmem_limit_bytes=mib * MIB)


def dot(left, right):
    return jnp.dot(left, right, preferred_element_type=F32)


def dot_nt(left, right):
    return lax.dot_general(left, right, (((1,), (1,)), ((), ())), preferred_element_type=F32)


def choose(index, values):
    out = jnp.int32(values[0])
    for n in range(1, len(values)):
        out = jnp.where(index == n, jnp.int32(values[n]), out)
    return out


def aligned(start, size):
    return pl.ds(pl.multiple_of(start, size), size)


def travel_order(tp_count, rb_count):
    half, quarter = tp_count // 2, tp_count // 4

    def both(distances):
        return [(far, side) for far in distances for side in range(rb_count)]

    long, late = both(range(half, half + quarter)), both(range(half + quarter, tp_count))
    near, rest = both(reversed(range(quarter, half))), both(range(1, quarter))
    own, other = (0, 0), [(0, side) for side in range(1, rb_count)]
    step = len(long) // 4
    head = long[: 2 * step] + near[: 2 * step] + long[2 * step : 3 * step]
    tail = near[3 * step :] + other + near[2 * step : 3 * step] + long[3 * step :] + rest
    return head, tail, late, [own]


def distance(far, tp_rank, tp_count):
    if far < tp_count // 2:
        return far
    return lax.bitwise_xor(jnp.int32(far), jnp.where(tp_rank < tp_count // 2, jnp.int32(tp_count // 4), jnp.int32(0)))


def pick_kernel(keys, times, table, *refs):
    outs, (held, wide, taken_times, sem, times_sem) = refs[:-5], refs[-5:]
    tp_rank, rb_rank = lax.axis_index("tp"), lax.axis_index("rb")
    rows, _, packed, _ = table.shape

    def fetch(chunk):
        where = aligned(chunk * STEP, STEP)
        return pltpu.make_async_copy(table.at[where], held.at[where], sem.at[chunk])

    copy = pltpu.make_async_copy(times, taken_times, times_sem)
    copy.start()
    for chunk in range(rows // STEP):
        fetch(chunk).start()
    copy.wait()

    def step(chunk, carry):
        fetch(chunk).wait()
        where = aligned(chunk * STEP, STEP)
        for n, (far, side) in enumerate(keys):
            owner = lax.bitwise_xor(tp_rank, distance(far, tp_rank, taken_times.shape[1]))
            time = taken_times[lax.bitwise_xor(rb_rank, side), owner]
            slot = n % wide.shape[0]
            wide[slot] = held[where, time].astype(F32).reshape(STEP * packed, LANES)
            for tile in range(packed // 2):
                for part in range(2):
                    taken = wide[slot, pl.ds(2 * tile + part, STEP, stride=packed), :]
                    outs[n][part, where, tile * LANES : (tile + 1) * LANES] = taken.astype(BF16)
        return carry

    lax.fori_loop(0, rows // STEP, step, 0)


def pick(owner_times, peram, keys, name, spare):
    rows, times, parts, width = peram.shape
    tiles = width // LANES
    table = peram.reshape(rows, times, parts, tiles, LANES).swapaxes(2, 3)
    table = table.reshape(rows, times, tiles * parts, LANES)
    picked = pl.pallas_call(
        functools.partial(pick_kernel, keys),
        out_shape=[jax.ShapeDtypeStruct((parts, rows, width), BF16)] * len(keys) + spare,
        in_specs=[ANY, ANY],
        out_specs=[VMEM] * len(keys) + [ANY] * len(spare),
        scratch_shapes=[
            pltpu.VMEM(table.shape, BF16),
            pltpu.VMEM((4, STEP * tiles * parts, LANES), F32),
            pltpu.SMEM(owner_times.shape[::-1], jnp.int32),
            pltpu.SemaphoreType.DMA((rows // STEP,)),
            pltpu.SemaphoreType.DMA,
        ],
        compiler_params=params(32),
        cost_estimate=LITTLE,
        name=name,
    )(in_hbm(owner_times.T), in_hbm(table))
    return dict(zip(keys, picked))


def place(far, per_spin):
    low = lax.axis_index("tp") % per_spin
    return (far // per_spin) * per_spin + lax.bitwise_xor(jnp.int32(far % per_spin), low)


def gram_block(left, right):
    depth = left.shape[1] // 2
    real = dot_nt(left, right)
    imag = dot_nt(left[:, :depth], right[:, depth:]) - dot_nt(left[:, depth:], right[:, :depth])
    return real.astype(BF16), imag.astype(BF16)


def fold(values):
    rows, columns = values.shape
    folded = jnp.sum(values.reshape(rows // SUBLANES, SUBLANES, columns), axis=0)
    return functools.reduce(jnp.add, [folded[:, n : n + LANES] for n in range(0, columns, LANES)])


def direct_sums(diagonal, own, out, carried=None):
    real = functools.reduce(jnp.add, [block[0].astype(F32) for block in diagonal])
    imag = functools.reduce(jnp.add, [block[1].astype(F32) for block in diagonal])
    for slot in range(own.shape[0]):
        elem_re, elem_im = own[slot, 0].astype(F32), own[slot, 1].astype(F32)
        sums = [fold(elem_re * real + elem_im * imag), fold(elem_im * real - elem_re * imag)]
        for part in range(2):
            n = 2 * slot + part
            out[n] = sums[part] if carried is None else sums[part] + carried[n]


def sums_shape(count):
    return jax.ShapeDtypeStruct((count, SUBLANES, LANES), F32)


def early_blocks(spins):
    off = [(s, t) for s in range(spins - 1) for t in range(s + 1, spins - 1)]
    return off + [(s, s) for s in range(spins - 1)]


def early_kernel(eig, keys, rb_count, blocks, *refs):
    pieces, (own, flat, out, traces, sem) = refs[:-5], refs[-5:]
    rows, width = pieces[0].shape[1:]
    depth = rb_count * width
    copies = []
    for n, ((far, side), piece) in enumerate(zip(keys, pieces)):
        where = aligned(place(far, eig // rows) * rows, rows)
        for part in range(2):
            columns = pl.ds(part * depth + side * width, width)
            copies.append(pltpu.make_async_copy(piece.at[part], flat.at[where, columns], sem.at[2 * n + part]))
    for copy in copies:
        copy.start()
    for copy in copies:
        copy.wait()

    def step(n, carry):
        top, side = choose(n, [b[0] for b in blocks]), choose(n, [b[1] for b in blocks])
        out[n, 0], out[n, 1] = gram_block(flat[aligned(top * eig, eig), :], flat[aligned(side * eig, eig), :])
        return carry

    lax.fori_loop(0, len(blocks), step, 0)
    diagonal = [out.at[n] for n, block in enumerate(blocks) if block[0] == block[1]]
    direct_sums(diagonal, own, traces)


def early_gram(keys, pieces, own_elems, spins, eig, rb_count):
    blocks = early_blocks(spins)
    depth = 2 * rb_count * pieces[0].shape[2]
    return pl.pallas_call(
        functools.partial(early_kernel, eig, keys, rb_count, blocks),
        out_shape=(
            jax.ShapeDtypeStruct(((spins - 1) * eig, depth), BF16),
            jax.ShapeDtypeStruct((len(blocks), 2, eig, eig), BF16),
            sums_shape(2 * own_elems.shape[0]),
        ),
        in_specs=[ANY] * len(pieces) + [VMEM],
        out_specs=(VMEM, VMEM, VMEM),
        scratch_shapes=[pltpu.SemaphoreType.DMA((2 * len(pieces),))],
        compiler_params=params(32),
        cost_estimate=LONG,
        name="early_gram",
    )(*pieces, own_elems)


def side_columns(ref, rows, side, width, rb_count):
    return [ref[rows, (part * rb_count + side) * width : (part * rb_count + side + 1) * width] for part in range(2)]


def half_products(left, right):
    real = dot_nt(left[0], right[0]) + dot_nt(left[1], right[1])
    imag = dot_nt(left[0], right[1]) - dot_nt(left[1], right[0])
    return real, imag


def gather_last(eig, keys, others, pieces, last):
    rows, width = pieces[0].shape[1:]
    for (far, _), piece in zip(keys, pieces):
        where = aligned((place(far, eig // rows) - others * (eig // rows)) * rows, rows)
        for part in range(2):
            last[where, part * width : (part + 1) * width] = piece[part]


def late_begin_kernel(eig, keys, rb_count, flat, begun, *refs):
    pieces, (out, last) = refs[:-2], refs[-2:]
    side, width, others = keys[0][1], pieces[0].shape[2], flat.shape[0] // eig
    gather_last(eig, keys, others, pieces, last)
    right = [last[:, :width], last[:, width:]]
    for n in range(others):
        left = side_columns(flat, slice(n * eig, (n + 1) * eig), side, width, rb_count)
        out[n, 0], out[n, 1] = half_products(left, right)
    out[others, 0], out[others, 1] = half_products(right, right)


def late_begin(keys, flat, begun, pieces, spins, eig, rb_count):
    return pl.pallas_call(
        functools.partial(late_begin_kernel, eig, keys, rb_count),
        out_shape=jax.ShapeDtypeStruct((spins, 2, eig, eig), F32),
        in_specs=[VMEM, ANY] + [VMEM] * len(pieces),
        out_specs=VMEM,
        scratch_shapes=[pltpu.VMEM((eig, 2 * pieces[0].shape[2]), BF16)],
        compiler_params=params(32),
        cost_estimate=LITTLE,
        name="late_begin",
    )(flat, begun, *pieces)


def late_rows_kernel(eig, keys, rb_count, flat, partial, *refs):
    pieces, (out, last) = refs[:-2], refs[-2:]
    side, width = keys[0][1], pieces[0].shape[2]
    gather_last(eig, keys, flat.shape[0] // eig, pieces, last)
    right = [last[:, :width], last[:, width:]]
    for n in range(out.shape[0]):
        left = side_columns(flat, slice(n * eig, (n + 1) * eig), side, width, rb_count)
        real, imag = half_products(left, right)
        out[n, 0], out[n, 1] = (partial[n, 0] + real).astype(BF16), (partial[n, 1] + imag).astype(BF16)


def late_rest_kernel(eig, side, rb_count, flat, partial, last, out):
    count, width = out.shape[0] - 1, last.shape[1] // 2
    others = flat.shape[0] // eig
    right = [last[:, :width], last[:, width:]]
    for n in range(count + 1):
        spin = others - count + n
        left = right
        if n < count:
            left = side_columns(flat, slice(spin * eig, (spin + 1) * eig), side, width, rb_count)
        real, imag = half_products(left, right)
        out[n, 0], out[n, 1] = (partial[spin, 0] + real).astype(BF16), (partial[spin, 1] + imag).astype(BF16)


def late_rows(keys, flat, partial, pieces, spins, eig, rb_count):
    return pl.pallas_call(
        functools.partial(late_rows_kernel, eig, keys, rb_count),
        out_shape=(
            jax.ShapeDtypeStruct((spins // 2, 2, eig, eig), BF16),
            jax.ShapeDtypeStruct((eig, 2 * pieces[0].shape[2]), BF16),
        ),
        in_specs=[VMEM] * (2 + len(pieces)),
        out_specs=(VMEM, VMEM),
        compiler_params=params(32),
        cost_estimate=LONG,
        name="late_rows",
    )(flat, partial, *pieces)


def late_rest(side, flat, partial, last, spins, eig, rb_count):
    return pl.pallas_call(
        functools.partial(late_rest_kernel, eig, side, rb_count),
        out_shape=jax.ShapeDtypeStruct((spins - spins // 2, 2, eig, eig), BF16),
        in_specs=[VMEM] * 3,
        out_specs=VMEM,
        compiler_params=params(32),
        cost_estimate=LITTLE,
        name="late_rest",
    )(flat, partial, last)


def factors_kernel(diag_mom, elems, right_ref, left_ref, own_ref, held, sem):
    rank = lax.axis_index("rb")
    eig = held.shape[-1]
    copies = []
    for time in range(2):
        which = diag_mom[0, rank, lax.bitwise_xor(rank, time)]
        copies.append(pltpu.make_async_copy(elems.at[which], held.at[time], sem.at[time]))
    for slot in range(own_ref.shape[0]):
        copies.append(pltpu.make_async_copy(elems.at[diag_mom[0, slot, rank]], own_ref.at[slot], sem.at[2 + slot]))
    for copy in copies:
        copy.start()
    for copy in copies:
        copy.wait()
    for time in range(2):
        re, im = held[time, 0], held[time, 1]
        right_ref[time, :eig, :eig] = re
        right_ref[time, :eig, eig:] = im
        right_ref[time, eig:, :eig] = -im
        right_ref[time, eig:, eig:] = re
        re_t = re.astype(F32).T.astype(BF16)
        im_t = im.astype(F32).T.astype(BF16)
        left_ref[time, :eig, :eig] = re_t
        left_ref[time, :eig, eig:] = im_t
        left_ref[time, eig:, :eig] = im_t
        left_ref[time, eig:, eig:] = -re_t


def factors(diag_mom, src_elems):
    slots, eig = diag_mom.shape[1], src_elems.shape[-1]
    form = jax.ShapeDtypeStruct((2, 2 * eig, 2 * eig), BF16)
    return pl.pallas_call(
        factors_kernel,
        out_shape=(form, form, jax.ShapeDtypeStruct((slots, 2, eig, eig), BF16)),
        in_specs=[SMEM, ANY],
        out_specs=(VMEM, VMEM, VMEM),
        scratch_shapes=[pltpu.VMEM((2, 2, eig, eig), BF16), pltpu.SemaphoreType.DMA((2 + slots,))],
        compiler_params=params(32),
        cost_estimate=LITTLE,
        name="factors",
    )(diag_mom, src_elems)


def late_direct_kernel(rest, own, carried, out):
    direct_sums([rest.at[rest.shape[0] - 1]], own, out, carried)


def late_direct(rest, own, carried):
    return pl.pallas_call(
        late_direct_kernel,
        out_shape=sums_shape(carried.shape[0]),
        in_specs=[VMEM] * 3,
        out_specs=VMEM,
        compiler_params=params(32),
        cost_estimate=LITTLE,
        name="late_direct",
    )(rest, own, carried)


def cross_kernel(offs, own, other, right, left, *refs):
    carried, out = refs[:-1], refs[-1]
    eig = own.shape[-1]
    if len(other.shape) > len(own.shape):
        other = other.at[1 - lax.axis_index("rb")]
    real, imag = [], []

    def add(x, y, count, from_right, from_left):
        rows = [jnp.concatenate([x[n, 0], x[n, 1]], axis=1) for n in range(count)]
        product = dot(jnp.concatenate(rows, axis=0), from_right)
        for n in range(count):
            partner = dot(from_left, y[n].reshape(2 * eig, eig))
            mine = product[n * eig : (n + 1) * eig]
            p_re, p_im = mine[:, :eig], mine[:, eig:]
            w_re, w_im = partner[:eig], partner[eig:]
            real.append(fold(p_re * w_re - p_im * w_im))
            imag.append(fold(p_re * w_im + p_im * w_re))

    add(other, own, own.shape[0], right[1], left[0])
    add(own, other, offs, right[0], left[1])
    out[0] = functools.reduce(jnp.add, real + [ref[0] for ref in carried])
    out[1] = functools.reduce(jnp.add, imag + [ref[1] for ref in carried])


def cross_traces(offs, own, other, right, left, carried, name):
    return pl.pallas_call(
        functools.partial(cross_kernel, offs),
        out_shape=sums_shape(2),
        in_specs=[VMEM] * (4 + len(carried)),
        out_specs=VMEM,
        compiler_params=params(32),
        cost_estimate=LITTLE,
        name=name,
    )(own, other, right, left, *carried)


def last_cross_kernel(offs, own, other, right, left, direct, carried, out):
    count = direct.shape[0]
    for n in range(count):
        out[n] = direct[n]
    cross_kernel(offs, own, other, right, left, carried, out.at[pl.ds(count, 2)])


def last_cross(offs, own, other, right, left, direct, carried):
    return pl.pallas_call(
        functools.partial(last_cross_kernel, offs),
        out_shape=sums_shape(direct.shape[0] + 2),
        in_specs=[VMEM] * 6,
        out_specs=VMEM,
        compiler_params=params(32),
        cost_estimate=LITTLE,
        name="last_cross",
    )(own, other, right, left, direct, carried)


def final_kernel(slots, mine, theirs, count, out):
    rank = lax.axis_index("rb")
    lane = lax.broadcasted_iota(jnp.int32, (1, LANES), 1)

    def totals(ref):
        rows = jnp.concatenate([jnp.sum(ref[n], axis=0, keepdims=True) for n in range(ref.shape[0])], axis=0)
        sums = jnp.broadcast_to(jnp.sum(rows, axis=1, keepdims=True), rows.shape)
        return [sums[n : n + 1] for n in range(ref.shape[0])]

    def put(slot, kind, re, im):
        value = jnp.where(lane == 0, re, im) * 0.25
        out[0, slot, kind : kind + 1, :] = jnp.where(slot < count[0], value, 0.0)[:, :2]

    m, t = totals(mine), totals(theirs)
    for slot in range(slots):
        m_re, m_im, t_re, t_im = m[2 * slot], m[2 * slot + 1], t[2 * slot], t[2 * slot + 1]
        put(slot, 0, m_re * t_re - m_im * t_im, m_re * t_im + m_im * t_re)
        here = rank == slot
        put(slot, 1, jnp.where(here, m[2 * slots], t[2 * slots]), jnp.where(here, m[2 * slots + 1], t[2 * slots + 1]))


def final(mine, theirs, diag_count, slots):
    return pl.pallas_call(
        functools.partial(final_kernel, slots),
        out_shape=jax.ShapeDtypeStruct((1, slots, 2, 2), F32),
        in_specs=[VMEM, VMEM, SMEM],
        out_specs=VMEM,
        compiler_params=params(32),
        name="final",
    )(mine, theirs, diag_count)


def shards(peram, src_elems, owner_times, diag_mom, diag_count):
    tp_count, rb_count = lax.axis_size("tp"), lax.axis_size("rb")
    eig = src_elems.shape[-1]
    spins = tp_count * peram.shape[0] // eig
    slots = diag_mom.shape[1]

    head, tail, late, own = travel_order(tp_count, rb_count)
    early_keys = head + tail
    picked = pick(owner_times, peram, head, "pick_head", [jax.ShapeDtypeStruct((4, *peram.shape), BF16)])
    picked.update(pick(owner_times, peram, tail + late + own, "pick_tail", []))

    def send(key):
        far, side = key
        swapped = tp_count // 4 if far >= tp_count // 2 else 0
        pairs = [
            (tp * rb_count + rb, (tp ^ far ^ (swapped if tp < tp_count // 2 else 0)) * rb_count + (rb ^ side))
            for tp in range(tp_count)
            for rb in range(rb_count)
        ]
        return lax.ppermute(picked[key], ("tp", "rb"), pairs)

    swap = [(rb, rb ^ 1) for rb in range(rb_count)]
    right, left, own_elems = factors(diag_mom, src_elems)
    arrived = [send(key) for key in early_keys] + [picked[key] for key in own]
    flat, early, direct = early_gram(early_keys + own, arrived, own_elems, spins, eig, rb_count)
    early_both = lax.all_to_all(jnp.stack([early] * rb_count), "rb", 0, 0)
    offs = early.shape[0] - (spins - 1)
    begun = cross_traces(offs, early, early_both, right, left, [], "early_cross")

    halves = [[key for key in late if key[1] == side] for side in range(rb_count)]
    sent = [[send(key) for key in keys] for keys in halves]
    half = late_begin(halves[0], flat, begun, sent[0], spins, eig, rb_count)
    blocks, last = late_rows(halves[1], flat, half, sent[1], spins, eig, rb_count)
    swapped = lax.ppermute(blocks, "rb", swap)
    rest = late_rest(1, flat, half, last, spins, eig, rb_count)
    rest_swapped = lax.ppermute(rest, "rb", swap)
    traces = late_direct(rest, own_elems, direct)
    partial = cross_traces(blocks.shape[0], blocks, swapped, right, left, [begun], "late_cross")
    mine = last_cross(rest.shape[0] - 1, rest, rest_swapped, right, left, traces, partial)
    theirs = lax.ppermute(mine, "rb", swap)
    return final(mine, theirs, diag_count, slots)


def solution(mesh):
    in_specs = (
        P(("grp", "tp"), None, None, "rb"),
        P("grp", None, None, None),
        P("grp", None),
        P(("grp", "tp"), None, None),
        P(("grp", "tp")),
    )
    out_specs = P(("grp", "tp"), None, None, None)
    return jax.shard_map(shards, mesh=mesh, in_specs=in_specs, out_specs=out_specs, check_vma=False)
```

```python
import functools

import jax
import jax.numpy as jnp
from jax import lax
from jax.experimental import pallas as pl
from jax.experimental.pallas import tpu as pltpu
from jax.sharding import PartitionSpec as P

F32 = jnp.float32
BF16 = jnp.bfloat16
ANY = pl.BlockSpec(memory_space=pl.ANY)
SMEM = pl.BlockSpec(memory_space=pltpu.SMEM)
VMEM = pl.BlockSpec(memory_space=pltpu.VMEM)
SUBLANES = 8
LANES = 128
STEP = 16
MIB = 1 << 20
LITTLE = pl.CostEstimate(flops=1000, bytes_accessed=1000, transcendentals=0)
LONG = pl.CostEstimate(flops=5 * 10**10, bytes_accessed=1000, transcendentals=0)


def in_hbm(array):
    return pltpu.with_memory_space_constraint(array, pltpu.HBM)


def params(mib):
    return pltpu.CompilerParams(vmem_limit_bytes=mib * MIB)


def dot(left, right):
    return jnp.dot(left, right, preferred_element_type=F32)


def dot_nt(left, right):
    return lax.dot_general(left, right, (((1,), (1,)), ((), ())), preferred_element_type=F32)


def choose(index, values):
    out = jnp.int32(values[0])
    for n in range(1, len(values)):
        out = jnp.where(index == n, jnp.int32(values[n]), out)
    return out


def aligned(start, size):
    return pl.ds(pl.multiple_of(start, size), size)


def travel_order(tp_count, rb_count):
    half, quarter = tp_count // 2, tp_count // 4

    def both(distances):
        return [(far, side) for far in distances for side in range(rb_count)]

    long, late = both(range(half, half + quarter)), both(range(half + quarter, tp_count))
    near, rest = both(reversed(range(quarter, half))), both(range(1, quarter))
    own, other = (0, 0), [(0, side) for side in range(1, rb_count)]
    step, part = len(long) // 4, len(rest) // 2
    head = long[: 2 * step] + near[: 2 * step] + long[2 * step : 3 * step]
    tail = rest[:part] + other + near[2 * step : 3 * step] + long[3 * step :] + rest[part:] + near[3 * step :]
    return head, tail, late, [own]


def distance(far, tp_rank, tp_count):
    if far < tp_count // 2:
        return far
    return lax.bitwise_xor(jnp.int32(far), jnp.where(tp_rank < tp_count // 2, jnp.int32(tp_count // 4), jnp.int32(0)))


def pick_kernel(keys, times, table, *refs):
    outs, (held, wide, taken_times, sem, times_sem) = refs[:-5], refs[-5:]
    tp_rank, rb_rank = lax.axis_index("tp"), lax.axis_index("rb")
    rows, _, packed, _ = table.shape

    def fetch(chunk):
        where = aligned(chunk * STEP, STEP)
        return pltpu.make_async_copy(table.at[where], held.at[where], sem.at[chunk])

    copy = pltpu.make_async_copy(times, taken_times, times_sem)
    copy.start()
    for chunk in range(rows // STEP):
        fetch(chunk).start()
    copy.wait()

    def step(chunk, carry):
        fetch(chunk).wait()
        where = aligned(chunk * STEP, STEP)
        for n, (far, side) in enumerate(keys):
            owner = lax.bitwise_xor(tp_rank, distance(far, tp_rank, taken_times.shape[1]))
            time = taken_times[lax.bitwise_xor(rb_rank, side), owner]
            slot = n % wide.shape[0]
            wide[slot] = held[where, time].astype(F32).reshape(STEP * packed, LANES)
            for tile in range(packed // 2):
                for part in range(2):
                    taken = wide[slot, pl.ds(2 * tile + part, STEP, stride=packed), :]
                    outs[n][part, where, tile * LANES : (tile + 1) * LANES] = taken.astype(BF16)
        return carry

    lax.fori_loop(0, rows // STEP, step, 0)


def pick(owner_times, peram, keys, name, spare):
    rows, times, parts, width = peram.shape
    tiles = width // LANES
    table = peram.reshape(rows, times, parts, tiles, LANES).swapaxes(2, 3)
    table = table.reshape(rows, times, tiles * parts, LANES)
    picked = pl.pallas_call(
        functools.partial(pick_kernel, keys),
        out_shape=[jax.ShapeDtypeStruct((parts, rows, width), BF16)] * len(keys) + spare,
        in_specs=[ANY, ANY],
        out_specs=[VMEM] * len(keys) + [ANY] * len(spare),
        scratch_shapes=[
            pltpu.VMEM(table.shape, BF16),
            pltpu.VMEM((4, STEP * tiles * parts, LANES), F32),
            pltpu.SMEM(owner_times.shape[::-1], jnp.int32),
            pltpu.SemaphoreType.DMA((rows // STEP,)),
            pltpu.SemaphoreType.DMA,
        ],
        compiler_params=params(32),
        cost_estimate=LITTLE,
        name=name,
    )(in_hbm(owner_times.T), in_hbm(table))
    return dict(zip(keys, picked))


def place(far, per_spin):
    low = lax.axis_index("tp") % per_spin
    return (far // per_spin) * per_spin + lax.bitwise_xor(jnp.int32(far % per_spin), low)


def gram_block(left, right):
    depth = left.shape[1] // 2
    real = dot_nt(left, right)
    imag = dot_nt(left[:, :depth], right[:, depth:]) - dot_nt(left[:, depth:], right[:, :depth])
    return real.astype(BF16), imag.astype(BF16)


def fold(values):
    rows, columns = values.shape
    folded = jnp.sum(values.reshape(rows // SUBLANES, SUBLANES, columns), axis=0)
    return functools.reduce(jnp.add, [folded[:, n : n + LANES] for n in range(0, columns, LANES)])


def direct_sums(diagonal, own, out, carried=None):
    real = functools.reduce(jnp.add, [block[0].astype(F32) for block in diagonal])
    imag = functools.reduce(jnp.add, [block[1].astype(F32) for block in diagonal])
    for slot in range(own.shape[0]):
        elem_re, elem_im = own[slot, 0].astype(F32), own[slot, 1].astype(F32)
        sums = [fold(elem_re * real + elem_im * imag), fold(elem_im * real - elem_re * imag)]
        for part in range(2):
            n = 2 * slot + part
            out[n] = sums[part] if carried is None else sums[part] + carried[n]


def sums_shape(count):
    return jax.ShapeDtypeStruct((count, SUBLANES, LANES), F32)


def early_blocks(spins):
    off = [(s, t) for s in range(spins - 1) for t in range(s + 1, spins - 1)]
    return off + [(s, s) for s in range(spins - 1)]


def early_kernel(eig, keys, rb_count, blocks, *refs):
    pieces, (own, flat, out, traces, sem) = refs[:-5], refs[-5:]
    rows, width = pieces[0].shape[1:]
    depth = rb_count * width
    copies = []
    for n, ((far, side), piece) in enumerate(zip(keys, pieces)):
        where = aligned(place(far, eig // rows) * rows, rows)
        for part in range(2):
            columns = pl.ds(part * depth + side * width, width)
            copies.append(pltpu.make_async_copy(piece.at[part], flat.at[where, columns], sem.at[2 * n + part]))
    for copy in copies:
        copy.start()
    for copy in copies:
        copy.wait()

    def step(n, carry):
        top, side = choose(n, [b[0] for b in blocks]), choose(n, [b[1] for b in blocks])
        out[n, 0], out[n, 1] = gram_block(flat[aligned(top * eig, eig), :], flat[aligned(side * eig, eig), :])
        return carry

    lax.fori_loop(0, len(blocks), step, 0)
    diagonal = [out.at[n] for n, block in enumerate(blocks) if block[0] == block[1]]
    direct_sums(diagonal, own, traces)


def early_gram(keys, pieces, own_elems, spins, eig, rb_count):
    blocks = early_blocks(spins)
    depth = 2 * rb_count * pieces[0].shape[2]
    return pl.pallas_call(
        functools.partial(early_kernel, eig, keys, rb_count, blocks),
        out_shape=(
            jax.ShapeDtypeStruct(((spins - 1) * eig, depth), BF16),
            jax.ShapeDtypeStruct((len(blocks), 2, eig, eig), BF16),
            sums_shape(2 * own_elems.shape[0]),
        ),
        in_specs=[ANY] * len(pieces) + [VMEM],
        out_specs=(VMEM, VMEM, VMEM),
        scratch_shapes=[pltpu.SemaphoreType.DMA((2 * len(pieces),))],
        compiler_params=params(32),
        cost_estimate=LONG,
        name="early_gram",
    )(*pieces, own_elems)


def side_columns(ref, rows, side, width, rb_count):
    return [ref[rows, (part * rb_count + side) * width : (part * rb_count + side + 1) * width] for part in range(2)]


def half_products(left, right):
    real = dot_nt(left[0], right[0]) + dot_nt(left[1], right[1])
    imag = dot_nt(left[0], right[1]) - dot_nt(left[1], right[0])
    return real, imag


def gather_last(eig, keys, others, pieces, last):
    rows, width = pieces[0].shape[1:]
    for (far, _), piece in zip(keys, pieces):
        where = aligned((place(far, eig // rows) - others * (eig // rows)) * rows, rows)
        for part in range(2):
            last[where, part * width : (part + 1) * width] = piece[part]


def late_begin_kernel(eig, keys, rb_count, flat, begun, *refs):
    pieces, (out, last) = refs[:-2], refs[-2:]
    side, width, others = keys[0][1], pieces[0].shape[2], flat.shape[0] // eig
    gather_last(eig, keys, others, pieces, last)
    right = [last[:, :width], last[:, width:]]
    for n in range(others):
        left = side_columns(flat, slice(n * eig, (n + 1) * eig), side, width, rb_count)
        out[n, 0], out[n, 1] = half_products(left, right)
    out[others, 0], out[others, 1] = half_products(right, right)


def late_begin(keys, flat, begun, pieces, spins, eig, rb_count):
    return pl.pallas_call(
        functools.partial(late_begin_kernel, eig, keys, rb_count),
        out_shape=jax.ShapeDtypeStruct((spins, 2, eig, eig), F32),
        in_specs=[VMEM, ANY] + [VMEM] * len(pieces),
        out_specs=VMEM,
        scratch_shapes=[pltpu.VMEM((eig, 2 * pieces[0].shape[2]), BF16)],
        compiler_params=params(32),
        cost_estimate=LITTLE,
        name="late_begin",
    )(flat, begun, *pieces)


def late_rows_kernel(eig, keys, rb_count, flat, partial, *refs):
    pieces, (out, last) = refs[:-2], refs[-2:]
    side, width = keys[0][1], pieces[0].shape[2]
    gather_last(eig, keys, flat.shape[0] // eig, pieces, last)
    right = [last[:, :width], last[:, width:]]
    for n in range(out.shape[0]):
        left = side_columns(flat, slice(n * eig, (n + 1) * eig), side, width, rb_count)
        real, imag = half_products(left, right)
        out[n, 0], out[n, 1] = (partial[n, 0] + real).astype(BF16), (partial[n, 1] + imag).astype(BF16)


def late_rest_kernel(eig, side, rb_count, flat, partial, last, out):
    count, width = out.shape[0] - 1, last.shape[1] // 2
    others = flat.shape[0] // eig
    right = [last[:, :width], last[:, width:]]
    for n in range(count + 1):
        spin = others - count + n
        left = right
        if n < count:
            left = side_columns(flat, slice(spin * eig, (spin + 1) * eig), side, width, rb_count)
        real, imag = half_products(left, right)
        out[n, 0], out[n, 1] = (partial[spin, 0] + real).astype(BF16), (partial[spin, 1] + imag).astype(BF16)


def late_rows(keys, flat, partial, pieces, spins, eig, rb_count):
    return pl.pallas_call(
        functools.partial(late_rows_kernel, eig, keys, rb_count),
        out_shape=(
            jax.ShapeDtypeStruct((spins // 2, 2, eig, eig), BF16),
            jax.ShapeDtypeStruct((eig, 2 * pieces[0].shape[2]), BF16),
        ),
        in_specs=[VMEM] * (2 + len(pieces)),
        out_specs=(VMEM, VMEM),
        compiler_params=params(32),
        cost_estimate=LONG,
        name="late_rows",
    )(flat, partial, *pieces)


def late_rest(side, flat, partial, last, spins, eig, rb_count):
    return pl.pallas_call(
        functools.partial(late_rest_kernel, eig, side, rb_count),
        out_shape=jax.ShapeDtypeStruct((spins - spins // 2, 2, eig, eig), BF16),
        in_specs=[VMEM] * 3,
        out_specs=VMEM,
        compiler_params=params(32),
        cost_estimate=LITTLE,
        name="late_rest",
    )(flat, partial, last)


def factors_kernel(diag_mom, elems, right_ref, left_ref, own_ref, held, sem):
    rank = lax.axis_index("rb")
    eig = held.shape[-1]
    copies = []
    for time in range(2):
        which = diag_mom[0, rank, lax.bitwise_xor(rank, time)]
        copies.append(pltpu.make_async_copy(elems.at[which], held.at[time], sem.at[time]))
    for slot in range(own_ref.shape[0]):
        copies.append(pltpu.make_async_copy(elems.at[diag_mom[0, slot, rank]], own_ref.at[slot], sem.at[2 + slot]))
    for copy in copies:
        copy.start()
    for copy in copies:
        copy.wait()
    for time in range(2):
        re, im = held[time, 0], held[time, 1]
        right_ref[time, :eig, :eig] = re
        right_ref[time, :eig, eig:] = im
        right_ref[time, eig:, :eig] = -im
        right_ref[time, eig:, eig:] = re
        re_t = re.astype(F32).T.astype(BF16)
        im_t = im.astype(F32).T.astype(BF16)
        left_ref[time, :eig, :eig] = re_t
        left_ref[time, :eig, eig:] = im_t
        left_ref[time, eig:, :eig] = im_t
        left_ref[time, eig:, eig:] = -re_t


def factors(diag_mom, src_elems):
    slots, eig = diag_mom.shape[1], src_elems.shape[-1]
    form = jax.ShapeDtypeStruct((2, 2 * eig, 2 * eig), BF16)
    return pl.pallas_call(
        factors_kernel,
        out_shape=(form, form, jax.ShapeDtypeStruct((slots, 2, eig, eig), BF16)),
        in_specs=[SMEM, ANY],
        out_specs=(VMEM, VMEM, VMEM),
        scratch_shapes=[pltpu.VMEM((2, 2, eig, eig), BF16), pltpu.SemaphoreType.DMA((2 + slots,))],
        compiler_params=params(32),
        cost_estimate=LITTLE,
        name="factors",
    )(diag_mom, src_elems)


def late_direct_kernel(rest, own, carried, out):
    direct_sums([rest.at[rest.shape[0] - 1]], own, out, carried)


def late_direct(rest, own, carried):
    return pl.pallas_call(
        late_direct_kernel,
        out_shape=sums_shape(carried.shape[0]),
        in_specs=[VMEM] * 3,
        out_specs=VMEM,
        compiler_params=params(32),
        cost_estimate=LITTLE,
        name="late_direct",
    )(rest, own, carried)


def cross_kernel(offs, own, other, right, left, *refs):
    carried, out = refs[:-1], refs[-1]
    eig = own.shape[-1]
    if len(other.shape) > len(own.shape):
        other = other.at[1 - lax.axis_index("rb")]
    real, imag = [], []

    def add(x, y, count, from_right, from_left):
        rows = [jnp.concatenate([x[n, 0], x[n, 1]], axis=1) for n in range(count)]
        product = dot(jnp.concatenate(rows, axis=0), from_right)
        for n in range(count):
            partner = dot(from_left, y[n].reshape(2 * eig, eig))
            mine = product[n * eig : (n + 1) * eig]
            p_re, p_im = mine[:, :eig], mine[:, eig:]
            w_re, w_im = partner[:eig], partner[eig:]
            real.append(fold(p_re * w_re - p_im * w_im))
            imag.append(fold(p_re * w_im + p_im * w_re))

    add(other, own, own.shape[0], right[1], left[0])
    add(own, other, offs, right[0], left[1])
    out[0] = functools.reduce(jnp.add, real + [ref[0] for ref in carried])
    out[1] = functools.reduce(jnp.add, imag + [ref[1] for ref in carried])


def cross_traces(offs, own, other, right, left, carried, name):
    return pl.pallas_call(
        functools.partial(cross_kernel, offs),
        out_shape=sums_shape(2),
        in_specs=[VMEM] * (4 + len(carried)),
        out_specs=VMEM,
        compiler_params=params(32),
        cost_estimate=LITTLE,
        name=name,
    )(own, other, right, left, *carried)


def last_cross_kernel(offs, own, other, right, left, direct, carried, out):
    count = direct.shape[0]
    for n in range(count):
        out[n] = direct[n]
    cross_kernel(offs, own, other, right, left, carried, out.at[pl.ds(count, 2)])


def last_cross(offs, own, other, right, left, direct, carried):
    return pl.pallas_call(
        functools.partial(last_cross_kernel, offs),
        out_shape=sums_shape(direct.shape[0] + 2),
        in_specs=[VMEM] * 6,
        out_specs=VMEM,
        compiler_params=params(32),
        cost_estimate=LITTLE,
        name="last_cross",
    )(own, other, right, left, direct, carried)


def final_kernel(slots, mine, theirs, count, out):
    rank = lax.axis_index("rb")
    lane = lax.broadcasted_iota(jnp.int32, (1, LANES), 1)

    def totals(ref):
        rows = jnp.concatenate([jnp.sum(ref[n], axis=0, keepdims=True) for n in range(ref.shape[0])], axis=0)
        sums = jnp.broadcast_to(jnp.sum(rows, axis=1, keepdims=True), rows.shape)
        return [sums[n : n + 1] for n in range(ref.shape[0])]

    def put(slot, kind, re, im):
        value = jnp.where(lane == 0, re, im) * 0.25
        out[0, slot, kind : kind + 1, :] = jnp.where(slot < count[0], value, 0.0)[:, :2]

    m, t = totals(mine), totals(theirs)
    for slot in range(slots):
        m_re, m_im, t_re, t_im = m[2 * slot], m[2 * slot + 1], t[2 * slot], t[2 * slot + 1]
        put(slot, 0, m_re * t_re - m_im * t_im, m_re * t_im + m_im * t_re)
        here = rank == slot
        put(slot, 1, jnp.where(here, m[2 * slots], t[2 * slots]), jnp.where(here, m[2 * slots + 1], t[2 * slots + 1]))


def final(mine, theirs, diag_count, slots):
    return pl.pallas_call(
        functools.partial(final_kernel, slots),
        out_shape=jax.ShapeDtypeStruct((1, slots, 2, 2), F32),
        in_specs=[VMEM, VMEM, SMEM],
        out_specs=VMEM,
        compiler_params=params(32),
        name="final",
    )(mine, theirs, diag_count)


def shards(peram, src_elems, owner_times, diag_mom, diag_count):
    tp_count, rb_count = lax.axis_size("tp"), lax.axis_size("rb")
    eig = src_elems.shape[-1]
    spins = tp_count * peram.shape[0] // eig
    slots = diag_mom.shape[1]

    head, tail, late, own = travel_order(tp_count, rb_count)
    early_keys = head + tail
    picked = pick(owner_times, peram, head, "pick_head", [jax.ShapeDtypeStruct((4, *peram.shape), BF16)])
    picked.update(pick(owner_times, peram, tail + late + own, "pick_tail", []))

    def send(key):
        far, side = key
        swapped = tp_count // 4 if far >= tp_count // 2 else 0
        pairs = [
            (tp * rb_count + rb, (tp ^ far ^ (swapped if tp < tp_count // 2 else 0)) * rb_count + (rb ^ side))
            for tp in range(tp_count)
            for rb in range(rb_count)
        ]
        return lax.ppermute(picked[key], ("tp", "rb"), pairs)

    swap = [(rb, rb ^ 1) for rb in range(rb_count)]
    right, left, own_elems = factors(diag_mom, src_elems)
    arrived = [send(key) for key in early_keys] + [picked[key] for key in own]
    flat, early, direct = early_gram(early_keys + own, arrived, own_elems, spins, eig, rb_count)
    early_both = lax.all_to_all(jnp.stack([early] * rb_count), "rb", 0, 0)
    offs = early.shape[0] - (spins - 1)
    begun = cross_traces(offs, early, early_both, right, left, [], "early_cross")

    halves = [[key for key in late if key[1] == side] for side in range(rb_count)]
    sent = [[send(key) for key in keys] for keys in halves]
    half = late_begin(halves[0], flat, begun, sent[0], spins, eig, rb_count)
    blocks, last = late_rows(halves[1], flat, half, sent[1], spins, eig, rb_count)
    swapped = lax.ppermute(blocks, "rb", swap)
    rest = late_rest(1, flat, half, last, spins, eig, rb_count)
    rest_swapped = lax.ppermute(rest, "rb", swap)
    traces = late_direct(rest, own_elems, direct)
    partial = cross_traces(blocks.shape[0], blocks, swapped, right, left, [begun], "late_cross")
    mine = last_cross(rest.shape[0] - 1, rest, rest_swapped, right, left, traces, partial)
    theirs = lax.ppermute(mine, "rb", swap)
    return final(mine, theirs, diag_count, slots)


def solution(mesh):
    in_specs = (
        P(("grp", "tp"), None, None, "rb"),
        P("grp", None, None, None),
        P("grp", None),
        P(("grp", "tp"), None, None),
        P(("grp", "tp")),
    )
    out_specs = P(("grp", "tp"), None, None, None)
    return jax.shard_map(shards, mesh=mesh, in_specs=in_specs, out_specs=out_specs, check_vma=False)
```

```python
import functools

import jax
import jax.numpy as jnp
from jax import lax
from jax.experimental import pallas as pl
from jax.experimental.pallas import tpu as pltpu
from jax.sharding import PartitionSpec as P

F32 = jnp.float32
BF16 = jnp.bfloat16
ANY = pl.BlockSpec(memory_space=pl.ANY)
SMEM = pl.BlockSpec(memory_space=pltpu.SMEM)
VMEM = pl.BlockSpec(memory_space=pltpu.VMEM)
SUBLANES = 8
LANES = 128
STEP = 16
MIB = 1 << 20
LITTLE = pl.CostEstimate(flops=1000, bytes_accessed=1000, transcendentals=0)
LONG = pl.CostEstimate(flops=5 * 10**10, bytes_accessed=1000, transcendentals=0)


def in_hbm(array):
    return pltpu.with_memory_space_constraint(array, pltpu.HBM)


def params(mib):
    return pltpu.CompilerParams(vmem_limit_bytes=mib * MIB)


def dot(left, right):
    return jnp.dot(left, right, preferred_element_type=F32)


def dot_nt(left, right):
    return lax.dot_general(left, right, (((1,), (1,)), ((), ())), preferred_element_type=F32)


def choose(index, values):
    out = jnp.int32(values[0])
    for n in range(1, len(values)):
        out = jnp.where(index == n, jnp.int32(values[n]), out)
    return out


def aligned(start, size):
    return pl.ds(pl.multiple_of(start, size), size)


def travel_order(tp_count, rb_count):
    half, quarter = tp_count // 2, tp_count // 4

    def both(distances):
        return [(far, side) for far in distances for side in range(rb_count)]

    long, late = both(range(half, half + quarter)), both(range(half + quarter, tp_count))
    near, rest = both(reversed(range(quarter, half))), both(range(1, quarter))
    own, other = (0, 0), [(0, side) for side in range(1, rb_count)]
    step, part = len(long) // 4, len(rest) // 2
    head = long[: 2 * step]
    tail = near[: 2 * step] + long[2 * step : 3 * step] + rest[:part] + other + near[2 * step : 3 * step] + long[3 * step :] + rest[part:] + near[3 * step :]
    return head, tail, late, [own]


def distance(far, tp_rank, tp_count):
    if far < tp_count // 2:
        return far
    return lax.bitwise_xor(jnp.int32(far), jnp.where(tp_rank < tp_count // 2, jnp.int32(tp_count // 4), jnp.int32(0)))


def pick_kernel(keys, times, table, *refs):
    outs, (held, wide, taken_times, sem, times_sem) = refs[:-5], refs[-5:]
    tp_rank, rb_rank = lax.axis_index("tp"), lax.axis_index("rb")
    rows, _, packed, _ = table.shape

    def fetch(chunk):
        where = aligned(chunk * STEP, STEP)
        return pltpu.make_async_copy(table.at[where], held.at[where], sem.at[chunk])

    copy = pltpu.make_async_copy(times, taken_times, times_sem)
    copy.start()
    for chunk in range(rows // STEP):
        fetch(chunk).start()
    copy.wait()

    def step(chunk, carry):
        fetch(chunk).wait()
        where = aligned(chunk * STEP, STEP)
        for n, (far, side) in enumerate(keys):
            owner = lax.bitwise_xor(tp_rank, distance(far, tp_rank, taken_times.shape[1]))
            time = taken_times[lax.bitwise_xor(rb_rank, side), owner]
            slot = n % wide.shape[0]
            wide[slot] = held[where, time].astype(F32).reshape(STEP * packed, LANES)
            for tile in range(packed // 2):
                for part in range(2):
                    taken = wide[slot, pl.ds(2 * tile + part, STEP, stride=packed), :]
                    outs[n][part, where, tile * LANES : (tile + 1) * LANES] = taken.astype(BF16)
        return carry

    lax.fori_loop(0, rows // STEP, step, 0)


def pick(owner_times, peram, keys, name, spare):
    rows, times, parts, width = peram.shape
    tiles = width // LANES
    table = peram.reshape(rows, times, parts, tiles, LANES).swapaxes(2, 3)
    table = table.reshape(rows, times, tiles * parts, LANES)
    picked = pl.pallas_call(
        functools.partial(pick_kernel, keys),
        out_shape=[jax.ShapeDtypeStruct((parts, rows, width), BF16)] * len(keys) + spare,
        in_specs=[ANY, ANY],
        out_specs=[VMEM] * len(keys) + [ANY] * len(spare),
        scratch_shapes=[
            pltpu.VMEM(table.shape, BF16),
            pltpu.VMEM((4, STEP * tiles * parts, LANES), F32),
            pltpu.SMEM(owner_times.shape[::-1], jnp.int32),
            pltpu.SemaphoreType.DMA((rows // STEP,)),
            pltpu.SemaphoreType.DMA,
        ],
        compiler_params=params(32),
        cost_estimate=LITTLE,
        name=name,
    )(in_hbm(owner_times.T), in_hbm(table))
    return dict(zip(keys, picked))


def place(far, per_spin):
    low = lax.axis_index("tp") % per_spin
    return (far // per_spin) * per_spin + lax.bitwise_xor(jnp.int32(far % per_spin), low)


def gram_block(left, right):
    depth = left.shape[1] // 2
    real = dot_nt(left, right)
    imag = dot_nt(left[:, :depth], right[:, depth:]) - dot_nt(left[:, depth:], right[:, :depth])
    return real.astype(BF16), imag.astype(BF16)


def fold(values):
    rows, columns = values.shape
    folded = jnp.sum(values.reshape(rows // SUBLANES, SUBLANES, columns), axis=0)
    return functools.reduce(jnp.add, [folded[:, n : n + LANES] for n in range(0, columns, LANES)])


def direct_sums(diagonal, own, out, carried=None):
    real = functools.reduce(jnp.add, [block[0].astype(F32) for block in diagonal])
    imag = functools.reduce(jnp.add, [block[1].astype(F32) for block in diagonal])
    for slot in range(own.shape[0]):
        elem_re, elem_im = own[slot, 0].astype(F32), own[slot, 1].astype(F32)
        sums = [fold(elem_re * real + elem_im * imag), fold(elem_im * real - elem_re * imag)]
        for part in range(2):
            n = 2 * slot + part
            out[n] = sums[part] if carried is None else sums[part] + carried[n]


def sums_shape(count):
    return jax.ShapeDtypeStruct((count, SUBLANES, LANES), F32)


def early_blocks(spins):
    off = [(s, t) for s in range(spins - 1) for t in range(s + 1, spins - 1)]
    return off + [(s, s) for s in range(spins - 1)]


def early_kernel(eig, keys, rb_count, blocks, *refs):
    pieces, (own, flat, out, traces, sem) = refs[:-5], refs[-5:]
    rows, width = pieces[0].shape[1:]
    depth = rb_count * width
    copies = []
    for n, ((far, side), piece) in enumerate(zip(keys, pieces)):
        where = aligned(place(far, eig // rows) * rows, rows)
        for part in range(2):
            columns = pl.ds(part * depth + side * width, width)
            copies.append(pltpu.make_async_copy(piece.at[part], flat.at[where, columns], sem.at[2 * n + part]))
    for copy in copies:
        copy.start()
    for copy in copies:
        copy.wait()

    def step(n, carry):
        top, side = choose(n, [b[0] for b in blocks]), choose(n, [b[1] for b in blocks])
        out[n, 0], out[n, 1] = gram_block(flat[aligned(top * eig, eig), :], flat[aligned(side * eig, eig), :])
        return carry

    lax.fori_loop(0, len(blocks), step, 0)
    diagonal = [out.at[n] for n, block in enumerate(blocks) if block[0] == block[1]]
    direct_sums(diagonal, own, traces)


def early_gram(keys, pieces, own_elems, spins, eig, rb_count):
    blocks = early_blocks(spins)
    depth = 2 * rb_count * pieces[0].shape[2]
    return pl.pallas_call(
        functools.partial(early_kernel, eig, keys, rb_count, blocks),
        out_shape=(
            jax.ShapeDtypeStruct(((spins - 1) * eig, depth), BF16),
            jax.ShapeDtypeStruct((len(blocks), 2, eig, eig), BF16),
            sums_shape(2 * own_elems.shape[0]),
        ),
        in_specs=[ANY] * len(pieces) + [VMEM],
        out_specs=(VMEM, VMEM, VMEM),
        scratch_shapes=[pltpu.SemaphoreType.DMA((2 * len(pieces),))],
        compiler_params=params(32),
        cost_estimate=LONG,
        name="early_gram",
    )(*pieces, own_elems)


def side_columns(ref, rows, side, width, rb_count):
    return [ref[rows, (part * rb_count + side) * width : (part * rb_count + side + 1) * width] for part in range(2)]


def half_products(left, right):
    real = dot_nt(left[0], right[0]) + dot_nt(left[1], right[1])
    imag = dot_nt(left[0], right[1]) - dot_nt(left[1], right[0])
    return real, imag


def gather_last(eig, keys, others, pieces, last):
    rows, width = pieces[0].shape[1:]
    for (far, _), piece in zip(keys, pieces):
        where = aligned((place(far, eig // rows) - others * (eig // rows)) * rows, rows)
        for part in range(2):
            last[where, part * width : (part + 1) * width] = piece[part]


def late_begin_kernel(eig, keys, rb_count, flat, begun, *refs):
    pieces, (out, last) = refs[:-2], refs[-2:]
    side, width, others = keys[0][1], pieces[0].shape[2], flat.shape[0] // eig
    gather_last(eig, keys, others, pieces, last)
    right = [last[:, :width], last[:, width:]]
    for n in range(others):
        left = side_columns(flat, slice(n * eig, (n + 1) * eig), side, width, rb_count)
        out[n, 0], out[n, 1] = half_products(left, right)
    out[others, 0], out[others, 1] = half_products(right, right)


def late_begin(keys, flat, begun, pieces, spins, eig, rb_count):
    return pl.pallas_call(
        functools.partial(late_begin_kernel, eig, keys, rb_count),
        out_shape=jax.ShapeDtypeStruct((spins, 2, eig, eig), F32),
        in_specs=[VMEM, ANY] + [VMEM] * len(pieces),
        out_specs=VMEM,
        scratch_shapes=[pltpu.VMEM((eig, 2 * pieces[0].shape[2]), BF16)],
        compiler_params=params(32),
        cost_estimate=LITTLE,
        name="late_begin",
    )(flat, begun, *pieces)


def late_rows_kernel(eig, keys, rb_count, flat, partial, *refs):
    pieces, (out, last) = refs[:-2], refs[-2:]
    side, width = keys[0][1], pieces[0].shape[2]
    gather_last(eig, keys, flat.shape[0] // eig, pieces, last)
    right = [last[:, :width], last[:, width:]]
    for n in range(out.shape[0]):
        left = side_columns(flat, slice(n * eig, (n + 1) * eig), side, width, rb_count)
        real, imag = half_products(left, right)
        out[n, 0], out[n, 1] = (partial[n, 0] + real).astype(BF16), (partial[n, 1] + imag).astype(BF16)


def late_rest_kernel(eig, side, rb_count, flat, partial, last, own, carried, out, traces):
    count, width = out.shape[0] - 1, last.shape[1] // 2
    others = flat.shape[0] // eig
    right = [last[:, :width], last[:, width:]]
    for n in range(count + 1):
        spin = others - count + n
        left = right
        if n < count:
            left = side_columns(flat, slice(spin * eig, (spin + 1) * eig), side, width, rb_count)
        real, imag = half_products(left, right)
        out[n, 0], out[n, 1] = (partial[spin, 0] + real).astype(BF16), (partial[spin, 1] + imag).astype(BF16)
    direct_sums([out.at[count]], own, traces, carried)


def late_rows(keys, flat, partial, pieces, spins, eig, rb_count):
    return pl.pallas_call(
        functools.partial(late_rows_kernel, eig, keys, rb_count),
        out_shape=(
            jax.ShapeDtypeStruct((spins // 2, 2, eig, eig), BF16),
            jax.ShapeDtypeStruct((eig, 2 * pieces[0].shape[2]), BF16),
        ),
        in_specs=[VMEM] * (2 + len(pieces)),
        out_specs=(VMEM, VMEM),
        compiler_params=params(32),
        cost_estimate=LONG,
        name="late_rows",
    )(flat, partial, *pieces)


def late_rest(side, flat, partial, last, own, carried, spins, eig, rb_count):
    return pl.pallas_call(
        functools.partial(late_rest_kernel, eig, side, rb_count),
        out_shape=(
            jax.ShapeDtypeStruct((spins - spins // 2, 2, eig, eig), BF16),
            sums_shape(carried.shape[0]),
        ),
        in_specs=[VMEM] * 5,
        out_specs=(VMEM, VMEM),
        compiler_params=params(32),
        cost_estimate=LITTLE,
        name="late_rest",
    )(flat, partial, last, own, carried)


def factors_kernel(diag_mom, elems, right_ref, left_ref, own_ref, held, sem):
    rank = lax.axis_index("rb")
    eig = held.shape[-1]
    copies = []
    for time in range(2):
        which = diag_mom[0, rank, lax.bitwise_xor(rank, time)]
        copies.append(pltpu.make_async_copy(elems.at[which], held.at[time], sem.at[time]))
    for slot in range(own_ref.shape[0]):
        copies.append(pltpu.make_async_copy(elems.at[diag_mom[0, slot, rank]], own_ref.at[slot], sem.at[2 + slot]))
    for copy in copies:
        copy.start()
    for copy in copies:
        copy.wait()
    for time in range(2):
        re, im = held[time, 0], held[time, 1]
        right_ref[time, :eig, :eig] = re
        right_ref[time, :eig, eig:] = im
        right_ref[time, eig:, :eig] = -im
        right_ref[time, eig:, eig:] = re
        re_t = re.astype(F32).T.astype(BF16)
        im_t = im.astype(F32).T.astype(BF16)
        left_ref[time, :eig, :eig] = re_t
        left_ref[time, :eig, eig:] = im_t
        left_ref[time, eig:, :eig] = im_t
        left_ref[time, eig:, eig:] = -re_t


def factors(diag_mom, src_elems):
    slots, eig = diag_mom.shape[1], src_elems.shape[-1]
    form = jax.ShapeDtypeStruct((2, 2 * eig, 2 * eig), BF16)
    return pl.pallas_call(
        factors_kernel,
        out_shape=(form, form, jax.ShapeDtypeStruct((slots, 2, eig, eig), BF16)),
        in_specs=[SMEM, ANY],
        out_specs=(VMEM, VMEM, VMEM),
        scratch_shapes=[pltpu.VMEM((2, 2, eig, eig), BF16), pltpu.SemaphoreType.DMA((2 + slots,))],
        compiler_params=params(32),
        cost_estimate=LITTLE,
        name="factors",
    )(diag_mom, src_elems)


def cross_kernel(offs, own, other, right, left, *refs):
    carried, out = refs[:-1], refs[-1]
    eig = own.shape[-1]
    if len(other.shape) > len(own.shape):
        other = other.at[1 - lax.axis_index("rb")]
    real, imag = [], []

    def add(x, y, count, from_right, from_left):
        rows = [jnp.concatenate([x[n, 0], x[n, 1]], axis=1) for n in range(count)]
        product = dot(jnp.concatenate(rows, axis=0), from_right)
        for n in range(count):
            partner = dot(from_left, y[n].reshape(2 * eig, eig))
            mine = product[n * eig : (n + 1) * eig]
            p_re, p_im = mine[:, :eig], mine[:, eig:]
            w_re, w_im = partner[:eig], partner[eig:]
            real.append(fold(p_re * w_re - p_im * w_im))
            imag.append(fold(p_re * w_im + p_im * w_re))

    add(other, own, own.shape[0], right[1], left[0])
    add(own, other, offs, right[0], left[1])
    out[0] = functools.reduce(jnp.add, real + [ref[0] for ref in carried])
    out[1] = functools.reduce(jnp.add, imag + [ref[1] for ref in carried])


def cross_traces(offs, own, other, right, left, carried, name):
    return pl.pallas_call(
        functools.partial(cross_kernel, offs),
        out_shape=sums_shape(2),
        in_specs=[VMEM] * (4 + len(carried)),
        out_specs=VMEM,
        compiler_params=params(32),
        cost_estimate=LITTLE,
        name=name,
    )(own, other, right, left, *carried)


def last_cross_kernel(offs, own, other, right, left, direct, carried, out):
    count = direct.shape[0]
    for n in range(count):
        out[n] = direct[n]
    cross_kernel(offs, own, other, right, left, carried, out.at[pl.ds(count, 2)])


def last_cross(offs, own, other, right, left, direct, carried):
    return pl.pallas_call(
        functools.partial(last_cross_kernel, offs),
        out_shape=sums_shape(direct.shape[0] + 2),
        in_specs=[VMEM] * 6,
        out_specs=VMEM,
        compiler_params=params(32),
        cost_estimate=LITTLE,
        name="last_cross",
    )(own, other, right, left, direct, carried)


def final_kernel(slots, mine, theirs, count, out):
    rank = lax.axis_index("rb")
    lane = lax.broadcasted_iota(jnp.int32, (1, LANES), 1)

    def totals(ref):
        rows = jnp.concatenate([jnp.sum(ref[n], axis=0, keepdims=True) for n in range(ref.shape[0])], axis=0)
        sums = jnp.broadcast_to(jnp.sum(rows, axis=1, keepdims=True), rows.shape)
        return [sums[n : n + 1] for n in range(ref.shape[0])]

    def put(slot, kind, re, im):
        value = jnp.where(lane == 0, re, im) * 0.25
        out[0, slot, kind : kind + 1, :] = jnp.where(slot < count[0], value, 0.0)[:, :2]

    m, t = totals(mine), totals(theirs)
    for slot in range(slots):
        m_re, m_im, t_re, t_im = m[2 * slot], m[2 * slot + 1], t[2 * slot], t[2 * slot + 1]
        put(slot, 0, m_re * t_re - m_im * t_im, m_re * t_im + m_im * t_re)
        here = rank == slot
        put(slot, 1, jnp.where(here, m[2 * slots], t[2 * slots]), jnp.where(here, m[2 * slots + 1], t[2 * slots + 1]))


def final(mine, theirs, diag_count, slots):
    return pl.pallas_call(
        functools.partial(final_kernel, slots),
        out_shape=jax.ShapeDtypeStruct((1, slots, 2, 2), F32),
        in_specs=[VMEM, VMEM, SMEM],
        out_specs=VMEM,
        compiler_params=params(32),
        name="final",
    )(mine, theirs, diag_count)


def shards(peram, src_elems, owner_times, diag_mom, diag_count):
    tp_count, rb_count = lax.axis_size("tp"), lax.axis_size("rb")
    eig = src_elems.shape[-1]
    spins = tp_count * peram.shape[0] // eig
    slots = diag_mom.shape[1]

    head, tail, late, own = travel_order(tp_count, rb_count)
    early_keys = head + tail
    picked = pick(owner_times, peram, head, "pick_head", [jax.ShapeDtypeStruct((4, *peram.shape), BF16)])
    picked.update(pick(owner_times, peram, tail + late + own, "pick_tail", []))

    def send(key):
        far, side = key
        swapped = tp_count // 4 if far >= tp_count // 2 else 0
        pairs = [
            (tp * rb_count + rb, (tp ^ far ^ (swapped if tp < tp_count // 2 else 0)) * rb_count + (rb ^ side))
            for tp in range(tp_count)
            for rb in range(rb_count)
        ]
        return lax.ppermute(picked[key], ("tp", "rb"), pairs)

    swap = [(rb, rb ^ 1) for rb in range(rb_count)]
    right, left, own_elems = factors(diag_mom, src_elems)
    arrived = [send(key) for key in early_keys] + [picked[key] for key in own]
    flat, early, direct = early_gram(early_keys + own, arrived, own_elems, spins, eig, rb_count)
    early_both = lax.all_to_all(jnp.stack([early] * rb_count), "rb", 0, 0)
    offs = early.shape[0] - (spins - 1)
    begun = cross_traces(offs, early, early_both, right, left, [], "early_cross")

    halves = [[key for key in late if key[1] == side] for side in range(rb_count)]
    sent = [[send(key) for key in keys] for keys in halves]
    half = late_begin(halves[0], flat, begun, sent[0], spins, eig, rb_count)
    blocks, last = late_rows(halves[1], flat, half, sent[1], spins, eig, rb_count)
    swapped = lax.ppermute(blocks, "rb", swap)
    rest, traces = late_rest(1, flat, half, last, own_elems, direct, spins, eig, rb_count)
    rest_swapped = lax.ppermute(rest, "rb", swap)
    partial = cross_traces(blocks.shape[0], blocks, swapped, right, left, [begun], "late_cross")
    mine = last_cross(rest.shape[0] - 1, rest, rest_swapped, right, left, traces, partial)
    theirs = lax.ppermute(mine, "rb", swap)
    return final(mine, theirs, diag_count, slots)


def solution(mesh):
    in_specs = (
        P(("grp", "tp"), None, None, "rb"),
        P("grp", None, None, None),
        P("grp", None),
        P(("grp", "tp"), None, None),
        P(("grp", "tp")),
    )
    out_specs = P(("grp", "tp"), None, None, None)
    return jax.shard_map(shards, mesh=mesh, in_specs=in_specs, out_specs=out_specs, check_vma=False)
```

```python
import functools

import jax
import jax.numpy as jnp
from jax import lax
from jax.experimental import pallas as pl
from jax.experimental.pallas import tpu as pltpu
from jax.sharding import PartitionSpec as P

F32 = jnp.float32
BF16 = jnp.bfloat16
ANY = pl.BlockSpec(memory_space=pl.ANY)
SMEM = pl.BlockSpec(memory_space=pltpu.SMEM)
VMEM = pl.BlockSpec(memory_space=pltpu.VMEM)
SUBLANES = 8
LANES = 128
STEP = 16
MIB = 1 << 20
LITTLE = pl.CostEstimate(flops=1000, bytes_accessed=1000, transcendentals=0)
LONG = pl.CostEstimate(flops=5 * 10**10, bytes_accessed=1000, transcendentals=0)


def in_hbm(array):
    return pltpu.with_memory_space_constraint(array, pltpu.HBM)


def params(mib):
    return pltpu.CompilerParams(vmem_limit_bytes=mib * MIB)


def dot(left, right):
    return jnp.dot(left, right, preferred_element_type=F32)


def dot_nt(left, right):
    return lax.dot_general(left, right, (((1,), (1,)), ((), ())), preferred_element_type=F32)


def choose(index, values):
    out = jnp.int32(values[0])
    for n in range(1, len(values)):
        out = jnp.where(index == n, jnp.int32(values[n]), out)
    return out


def aligned(start, size):
    return pl.ds(pl.multiple_of(start, size), size)


def travel_order(tp_count, rb_count):
    half, quarter = tp_count // 2, tp_count // 4

    def both(distances):
        return [(far, side) for far in distances for side in range(rb_count)]

    long, late = both(range(half, half + quarter)), both(range(half + quarter, tp_count))
    near, rest = both(reversed(range(quarter, half))), both(range(1, quarter))
    own, other = (0, 0), [(0, side) for side in range(1, rb_count)]
    step, part = len(long) // 4, len(rest) // 2
    head = long[: 2 * step] + near[: 2 * step] + long[2 * step : 3 * step]
    tail = rest[:part] + other + near[2 * step : 3 * step] + long[3 * step :] + rest[part:] + near[3 * step :]
    return head, tail, late, [own]


def distance(far, tp_rank, tp_count):
    if far < tp_count // 2:
        return far
    return lax.bitwise_xor(jnp.int32(far), jnp.where(tp_rank < tp_count // 2, jnp.int32(tp_count // 4), jnp.int32(0)))


def pick_kernel(keys, times, table, *refs):
    outs, (held, wide, taken_times, sem, times_sem) = refs[:-5], refs[-5:]
    tp_rank, rb_rank = lax.axis_index("tp"), lax.axis_index("rb")
    rows, _, packed, _ = table.shape

    def fetch(chunk):
        where = aligned(chunk * STEP, STEP)
        return pltpu.make_async_copy(table.at[where], held.at[where], sem.at[chunk])

    copy = pltpu.make_async_copy(times, taken_times, times_sem)
    copy.start()
    for chunk in range(rows // STEP):
        fetch(chunk).start()
    copy.wait()

    def step(chunk, carry):
        fetch(chunk).wait()
        where = aligned(chunk * STEP, STEP)
        for n, (far, side) in enumerate(keys):
            owner = lax.bitwise_xor(tp_rank, distance(far, tp_rank, taken_times.shape[1]))
            time = taken_times[lax.bitwise_xor(rb_rank, side), owner]
            slot = n % wide.shape[0]
            wide[slot] = held[where, time].astype(F32).reshape(STEP * packed, LANES)
            for tile in range(packed // 2):
                for part in range(2):
                    taken = wide[slot, pl.ds(2 * tile + part, STEP, stride=packed), :]
                    outs[n][part, where, tile * LANES : (tile + 1) * LANES] = taken.astype(BF16)
        return carry

    lax.fori_loop(0, rows // STEP, step, 0)


def pick(owner_times, peram, keys, name, spare):
    rows, times, parts, width = peram.shape
    tiles = width // LANES
    table = peram.reshape(rows, times, parts, tiles, LANES).swapaxes(2, 3)
    table = table.reshape(rows, times, tiles * parts, LANES)
    picked = pl.pallas_call(
        functools.partial(pick_kernel, keys),
        out_shape=[jax.ShapeDtypeStruct((parts, rows, width), BF16)] * len(keys) + spare,
        in_specs=[ANY, ANY],
        out_specs=[VMEM] * len(keys) + [ANY] * len(spare),
        scratch_shapes=[
            pltpu.VMEM(table.shape, BF16),
            pltpu.VMEM((4, STEP * tiles * parts, LANES), F32),
            pltpu.SMEM(owner_times.shape[::-1], jnp.int32),
            pltpu.SemaphoreType.DMA((rows // STEP,)),
            pltpu.SemaphoreType.DMA,
        ],
        compiler_params=params(32),
        cost_estimate=LITTLE,
        name=name,
    )(in_hbm(owner_times.T), in_hbm(table))
    return dict(zip(keys, picked))


def place(far, per_spin):
    low = lax.axis_index("tp") % per_spin
    return (far // per_spin) * per_spin + lax.bitwise_xor(jnp.int32(far % per_spin), low)


def gram_block(left, right):
    depth = left.shape[1] // 2
    real = dot_nt(left, right)
    imag = dot_nt(left[:, :depth], right[:, depth:]) - dot_nt(left[:, depth:], right[:, :depth])
    return real.astype(BF16), imag.astype(BF16)


def fold(values):
    rows, columns = values.shape
    folded = jnp.sum(values.reshape(rows // SUBLANES, SUBLANES, columns), axis=0)
    return functools.reduce(jnp.add, [folded[:, n : n + LANES] for n in range(0, columns, LANES)])


def direct_sums(diagonal, own, out, carried=None):
    real = functools.reduce(jnp.add, [block[0].astype(F32) for block in diagonal])
    imag = functools.reduce(jnp.add, [block[1].astype(F32) for block in diagonal])
    for slot in range(own.shape[0]):
        elem_re, elem_im = own[slot, 0].astype(F32), own[slot, 1].astype(F32)
        sums = [fold(elem_re * real + elem_im * imag), fold(elem_im * real - elem_re * imag)]
        for part in range(2):
            n = 2 * slot + part
            out[n] = sums[part] if carried is None else sums[part] + carried[n]


def sums_shape(count):
    return jax.ShapeDtypeStruct((count, SUBLANES, LANES), F32)


def early_blocks(spins):
    off = [(s, t) for s in range(spins - 1) for t in range(s + 1, spins - 1)]
    return off + [(s, s) for s in range(spins - 1)]


def early_kernel(eig, keys, rb_count, blocks, *refs):
    pieces, (own, flat, out, traces, sem) = refs[:-5], refs[-5:]
    rows, width = pieces[0].shape[1:]
    depth = rb_count * width
    copies = []
    for n, ((far, side), piece) in enumerate(zip(keys, pieces)):
        where = aligned(place(far, eig // rows) * rows, rows)
        for part in range(2):
            columns = pl.ds(part * depth + side * width, width)
            copies.append(pltpu.make_async_copy(piece.at[part], flat.at[where, columns], sem.at[2 * n + part]))
    for copy in copies:
        copy.start()
    for copy in copies:
        copy.wait()

    def step(n, carry):
        top, side = choose(n, [b[0] for b in blocks]), choose(n, [b[1] for b in blocks])
        out[n, 0], out[n, 1] = gram_block(flat[aligned(top * eig, eig), :], flat[aligned(side * eig, eig), :])
        return carry

    lax.fori_loop(0, len(blocks), step, 0)
    diagonal = [out.at[n] for n, block in enumerate(blocks) if block[0] == block[1]]
    direct_sums(diagonal, own, traces)


def early_gram(keys, pieces, own_elems, spins, eig, rb_count):
    blocks = early_blocks(spins)
    depth = 2 * rb_count * pieces[0].shape[2]
    return pl.pallas_call(
        functools.partial(early_kernel, eig, keys, rb_count, blocks),
        out_shape=(
            jax.ShapeDtypeStruct(((spins - 1) * eig, depth), BF16),
            jax.ShapeDtypeStruct((len(blocks), 2, eig, eig), BF16),
            sums_shape(2 * own_elems.shape[0]),
        ),
        in_specs=[ANY] * len(pieces) + [VMEM],
        out_specs=(VMEM, VMEM, VMEM),
        scratch_shapes=[pltpu.SemaphoreType.DMA((2 * len(pieces),))],
        compiler_params=params(32),
        cost_estimate=LONG,
        name="early_gram",
    )(*pieces, own_elems)


def side_columns(ref, rows, side, width, rb_count):
    return [ref[rows, (part * rb_count + side) * width : (part * rb_count + side + 1) * width] for part in range(2)]


def half_products(left, right):
    real = dot_nt(left[0], right[0]) + dot_nt(left[1], right[1])
    imag = dot_nt(left[0], right[1]) - dot_nt(left[1], right[0])
    return real, imag


def gather_last(eig, keys, others, pieces, last):
    rows, width = pieces[0].shape[1:]
    for (far, _), piece in zip(keys, pieces):
        where = aligned((place(far, eig // rows) - others * (eig // rows)) * rows, rows)
        for part in range(2):
            last[where, part * width : (part + 1) * width] = piece[part]


def late_begin_kernel(eig, keys, rb_count, flat, begun, *refs):
    pieces, (out, last) = refs[:-2], refs[-2:]
    side, width, others = keys[0][1], pieces[0].shape[2], flat.shape[0] // eig
    gather_last(eig, keys, others, pieces, last)
    right = [last[:, :width], last[:, width:]]
    for n in range(others):
        left = side_columns(flat, slice(n * eig, (n + 1) * eig), side, width, rb_count)
        out[n, 0], out[n, 1] = half_products(left, right)
    out[others, 0], out[others, 1] = half_products(right, right)


def late_begin(keys, flat, begun, pieces, spins, eig, rb_count):
    return pl.pallas_call(
        functools.partial(late_begin_kernel, eig, keys, rb_count),
        out_shape=jax.ShapeDtypeStruct((spins, 2, eig, eig), F32),
        in_specs=[VMEM, ANY] + [VMEM] * len(pieces),
        out_specs=VMEM,
        scratch_shapes=[pltpu.VMEM((eig, 2 * pieces[0].shape[2]), BF16)],
        compiler_params=params(32),
        cost_estimate=LITTLE,
        name="late_begin",
    )(flat, begun, *pieces)


def late_rows_kernel(eig, keys, rb_count, flat, partial, *refs):
    pieces, (out, last) = refs[:-2], refs[-2:]
    side, width = keys[0][1], pieces[0].shape[2]
    gather_last(eig, keys, flat.shape[0] // eig, pieces, last)
    right = [last[:, :width], last[:, width:]]
    for n in range(out.shape[0]):
        left = side_columns(flat, slice(n * eig, (n + 1) * eig), side, width, rb_count)
        real, imag = half_products(left, right)
        out[n, 0], out[n, 1] = (partial[n, 0] + real).astype(BF16), (partial[n, 1] + imag).astype(BF16)


def late_rest_kernel(eig, side, rb_count, flat, partial, last, out):
    count, width = out.shape[0] - 1, last.shape[1] // 2
    others = flat.shape[0] // eig
    right = [last[:, :width], last[:, width:]]
    for n in range(count + 1):
        spin = others - count + n
        left = right
        if n < count:
            left = side_columns(flat, slice(spin * eig, (spin + 1) * eig), side, width, rb_count)
        real, imag = half_products(left, right)
        out[n, 0], out[n, 1] = (partial[spin, 0] + real).astype(BF16), (partial[spin, 1] + imag).astype(BF16)


def late_rows(keys, flat, partial, pieces, spins, eig, rb_count):
    return pl.pallas_call(
        functools.partial(late_rows_kernel, eig, keys, rb_count),
        out_shape=(
            jax.ShapeDtypeStruct((spins // 2, 2, eig, eig), BF16),
            jax.ShapeDtypeStruct((eig, 2 * pieces[0].shape[2]), BF16),
        ),
        in_specs=[VMEM] * (2 + len(pieces)),
        out_specs=(VMEM, VMEM),
        compiler_params=params(32),
        cost_estimate=LONG,
        name="late_rows",
    )(flat, partial, *pieces)


def late_rest(side, flat, partial, last, spins, eig, rb_count):
    return pl.pallas_call(
        functools.partial(late_rest_kernel, eig, side, rb_count),
        out_shape=jax.ShapeDtypeStruct((spins - spins // 2, 2, eig, eig), BF16),
        in_specs=[VMEM] * 3,
        out_specs=VMEM,
        compiler_params=params(32),
        cost_estimate=LITTLE,
        name="late_rest",
    )(flat, partial, last)


def factors_kernel(diag_mom, elems, right_ref, left_ref, own_ref, held, sem):
    rank = lax.axis_index("rb")
    eig = held.shape[-1]
    copies = []
    for time in range(2):
        which = diag_mom[0, rank, lax.bitwise_xor(rank, time)]
        copies.append(pltpu.make_async_copy(elems.at[which], held.at[time], sem.at[time]))
    for slot in range(own_ref.shape[0]):
        copies.append(pltpu.make_async_copy(elems.at[diag_mom[0, slot, rank]], own_ref.at[slot], sem.at[2 + slot]))
    for copy in copies:
        copy.start()
    for copy in copies:
        copy.wait()
    for time in range(2):
        re, im = held[time, 0], held[time, 1]
        right_ref[time, :eig, :eig] = re
        right_ref[time, :eig, eig:] = im
        right_ref[time, eig:, :eig] = -im
        right_ref[time, eig:, eig:] = re
        re_t = re.astype(F32).T.astype(BF16)
        im_t = im.astype(F32).T.astype(BF16)
        left_ref[time, :eig, :eig] = re_t
        left_ref[time, :eig, eig:] = im_t
        left_ref[time, eig:, :eig] = im_t
        left_ref[time, eig:, eig:] = -re_t


def factors(diag_mom, src_elems):
    slots, eig = diag_mom.shape[1], src_elems.shape[-1]
    form = jax.ShapeDtypeStruct((2, 2 * eig, 2 * eig), BF16)
    return pl.pallas_call(
        factors_kernel,
        out_shape=(form, form, jax.ShapeDtypeStruct((slots, 2, eig, eig), BF16)),
        in_specs=[SMEM, ANY],
        out_specs=(VMEM, VMEM, VMEM),
        scratch_shapes=[pltpu.VMEM((2, 2, eig, eig), BF16), pltpu.SemaphoreType.DMA((2 + slots,))],
        compiler_params=params(32),
        cost_estimate=LITTLE,
        name="factors",
    )(diag_mom, src_elems)


def late_direct_kernel(rest, own, carried, out):
    direct_sums([rest.at[rest.shape[0] - 1]], own, out, carried)


def late_direct(rest, own, carried):
    return pl.pallas_call(
        late_direct_kernel,
        out_shape=sums_shape(carried.shape[0]),
        in_specs=[VMEM] * 3,
        out_specs=VMEM,
        compiler_params=params(32),
        cost_estimate=LITTLE,
        name="late_direct",
    )(rest, own, carried)


def cross_kernel(offs, own, other, right, left, *refs):
    carried, out = refs[:-1], refs[-1]
    eig = own.shape[-1]
    if len(other.shape) > len(own.shape):
        other = other.at[1 - lax.axis_index("rb")]
    real, imag = [], []

    def add(x, y, count, from_right, from_left):
        rows = [jnp.concatenate([x[n, 0], x[n, 1]], axis=1) for n in range(count)]
        product = dot(jnp.concatenate(rows, axis=0), from_right)
        for n in range(count):
            partner = dot(from_left, y[n].reshape(2 * eig, eig))
            mine = product[n * eig : (n + 1) * eig]
            p_re, p_im = mine[:, :eig], mine[:, eig:]
            w_re, w_im = partner[:eig], partner[eig:]
            real.append(fold(p_re * w_re - p_im * w_im))
            imag.append(fold(p_re * w_im + p_im * w_re))

    add(other, own, own.shape[0], right[1], left[0])
    add(own, other, offs, right[0], left[1])
    out[0] = functools.reduce(jnp.add, real + [ref[0] for ref in carried])
    out[1] = functools.reduce(jnp.add, imag + [ref[1] for ref in carried])


def cross_traces(offs, own, other, right, left, carried, name):
    return pl.pallas_call(
        functools.partial(cross_kernel, offs),
        out_shape=sums_shape(2),
        in_specs=[VMEM] * (4 + len(carried)),
        out_specs=VMEM,
        compiler_params=params(32),
        cost_estimate=LITTLE,
        name=name,
    )(own, other, right, left, *carried)


def last_cross_kernel(offs, own, other, right, left, direct, carried, out):
    count = direct.shape[0]
    for n in range(count):
        out[n] = direct[n]
    cross_kernel(offs, own, other, right, left, carried, out.at[pl.ds(count, 2)])


def last_cross(offs, own, other, right, left, direct, carried):
    return pl.pallas_call(
        functools.partial(last_cross_kernel, offs),
        out_shape=sums_shape(direct.shape[0] + 2),
        in_specs=[VMEM] * 6,
        out_specs=VMEM,
        compiler_params=params(32),
        cost_estimate=LITTLE,
        name="last_cross",
    )(own, other, right, left, direct, carried)


def final_kernel(slots, mine, theirs, count, out):
    rank = lax.axis_index("rb")
    lane = lax.broadcasted_iota(jnp.int32, (1, LANES), 1)

    def totals(ref):
        rows = jnp.concatenate([jnp.sum(ref[n], axis=0, keepdims=True) for n in range(ref.shape[0])], axis=0)
        sums = jnp.broadcast_to(jnp.sum(rows, axis=1, keepdims=True), rows.shape)
        return [sums[n : n + 1] for n in range(ref.shape[0])]

    def put(slot, kind, re, im):
        value = jnp.where(lane == 0, re, im) * 0.25
        out[0, slot, kind : kind + 1, :] = jnp.where(slot < count[0], value, 0.0)[:, :2]

    m, t = totals(mine), totals(theirs)
    for slot in range(slots):
        m_re, m_im, t_re, t_im = m[2 * slot], m[2 * slot + 1], t[2 * slot], t[2 * slot + 1]
        put(slot, 0, m_re * t_re - m_im * t_im, m_re * t_im + m_im * t_re)
        here = rank == slot
        put(slot, 1, jnp.where(here, m[2 * slots], t[2 * slots]), jnp.where(here, m[2 * slots + 1], t[2 * slots + 1]))


def final(mine, theirs, diag_count, slots):
    return pl.pallas_call(
        functools.partial(final_kernel, slots),
        out_shape=jax.ShapeDtypeStruct((1, slots, 2, 2), F32),
        in_specs=[VMEM, VMEM, SMEM],
        out_specs=VMEM,
        compiler_params=params(32),
        name="final",
    )(mine, theirs, diag_count)


def shards(peram, src_elems, owner_times, diag_mom, diag_count):
    tp_count, rb_count = lax.axis_size("tp"), lax.axis_size("rb")
    eig = src_elems.shape[-1]
    spins = tp_count * peram.shape[0] // eig
    slots = diag_mom.shape[1]

    head, tail, late, own = travel_order(tp_count, rb_count)
    early_keys = head + tail
    picked = pick(owner_times, peram, head, "pick_head", [jax.ShapeDtypeStruct((4, *peram.shape), BF16)])
    picked.update(pick(owner_times, peram, tail + late + own, "pick_tail", []))

    def send(key):
        far, side = key
        swapped = tp_count // 4 if far >= tp_count // 2 else 0
        pairs = [
            (tp * rb_count + rb, (tp ^ far ^ (swapped if tp < tp_count // 2 else 0)) * rb_count + (rb ^ side))
            for tp in range(tp_count)
            for rb in range(rb_count)
        ]
        return lax.ppermute(picked[key], ("tp", "rb"), pairs)

    swap = [(rb, rb ^ 1) for rb in range(rb_count)]
    right, left, own_elems = factors(diag_mom, src_elems)
    arrived = [send(key) for key in early_keys] + [picked[key] for key in own]
    flat, early, direct = early_gram(early_keys + own, arrived, own_elems, spins, eig, rb_count)
    early_both = lax.all_to_all(jnp.stack([early] * rb_count), "rb", 0, 0)
    offs = early.shape[0] - (spins - 1)
    begun = cross_traces(offs, early, early_both, right, left, [], "early_cross")

    halves = [[key for key in late if key[1] == side] for side in reversed(range(rb_count))]
    sent = [[send(key) for key in keys] for keys in halves]
    half = late_begin(halves[0], flat, begun, sent[0], spins, eig, rb_count)
    blocks, last = late_rows(halves[1], flat, half, sent[1], spins, eig, rb_count)
    swapped = lax.ppermute(blocks, "rb", swap)
    rest = late_rest(0, flat, half, last, spins, eig, rb_count)
    rest_swapped = lax.ppermute(rest, "rb", swap)
    traces = late_direct(rest, own_elems, direct)
    partial = cross_traces(blocks.shape[0], blocks, swapped, right, left, [begun], "late_cross")
    mine = last_cross(rest.shape[0] - 1, rest, rest_swapped, right, left, traces, partial)
    theirs = lax.ppermute(mine, "rb", swap)
    return final(mine, theirs, diag_count, slots)


def solution(mesh):
    in_specs = (
        P(("grp", "tp"), None, None, "rb"),
        P("grp", None, None, None),
        P("grp", None),
        P(("grp", "tp"), None, None),
        P(("grp", "tp")),
    )
    out_specs = P(("grp", "tp"), None, None, None)
    return jax.shard_map(shards, mesh=mesh, in_specs=in_specs, out_specs=out_specs, check_vma=False)
```

```python
import functools

import jax
import jax.numpy as jnp
from jax import lax
from jax.experimental import pallas as pl
from jax.experimental.pallas import tpu as pltpu
from jax.sharding import PartitionSpec as P

F32 = jnp.float32
BF16 = jnp.bfloat16
ANY = pl.BlockSpec(memory_space=pl.ANY)
SMEM = pl.BlockSpec(memory_space=pltpu.SMEM)
VMEM = pl.BlockSpec(memory_space=pltpu.VMEM)
SUBLANES = 8
LANES = 128
STEP = 16
MIB = 1 << 20
LITTLE = pl.CostEstimate(flops=1000, bytes_accessed=1000, transcendentals=0)
LONG = pl.CostEstimate(flops=5 * 10**10, bytes_accessed=1000, transcendentals=0)


def in_hbm(array):
    return pltpu.with_memory_space_constraint(array, pltpu.HBM)


def params(mib):
    return pltpu.CompilerParams(vmem_limit_bytes=mib * MIB)


def dot(left, right):
    return jnp.dot(left, right, preferred_element_type=F32)


def dot_nt(left, right):
    return lax.dot_general(left, right, (((1,), (1,)), ((), ())), preferred_element_type=F32)


def choose(index, values):
    out = jnp.int32(values[0])
    for n in range(1, len(values)):
        out = jnp.where(index == n, jnp.int32(values[n]), out)
    return out


def aligned(start, size):
    return pl.ds(pl.multiple_of(start, size), size)


def travel_order(tp_count, rb_count):
    half, quarter = tp_count // 2, tp_count // 4

    def both(distances):
        return [(far, side) for far in distances for side in range(rb_count)]

    long, late = both(range(half, half + quarter)), both(range(half + quarter, tp_count))
    near, rest = both(reversed(range(quarter, half))), both(range(1, quarter))
    own, other = (0, 0), [(0, side) for side in range(1, rb_count)]
    step, part = len(long) // 4, len(rest) // 2
    head = long[: 2 * step] + near[: 2 * step] + long[2 * step : 3 * step]
    tail = rest[:part] + other + near[2 * step : 3 * step] + long[3 * step :] + rest[part:] + near[3 * step :]
    return head, tail, late, [own]


def distance(far, tp_rank, tp_count):
    if far < tp_count // 2:
        return far
    return lax.bitwise_xor(jnp.int32(far), jnp.where(tp_rank < tp_count // 2, jnp.int32(tp_count // 4), jnp.int32(0)))


def pick_kernel(keys, times, table, *refs):
    outs, (held, wide, taken_times, sem, times_sem) = refs[:-5], refs[-5:]
    tp_rank, rb_rank = lax.axis_index("tp"), lax.axis_index("rb")
    rows, _, packed, _ = table.shape

    def fetch(chunk):
        where = aligned(chunk * STEP, STEP)
        return pltpu.make_async_copy(table.at[where], held.at[where], sem.at[chunk])

    copy = pltpu.make_async_copy(times, taken_times, times_sem)
    copy.start()
    for chunk in range(rows // STEP):
        fetch(chunk).start()
    copy.wait()

    def step(chunk, carry):
        fetch(chunk).wait()
        where = aligned(chunk * STEP, STEP)
        for n, (far, side) in enumerate(keys):
            owner = lax.bitwise_xor(tp_rank, distance(far, tp_rank, taken_times.shape[1]))
            time = taken_times[lax.bitwise_xor(rb_rank, side), owner]
            slot = n % wide.shape[0]
            wide[slot] = held[where, time].astype(F32).reshape(STEP * packed, LANES)
            for tile in range(packed // 2):
                for part in range(2):
                    taken = wide[slot, pl.ds(2 * tile + part, STEP, stride=packed), :]
                    outs[n][part, where, tile * LANES : (tile + 1) * LANES] = taken.astype(BF16)
        return carry

    lax.fori_loop(0, rows // STEP, step, 0)


def pick(owner_times, peram, keys, name, spare):
    rows, times, parts, width = peram.shape
    tiles = width // LANES
    table = peram.reshape(rows, times, parts, tiles, LANES).swapaxes(2, 3)
    table = table.reshape(rows, times, tiles * parts, LANES)
    picked = pl.pallas_call(
        functools.partial(pick_kernel, keys),
        out_shape=[jax.ShapeDtypeStruct((parts, rows, width), BF16)] * len(keys) + spare,
        in_specs=[ANY, ANY],
        out_specs=[VMEM] * len(keys) + [ANY] * len(spare),
        scratch_shapes=[
            pltpu.VMEM(table.shape, BF16),
            pltpu.VMEM((4, STEP * tiles * parts, LANES), F32),
            pltpu.SMEM(owner_times.shape[::-1], jnp.int32),
            pltpu.SemaphoreType.DMA((rows // STEP,)),
            pltpu.SemaphoreType.DMA,
        ],
        compiler_params=params(32),
        cost_estimate=LITTLE,
        name=name,
    )(in_hbm(owner_times.T), in_hbm(table))
    return dict(zip(keys, picked))


def place(far, per_spin):
    low = lax.axis_index("tp") % per_spin
    return (far // per_spin) * per_spin + lax.bitwise_xor(jnp.int32(far % per_spin), low)


def gram_block(left, right):
    depth = left.shape[1] // 2
    real = dot_nt(left, right)
    imag = dot_nt(left[:, :depth], right[:, depth:]) - dot_nt(left[:, depth:], right[:, :depth])
    return real.astype(BF16), imag.astype(BF16)


def fold(values):
    rows, columns = values.shape
    folded = jnp.sum(values.reshape(rows // SUBLANES, SUBLANES, columns), axis=0)
    return functools.reduce(jnp.add, [folded[:, n : n + LANES] for n in range(0, columns, LANES)])


def direct_sums(diagonal, own, out, carried=None):
    real = functools.reduce(jnp.add, [block[0].astype(F32) for block in diagonal])
    imag = functools.reduce(jnp.add, [block[1].astype(F32) for block in diagonal])
    for slot in range(own.shape[0]):
        elem_re, elem_im = own[slot, 0].astype(F32), own[slot, 1].astype(F32)
        sums = [fold(elem_re * real + elem_im * imag), fold(elem_im * real - elem_re * imag)]
        for part in range(2):
            n = 2 * slot + part
            out[n] = sums[part] if carried is None else sums[part] + carried[n]


def sums_shape(count):
    return jax.ShapeDtypeStruct((count, SUBLANES, LANES), F32)


def early_blocks(spins):
    off = [(s, t) for s in range(spins - 1) for t in range(s + 1, spins - 1)]
    return off + [(s, s) for s in range(spins - 1)]


def early_kernel(eig, keys, rb_count, blocks, *refs):
    pieces, (own, flat, out, traces, sem) = refs[:-5], refs[-5:]
    rows, width = pieces[0].shape[1:]
    depth = rb_count * width
    copies = []
    for n, ((far, side), piece) in enumerate(zip(keys, pieces)):
        where = aligned(place(far, eig // rows) * rows, rows)
        for part in range(2):
            columns = pl.ds(part * depth + side * width, width)
            copies.append(pltpu.make_async_copy(piece.at[part], flat.at[where, columns], sem.at[2 * n + part]))
    for copy in copies:
        copy.start()
    for copy in copies:
        copy.wait()

    def step(n, carry):
        top, side = choose(n, [b[0] for b in blocks]), choose(n, [b[1] for b in blocks])
        out[n, 0], out[n, 1] = gram_block(flat[aligned(top * eig, eig), :], flat[aligned(side * eig, eig), :])
        return carry

    lax.fori_loop(0, len(blocks), step, 0)
    diagonal = [out.at[n] for n, block in enumerate(blocks) if block[0] == block[1]]
    direct_sums(diagonal, own, traces)


def early_gram(keys, pieces, own_elems, spins, eig, rb_count):
    blocks = early_blocks(spins)
    depth = 2 * rb_count * pieces[0].shape[2]
    return pl.pallas_call(
        functools.partial(early_kernel, eig, keys, rb_count, blocks),
        out_shape=(
            jax.ShapeDtypeStruct(((spins - 1) * eig, depth), BF16),
            jax.ShapeDtypeStruct((len(blocks), 2, eig, eig), BF16),
            sums_shape(2 * own_elems.shape[0]),
        ),
        in_specs=[ANY] * len(pieces) + [VMEM],
        out_specs=(VMEM, VMEM, VMEM),
        scratch_shapes=[pltpu.SemaphoreType.DMA((2 * len(pieces),))],
        compiler_params=params(32),
        cost_estimate=LONG,
        name="early_gram",
    )(*pieces, own_elems)


def side_columns(ref, rows, side, width, rb_count):
    return [ref[rows, (part * rb_count + side) * width : (part * rb_count + side + 1) * width] for part in range(2)]


def half_products(left, right):
    real = dot_nt(left[0], right[0]) + dot_nt(left[1], right[1])
    imag = dot_nt(left[0], right[1]) - dot_nt(left[1], right[0])
    return real, imag


def gather_last(eig, keys, others, pieces, last):
    rows, width = pieces[0].shape[1:]
    for (far, _), piece in zip(keys, pieces):
        where = aligned((place(far, eig // rows) - others * (eig // rows)) * rows, rows)
        for part in range(2):
            last[where, part * width : (part + 1) * width] = piece[part]


def late_begin_kernel(eig, keys, rb_count, flat, begun, *refs):
    pieces, (out, last) = refs[:-2], refs[-2:]
    side, width, others = keys[0][1], pieces[0].shape[2], flat.shape[0] // eig
    gather_last(eig, keys, others, pieces, last)
    right = [last[:, :width], last[:, width:]]
    for n in range(others):
        left = side_columns(flat, slice(n * eig, (n + 1) * eig), side, width, rb_count)
        out[n, 0], out[n, 1] = half_products(left, right)
    out[others, 0], out[others, 1] = half_products(right, right)


def late_begin(keys, flat, begun, pieces, spins, eig, rb_count):
    return pl.pallas_call(
        functools.partial(late_begin_kernel, eig, keys, rb_count),
        out_shape=jax.ShapeDtypeStruct((spins, 2, eig, eig), F32),
        in_specs=[VMEM, ANY] + [VMEM] * len(pieces),
        out_specs=VMEM,
        scratch_shapes=[pltpu.VMEM((eig, 2 * pieces[0].shape[2]), BF16)],
        compiler_params=params(32),
        cost_estimate=LITTLE,
        name="late_begin",
    )(flat, begun, *pieces)


def late_rows_kernel(eig, keys, rb_count, flat, partial, *refs):
    pieces, (out, last) = refs[:-2], refs[-2:]
    side, width = keys[0][1], pieces[0].shape[2]
    gather_last(eig, keys, flat.shape[0] // eig, pieces, last)
    right = [last[:, :width], last[:, width:]]
    for n in range(out.shape[0]):
        left = side_columns(flat, slice(n * eig, (n + 1) * eig), side, width, rb_count)
        real, imag = half_products(left, right)
        out[n, 0], out[n, 1] = (partial[n, 0] + real).astype(BF16), (partial[n, 1] + imag).astype(BF16)


def late_rest_kernel(eig, side, rb_count, flat, partial, last, own, carried, out, traces):
    count, width = out.shape[0] - 1, last.shape[1] // 2
    others = flat.shape[0] // eig
    right = [last[:, :width], last[:, width:]]
    for n in range(count + 1):
        spin = others - count + n
        left = right
        if n < count:
            left = side_columns(flat, slice(spin * eig, (spin + 1) * eig), side, width, rb_count)
        real, imag = half_products(left, right)
        out[n, 0], out[n, 1] = (partial[spin, 0] + real).astype(BF16), (partial[spin, 1] + imag).astype(BF16)
    direct_sums([out.at[count]], own, traces, carried)


def late_rows(keys, flat, partial, pieces, spins, eig, rb_count):
    return pl.pallas_call(
        functools.partial(late_rows_kernel, eig, keys, rb_count),
        out_shape=(
            jax.ShapeDtypeStruct((spins // 2, 2, eig, eig), BF16),
            jax.ShapeDtypeStruct((eig, 2 * pieces[0].shape[2]), BF16),
        ),
        in_specs=[VMEM] * (2 + len(pieces)),
        out_specs=(VMEM, VMEM),
        compiler_params=params(32),
        cost_estimate=LONG,
        name="late_rows",
    )(flat, partial, *pieces)


def late_rest(side, flat, partial, last, own, carried, spins, eig, rb_count):
    return pl.pallas_call(
        functools.partial(late_rest_kernel, eig, side, rb_count),
        out_shape=(
            jax.ShapeDtypeStruct((spins - spins // 2, 2, eig, eig), BF16),
            sums_shape(carried.shape[0]),
        ),
        in_specs=[VMEM] * 5,
        out_specs=(VMEM, VMEM),
        compiler_params=params(32),
        cost_estimate=LITTLE,
        name="late_rest",
    )(flat, partial, last, own, carried)


def factors_kernel(diag_mom, elems, right_ref, left_ref, own_ref, held, sem):
    rank = lax.axis_index("rb")
    eig = held.shape[-1]
    copies = []
    for time in range(2):
        which = diag_mom[0, rank, lax.bitwise_xor(rank, time)]
        copies.append(pltpu.make_async_copy(elems.at[which], held.at[time], sem.at[time]))
    for slot in range(own_ref.shape[0]):
        copies.append(pltpu.make_async_copy(elems.at[diag_mom[0, slot, rank]], own_ref.at[slot], sem.at[2 + slot]))
    for copy in copies:
        copy.start()
    for copy in copies:
        copy.wait()
    for time in range(2):
        re, im = held[time, 0], held[time, 1]
        right_ref[time, :eig, :eig] = re
        right_ref[time, :eig, eig:] = im
        right_ref[time, eig:, :eig] = -im
        right_ref[time, eig:, eig:] = re
        re_t = re.astype(F32).T.astype(BF16)
        im_t = im.astype(F32).T.astype(BF16)
        left_ref[time, :eig, :eig] = re_t
        left_ref[time, :eig, eig:] = im_t
        left_ref[time, eig:, :eig] = im_t
        left_ref[time, eig:, eig:] = -re_t


def factors(diag_mom, src_elems):
    slots, eig = diag_mom.shape[1], src_elems.shape[-1]
    form = jax.ShapeDtypeStruct((2, 2 * eig, 2 * eig), BF16)
    return pl.pallas_call(
        factors_kernel,
        out_shape=(form, form, jax.ShapeDtypeStruct((slots, 2, eig, eig), BF16)),
        in_specs=[SMEM, ANY],
        out_specs=(VMEM, VMEM, VMEM),
        scratch_shapes=[pltpu.VMEM((2, 2, eig, eig), BF16), pltpu.SemaphoreType.DMA((2 + slots,))],
        compiler_params=params(32),
        cost_estimate=LITTLE,
        name="factors",
    )(diag_mom, src_elems)


def right_products(x, count, from_right):
    rows = [jnp.concatenate([x[n, 0], x[n, 1]], axis=1) for n in range(count)]
    return dot(jnp.concatenate(rows, axis=0), from_right)


def left_product(y, n, from_left):
    eig = y.shape[-1]
    return dot(from_left, y[n].reshape(2 * eig, eig))


def paired(product, partner):
    eig = partner.shape[1]
    p_re, p_im = product[:, :eig], product[:, eig:]
    w_re, w_im = partner[:eig], partner[eig:]
    return fold(p_re * w_re - p_im * w_im), fold(p_re * w_im + p_im * w_re)


def own_products_kernel(own, right, left, products, partners):
    count = own.shape[0]
    products[...] = right_products(own, count, right[0])
    for n in range(count):
        partners[n] = left_product(own, n, left[0])


def own_products(own, right, left):
    count, eig = own.shape[0], own.shape[-1]
    return pl.pallas_call(
        own_products_kernel,
        out_shape=(
            jax.ShapeDtypeStruct((count * eig, 2 * eig), F32),
            jax.ShapeDtypeStruct((count, 2 * eig, eig), F32),
        ),
        in_specs=[VMEM] * 3,
        out_specs=(VMEM, VMEM),
        compiler_params=params(32),
        cost_estimate=LITTLE,
        name="own_products",
    )(own, right, left)


def joined_kernel(other, right, left, products, partners, carried, out):
    count, eig = other.shape[0], other.shape[-1]
    theirs = right_products(other, count, right[1])
    real, imag = [carried[0]], [carried[1]]
    for n in range(count):
        rows = slice(n * eig, (n + 1) * eig)
        sums = [paired(theirs[rows], partners[n]), paired(products[rows, :], left_product(other, n, left[1]))]
        real += [pair[0] for pair in sums]
        imag += [pair[1] for pair in sums]
    out[0] = functools.reduce(jnp.add, real)
    out[1] = functools.reduce(jnp.add, imag)


def joined_traces(other, right, left, products, partners, carried):
    return pl.pallas_call(
        joined_kernel,
        out_shape=sums_shape(2),
        in_specs=[VMEM] * 6,
        out_specs=VMEM,
        compiler_params=params(32),
        cost_estimate=LITTLE,
        name="late_cross",
    )(other, right, left, products, partners, carried)


def cross_kernel(offs, own, other, right, left, *refs):
    carried, out = refs[:-1], refs[-1]
    eig = own.shape[-1]
    if len(other.shape) > len(own.shape):
        other = other.at[1 - lax.axis_index("rb")]
    real, imag = [], []

    def add(x, y, count, from_right, from_left):
        product = right_products(x, count, from_right)
        for n in range(count):
            pair = paired(product[n * eig : (n + 1) * eig], left_product(y, n, from_left))
            real.append(pair[0])
            imag.append(pair[1])

    add(other, own, own.shape[0], right[1], left[0])
    add(own, other, offs, right[0], left[1])
    out[0] = functools.reduce(jnp.add, real + [ref[0] for ref in carried])
    out[1] = functools.reduce(jnp.add, imag + [ref[1] for ref in carried])


def cross_traces(offs, own, other, right, left, carried, name):
    return pl.pallas_call(
        functools.partial(cross_kernel, offs),
        out_shape=sums_shape(2),
        in_specs=[VMEM] * (4 + len(carried)),
        out_specs=VMEM,
        compiler_params=params(32),
        cost_estimate=LITTLE,
        name=name,
    )(own, other, right, left, *carried)


def last_cross_kernel(offs, own, other, right, left, direct, carried, out):
    count = direct.shape[0]
    for n in range(count):
        out[n] = direct[n]
    cross_kernel(offs, own, other, right, left, carried, out.at[pl.ds(count, 2)])


def last_cross(offs, own, other, right, left, direct, carried):
    return pl.pallas_call(
        functools.partial(last_cross_kernel, offs),
        out_shape=sums_shape(direct.shape[0] + 2),
        in_specs=[VMEM] * 6,
        out_specs=VMEM,
        compiler_params=params(32),
        cost_estimate=LITTLE,
        name="last_cross",
    )(own, other, right, left, direct, carried)


def final_kernel(slots, mine, theirs, count, out):
    rank = lax.axis_index("rb")
    lane = lax.broadcasted_iota(jnp.int32, (1, LANES), 1)

    def totals(ref):
        rows = jnp.concatenate([jnp.sum(ref[n], axis=0, keepdims=True) for n in range(ref.shape[0])], axis=0)
        sums = jnp.broadcast_to(jnp.sum(rows, axis=1, keepdims=True), rows.shape)
        return [sums[n : n + 1] for n in range(ref.shape[0])]

    def put(slot, kind, re, im):
        value = jnp.where(lane == 0, re, im) * 0.25
        out[0, slot, kind : kind + 1, :] = jnp.where(slot < count[0], value, 0.0)[:, :2]

    m, t = totals(mine), totals(theirs)
    for slot in range(slots):
        m_re, m_im, t_re, t_im = m[2 * slot], m[2 * slot + 1], t[2 * slot], t[2 * slot + 1]
        put(slot, 0, m_re * t_re - m_im * t_im, m_re * t_im + m_im * t_re)
        here = rank == slot
        put(slot, 1, jnp.where(here, m[2 * slots], t[2 * slots]), jnp.where(here, m[2 * slots + 1], t[2 * slots + 1]))


def final(mine, theirs, diag_count, slots):
    return pl.pallas_call(
        functools.partial(final_kernel, slots),
        out_shape=jax.ShapeDtypeStruct((1, slots, 2, 2), F32),
        in_specs=[VMEM, VMEM, SMEM],
        out_specs=VMEM,
        compiler_params=params(32),
        name="final",
    )(mine, theirs, diag_count)


def shards(peram, src_elems, owner_times, diag_mom, diag_count):
    tp_count, rb_count = lax.axis_size("tp"), lax.axis_size("rb")
    eig = src_elems.shape[-1]
    spins = tp_count * peram.shape[0] // eig
    slots = diag_mom.shape[1]

    head, tail, late, own = travel_order(tp_count, rb_count)
    early_keys = head + tail
    picked = pick(owner_times, peram, head, "pick_head", [jax.ShapeDtypeStruct((4, *peram.shape), BF16)])
    picked.update(pick(owner_times, peram, tail + late + own, "pick_tail", []))

    def send(key):
        far, side = key
        swapped = tp_count // 4 if far >= tp_count // 2 else 0
        pairs = [
            (tp * rb_count + rb, (tp ^ far ^ (swapped if tp < tp_count // 2 else 0)) * rb_count + (rb ^ side))
            for tp in range(tp_count)
            for rb in range(rb_count)
        ]
        return lax.ppermute(picked[key], ("tp", "rb"), pairs)

    swap = [(rb, rb ^ 1) for rb in range(rb_count)]
    right, left, own_elems = factors(diag_mom, src_elems)
    arrived = [send(key) for key in early_keys] + [picked[key] for key in own]
    flat, early, direct = early_gram(early_keys + own, arrived, own_elems, spins, eig, rb_count)
    early_both = lax.all_to_all(jnp.stack([early] * rb_count), "rb", 0, 0)
    offs = early.shape[0] - (spins - 1)
    begun = cross_traces(offs, early, early_both, right, left, [], "early_cross")

    halves = [[key for key in late if key[1] == side] for side in range(rb_count)]
    sent = [[send(key) for key in keys] for keys in halves]
    half = late_begin(halves[0], flat, begun, sent[0], spins, eig, rb_count)
    blocks, last = late_rows(halves[1], flat, half, sent[1], spins, eig, rb_count)
    swapped = lax.ppermute(blocks, "rb", swap)
    rest, traces = late_rest(1, flat, half, last, own_elems, direct, spins, eig, rb_count)
    rest_swapped = lax.ppermute(rest, "rb", swap)
    products, partners = own_products(blocks, right, left)
    partial = joined_traces(swapped, right, left, products, partners, begun)
    mine = last_cross(rest.shape[0] - 1, rest, rest_swapped, right, left, traces, partial)
    theirs = lax.ppermute(mine, "rb", swap)
    return final(mine, theirs, diag_count, slots)


def solution(mesh):
    in_specs = (
        P(("grp", "tp"), None, None, "rb"),
        P("grp", None, None, None),
        P("grp", None),
        P(("grp", "tp"), None, None),
        P(("grp", "tp")),
    )
    out_specs = P(("grp", "tp"), None, None, None)
    return jax.shard_map(shards, mesh=mesh, in_specs=in_specs, out_specs=out_specs, check_vma=False)
```

```python
import functools

import jax
import jax.numpy as jnp
from jax import lax
from jax.experimental import pallas as pl
from jax.experimental.pallas import tpu as pltpu
from jax.sharding import PartitionSpec as P

F32 = jnp.float32
BF16 = jnp.bfloat16
ANY = pl.BlockSpec(memory_space=pl.ANY)
SMEM = pl.BlockSpec(memory_space=pltpu.SMEM)
VMEM = pl.BlockSpec(memory_space=pltpu.VMEM)
SUBLANES = 8
LANES = 128
STEP = 16
MIB = 1 << 20
LITTLE = pl.CostEstimate(flops=1000, bytes_accessed=1000, transcendentals=0)
LONG = pl.CostEstimate(flops=5 * 10**10, bytes_accessed=1000, transcendentals=0)


def in_hbm(array):
    return pltpu.with_memory_space_constraint(array, pltpu.HBM)


def params(mib):
    return pltpu.CompilerParams(vmem_limit_bytes=mib * MIB)


def dot(left, right):
    return jnp.dot(left, right, preferred_element_type=F32)


def dot_nt(left, right):
    return lax.dot_general(left, right, (((1,), (1,)), ((), ())), preferred_element_type=F32)


def choose(index, values):
    out = jnp.int32(values[0])
    for n in range(1, len(values)):
        out = jnp.where(index == n, jnp.int32(values[n]), out)
    return out


def aligned(start, size):
    return pl.ds(pl.multiple_of(start, size), size)


def travel_order(tp_count, rb_count):
    half, quarter = tp_count // 2, tp_count // 4

    def both(distances):
        return [(far, side) for far in distances for side in range(rb_count)]

    long, late = both(range(half, half + quarter)), both(range(half + quarter, tp_count))
    near, rest = both(reversed(range(quarter, half))), both(range(1, quarter))
    own, other = (0, 0), [(0, side) for side in range(1, rb_count)]
    step = len(long) // 4
    head = long[: 2 * step] + near[: 2 * step] + long[2 * step : 3 * step]
    tail = long[3 * step :] + other + near[2 * step : 3 * step] + rest + near[3 * step :]
    return head, tail, late, [own]


def distance(far, tp_rank, tp_count):
    if far < tp_count // 2:
        return far
    return lax.bitwise_xor(jnp.int32(far), jnp.where(tp_rank < tp_count // 2, jnp.int32(tp_count // 4), jnp.int32(0)))


def pick_kernel(keys, times, table, *refs):
    outs, (held, wide, taken_times, sem, times_sem) = refs[:-5], refs[-5:]
    tp_rank, rb_rank = lax.axis_index("tp"), lax.axis_index("rb")
    rows, _, packed, _ = table.shape

    def fetch(chunk):
        where = aligned(chunk * STEP, STEP)
        return pltpu.make_async_copy(table.at[where], held.at[where], sem.at[chunk])

    copy = pltpu.make_async_copy(times, taken_times, times_sem)
    copy.start()
    for chunk in range(rows // STEP):
        fetch(chunk).start()
    copy.wait()

    def step(chunk, carry):
        fetch(chunk).wait()
        where = aligned(chunk * STEP, STEP)
        for n, (far, side) in enumerate(keys):
            owner = lax.bitwise_xor(tp_rank, distance(far, tp_rank, taken_times.shape[1]))
            time = taken_times[lax.bitwise_xor(rb_rank, side), owner]
            slot = n % wide.shape[0]
            wide[slot] = held[where, time].astype(F32).reshape(STEP * packed, LANES)
            for tile in range(packed // 2):
                for part in range(2):
                    taken = wide[slot, pl.ds(2 * tile + part, STEP, stride=packed), :]
                    outs[n][part, where, tile * LANES : (tile + 1) * LANES] = taken.astype(BF16)
        return carry

    lax.fori_loop(0, rows // STEP, step, 0)


def pick(owner_times, peram, keys, name, spare):
    rows, times, parts, width = peram.shape
    tiles = width // LANES
    table = peram.reshape(rows, times, parts, tiles, LANES).swapaxes(2, 3)
    table = table.reshape(rows, times, tiles * parts, LANES)
    picked = pl.pallas_call(
        functools.partial(pick_kernel, keys),
        out_shape=[jax.ShapeDtypeStruct((parts, rows, width), BF16)] * len(keys) + spare,
        in_specs=[ANY, ANY],
        out_specs=[VMEM] * len(keys) + [ANY] * len(spare),
        scratch_shapes=[
            pltpu.VMEM(table.shape, BF16),
            pltpu.VMEM((4, STEP * tiles * parts, LANES), F32),
            pltpu.SMEM(owner_times.shape[::-1], jnp.int32),
            pltpu.SemaphoreType.DMA((rows // STEP,)),
            pltpu.SemaphoreType.DMA,
        ],
        compiler_params=params(32),
        cost_estimate=LITTLE,
        name=name,
    )(in_hbm(owner_times.T), in_hbm(table))
    return dict(zip(keys, picked))


def place(far, per_spin):
    low = lax.axis_index("tp") % per_spin
    return (far // per_spin) * per_spin + lax.bitwise_xor(jnp.int32(far % per_spin), low)


def gram_block(left, right):
    depth = left.shape[1] // 2
    real = dot_nt(left, right)
    imag = dot_nt(left[:, :depth], right[:, depth:]) - dot_nt(left[:, depth:], right[:, :depth])
    return real.astype(BF16), imag.astype(BF16)


def fold(values):
    rows, columns = values.shape
    folded = jnp.sum(values.reshape(rows // SUBLANES, SUBLANES, columns), axis=0)
    return functools.reduce(jnp.add, [folded[:, n : n + LANES] for n in range(0, columns, LANES)])


def direct_sums(diagonal, own, out, carried=None):
    real = functools.reduce(jnp.add, [block[0].astype(F32) for block in diagonal])
    imag = functools.reduce(jnp.add, [block[1].astype(F32) for block in diagonal])
    for slot in range(own.shape[0]):
        elem_re, elem_im = own[slot, 0].astype(F32), own[slot, 1].astype(F32)
        sums = [fold(elem_re * real + elem_im * imag), fold(elem_im * real - elem_re * imag)]
        for part in range(2):
            n = 2 * slot + part
            out[n] = sums[part] if carried is None else sums[part] + carried[n]


def sums_shape(count):
    return jax.ShapeDtypeStruct((count, SUBLANES, LANES), F32)


def early_blocks(spins):
    off = [(s, t) for s in range(spins - 1) for t in range(s + 1, spins - 1)]
    return off + [(s, s) for s in range(spins - 1)]


def early_kernel(eig, keys, rb_count, blocks, *refs):
    pieces, (own, flat, out, traces, sem) = refs[:-5], refs[-5:]
    rows, width = pieces[0].shape[1:]
    depth = rb_count * width
    copies = []
    for n, ((far, side), piece) in enumerate(zip(keys, pieces)):
        where = aligned(place(far, eig // rows) * rows, rows)
        for part in range(2):
            columns = pl.ds(part * depth + side * width, width)
            copies.append(pltpu.make_async_copy(piece.at[part], flat.at[where, columns], sem.at[2 * n + part]))
    for copy in copies:
        copy.start()
    for copy in copies:
        copy.wait()

    def step(n, carry):
        top, side = choose(n, [b[0] for b in blocks]), choose(n, [b[1] for b in blocks])
        out[n, 0], out[n, 1] = gram_block(flat[aligned(top * eig, eig), :], flat[aligned(side * eig, eig), :])
        return carry

    lax.fori_loop(0, len(blocks), step, 0)
    diagonal = [out.at[n] for n, block in enumerate(blocks) if block[0] == block[1]]
    direct_sums(diagonal, own, traces)


def early_gram(keys, pieces, own_elems, spins, eig, rb_count):
    blocks = early_blocks(spins)
    depth = 2 * rb_count * pieces[0].shape[2]
    return pl.pallas_call(
        functools.partial(early_kernel, eig, keys, rb_count, blocks),
        out_shape=(
            jax.ShapeDtypeStruct(((spins - 1) * eig, depth), BF16),
            jax.ShapeDtypeStruct((len(blocks), 2, eig, eig), BF16),
            sums_shape(2 * own_elems.shape[0]),
        ),
        in_specs=[ANY] * len(pieces) + [VMEM],
        out_specs=(VMEM, VMEM, VMEM),
        scratch_shapes=[pltpu.SemaphoreType.DMA((2 * len(pieces),))],
        compiler_params=params(32),
        cost_estimate=LONG,
        name="early_gram",
    )(*pieces, own_elems)


def side_columns(ref, rows, side, width, rb_count):
    return [ref[rows, (part * rb_count + side) * width : (part * rb_count + side + 1) * width] for part in range(2)]


def half_products(left, right):
    real = dot_nt(left[0], right[0]) + dot_nt(left[1], right[1])
    imag = dot_nt(left[0], right[1]) - dot_nt(left[1], right[0])
    return real, imag


def gather_last(eig, keys, others, pieces, last):
    rows, width = pieces[0].shape[1:]
    for (far, _), piece in zip(keys, pieces):
        where = aligned((place(far, eig // rows) - others * (eig // rows)) * rows, rows)
        for part in range(2):
            last[where, part * width : (part + 1) * width] = piece[part]


def late_begin_kernel(eig, keys, rb_count, flat, begun, *refs):
    pieces, (out, last) = refs[:-2], refs[-2:]
    side, width, others = keys[0][1], pieces[0].shape[2], flat.shape[0] // eig
    gather_last(eig, keys, others, pieces, last)
    right = [last[:, :width], last[:, width:]]
    for n in range(others):
        left = side_columns(flat, slice(n * eig, (n + 1) * eig), side, width, rb_count)
        out[n, 0], out[n, 1] = half_products(left, right)
    out[others, 0], out[others, 1] = half_products(right, right)


def late_begin(keys, flat, begun, pieces, spins, eig, rb_count):
    return pl.pallas_call(
        functools.partial(late_begin_kernel, eig, keys, rb_count),
        out_shape=jax.ShapeDtypeStruct((spins, 2, eig, eig), F32),
        in_specs=[VMEM, ANY] + [VMEM] * len(pieces),
        out_specs=VMEM,
        scratch_shapes=[pltpu.VMEM((eig, 2 * pieces[0].shape[2]), BF16)],
        compiler_params=params(32),
        cost_estimate=LITTLE,
        name="late_begin",
    )(flat, begun, *pieces)


def late_rows_kernel(eig, keys, rb_count, flat, partial, *refs):
    pieces, (out, last) = refs[:-2], refs[-2:]
    side, width = keys[0][1], pieces[0].shape[2]
    gather_last(eig, keys, flat.shape[0] // eig, pieces, last)
    right = [last[:, :width], last[:, width:]]
    for n in range(out.shape[0]):
        left = side_columns(flat, slice(n * eig, (n + 1) * eig), side, width, rb_count)
        real, imag = half_products(left, right)
        out[n, 0], out[n, 1] = (partial[n, 0] + real).astype(BF16), (partial[n, 1] + imag).astype(BF16)


def late_rest_kernel(eig, side, rb_count, flat, partial, last, own, carried, out, traces):
    count, width = out.shape[0] - 1, last.shape[1] // 2
    others = flat.shape[0] // eig
    right = [last[:, :width], last[:, width:]]
    for n in range(count + 1):
        spin = others - count + n
        left = right
        if n < count:
            left = side_columns(flat, slice(spin * eig, (spin + 1) * eig), side, width, rb_count)
        real, imag = half_products(left, right)
        out[n, 0], out[n, 1] = (partial[spin, 0] + real).astype(BF16), (partial[spin, 1] + imag).astype(BF16)
    direct_sums([out.at[count]], own, traces, carried)


def late_rows(keys, flat, partial, pieces, spins, eig, rb_count):
    return pl.pallas_call(
        functools.partial(late_rows_kernel, eig, keys, rb_count),
        out_shape=(
            jax.ShapeDtypeStruct((spins // 2, 2, eig, eig), BF16),
            jax.ShapeDtypeStruct((eig, 2 * pieces[0].shape[2]), BF16),
        ),
        in_specs=[VMEM] * (2 + len(pieces)),
        out_specs=(VMEM, VMEM),
        compiler_params=params(32),
        cost_estimate=LONG,
        name="late_rows",
    )(flat, partial, *pieces)


def late_rest(side, flat, partial, last, own, carried, spins, eig, rb_count):
    return pl.pallas_call(
        functools.partial(late_rest_kernel, eig, side, rb_count),
        out_shape=(
            jax.ShapeDtypeStruct((spins - spins // 2, 2, eig, eig), BF16),
            sums_shape(carried.shape[0]),
        ),
        in_specs=[VMEM] * 5,
        out_specs=(VMEM, VMEM),
        compiler_params=params(32),
        cost_estimate=LITTLE,
        name="late_rest",
    )(flat, partial, last, own, carried)


def factors_kernel(diag_mom, elems, right_ref, left_ref, own_ref, held, sem):
    rank = lax.axis_index("rb")
    eig = held.shape[-1]
    copies = []
    for time in range(2):
        which = diag_mom[0, rank, lax.bitwise_xor(rank, time)]
        copies.append(pltpu.make_async_copy(elems.at[which], held.at[time], sem.at[time]))
    for slot in range(own_ref.shape[0]):
        copies.append(pltpu.make_async_copy(elems.at[diag_mom[0, slot, rank]], own_ref.at[slot], sem.at[2 + slot]))
    for copy in copies:
        copy.start()
    for copy in copies:
        copy.wait()
    for time in range(2):
        re, im = held[time, 0], held[time, 1]
        right_ref[time, :eig, :eig] = re
        right_ref[time, :eig, eig:] = im
        right_ref[time, eig:, :eig] = -im
        right_ref[time, eig:, eig:] = re
        re_t = re.astype(F32).T.astype(BF16)
        im_t = im.astype(F32).T.astype(BF16)
        left_ref[time, :eig, :eig] = re_t
        left_ref[time, :eig, eig:] = im_t
        left_ref[time, eig:, :eig] = im_t
        left_ref[time, eig:, eig:] = -re_t


def factors(diag_mom, src_elems):
    slots, eig = diag_mom.shape[1], src_elems.shape[-1]
    form = jax.ShapeDtypeStruct((2, 2 * eig, 2 * eig), BF16)
    return pl.pallas_call(
        factors_kernel,
        out_shape=(form, form, jax.ShapeDtypeStruct((slots, 2, eig, eig), BF16)),
        in_specs=[SMEM, ANY],
        out_specs=(VMEM, VMEM, VMEM),
        scratch_shapes=[pltpu.VMEM((2, 2, eig, eig), BF16), pltpu.SemaphoreType.DMA((2 + slots,))],
        compiler_params=params(32),
        cost_estimate=LITTLE,
        name="factors",
    )(diag_mom, src_elems)


def right_products(x, count, from_right):
    rows = [jnp.concatenate([x[n, 0], x[n, 1]], axis=1) for n in range(count)]
    return dot(jnp.concatenate(rows, axis=0), from_right)


def left_product(y, n, from_left):
    eig = y.shape[-1]
    return dot(from_left, y[n].reshape(2 * eig, eig))


def paired(product, partner):
    eig = partner.shape[1]
    p_re, p_im = product[:, :eig], product[:, eig:]
    w_re, w_im = partner[:eig], partner[eig:]
    return fold(p_re * w_re - p_im * w_im), fold(p_re * w_im + p_im * w_re)


def own_products_kernel(own, right, left, products, partners):
    count = own.shape[0]
    products[...] = right_products(own, count, right[0])
    for n in range(count):
        partners[n] = left_product(own, n, left[0])


def own_products(own, right, left):
    count, eig = own.shape[0], own.shape[-1]
    return pl.pallas_call(
        own_products_kernel,
        out_shape=(
            jax.ShapeDtypeStruct((count * eig, 2 * eig), F32),
            jax.ShapeDtypeStruct((count, 2 * eig, eig), F32),
        ),
        in_specs=[VMEM] * 3,
        out_specs=(VMEM, VMEM),
        compiler_params=params(32),
        cost_estimate=LITTLE,
        name="own_products",
    )(own, right, left)


def joined_kernel(other, right, left, products, partners, carried, out):
    count, eig = other.shape[0], other.shape[-1]
    theirs = right_products(other, count, right[1])
    real, imag = [carried[0]], [carried[1]]
    for n in range(count):
        rows = slice(n * eig, (n + 1) * eig)
        sums = [paired(theirs[rows], partners[n]), paired(products[rows, :], left_product(other, n, left[1]))]
        real += [pair[0] for pair in sums]
        imag += [pair[1] for pair in sums]
    out[0] = functools.reduce(jnp.add, real)
    out[1] = functools.reduce(jnp.add, imag)


def joined_traces(other, right, left, products, partners, carried):
    return pl.pallas_call(
        joined_kernel,
        out_shape=sums_shape(2),
        in_specs=[VMEM] * 6,
        out_specs=VMEM,
        compiler_params=params(32),
        cost_estimate=LITTLE,
        name="late_cross",
    )(other, right, left, products, partners, carried)


def cross_kernel(offs, own, other, right, left, *refs):
    carried, out = refs[:-1], refs[-1]
    eig = own.shape[-1]
    if len(other.shape) > len(own.shape):
        other = other.at[1 - lax.axis_index("rb")]
    real, imag = [], []

    def add(x, y, count, from_right, from_left):
        product = right_products(x, count, from_right)
        for n in range(count):
            pair = paired(product[n * eig : (n + 1) * eig], left_product(y, n, from_left))
            real.append(pair[0])
            imag.append(pair[1])

    add(other, own, own.shape[0], right[1], left[0])
    add(own, other, offs, right[0], left[1])
    out[0] = functools.reduce(jnp.add, real + [ref[0] for ref in carried])
    out[1] = functools.reduce(jnp.add, imag + [ref[1] for ref in carried])


def cross_traces(offs, own, other, right, left, carried, name):
    return pl.pallas_call(
        functools.partial(cross_kernel, offs),
        out_shape=sums_shape(2),
        in_specs=[VMEM] * (4 + len(carried)),
        out_specs=VMEM,
        compiler_params=params(32),
        cost_estimate=LITTLE,
        name=name,
    )(own, other, right, left, *carried)


def last_cross_kernel(offs, own, other, right, left, direct, carried, out):
    count = direct.shape[0]
    for n in range(count):
        out[n] = direct[n]
    cross_kernel(offs, own, other, right, left, carried, out.at[pl.ds(count, 2)])


def last_cross(offs, own, other, right, left, direct, carried):
    return pl.pallas_call(
        functools.partial(last_cross_kernel, offs),
        out_shape=sums_shape(direct.shape[0] + 2),
        in_specs=[VMEM] * 6,
        out_specs=VMEM,
        compiler_params=params(32),
        cost_estimate=LITTLE,
        name="last_cross",
    )(own, other, right, left, direct, carried)


def final_kernel(slots, mine, theirs, count, out):
    rank = lax.axis_index("rb")
    lane = lax.broadcasted_iota(jnp.int32, (1, LANES), 1)

    def totals(ref):
        rows = jnp.concatenate([jnp.sum(ref[n], axis=0, keepdims=True) for n in range(ref.shape[0])], axis=0)
        sums = jnp.broadcast_to(jnp.sum(rows, axis=1, keepdims=True), rows.shape)
        return [sums[n : n + 1] for n in range(ref.shape[0])]

    def put(slot, kind, re, im):
        value = jnp.where(lane == 0, re, im) * 0.25
        out[0, slot, kind : kind + 1, :] = jnp.where(slot < count[0], value, 0.0)[:, :2]

    m, t = totals(mine), totals(theirs)
    for slot in range(slots):
        m_re, m_im, t_re, t_im = m[2 * slot], m[2 * slot + 1], t[2 * slot], t[2 * slot + 1]
        put(slot, 0, m_re * t_re - m_im * t_im, m_re * t_im + m_im * t_re)
        here = rank == slot
        put(slot, 1, jnp.where(here, m[2 * slots], t[2 * slots]), jnp.where(here, m[2 * slots + 1], t[2 * slots + 1]))


def final(mine, theirs, diag_count, slots):
    return pl.pallas_call(
        functools.partial(final_kernel, slots),
        out_shape=jax.ShapeDtypeStruct((1, slots, 2, 2), F32),
        in_specs=[VMEM, VMEM, SMEM],
        out_specs=VMEM,
        compiler_params=params(32),
        name="final",
    )(mine, theirs, diag_count)


def shards(peram, src_elems, owner_times, diag_mom, diag_count):
    tp_count, rb_count = lax.axis_size("tp"), lax.axis_size("rb")
    eig = src_elems.shape[-1]
    spins = tp_count * peram.shape[0] // eig
    slots = diag_mom.shape[1]

    head, tail, late, own = travel_order(tp_count, rb_count)
    early_keys = head + tail
    picked = pick(owner_times, peram, head, "pick_head", [jax.ShapeDtypeStruct((4, *peram.shape), BF16)])
    picked.update(pick(owner_times, peram, tail + late + own, "pick_tail", []))

    def send(key):
        far, side = key
        swapped = tp_count // 4 if far >= tp_count // 2 else 0
        pairs = [
            (tp * rb_count + rb, (tp ^ far ^ (swapped if tp < tp_count // 2 else 0)) * rb_count + (rb ^ side))
            for tp in range(tp_count)
            for rb in range(rb_count)
        ]
        return lax.ppermute(picked[key], ("tp", "rb"), pairs)

    swap = [(rb, rb ^ 1) for rb in range(rb_count)]
    right, left, own_elems = factors(diag_mom, src_elems)
    arrived = [send(key) for key in early_keys] + [picked[key] for key in own]
    flat, early, direct = early_gram(early_keys + own, arrived, own_elems, spins, eig, rb_count)
    early_both = lax.all_to_all(jnp.stack([early] * rb_count), "rb", 0, 0)
    offs = early.shape[0] - (spins - 1)
    begun = cross_traces(offs, early, early_both, right, left, [], "early_cross")

    halves = [[key for key in late if key[1] == side] for side in range(rb_count)]
    sent = [[send(key) for key in keys] for keys in halves]
    half = late_begin(halves[0], flat, begun, sent[0], spins, eig, rb_count)
    blocks, last = late_rows(halves[1], flat, half, sent[1], spins, eig, rb_count)
    swapped = lax.ppermute(blocks, "rb", swap)
    rest, traces = late_rest(1, flat, half, last, own_elems, direct, spins, eig, rb_count)
    rest_swapped = lax.ppermute(rest, "rb", swap)
    products, partners = own_products(blocks, right, left)
    partial = joined_traces(swapped, right, left, products, partners, begun)
    mine = last_cross(rest.shape[0] - 1, rest, rest_swapped, right, left, traces, partial)
    theirs = lax.ppermute(mine, "rb", swap)
    return final(mine, theirs, diag_count, slots)


def solution(mesh):
    in_specs = (
        P(("grp", "tp"), None, None, "rb"),
        P("grp", None, None, None),
        P("grp", None),
        P(("grp", "tp"), None, None),
        P(("grp", "tp")),
    )
    out_specs = P(("grp", "tp"), None, None, None)
    return jax.shard_map(shards, mesh=mesh, in_specs=in_specs, out_specs=out_specs, check_vma=False)
```

```python
import functools

import jax
import jax.numpy as jnp
from jax import lax
from jax.experimental import pallas as pl
from jax.experimental.pallas import tpu as pltpu
from jax.sharding import PartitionSpec as P

F32 = jnp.float32
BF16 = jnp.bfloat16
ANY = pl.BlockSpec(memory_space=pl.ANY)
SMEM = pl.BlockSpec(memory_space=pltpu.SMEM)
VMEM = pl.BlockSpec(memory_space=pltpu.VMEM)
SUBLANES = 8
LANES = 128
STEP = 16
MIB = 1 << 20
LITTLE = pl.CostEstimate(flops=1000, bytes_accessed=1000, transcendentals=0)
LONG = pl.CostEstimate(flops=5 * 10**10, bytes_accessed=1000, transcendentals=0)


def in_hbm(array):
    return pltpu.with_memory_space_constraint(array, pltpu.HBM)


def params(mib):
    return pltpu.CompilerParams(vmem_limit_bytes=mib * MIB)


def dot(left, right):
    return jnp.dot(left, right, preferred_element_type=F32)


def dot_nt(left, right):
    return lax.dot_general(left, right, (((1,), (1,)), ((), ())), preferred_element_type=F32)


def choose(index, values):
    out = jnp.int32(values[0])
    for n in range(1, len(values)):
        out = jnp.where(index == n, jnp.int32(values[n]), out)
    return out


def aligned(start, size):
    return pl.ds(pl.multiple_of(start, size), size)


def travel_order(tp_count, rb_count):
    half, quarter = tp_count // 2, tp_count // 4

    def both(distances):
        return [(far, side) for far in distances for side in range(rb_count)]

    long, late = both(range(half, half + quarter)), both(range(half + quarter, tp_count))
    near, rest = both(reversed(range(quarter, half))), both(range(1, quarter))
    own, other = (0, 0), [(0, side) for side in range(1, rb_count)]
    step, part = len(long) // 4, len(rest) // 2
    head = long[: 2 * step] + near[: 2 * step] + long[2 * step : 3 * step]
    tail = rest[:part] + other + long[3 * step :] + near[2 * step : 3 * step] + rest[part:] + near[3 * step :]
    return head, tail, late, [own]


def distance(far, tp_rank, tp_count):
    if far < tp_count // 2:
        return far
    return lax.bitwise_xor(jnp.int32(far), jnp.where(tp_rank < tp_count // 2, jnp.int32(tp_count // 4), jnp.int32(0)))


def pick_kernel(keys, times, table, *refs):
    outs, (held, wide, taken_times, sem, times_sem) = refs[:-5], refs[-5:]
    tp_rank, rb_rank = lax.axis_index("tp"), lax.axis_index("rb")
    rows, _, packed, _ = table.shape

    def fetch(chunk):
        where = aligned(chunk * STEP, STEP)
        return pltpu.make_async_copy(table.at[where], held.at[where], sem.at[chunk])

    copy = pltpu.make_async_copy(times, taken_times, times_sem)
    copy.start()
    for chunk in range(rows // STEP):
        fetch(chunk).start()
    copy.wait()

    def step(chunk, carry):
        fetch(chunk).wait()
        where = aligned(chunk * STEP, STEP)
        for n, (far, side) in enumerate(keys):
            owner = lax.bitwise_xor(tp_rank, distance(far, tp_rank, taken_times.shape[1]))
            time = taken_times[lax.bitwise_xor(rb_rank, side), owner]
            slot = n % wide.shape[0]
            wide[slot] = held[where, time].astype(F32).reshape(STEP * packed, LANES)
            for tile in range(packed // 2):
                for part in range(2):
                    taken = wide[slot, pl.ds(2 * tile + part, STEP, stride=packed), :]
                    outs[n][part, where, tile * LANES : (tile + 1) * LANES] = taken.astype(BF16)
        return carry

    lax.fori_loop(0, rows // STEP, step, 0)


def pick(owner_times, peram, keys, name, spare):
    rows, times, parts, width = peram.shape
    tiles = width // LANES
    table = peram.reshape(rows, times, parts, tiles, LANES).swapaxes(2, 3)
    table = table.reshape(rows, times, tiles * parts, LANES)
    picked = pl.pallas_call(
        functools.partial(pick_kernel, keys),
        out_shape=[jax.ShapeDtypeStruct((parts, rows, width), BF16)] * len(keys) + spare,
        in_specs=[ANY, ANY],
        out_specs=[VMEM] * len(keys) + [ANY] * len(spare),
        scratch_shapes=[
            pltpu.VMEM(table.shape, BF16),
            pltpu.VMEM((4, STEP * tiles * parts, LANES), F32),
            pltpu.SMEM(owner_times.shape[::-1], jnp.int32),
            pltpu.SemaphoreType.DMA((rows // STEP,)),
            pltpu.SemaphoreType.DMA,
        ],
        compiler_params=params(32),
        cost_estimate=LITTLE,
        name=name,
    )(in_hbm(owner_times.T), in_hbm(table))
    return dict(zip(keys, picked))


def place(far, per_spin):
    low = lax.axis_index("tp") % per_spin
    return (far // per_spin) * per_spin + lax.bitwise_xor(jnp.int32(far % per_spin), low)


def gram_block(left, right):
    depth = left.shape[1] // 2
    real = dot_nt(left, right)
    imag = dot_nt(left[:, :depth], right[:, depth:]) - dot_nt(left[:, depth:], right[:, :depth])
    return real.astype(BF16), imag.astype(BF16)


def fold(values):
    rows, columns = values.shape
    folded = jnp.sum(values.reshape(rows // SUBLANES, SUBLANES, columns), axis=0)
    return functools.reduce(jnp.add, [folded[:, n : n + LANES] for n in range(0, columns, LANES)])


def direct_sums(diagonal, own, out, carried=None):
    real = functools.reduce(jnp.add, [block[0].astype(F32) for block in diagonal])
    imag = functools.reduce(jnp.add, [block[1].astype(F32) for block in diagonal])
    for slot in range(own.shape[0]):
        elem_re, elem_im = own[slot, 0].astype(F32), own[slot, 1].astype(F32)
        sums = [fold(elem_re * real + elem_im * imag), fold(elem_im * real - elem_re * imag)]
        for part in range(2):
            n = 2 * slot + part
            out[n] = sums[part] if carried is None else sums[part] + carried[n]


def sums_shape(count):
    return jax.ShapeDtypeStruct((count, SUBLANES, LANES), F32)


def early_blocks(spins):
    off = [(s, t) for s in range(spins - 1) for t in range(s + 1, spins - 1)]
    return off + [(s, s) for s in range(spins - 1)]


def early_kernel(eig, keys, rb_count, blocks, *refs):
    pieces, (own, flat, out, traces, sem) = refs[:-5], refs[-5:]
    rows, width = pieces[0].shape[1:]
    depth = rb_count * width
    copies = []
    for n, ((far, side), piece) in enumerate(zip(keys, pieces)):
        where = aligned(place(far, eig // rows) * rows, rows)
        for part in range(2):
            columns = pl.ds(part * depth + side * width, width)
            copies.append(pltpu.make_async_copy(piece.at[part], flat.at[where, columns], sem.at[2 * n + part]))
    for copy in copies:
        copy.start()
    for copy in copies:
        copy.wait()

    def step(n, carry):
        top, side = choose(n, [b[0] for b in blocks]), choose(n, [b[1] for b in blocks])
        out[n, 0], out[n, 1] = gram_block(flat[aligned(top * eig, eig), :], flat[aligned(side * eig, eig), :])
        return carry

    lax.fori_loop(0, len(blocks), step, 0)
    diagonal = [out.at[n] for n, block in enumerate(blocks) if block[0] == block[1]]
    direct_sums(diagonal, own, traces)


def early_gram(keys, pieces, own_elems, spins, eig, rb_count):
    blocks = early_blocks(spins)
    depth = 2 * rb_count * pieces[0].shape[2]
    return pl.pallas_call(
        functools.partial(early_kernel, eig, keys, rb_count, blocks),
        out_shape=(
            jax.ShapeDtypeStruct(((spins - 1) * eig, depth), BF16),
            jax.ShapeDtypeStruct((len(blocks), 2, eig, eig), BF16),
            sums_shape(2 * own_elems.shape[0]),
        ),
        in_specs=[ANY] * len(pieces) + [VMEM],
        out_specs=(VMEM, VMEM, VMEM),
        scratch_shapes=[pltpu.SemaphoreType.DMA((2 * len(pieces),))],
        compiler_params=params(32),
        cost_estimate=LONG,
        name="early_gram",
    )(*pieces, own_elems)


def side_columns(ref, rows, side, width, rb_count):
    return [ref[rows, (part * rb_count + side) * width : (part * rb_count + side + 1) * width] for part in range(2)]


def half_products(left, right):
    real = dot_nt(left[0], right[0]) + dot_nt(left[1], right[1])
    imag = dot_nt(left[0], right[1]) - dot_nt(left[1], right[0])
    return real, imag


def gather_last(eig, keys, others, pieces, last):
    rows, width = pieces[0].shape[1:]
    for (far, _), piece in zip(keys, pieces):
        where = aligned((place(far, eig // rows) - others * (eig // rows)) * rows, rows)
        for part in range(2):
            last[where, part * width : (part + 1) * width] = piece[part]


def late_begin_kernel(eig, keys, rb_count, flat, begun, *refs):
    pieces, (out, last) = refs[:-2], refs[-2:]
    side, width, others = keys[0][1], pieces[0].shape[2], flat.shape[0] // eig
    gather_last(eig, keys, others, pieces, last)
    right = [last[:, :width], last[:, width:]]
    for n in range(others):
        left = side_columns(flat, slice(n * eig, (n + 1) * eig), side, width, rb_count)
        out[n, 0], out[n, 1] = half_products(left, right)
    out[others, 0], out[others, 1] = half_products(right, right)


def late_begin(keys, flat, begun, pieces, spins, eig, rb_count):
    return pl.pallas_call(
        functools.partial(late_begin_kernel, eig, keys, rb_count),
        out_shape=jax.ShapeDtypeStruct((spins, 2, eig, eig), F32),
        in_specs=[VMEM, ANY] + [VMEM] * len(pieces),
        out_specs=VMEM,
        scratch_shapes=[pltpu.VMEM((eig, 2 * pieces[0].shape[2]), BF16)],
        compiler_params=params(32),
        cost_estimate=LITTLE,
        name="late_begin",
    )(flat, begun, *pieces)


def late_rows_kernel(eig, keys, rb_count, flat, partial, *refs):
    pieces, (out, last) = refs[:-2], refs[-2:]
    side, width = keys[0][1], pieces[0].shape[2]
    gather_last(eig, keys, flat.shape[0] // eig, pieces, last)
    right = [last[:, :width], last[:, width:]]
    for n in range(out.shape[0]):
        left = side_columns(flat, slice(n * eig, (n + 1) * eig), side, width, rb_count)
        real, imag = half_products(left, right)
        out[n, 0], out[n, 1] = (partial[n, 0] + real).astype(BF16), (partial[n, 1] + imag).astype(BF16)


def late_rest_kernel(eig, side, rb_count, flat, partial, last, own, carried, out, traces):
    count, width = out.shape[0] - 1, last.shape[1] // 2
    others = flat.shape[0] // eig
    right = [last[:, :width], last[:, width:]]
    for n in range(count + 1):
        spin = others - count + n
        left = right
        if n < count:
            left = side_columns(flat, slice(spin * eig, (spin + 1) * eig), side, width, rb_count)
        real, imag = half_products(left, right)
        out[n, 0], out[n, 1] = (partial[spin, 0] + real).astype(BF16), (partial[spin, 1] + imag).astype(BF16)
    direct_sums([out.at[count]], own, traces, carried)


def late_rows(keys, flat, partial, pieces, spins, eig, rb_count):
    return pl.pallas_call(
        functools.partial(late_rows_kernel, eig, keys, rb_count),
        out_shape=(
            jax.ShapeDtypeStruct((spins // 2, 2, eig, eig), BF16),
            jax.ShapeDtypeStruct((eig, 2 * pieces[0].shape[2]), BF16),
        ),
        in_specs=[VMEM] * (2 + len(pieces)),
        out_specs=(VMEM, VMEM),
        compiler_params=params(32),
        cost_estimate=LONG,
        name="late_rows",
    )(flat, partial, *pieces)


def late_rest(side, flat, partial, last, own, carried, spins, eig, rb_count):
    return pl.pallas_call(
        functools.partial(late_rest_kernel, eig, side, rb_count),
        out_shape=(
            jax.ShapeDtypeStruct((spins - spins // 2, 2, eig, eig), BF16),
            sums_shape(carried.shape[0]),
        ),
        in_specs=[VMEM] * 5,
        out_specs=(VMEM, VMEM),
        compiler_params=params(32),
        cost_estimate=LITTLE,
        name="late_rest",
    )(flat, partial, last, own, carried)


def factors_kernel(diag_mom, elems, right_ref, left_ref, own_ref, held, sem):
    rank = lax.axis_index("rb")
    eig = held.shape[-1]
    copies = []
    for time in range(2):
        which = diag_mom[0, rank, lax.bitwise_xor(rank, time)]
        copies.append(pltpu.make_async_copy(elems.at[which], held.at[time], sem.at[time]))
    for slot in range(own_ref.shape[0]):
        copies.append(pltpu.make_async_copy(elems.at[diag_mom[0, slot, rank]], own_ref.at[slot], sem.at[2 + slot]))
    for copy in copies:
        copy.start()
    for copy in copies:
        copy.wait()
    for time in range(2):
        re, im = held[time, 0], held[time, 1]
        right_ref[time, :eig, :eig] = re
        right_ref[time, :eig, eig:] = im
        right_ref[time, eig:, :eig] = -im
        right_ref[time, eig:, eig:] = re
        re_t = re.astype(F32).T.astype(BF16)
        im_t = im.astype(F32).T.astype(BF16)
        left_ref[time, :eig, :eig] = re_t
        left_ref[time, :eig, eig:] = im_t
        left_ref[time, eig:, :eig] = im_t
        left_ref[time, eig:, eig:] = -re_t


def factors(diag_mom, src_elems):
    slots, eig = diag_mom.shape[1], src_elems.shape[-1]
    form = jax.ShapeDtypeStruct((2, 2 * eig, 2 * eig), BF16)
    return pl.pallas_call(
        factors_kernel,
        out_shape=(form, form, jax.ShapeDtypeStruct((slots, 2, eig, eig), BF16)),
        in_specs=[SMEM, ANY],
        out_specs=(VMEM, VMEM, VMEM),
        scratch_shapes=[pltpu.VMEM((2, 2, eig, eig), BF16), pltpu.SemaphoreType.DMA((2 + slots,))],
        compiler_params=params(32),
        cost_estimate=LITTLE,
        name="factors",
    )(diag_mom, src_elems)


def right_products(x, count, from_right):
    rows = [jnp.concatenate([x[n, 0], x[n, 1]], axis=1) for n in range(count)]
    return dot(jnp.concatenate(rows, axis=0), from_right)


def left_product(y, n, from_left):
    eig = y.shape[-1]
    return dot(from_left, y[n].reshape(2 * eig, eig))


def paired(product, partner):
    eig = partner.shape[1]
    p_re, p_im = product[:, :eig], product[:, eig:]
    w_re, w_im = partner[:eig], partner[eig:]
    return fold(p_re * w_re - p_im * w_im), fold(p_re * w_im + p_im * w_re)


def own_products_kernel(own, right, left, products, partners):
    count = own.shape[0]
    products[...] = right_products(own, count, right[0])
    for n in range(count):
        partners[n] = left_product(own, n, left[0])


def own_products(own, right, left):
    count, eig = own.shape[0], own.shape[-1]
    return pl.pallas_call(
        own_products_kernel,
        out_shape=(
            jax.ShapeDtypeStruct((count * eig, 2 * eig), F32),
            jax.ShapeDtypeStruct((count, 2 * eig, eig), F32),
        ),
        in_specs=[VMEM] * 3,
        out_specs=(VMEM, VMEM),
        compiler_params=params(32),
        cost_estimate=LITTLE,
        name="own_products",
    )(own, right, left)


def joined_kernel(other, right, left, products, partners, carried, out):
    count, eig = other.shape[0], other.shape[-1]
    theirs = right_products(other, count, right[1])
    real, imag = [carried[0]], [carried[1]]
    for n in range(count):
        rows = slice(n * eig, (n + 1) * eig)
        sums = [paired(theirs[rows], partners[n]), paired(products[rows, :], left_product(other, n, left[1]))]
        real += [pair[0] for pair in sums]
        imag += [pair[1] for pair in sums]
    out[0] = functools.reduce(jnp.add, real)
    out[1] = functools.reduce(jnp.add, imag)


def joined_traces(other, right, left, products, partners, carried):
    return pl.pallas_call(
        joined_kernel,
        out_shape=sums_shape(2),
        in_specs=[VMEM] * 6,
        out_specs=VMEM,
        compiler_params=params(32),
        cost_estimate=LITTLE,
        name="late_cross",
    )(other, right, left, products, partners, carried)


def cross_kernel(offs, own, other, right, left, *refs):
    carried, out = refs[:-1], refs[-1]
    eig = own.shape[-1]
    if len(other.shape) > len(own.shape):
        other = other.at[1 - lax.axis_index("rb")]
    real, imag = [], []

    def add(x, y, count, from_right, from_left):
        product = right_products(x, count, from_right)
        for n in range(count):
            pair = paired(product[n * eig : (n + 1) * eig], left_product(y, n, from_left))
            real.append(pair[0])
            imag.append(pair[1])

    add(other, own, own.shape[0], right[1], left[0])
    add(own, other, offs, right[0], left[1])
    out[0] = functools.reduce(jnp.add, real + [ref[0] for ref in carried])
    out[1] = functools.reduce(jnp.add, imag + [ref[1] for ref in carried])


def cross_traces(offs, own, other, right, left, carried, name):
    return pl.pallas_call(
        functools.partial(cross_kernel, offs),
        out_shape=sums_shape(2),
        in_specs=[VMEM] * (4 + len(carried)),
        out_specs=VMEM,
        compiler_params=params(32),
        cost_estimate=LITTLE,
        name=name,
    )(own, other, right, left, *carried)


def last_cross_kernel(offs, own, other, right, left, direct, carried, out):
    count = direct.shape[0]
    for n in range(count):
        out[n] = direct[n]
    cross_kernel(offs, own, other, right, left, carried, out.at[pl.ds(count, 2)])


def last_cross(offs, own, other, right, left, direct, carried):
    return pl.pallas_call(
        functools.partial(last_cross_kernel, offs),
        out_shape=sums_shape(direct.shape[0] + 2),
        in_specs=[VMEM] * 6,
        out_specs=VMEM,
        compiler_params=params(32),
        cost_estimate=LITTLE,
        name="last_cross",
    )(own, other, right, left, direct, carried)


def final_kernel(slots, mine, theirs, count, out):
    rank = lax.axis_index("rb")
    lane = lax.broadcasted_iota(jnp.int32, (1, LANES), 1)

    def totals(ref):
        rows = jnp.concatenate([jnp.sum(ref[n], axis=0, keepdims=True) for n in range(ref.shape[0])], axis=0)
        sums = jnp.broadcast_to(jnp.sum(rows, axis=1, keepdims=True), rows.shape)
        return [sums[n : n + 1] for n in range(ref.shape[0])]

    def put(slot, kind, re, im):
        value = jnp.where(lane == 0, re, im) * 0.25
        out[0, slot, kind : kind + 1, :] = jnp.where(slot < count[0], value, 0.0)[:, :2]

    m, t = totals(mine), totals(theirs)
    for slot in range(slots):
        m_re, m_im, t_re, t_im = m[2 * slot], m[2 * slot + 1], t[2 * slot], t[2 * slot + 1]
        put(slot, 0, m_re * t_re - m_im * t_im, m_re * t_im + m_im * t_re)
        here = rank == slot
        put(slot, 1, jnp.where(here, m[2 * slots], t[2 * slots]), jnp.where(here, m[2 * slots + 1], t[2 * slots + 1]))


def final(mine, theirs, diag_count, slots):
    return pl.pallas_call(
        functools.partial(final_kernel, slots),
        out_shape=jax.ShapeDtypeStruct((1, slots, 2, 2), F32),
        in_specs=[VMEM, VMEM, SMEM],
        out_specs=VMEM,
        compiler_params=params(32),
        name="final",
    )(mine, theirs, diag_count)


def shards(peram, src_elems, owner_times, diag_mom, diag_count):
    tp_count, rb_count = lax.axis_size("tp"), lax.axis_size("rb")
    eig = src_elems.shape[-1]
    spins = tp_count * peram.shape[0] // eig
    slots = diag_mom.shape[1]

    head, tail, late, own = travel_order(tp_count, rb_count)
    early_keys = head + tail
    picked = pick(owner_times, peram, head, "pick_head", [jax.ShapeDtypeStruct((4, *peram.shape), BF16)])
    picked.update(pick(owner_times, peram, tail + late + own, "pick_tail", []))

    def send(key):
        far, side = key
        swapped = tp_count // 4 if far >= tp_count // 2 else 0
        pairs = [
            (tp * rb_count + rb, (tp ^ far ^ (swapped if tp < tp_count // 2 else 0)) * rb_count + (rb ^ side))
            for tp in range(tp_count)
            for rb in range(rb_count)
        ]
        return lax.ppermute(picked[key], ("tp", "rb"), pairs)

    swap = [(rb, rb ^ 1) for rb in range(rb_count)]
    right, left, own_elems = factors(diag_mom, src_elems)
    arrived = [send(key) for key in early_keys] + [picked[key] for key in own]
    flat, early, direct = early_gram(early_keys + own, arrived, own_elems, spins, eig, rb_count)
    early_both = lax.all_to_all(jnp.stack([early] * rb_count), "rb", 0, 0)
    offs = early.shape[0] - (spins - 1)
    begun = cross_traces(offs, early, early_both, right, left, [], "early_cross")

    halves = [[key for key in late if key[1] == side] for side in range(rb_count)]
    sent = [[send(key) for key in keys] for keys in halves]
    half = late_begin(halves[0], flat, begun, sent[0], spins, eig, rb_count)
    blocks, last = late_rows(halves[1], flat, half, sent[1], spins, eig, rb_count)
    swapped = lax.ppermute(blocks, "rb", swap)
    rest, traces = late_rest(1, flat, half, last, own_elems, direct, spins, eig, rb_count)
    rest_swapped = lax.ppermute(rest, "rb", swap)
    products, partners = own_products(blocks, right, left)
    partial = joined_traces(swapped, right, left, products, partners, begun)
    mine = last_cross(rest.shape[0] - 1, rest, rest_swapped, right, left, traces, partial)
    theirs = lax.ppermute(mine, "rb", swap)
    return final(mine, theirs, diag_count, slots)


def solution(mesh):
    in_specs = (
        P(("grp", "tp"), None, None, "rb"),
        P("grp", None, None, None),
        P("grp", None),
        P(("grp", "tp"), None, None),
        P(("grp", "tp")),
    )
    out_specs = P(("grp", "tp"), None, None, None)
    return jax.shard_map(shards, mesh=mesh, in_specs=in_specs, out_specs=out_specs, check_vma=False)
```

```python
import functools

import jax
import jax.numpy as jnp
from jax import lax
from jax.experimental import pallas as pl
from jax.experimental.pallas import tpu as pltpu
from jax.sharding import PartitionSpec as P

F32 = jnp.float32
BF16 = jnp.bfloat16
ANY = pl.BlockSpec(memory_space=pl.ANY)
SMEM = pl.BlockSpec(memory_space=pltpu.SMEM)
VMEM = pl.BlockSpec(memory_space=pltpu.VMEM)
SUBLANES = 8
LANES = 128
STEP = 16
MIB = 1 << 20
LITTLE = pl.CostEstimate(flops=1000, bytes_accessed=1000, transcendentals=0)
LONG = pl.CostEstimate(flops=5 * 10**10, bytes_accessed=1000, transcendentals=0)


def in_hbm(array):
    return pltpu.with_memory_space_constraint(array, pltpu.HBM)


def params(mib):
    return pltpu.CompilerParams(vmem_limit_bytes=mib * MIB)


def dot(left, right):
    return jnp.dot(left, right, preferred_element_type=F32)


def dot_nt(left, right):
    return lax.dot_general(left, right, (((1,), (1,)), ((), ())), preferred_element_type=F32)


def choose(index, values):
    out = jnp.int32(values[0])
    for n in range(1, len(values)):
        out = jnp.where(index == n, jnp.int32(values[n]), out)
    return out


def aligned(start, size):
    return pl.ds(pl.multiple_of(start, size), size)


def travel_order(tp_count, rb_count):
    half, quarter = tp_count // 2, tp_count // 4

    def both(distances):
        return [(far, side) for far in distances for side in range(rb_count)]

    long, late = both(range(half, half + quarter)), both(range(half + quarter, tp_count))
    near, rest = both(range(quarter, half)), both(range(1, quarter))
    own, other = (0, 0), [(0, side) for side in range(1, rb_count)]
    step, part = len(long) // 4, len(rest) // 2
    head = long[: 2 * step] + near[: 2 * step] + long[2 * step : 3 * step]
    tail = rest[:part] + other + near[2 * step : 3 * step] + long[3 * step :] + rest[part:] + near[3 * step :]
    return head, tail, late, [own]


def distance(far, tp_rank, tp_count):
    if far < tp_count // 2:
        return far
    return lax.bitwise_xor(jnp.int32(far), jnp.where(tp_rank < tp_count // 2, jnp.int32(tp_count // 4), jnp.int32(0)))


def pick_kernel(keys, times, table, *refs):
    outs, (held, wide, taken_times, sem, times_sem) = refs[:-5], refs[-5:]
    tp_rank, rb_rank = lax.axis_index("tp"), lax.axis_index("rb")
    rows, _, packed, _ = table.shape

    def fetch(chunk):
        where = aligned(chunk * STEP, STEP)
        return pltpu.make_async_copy(table.at[where], held.at[where], sem.at[chunk])

    copy = pltpu.make_async_copy(times, taken_times, times_sem)
    copy.start()
    for chunk in range(rows // STEP):
        fetch(chunk).start()
    copy.wait()

    def step(chunk, carry):
        fetch(chunk).wait()
        where = aligned(chunk * STEP, STEP)
        for n, (far, side) in enumerate(keys):
            owner = lax.bitwise_xor(tp_rank, distance(far, tp_rank, taken_times.shape[1]))
            time = taken_times[lax.bitwise_xor(rb_rank, side), owner]
            slot = n % wide.shape[0]
            wide[slot] = held[where, time].astype(F32).reshape(STEP * packed, LANES)
            for tile in range(packed // 2):
                for part in range(2):
                    taken = wide[slot, pl.ds(2 * tile + part, STEP, stride=packed), :]
                    outs[n][part, where, tile * LANES : (tile + 1) * LANES] = taken.astype(BF16)
        return carry

    lax.fori_loop(0, rows // STEP, step, 0)


def pick(owner_times, peram, keys, name, spare):
    rows, times, parts, width = peram.shape
    tiles = width // LANES
    table = peram.reshape(rows, times, parts, tiles, LANES).swapaxes(2, 3)
    table = table.reshape(rows, times, tiles * parts, LANES)
    picked = pl.pallas_call(
        functools.partial(pick_kernel, keys),
        out_shape=[jax.ShapeDtypeStruct((parts, rows, width), BF16)] * len(keys) + spare,
        in_specs=[ANY, ANY],
        out_specs=[VMEM] * len(keys) + [ANY] * len(spare),
        scratch_shapes=[
            pltpu.VMEM(table.shape, BF16),
            pltpu.VMEM((4, STEP * tiles * parts, LANES), F32),
            pltpu.SMEM(owner_times.shape[::-1], jnp.int32),
            pltpu.SemaphoreType.DMA((rows // STEP,)),
            pltpu.SemaphoreType.DMA,
        ],
        compiler_params=params(32),
        cost_estimate=LITTLE,
        name=name,
    )(in_hbm(owner_times.T), in_hbm(table))
    return dict(zip(keys, picked))


def place(far, per_spin):
    low = lax.axis_index("tp") % per_spin
    return (far // per_spin) * per_spin + lax.bitwise_xor(jnp.int32(far % per_spin), low)


def gram_block(left, right):
    depth = left.shape[1] // 2
    real = dot_nt(left, right)
    imag = dot_nt(left[:, :depth], right[:, depth:]) - dot_nt(left[:, depth:], right[:, :depth])
    return real.astype(BF16), imag.astype(BF16)


def fold(values):
    rows, columns = values.shape
    folded = jnp.sum(values.reshape(rows // SUBLANES, SUBLANES, columns), axis=0)
    return functools.reduce(jnp.add, [folded[:, n : n + LANES] for n in range(0, columns, LANES)])


def direct_sums(diagonal, own, out, carried=None):
    real = functools.reduce(jnp.add, [block[0].astype(F32) for block in diagonal])
    imag = functools.reduce(jnp.add, [block[1].astype(F32) for block in diagonal])
    for slot in range(own.shape[0]):
        elem_re, elem_im = own[slot, 0].astype(F32), own[slot, 1].astype(F32)
        sums = [fold(elem_re * real + elem_im * imag), fold(elem_im * real - elem_re * imag)]
        for part in range(2):
            n = 2 * slot + part
            out[n] = sums[part] if carried is None else sums[part] + carried[n]


def sums_shape(count):
    return jax.ShapeDtypeStruct((count, SUBLANES, LANES), F32)


def early_blocks(spins):
    off = [(s, t) for s in range(spins - 1) for t in range(s + 1, spins - 1)]
    return off + [(s, s) for s in range(spins - 1)]


def early_kernel(eig, keys, rb_count, blocks, *refs):
    pieces, (own, flat, out, traces, sem) = refs[:-5], refs[-5:]
    rows, width = pieces[0].shape[1:]
    depth = rb_count * width
    copies = []
    for n, ((far, side), piece) in enumerate(zip(keys, pieces)):
        where = aligned(place(far, eig // rows) * rows, rows)
        for part in range(2):
            columns = pl.ds(part * depth + side * width, width)
            copies.append(pltpu.make_async_copy(piece.at[part], flat.at[where, columns], sem.at[2 * n + part]))
    for copy in copies:
        copy.start()
    for copy in copies:
        copy.wait()

    def step(n, carry):
        top, side = choose(n, [b[0] for b in blocks]), choose(n, [b[1] for b in blocks])
        out[n, 0], out[n, 1] = gram_block(flat[aligned(top * eig, eig), :], flat[aligned(side * eig, eig), :])
        return carry

    lax.fori_loop(0, len(blocks), step, 0)
    diagonal = [out.at[n] for n, block in enumerate(blocks) if block[0] == block[1]]
    direct_sums(diagonal, own, traces)


def early_gram(keys, pieces, own_elems, spins, eig, rb_count):
    blocks = early_blocks(spins)
    depth = 2 * rb_count * pieces[0].shape[2]
    return pl.pallas_call(
        functools.partial(early_kernel, eig, keys, rb_count, blocks),
        out_shape=(
            jax.ShapeDtypeStruct(((spins - 1) * eig, depth), BF16),
            jax.ShapeDtypeStruct((len(blocks), 2, eig, eig), BF16),
            sums_shape(2 * own_elems.shape[0]),
        ),
        in_specs=[ANY] * len(pieces) + [VMEM],
        out_specs=(VMEM, VMEM, VMEM),
        scratch_shapes=[pltpu.SemaphoreType.DMA((2 * len(pieces),))],
        compiler_params=params(32),
        cost_estimate=LONG,
        name="early_gram",
    )(*pieces, own_elems)


def side_columns(ref, rows, side, width, rb_count):
    return [ref[rows, (part * rb_count + side) * width : (part * rb_count + side + 1) * width] for part in range(2)]


def half_products(left, right):
    real = dot_nt(left[0], right[0]) + dot_nt(left[1], right[1])
    imag = dot_nt(left[0], right[1]) - dot_nt(left[1], right[0])
    return real, imag


def gather_last(eig, keys, others, pieces, last):
    rows, width = pieces[0].shape[1:]
    for (far, _), piece in zip(keys, pieces):
        where = aligned((place(far, eig // rows) - others * (eig // rows)) * rows, rows)
        for part in range(2):
            last[where, part * width : (part + 1) * width] = piece[part]


def late_begin_kernel(eig, keys, rb_count, flat, begun, *refs):
    pieces, (out, last) = refs[:-2], refs[-2:]
    side, width, others = keys[0][1], pieces[0].shape[2], flat.shape[0] // eig
    gather_last(eig, keys, others, pieces, last)
    right = [last[:, :width], last[:, width:]]
    for n in range(others):
        left = side_columns(flat, slice(n * eig, (n + 1) * eig), side, width, rb_count)
        out[n, 0], out[n, 1] = half_products(left, right)
    out[others, 0], out[others, 1] = half_products(right, right)


def late_begin(keys, flat, begun, pieces, spins, eig, rb_count):
    return pl.pallas_call(
        functools.partial(late_begin_kernel, eig, keys, rb_count),
        out_shape=jax.ShapeDtypeStruct((spins, 2, eig, eig), F32),
        in_specs=[VMEM, ANY] + [VMEM] * len(pieces),
        out_specs=VMEM,
        scratch_shapes=[pltpu.VMEM((eig, 2 * pieces[0].shape[2]), BF16)],
        compiler_params=params(32),
        cost_estimate=LITTLE,
        name="late_begin",
    )(flat, begun, *pieces)


def late_rows_kernel(eig, keys, rb_count, flat, partial, *refs):
    pieces, (out, last) = refs[:-2], refs[-2:]
    side, width = keys[0][1], pieces[0].shape[2]
    gather_last(eig, keys, flat.shape[0] // eig, pieces, last)
    right = [last[:, :width], last[:, width:]]
    for n in range(out.shape[0]):
        left = side_columns(flat, slice(n * eig, (n + 1) * eig), side, width, rb_count)
        real, imag = half_products(left, right)
        out[n, 0], out[n, 1] = (partial[n, 0] + real).astype(BF16), (partial[n, 1] + imag).astype(BF16)


def late_rest_kernel(eig, side, rb_count, flat, partial, last, own, carried, out, traces):
    count, width = out.shape[0] - 1, last.shape[1] // 2
    others = flat.shape[0] // eig
    right = [last[:, :width], last[:, width:]]
    for n in range(count + 1):
        spin = others - count + n
        left = right
        if n < count:
            left = side_columns(flat, slice(spin * eig, (spin + 1) * eig), side, width, rb_count)
        real, imag = half_products(left, right)
        out[n, 0], out[n, 1] = (partial[spin, 0] + real).astype(BF16), (partial[spin, 1] + imag).astype(BF16)
    direct_sums([out.at[count]], own, traces, carried)


def late_rows(keys, flat, partial, pieces, spins, eig, rb_count):
    return pl.pallas_call(
        functools.partial(late_rows_kernel, eig, keys, rb_count),
        out_shape=(
            jax.ShapeDtypeStruct((spins // 2, 2, eig, eig), BF16),
            jax.ShapeDtypeStruct((eig, 2 * pieces[0].shape[2]), BF16),
        ),
        in_specs=[VMEM] * (2 + len(pieces)),
        out_specs=(VMEM, VMEM),
        compiler_params=params(32),
        cost_estimate=LONG,
        name="late_rows",
    )(flat, partial, *pieces)


def late_rest(side, flat, partial, last, own, carried, spins, eig, rb_count):
    return pl.pallas_call(
        functools.partial(late_rest_kernel, eig, side, rb_count),
        out_shape=(
            jax.ShapeDtypeStruct((spins - spins // 2, 2, eig, eig), BF16),
            sums_shape(carried.shape[0]),
        ),
        in_specs=[VMEM] * 5,
        out_specs=(VMEM, VMEM),
        compiler_params=params(32),
        cost_estimate=LITTLE,
        name="late_rest",
    )(flat, partial, last, own, carried)


def factors_kernel(diag_mom, elems, right_ref, left_ref, own_ref, held, sem):
    rank = lax.axis_index("rb")
    eig = held.shape[-1]
    copies = []
    for time in range(2):
        which = diag_mom[0, rank, lax.bitwise_xor(rank, time)]
        copies.append(pltpu.make_async_copy(elems.at[which], held.at[time], sem.at[time]))
    for slot in range(own_ref.shape[0]):
        copies.append(pltpu.make_async_copy(elems.at[diag_mom[0, slot, rank]], own_ref.at[slot], sem.at[2 + slot]))
    for copy in copies:
        copy.start()
    for copy in copies:
        copy.wait()
    for time in range(2):
        re, im = held[time, 0], held[time, 1]
        right_ref[time, :eig, :eig] = re
        right_ref[time, :eig, eig:] = im
        right_ref[time, eig:, :eig] = -im
        right_ref[time, eig:, eig:] = re
        re_t = re.astype(F32).T.astype(BF16)
        im_t = im.astype(F32).T.astype(BF16)
        left_ref[time, :eig, :eig] = re_t
        left_ref[time, :eig, eig:] = im_t
        left_ref[time, eig:, :eig] = im_t
        left_ref[time, eig:, eig:] = -re_t


def factors(diag_mom, src_elems):
    slots, eig = diag_mom.shape[1], src_elems.shape[-1]
    form = jax.ShapeDtypeStruct((2, 2 * eig, 2 * eig), BF16)
    return pl.pallas_call(
        factors_kernel,
        out_shape=(form, form, jax.ShapeDtypeStruct((slots, 2, eig, eig), BF16)),
        in_specs=[SMEM, ANY],
        out_specs=(VMEM, VMEM, VMEM),
        scratch_shapes=[pltpu.VMEM((2, 2, eig, eig), BF16), pltpu.SemaphoreType.DMA((2 + slots,))],
        compiler_params=params(32),
        cost_estimate=LITTLE,
        name="factors",
    )(diag_mom, src_elems)


def right_products(x, count, from_right):
    rows = [jnp.concatenate([x[n, 0], x[n, 1]], axis=1) for n in range(count)]
    return dot(jnp.concatenate(rows, axis=0), from_right)


def left_product(y, n, from_left):
    eig = y.shape[-1]
    return dot(from_left, y[n].reshape(2 * eig, eig))


def paired(product, partner):
    eig = partner.shape[1]
    p_re, p_im = product[:, :eig], product[:, eig:]
    w_re, w_im = partner[:eig], partner[eig:]
    return fold(p_re * w_re - p_im * w_im), fold(p_re * w_im + p_im * w_re)


def own_products_kernel(own, right, left, products, partners):
    count = own.shape[0]
    products[...] = right_products(own, count, right[0])
    for n in range(count):
        partners[n] = left_product(own, n, left[0])


def own_products(own, right, left):
    count, eig = own.shape[0], own.shape[-1]
    return pl.pallas_call(
        own_products_kernel,
        out_shape=(
            jax.ShapeDtypeStruct((count * eig, 2 * eig), F32),
            jax.ShapeDtypeStruct((count, 2 * eig, eig), F32),
        ),
        in_specs=[VMEM] * 3,
        out_specs=(VMEM, VMEM),
        compiler_params=params(32),
        cost_estimate=LITTLE,
        name="own_products",
    )(own, right, left)


def joined_kernel(other, right, left, products, partners, carried, out):
    count, eig = other.shape[0], other.shape[-1]
    theirs = right_products(other, count, right[1])
    real, imag = [carried[0]], [carried[1]]
    for n in range(count):
        rows = slice(n * eig, (n + 1) * eig)
        sums = [paired(theirs[rows], partners[n]), paired(products[rows, :], left_product(other, n, left[1]))]
        real += [pair[0] for pair in sums]
        imag += [pair[1] for pair in sums]
    out[0] = functools.reduce(jnp.add, real)
    out[1] = functools.reduce(jnp.add, imag)


def joined_traces(other, right, left, products, partners, carried):
    return pl.pallas_call(
        joined_kernel,
        out_shape=sums_shape(2),
        in_specs=[VMEM] * 6,
        out_specs=VMEM,
        compiler_params=params(32),
        cost_estimate=LITTLE,
        name="late_cross",
    )(other, right, left, products, partners, carried)


def cross_kernel(offs, own, other, right, left, *refs):
    carried, out = refs[:-1], refs[-1]
    eig = own.shape[-1]
    if len(other.shape) > len(own.shape):
        other = other.at[1 - lax.axis_index("rb")]
    real, imag = [], []

    def add(x, y, count, from_right, from_left):
        product = right_products(x, count, from_right)
        for n in range(count):
            pair = paired(product[n * eig : (n + 1) * eig], left_product(y, n, from_left))
            real.append(pair[0])
            imag.append(pair[1])

    add(other, own, own.shape[0], right[1], left[0])
    add(own, other, offs, right[0], left[1])
    out[0] = functools.reduce(jnp.add, real + [ref[0] for ref in carried])
    out[1] = functools.reduce(jnp.add, imag + [ref[1] for ref in carried])


def cross_traces(offs, own, other, right, left, carried, name):
    return pl.pallas_call(
        functools.partial(cross_kernel, offs),
        out_shape=sums_shape(2),
        in_specs=[VMEM] * (4 + len(carried)),
        out_specs=VMEM,
        compiler_params=params(32),
        cost_estimate=LITTLE,
        name=name,
    )(own, other, right, left, *carried)


def last_cross_kernel(offs, own, other, right, left, direct, carried, out):
    count = direct.shape[0]
    for n in range(count):
        out[n] = direct[n]
    cross_kernel(offs, own, other, right, left, carried, out.at[pl.ds(count, 2)])


def last_cross(offs, own, other, right, left, direct, carried):
    return pl.pallas_call(
        functools.partial(last_cross_kernel, offs),
        out_shape=sums_shape(direct.shape[0] + 2),
        in_specs=[VMEM] * 6,
        out_specs=VMEM,
        compiler_params=params(32),
        cost_estimate=LITTLE,
        name="last_cross",
    )(own, other, right, left, direct, carried)


def final_kernel(slots, mine, theirs, count, out):
    rank = lax.axis_index("rb")
    lane = lax.broadcasted_iota(jnp.int32, (1, LANES), 1)

    def totals(ref):
        rows = jnp.concatenate([jnp.sum(ref[n], axis=0, keepdims=True) for n in range(ref.shape[0])], axis=0)
        sums = jnp.broadcast_to(jnp.sum(rows, axis=1, keepdims=True), rows.shape)
        return [sums[n : n + 1] for n in range(ref.shape[0])]

    def put(slot, kind, re, im):
        value = jnp.where(lane == 0, re, im) * 0.25
        out[0, slot, kind : kind + 1, :] = jnp.where(slot < count[0], value, 0.0)[:, :2]

    m, t = totals(mine), totals(theirs)
    for slot in range(slots):
        m_re, m_im, t_re, t_im = m[2 * slot], m[2 * slot + 1], t[2 * slot], t[2 * slot + 1]
        put(slot, 0, m_re * t_re - m_im * t_im, m_re * t_im + m_im * t_re)
        here = rank == slot
        put(slot, 1, jnp.where(here, m[2 * slots], t[2 * slots]), jnp.where(here, m[2 * slots + 1], t[2 * slots + 1]))


def final(mine, theirs, diag_count, slots):
    return pl.pallas_call(
        functools.partial(final_kernel, slots),
        out_shape=jax.ShapeDtypeStruct((1, slots, 2, 2), F32),
        in_specs=[VMEM, VMEM, SMEM],
        out_specs=VMEM,
        compiler_params=params(32),
        name="final",
    )(mine, theirs, diag_count)


def shards(peram, src_elems, owner_times, diag_mom, diag_count):
    tp_count, rb_count = lax.axis_size("tp"), lax.axis_size("rb")
    eig = src_elems.shape[-1]
    spins = tp_count * peram.shape[0] // eig
    slots = diag_mom.shape[1]

    head, tail, late, own = travel_order(tp_count, rb_count)
    early_keys = head + tail
    picked = pick(owner_times, peram, head, "pick_head", [jax.ShapeDtypeStruct((4, *peram.shape), BF16)])
    picked.update(pick(owner_times, peram, tail + late + own, "pick_tail", []))

    def send(key):
        far, side = key
        swapped = tp_count // 4 if far >= tp_count // 2 else 0
        pairs = [
            (tp * rb_count + rb, (tp ^ far ^ (swapped if tp < tp_count // 2 else 0)) * rb_count + (rb ^ side))
            for tp in range(tp_count)
            for rb in range(rb_count)
        ]
        return lax.ppermute(picked[key], ("tp", "rb"), pairs)

    swap = [(rb, rb ^ 1) for rb in range(rb_count)]
    right, left, own_elems = factors(diag_mom, src_elems)
    arrived = [send(key) for key in early_keys] + [picked[key] for key in own]
    flat, early, direct = early_gram(early_keys + own, arrived, own_elems, spins, eig, rb_count)
    early_both = lax.all_to_all(jnp.stack([early] * rb_count), "rb", 0, 0)
    offs = early.shape[0] - (spins - 1)
    begun = cross_traces(offs, early, early_both, right, left, [], "early_cross")

    halves = [[key for key in late if key[1] == side] for side in range(rb_count)]
    sent = [[send(key) for key in keys] for keys in halves]
    half = late_begin(halves[0], flat, begun, sent[0], spins, eig, rb_count)
    blocks, last = late_rows(halves[1], flat, half, sent[1], spins, eig, rb_count)
    swapped = lax.ppermute(blocks, "rb", swap)
    rest, traces = late_rest(1, flat, half, last, own_elems, direct, spins, eig, rb_count)
    rest_swapped = lax.ppermute(rest, "rb", swap)
    products, partners = own_products(blocks, right, left)
    partial = joined_traces(swapped, right, left, products, partners, begun)
    mine = last_cross(rest.shape[0] - 1, rest, rest_swapped, right, left, traces, partial)
    theirs = lax.ppermute(mine, "rb", swap)
    return final(mine, theirs, diag_count, slots)


def solution(mesh):
    in_specs = (
        P(("grp", "tp"), None, None, "rb"),
        P("grp", None, None, None),
        P("grp", None),
        P(("grp", "tp"), None, None),
        P(("grp", "tp")),
    )
    out_specs = P(("grp", "tp"), None, None, None)
    return jax.shard_map(shards, mesh=mesh, in_specs=in_specs, out_specs=out_specs, check_vma=False)
```

```python
import functools

import jax
import jax.numpy as jnp
from jax import lax
from jax.experimental import pallas as pl
from jax.experimental.pallas import tpu as pltpu
from jax.sharding import PartitionSpec as P

F32 = jnp.float32
BF16 = jnp.bfloat16
ANY = pl.BlockSpec(memory_space=pl.ANY)
SMEM = pl.BlockSpec(memory_space=pltpu.SMEM)
VMEM = pl.BlockSpec(memory_space=pltpu.VMEM)
SUBLANES = 8
LANES = 128
STEP = 16
MIB = 1 << 20
LITTLE = pl.CostEstimate(flops=1000, bytes_accessed=1000, transcendentals=0)
LONG = pl.CostEstimate(flops=5 * 10**10, bytes_accessed=1000, transcendentals=0)


def in_hbm(array):
    return pltpu.with_memory_space_constraint(array, pltpu.HBM)


def params(mib):
    return pltpu.CompilerParams(vmem_limit_bytes=mib * MIB)


def dot(left, right):
    return jnp.dot(left, right, preferred_element_type=F32)


def dot_nt(left, right):
    return lax.dot_general(left, right, (((1,), (1,)), ((), ())), preferred_element_type=F32)


def choose(index, values):
    out = jnp.int32(values[0])
    for n in range(1, len(values)):
        out = jnp.where(index == n, jnp.int32(values[n]), out)
    return out


def aligned(start, size):
    return pl.ds(pl.multiple_of(start, size), size)


def travel_order(tp_count, rb_count):
    half, quarter = tp_count // 2, tp_count // 4

    def both(distances):
        return [(far, side) for far in distances for side in range(rb_count)]

    long, late = both(reversed(range(half, half + quarter))), both(range(half + quarter, tp_count))
    near, rest = both(reversed(range(quarter, half))), both(range(1, quarter))
    own, other = (0, 0), [(0, side) for side in range(1, rb_count)]
    step, part = len(long) // 4, len(rest) // 2
    head = long[: 2 * step] + near[: 2 * step] + long[2 * step : 3 * step]
    tail = rest[:part] + other + near[2 * step : 3 * step] + long[3 * step :] + rest[part:] + near[3 * step :]
    return head, tail, late, [own]


def distance(far, tp_rank, tp_count):
    if far < tp_count // 2:
        return far
    return lax.bitwise_xor(jnp.int32(far), jnp.where(tp_rank < tp_count // 2, jnp.int32(tp_count // 4), jnp.int32(0)))


def pick_kernel(keys, times, table, *refs):
    outs, (held, wide, taken_times, sem, times_sem) = refs[:-5], refs[-5:]
    tp_rank, rb_rank = lax.axis_index("tp"), lax.axis_index("rb")
    rows, _, packed, _ = table.shape

    def fetch(chunk):
        where = aligned(chunk * STEP, STEP)
        return pltpu.make_async_copy(table.at[where], held.at[where], sem.at[chunk])

    copy = pltpu.make_async_copy(times, taken_times, times_sem)
    copy.start()
    for chunk in range(rows // STEP):
        fetch(chunk).start()
    copy.wait()

    def step(chunk, carry):
        fetch(chunk).wait()
        where = aligned(chunk * STEP, STEP)
        for n, (far, side) in enumerate(keys):
            owner = lax.bitwise_xor(tp_rank, distance(far, tp_rank, taken_times.shape[1]))
            time = taken_times[lax.bitwise_xor(rb_rank, side), owner]
            slot = n % wide.shape[0]
            wide[slot] = held[where, time].astype(F32).reshape(STEP * packed, LANES)
            for tile in range(packed // 2):
                for part in range(2):
                    taken = wide[slot, pl.ds(2 * tile + part, STEP, stride=packed), :]
                    outs[n][part, where, tile * LANES : (tile + 1) * LANES] = taken.astype(BF16)
        return carry

    lax.fori_loop(0, rows // STEP, step, 0)


def pick(owner_times, peram, keys, name, spare):
    rows, times, parts, width = peram.shape
    tiles = width // LANES
    table = peram.reshape(rows, times, parts, tiles, LANES).swapaxes(2, 3)
    table = table.reshape(rows, times, tiles * parts, LANES)
    picked = pl.pallas_call(
        functools.partial(pick_kernel, keys),
        out_shape=[jax.ShapeDtypeStruct((parts, rows, width), BF16)] * len(keys) + spare,
        in_specs=[ANY, ANY],
        out_specs=[VMEM] * len(keys) + [ANY] * len(spare),
        scratch_shapes=[
            pltpu.VMEM(table.shape, BF16),
            pltpu.VMEM((4, STEP * tiles * parts, LANES), F32),
            pltpu.SMEM(owner_times.shape[::-1], jnp.int32),
            pltpu.SemaphoreType.DMA((rows // STEP,)),
            pltpu.SemaphoreType.DMA,
        ],
        compiler_params=params(32),
        cost_estimate=LITTLE,
        name=name,
    )(in_hbm(owner_times.T), in_hbm(table))
    return dict(zip(keys, picked))


def place(far, per_spin):
    low = lax.axis_index("tp") % per_spin
    return (far // per_spin) * per_spin + lax.bitwise_xor(jnp.int32(far % per_spin), low)


def gram_block(left, right):
    depth = left.shape[1] // 2
    real = dot_nt(left, right)
    imag = dot_nt(left[:, :depth], right[:, depth:]) - dot_nt(left[:, depth:], right[:, :depth])
    return real.astype(BF16), imag.astype(BF16)


def fold(values):
    rows, columns = values.shape
    folded = jnp.sum(values.reshape(rows // SUBLANES, SUBLANES, columns), axis=0)
    return functools.reduce(jnp.add, [folded[:, n : n + LANES] for n in range(0, columns, LANES)])


def direct_sums(diagonal, own, out, carried=None):
    real = functools.reduce(jnp.add, [block[0].astype(F32) for block in diagonal])
    imag = functools.reduce(jnp.add, [block[1].astype(F32) for block in diagonal])
    for slot in range(own.shape[0]):
        elem_re, elem_im = own[slot, 0].astype(F32), own[slot, 1].astype(F32)
        sums = [fold(elem_re * real + elem_im * imag), fold(elem_im * real - elem_re * imag)]
        for part in range(2):
            n = 2 * slot + part
            out[n] = sums[part] if carried is None else sums[part] + carried[n]


def sums_shape(count):
    return jax.ShapeDtypeStruct((count, SUBLANES, LANES), F32)


def early_blocks(spins):
    off = [(s, t) for s in range(spins - 1) for t in range(s + 1, spins - 1)]
    return off + [(s, s) for s in range(spins - 1)]


def early_kernel(eig, keys, rb_count, blocks, *refs):
    pieces, (own, flat, out, traces, sem) = refs[:-5], refs[-5:]
    rows, width = pieces[0].shape[1:]
    depth = rb_count * width
    copies = []
    for n, ((far, side), piece) in enumerate(zip(keys, pieces)):
        where = aligned(place(far, eig // rows) * rows, rows)
        for part in range(2):
            columns = pl.ds(part * depth + side * width, width)
            copies.append(pltpu.make_async_copy(piece.at[part], flat.at[where, columns], sem.at[2 * n + part]))
    for copy in copies:
        copy.start()
    for copy in copies:
        copy.wait()

    def step(n, carry):
        top, side = choose(n, [b[0] for b in blocks]), choose(n, [b[1] for b in blocks])
        out[n, 0], out[n, 1] = gram_block(flat[aligned(top * eig, eig), :], flat[aligned(side * eig, eig), :])
        return carry

    lax.fori_loop(0, len(blocks), step, 0)
    diagonal = [out.at[n] for n, block in enumerate(blocks) if block[0] == block[1]]
    direct_sums(diagonal, own, traces)


def early_gram(keys, pieces, own_elems, spins, eig, rb_count):
    blocks = early_blocks(spins)
    depth = 2 * rb_count * pieces[0].shape[2]
    return pl.pallas_call(
        functools.partial(early_kernel, eig, keys, rb_count, blocks),
        out_shape=(
            jax.ShapeDtypeStruct(((spins - 1) * eig, depth), BF16),
            jax.ShapeDtypeStruct((len(blocks), 2, eig, eig), BF16),
            sums_shape(2 * own_elems.shape[0]),
        ),
        in_specs=[ANY] * len(pieces) + [VMEM],
        out_specs=(VMEM, VMEM, VMEM),
        scratch_shapes=[pltpu.SemaphoreType.DMA((2 * len(pieces),))],
        compiler_params=params(32),
        cost_estimate=LONG,
        name="early_gram",
    )(*pieces, own_elems)


def side_columns(ref, rows, side, width, rb_count):
    return [ref[rows, (part * rb_count + side) * width : (part * rb_count + side + 1) * width] for part in range(2)]


def half_products(left, right):
    real = dot_nt(left[0], right[0]) + dot_nt(left[1], right[1])
    imag = dot_nt(left[0], right[1]) - dot_nt(left[1], right[0])
    return real, imag


def gather_last(eig, keys, others, pieces, last):
    rows, width = pieces[0].shape[1:]
    for (far, _), piece in zip(keys, pieces):
        where = aligned((place(far, eig // rows) - others * (eig // rows)) * rows, rows)
        for part in range(2):
            last[where, part * width : (part + 1) * width] = piece[part]


def late_begin_kernel(eig, keys, rb_count, flat, begun, *refs):
    pieces, (out, last) = refs[:-2], refs[-2:]
    side, width, others = keys[0][1], pieces[0].shape[2], flat.shape[0] // eig
    gather_last(eig, keys, others, pieces, last)
    right = [last[:, :width], last[:, width:]]
    for n in range(others):
        left = side_columns(flat, slice(n * eig, (n + 1) * eig), side, width, rb_count)
        out[n, 0], out[n, 1] = half_products(left, right)
    out[others, 0], out[others, 1] = half_products(right, right)


def late_begin(keys, flat, begun, pieces, spins, eig, rb_count):
    return pl.pallas_call(
        functools.partial(late_begin_kernel, eig, keys, rb_count),
        out_shape=jax.ShapeDtypeStruct((spins, 2, eig, eig), F32),
        in_specs=[VMEM, ANY] + [VMEM] * len(pieces),
        out_specs=VMEM,
        scratch_shapes=[pltpu.VMEM((eig, 2 * pieces[0].shape[2]), BF16)],
        compiler_params=params(32),
        cost_estimate=LITTLE,
        name="late_begin",
    )(flat, begun, *pieces)


def late_rows_kernel(eig, keys, rb_count, flat, partial, *refs):
    pieces, (out, last) = refs[:-2], refs[-2:]
    side, width = keys[0][1], pieces[0].shape[2]
    gather_last(eig, keys, flat.shape[0] // eig, pieces, last)
    right = [last[:, :width], last[:, width:]]
    for n in range(out.shape[0]):
        left = side_columns(flat, slice(n * eig, (n + 1) * eig), side, width, rb_count)
        real, imag = half_products(left, right)
        out[n, 0], out[n, 1] = (partial[n, 0] + real).astype(BF16), (partial[n, 1] + imag).astype(BF16)


def late_rest_kernel(eig, side, rb_count, flat, partial, last, own, carried, out, traces):
    count, width = out.shape[0] - 1, last.shape[1] // 2
    others = flat.shape[0] // eig
    right = [last[:, :width], last[:, width:]]
    for n in range(count + 1):
        spin = others - count + n
        left = right
        if n < count:
            left = side_columns(flat, slice(spin * eig, (spin + 1) * eig), side, width, rb_count)
        real, imag = half_products(left, right)
        out[n, 0], out[n, 1] = (partial[spin, 0] + real).astype(BF16), (partial[spin, 1] + imag).astype(BF16)
    direct_sums([out.at[count]], own, traces, carried)


def late_rows(keys, flat, partial, pieces, spins, eig, rb_count):
    return pl.pallas_call(
        functools.partial(late_rows_kernel, eig, keys, rb_count),
        out_shape=(
            jax.ShapeDtypeStruct((spins // 2, 2, eig, eig), BF16),
            jax.ShapeDtypeStruct((eig, 2 * pieces[0].shape[2]), BF16),
        ),
        in_specs=[VMEM] * (2 + len(pieces)),
        out_specs=(VMEM, VMEM),
        compiler_params=params(32),
        cost_estimate=LONG,
        name="late_rows",
    )(flat, partial, *pieces)


def late_rest(side, flat, partial, last, own, carried, spins, eig, rb_count):
    return pl.pallas_call(
        functools.partial(late_rest_kernel, eig, side, rb_count),
        out_shape=(
            jax.ShapeDtypeStruct((spins - spins // 2, 2, eig, eig), BF16),
            sums_shape(carried.shape[0]),
        ),
        in_specs=[VMEM] * 5,
        out_specs=(VMEM, VMEM),
        compiler_params=params(32),
        cost_estimate=LITTLE,
        name="late_rest",
    )(flat, partial, last, own, carried)


def factors_kernel(diag_mom, elems, right_ref, left_ref, own_ref, held, sem):
    rank = lax.axis_index("rb")
    eig = held.shape[-1]
    copies = []
    for time in range(2):
        which = diag_mom[0, rank, lax.bitwise_xor(rank, time)]
        copies.append(pltpu.make_async_copy(elems.at[which], held.at[time], sem.at[time]))
    for slot in range(own_ref.shape[0]):
        copies.append(pltpu.make_async_copy(elems.at[diag_mom[0, slot, rank]], own_ref.at[slot], sem.at[2 + slot]))
    for copy in copies:
        copy.start()
    for copy in copies:
        copy.wait()
    for time in range(2):
        re, im = held[time, 0], held[time, 1]
        right_ref[time, :eig, :eig] = re
        right_ref[time, :eig, eig:] = im
        right_ref[time, eig:, :eig] = -im
        right_ref[time, eig:, eig:] = re
        re_t = re.astype(F32).T.astype(BF16)
        im_t = im.astype(F32).T.astype(BF16)
        left_ref[time, :eig, :eig] = re_t
        left_ref[time, :eig, eig:] = im_t
        left_ref[time, eig:, :eig] = im_t
        left_ref[time, eig:, eig:] = -re_t


def factors(diag_mom, src_elems):
    slots, eig = diag_mom.shape[1], src_elems.shape[-1]
    form = jax.ShapeDtypeStruct((2, 2 * eig, 2 * eig), BF16)
    return pl.pallas_call(
        factors_kernel,
        out_shape=(form, form, jax.ShapeDtypeStruct((slots, 2, eig, eig), BF16)),
        in_specs=[SMEM, ANY],
        out_specs=(VMEM, VMEM, VMEM),
        scratch_shapes=[pltpu.VMEM((2, 2, eig, eig), BF16), pltpu.SemaphoreType.DMA((2 + slots,))],
        compiler_params=params(32),
        cost_estimate=LITTLE,
        name="factors",
    )(diag_mom, src_elems)


def right_products(x, count, from_right):
    rows = [jnp.concatenate([x[n, 0], x[n, 1]], axis=1) for n in range(count)]
    return dot(jnp.concatenate(rows, axis=0), from_right)


def left_product(y, n, from_left):
    eig = y.shape[-1]
    return dot(from_left, y[n].reshape(2 * eig, eig))


def paired(product, partner):
    eig = partner.shape[1]
    p_re, p_im = product[:, :eig], product[:, eig:]
    w_re, w_im = partner[:eig], partner[eig:]
    return fold(p_re * w_re - p_im * w_im), fold(p_re * w_im + p_im * w_re)


def own_products_kernel(own, right, left, products, partners):
    count = own.shape[0]
    products[...] = right_products(own, count, right[0])
    for n in range(count):
        partners[n] = left_product(own, n, left[0])


def own_products(own, right, left):
    count, eig = own.shape[0], own.shape[-1]
    return pl.pallas_call(
        own_products_kernel,
        out_shape=(
            jax.ShapeDtypeStruct((count * eig, 2 * eig), F32),
            jax.ShapeDtypeStruct((count, 2 * eig, eig), F32),
        ),
        in_specs=[VMEM] * 3,
        out_specs=(VMEM, VMEM),
        compiler_params=params(32),
        cost_estimate=LITTLE,
        name="own_products",
    )(own, right, left)


def joined_kernel(other, right, left, products, partners, carried, out):
    count, eig = other.shape[0], other.shape[-1]
    theirs = right_products(other, count, right[1])
    real, imag = [carried[0]], [carried[1]]
    for n in range(count):
        rows = slice(n * eig, (n + 1) * eig)
        sums = [paired(theirs[rows], partners[n]), paired(products[rows, :], left_product(other, n, left[1]))]
        real += [pair[0] for pair in sums]
        imag += [pair[1] for pair in sums]
    out[0] = functools.reduce(jnp.add, real)
    out[1] = functools.reduce(jnp.add, imag)


def joined_traces(other, right, left, products, partners, carried):
    return pl.pallas_call(
        joined_kernel,
        out_shape=sums_shape(2),
        in_specs=[VMEM] * 6,
        out_specs=VMEM,
        compiler_params=params(32),
        cost_estimate=LITTLE,
        name="late_cross",
    )(other, right, left, products, partners, carried)


def cross_kernel(offs, own, other, right, left, *refs):
    carried, out = refs[:-1], refs[-1]
    eig = own.shape[-1]
    if len(other.shape) > len(own.shape):
        other = other.at[1 - lax.axis_index("rb")]
    real, imag = [], []

    def add(x, y, count, from_right, from_left):
        product = right_products(x, count, from_right)
        for n in range(count):
            pair = paired(product[n * eig : (n + 1) * eig], left_product(y, n, from_left))
            real.append(pair[0])
            imag.append(pair[1])

    add(other, own, own.shape[0], right[1], left[0])
    add(own, other, offs, right[0], left[1])
    out[0] = functools.reduce(jnp.add, real + [ref[0] for ref in carried])
    out[1] = functools.reduce(jnp.add, imag + [ref[1] for ref in carried])


def cross_traces(offs, own, other, right, left, carried, name):
    return pl.pallas_call(
        functools.partial(cross_kernel, offs),
        out_shape=sums_shape(2),
        in_specs=[VMEM] * (4 + len(carried)),
        out_specs=VMEM,
        compiler_params=params(32),
        cost_estimate=LITTLE,
        name=name,
    )(own, other, right, left, *carried)


def last_cross_kernel(offs, own, other, right, left, direct, carried, out):
    count = direct.shape[0]
    for n in range(count):
        out[n] = direct[n]
    cross_kernel(offs, own, other, right, left, carried, out.at[pl.ds(count, 2)])


def last_cross(offs, own, other, right, left, direct, carried):
    return pl.pallas_call(
        functools.partial(last_cross_kernel, offs),
        out_shape=sums_shape(direct.shape[0] + 2),
        in_specs=[VMEM] * 6,
        out_specs=VMEM,
        compiler_params=params(32),
        cost_estimate=LITTLE,
        name="last_cross",
    )(own, other, right, left, direct, carried)


def final_kernel(slots, mine, theirs, count, out):
    rank = lax.axis_index("rb")
    lane = lax.broadcasted_iota(jnp.int32, (1, LANES), 1)

    def totals(ref):
        rows = jnp.concatenate([jnp.sum(ref[n], axis=0, keepdims=True) for n in range(ref.shape[0])], axis=0)
        sums = jnp.broadcast_to(jnp.sum(rows, axis=1, keepdims=True), rows.shape)
        return [sums[n : n + 1] for n in range(ref.shape[0])]

    def put(slot, kind, re, im):
        value = jnp.where(lane == 0, re, im) * 0.25
        out[0, slot, kind : kind + 1, :] = jnp.where(slot < count[0], value, 0.0)[:, :2]

    m, t = totals(mine), totals(theirs)
    for slot in range(slots):
        m_re, m_im, t_re, t_im = m[2 * slot], m[2 * slot + 1], t[2 * slot], t[2 * slot + 1]
        put(slot, 0, m_re * t_re - m_im * t_im, m_re * t_im + m_im * t_re)
        here = rank == slot
        put(slot, 1, jnp.where(here, m[2 * slots], t[2 * slots]), jnp.where(here, m[2 * slots + 1], t[2 * slots + 1]))


def final(mine, theirs, diag_count, slots):
    return pl.pallas_call(
        functools.partial(final_kernel, slots),
        out_shape=jax.ShapeDtypeStruct((1, slots, 2, 2), F32),
        in_specs=[VMEM, VMEM, SMEM],
        out_specs=VMEM,
        compiler_params=params(32),
        name="final",
    )(mine, theirs, diag_count)


def shards(peram, src_elems, owner_times, diag_mom, diag_count):
    tp_count, rb_count = lax.axis_size("tp"), lax.axis_size("rb")
    eig = src_elems.shape[-1]
    spins = tp_count * peram.shape[0] // eig
    slots = diag_mom.shape[1]

    head, tail, late, own = travel_order(tp_count, rb_count)
    early_keys = head + tail
    picked = pick(owner_times, peram, head, "pick_head", [jax.ShapeDtypeStruct((4, *peram.shape), BF16)])
    picked.update(pick(owner_times, peram, tail + late + own, "pick_tail", []))

    def send(key):
        far, side = key
        swapped = tp_count // 4 if far >= tp_count // 2 else 0
        pairs = [
            (tp * rb_count + rb, (tp ^ far ^ (swapped if tp < tp_count // 2 else 0)) * rb_count + (rb ^ side))
            for tp in range(tp_count)
            for rb in range(rb_count)
        ]
        return lax.ppermute(picked[key], ("tp", "rb"), pairs)

    swap = [(rb, rb ^ 1) for rb in range(rb_count)]
    right, left, own_elems = factors(diag_mom, src_elems)
    arrived = [send(key) for key in early_keys] + [picked[key] for key in own]
    flat, early, direct = early_gram(early_keys + own, arrived, own_elems, spins, eig, rb_count)
    early_both = lax.all_to_all(jnp.stack([early] * rb_count), "rb", 0, 0)
    offs = early.shape[0] - (spins - 1)
    begun = cross_traces(offs, early, early_both, right, left, [], "early_cross")

    halves = [[key for key in late if key[1] == side] for side in range(rb_count)]
    sent = [[send(key) for key in keys] for keys in halves]
    half = late_begin(halves[0], flat, begun, sent[0], spins, eig, rb_count)
    blocks, last = late_rows(halves[1], flat, half, sent[1], spins, eig, rb_count)
    swapped = lax.ppermute(blocks, "rb", swap)
    rest, traces = late_rest(1, flat, half, last, own_elems, direct, spins, eig, rb_count)
    rest_swapped = lax.ppermute(rest, "rb", swap)
    products, partners = own_products(blocks, right, left)
    partial = joined_traces(swapped, right, left, products, partners, begun)
    mine = last_cross(rest.shape[0] - 1, rest, rest_swapped, right, left, traces, partial)
    theirs = lax.ppermute(mine, "rb", swap)
    return final(mine, theirs, diag_count, slots)


def solution(mesh):
    in_specs = (
        P(("grp", "tp"), None, None, "rb"),
        P("grp", None, None, None),
        P("grp", None),
        P(("grp", "tp"), None, None),
        P(("grp", "tp")),
    )
    out_specs = P(("grp", "tp"), None, None, None)
    return jax.shard_map(shards, mesh=mesh, in_specs=in_specs, out_specs=out_specs, check_vma=False)
```

```python
import functools

import jax
import jax.numpy as jnp
from jax import lax
from jax.experimental import pallas as pl
from jax.experimental.pallas import tpu as pltpu
from jax.sharding import PartitionSpec as P

F32 = jnp.float32
BF16 = jnp.bfloat16
ANY = pl.BlockSpec(memory_space=pl.ANY)
SMEM = pl.BlockSpec(memory_space=pltpu.SMEM)
VMEM = pl.BlockSpec(memory_space=pltpu.VMEM)
SUBLANES = 8
LANES = 128
STEP = 16
MIB = 1 << 20
LITTLE = pl.CostEstimate(flops=1000, bytes_accessed=1000, transcendentals=0)
LONG = pl.CostEstimate(flops=5 * 10**10, bytes_accessed=1000, transcendentals=0)


def in_hbm(array):
    return pltpu.with_memory_space_constraint(array, pltpu.HBM)


def params(mib):
    return pltpu.CompilerParams(vmem_limit_bytes=mib * MIB)


def dot(left, right):
    return jnp.dot(left, right, preferred_element_type=F32)


def dot_nt(left, right):
    return lax.dot_general(left, right, (((1,), (1,)), ((), ())), preferred_element_type=F32)


def choose(index, values):
    out = jnp.int32(values[0])
    for n in range(1, len(values)):
        out = jnp.where(index == n, jnp.int32(values[n]), out)
    return out


def aligned(start, size):
    return pl.ds(pl.multiple_of(start, size), size)


def travel_order(tp_count, rb_count):
    half, quarter = tp_count // 2, tp_count // 4

    def both(distances):
        return [(far, side) for far in distances for side in range(rb_count)]

    long, late = both(range(half, half + quarter)), both(reversed(range(half + quarter, tp_count)))
    near, rest = both(reversed(range(quarter, half))), both(range(1, quarter))
    own, other = (0, 0), [(0, side) for side in range(1, rb_count)]
    step, part = len(long) // 4, len(rest) // 2
    head = long[: 2 * step] + near[: 2 * step] + long[2 * step : 3 * step]
    tail = rest[:part] + other + near[2 * step : 3 * step] + long[3 * step :] + rest[part:] + near[3 * step :]
    return head, tail, late, [own]


def distance(far, tp_rank, tp_count):
    if far < tp_count // 2:
        return far
    return lax.bitwise_xor(jnp.int32(far), jnp.where(tp_rank < tp_count // 2, jnp.int32(tp_count // 4), jnp.int32(0)))


def pick_kernel(keys, times, table, *refs):
    outs, (held, wide, taken_times, sem, times_sem) = refs[:-5], refs[-5:]
    tp_rank, rb_rank = lax.axis_index("tp"), lax.axis_index("rb")
    rows, _, packed, _ = table.shape

    def fetch(chunk):
        where = aligned(chunk * STEP, STEP)
        return pltpu.make_async_copy(table.at[where], held.at[where], sem.at[chunk])

    copy = pltpu.make_async_copy(times, taken_times, times_sem)
    copy.start()
    for chunk in range(rows // STEP):
        fetch(chunk).start()
    copy.wait()

    def step(chunk, carry):
        fetch(chunk).wait()
        where = aligned(chunk * STEP, STEP)
        for n, (far, side) in enumerate(keys):
            owner = lax.bitwise_xor(tp_rank, distance(far, tp_rank, taken_times.shape[1]))
            time = taken_times[lax.bitwise_xor(rb_rank, side), owner]
            slot = n % wide.shape[0]
            wide[slot] = held[where, time].astype(F32).reshape(STEP * packed, LANES)
            for tile in range(packed // 2):
                for part in range(2):
                    taken = wide[slot, pl.ds(2 * tile + part, STEP, stride=packed), :]
                    outs[n][part, where, tile * LANES : (tile + 1) * LANES] = taken.astype(BF16)
        return carry

    lax.fori_loop(0, rows // STEP, step, 0)


def pick(owner_times, peram, keys, name, spare):
    rows, times, parts, width = peram.shape
    tiles = width // LANES
    table = peram.reshape(rows, times, parts, tiles, LANES).swapaxes(2, 3)
    table = table.reshape(rows, times, tiles * parts, LANES)
    picked = pl.pallas_call(
        functools.partial(pick_kernel, keys),
        out_shape=[jax.ShapeDtypeStruct((parts, rows, width), BF16)] * len(keys) + spare,
        in_specs=[ANY, ANY],
        out_specs=[VMEM] * len(keys) + [ANY] * len(spare),
        scratch_shapes=[
            pltpu.VMEM(table.shape, BF16),
            pltpu.VMEM((4, STEP * tiles * parts, LANES), F32),
            pltpu.SMEM(owner_times.shape[::-1], jnp.int32),
            pltpu.SemaphoreType.DMA((rows // STEP,)),
            pltpu.SemaphoreType.DMA,
        ],
        compiler_params=params(32),
        cost_estimate=LITTLE,
        name=name,
    )(in_hbm(owner_times.T), in_hbm(table))
    return dict(zip(keys, picked))


def place(far, per_spin):
    low = lax.axis_index("tp") % per_spin
    return (far // per_spin) * per_spin + lax.bitwise_xor(jnp.int32(far % per_spin), low)


def gram_block(left, right):
    depth = left.shape[1] // 2
    real = dot_nt(left, right)
    imag = dot_nt(left[:, :depth], right[:, depth:]) - dot_nt(left[:, depth:], right[:, :depth])
    return real.astype(BF16), imag.astype(BF16)


def fold(values):
    rows, columns = values.shape
    folded = jnp.sum(values.reshape(rows // SUBLANES, SUBLANES, columns), axis=0)
    return functools.reduce(jnp.add, [folded[:, n : n + LANES] for n in range(0, columns, LANES)])


def direct_sums(diagonal, own, out, carried=None):
    real = functools.reduce(jnp.add, [block[0].astype(F32) for block in diagonal])
    imag = functools.reduce(jnp.add, [block[1].astype(F32) for block in diagonal])
    for slot in range(own.shape[0]):
        elem_re, elem_im = own[slot, 0].astype(F32), own[slot, 1].astype(F32)
        sums = [fold(elem_re * real + elem_im * imag), fold(elem_im * real - elem_re * imag)]
        for part in range(2):
            n = 2 * slot + part
            out[n] = sums[part] if carried is None else sums[part] + carried[n]


def sums_shape(count):
    return jax.ShapeDtypeStruct((count, SUBLANES, LANES), F32)


def early_blocks(spins):
    off = [(s, t) for s in range(spins - 1) for t in range(s + 1, spins - 1)]
    return off + [(s, s) for s in range(spins - 1)]


def early_kernel(eig, keys, rb_count, blocks, *refs):
    pieces, (own, flat, out, traces, sem) = refs[:-5], refs[-5:]
    rows, width = pieces[0].shape[1:]
    depth = rb_count * width
    copies = []
    for n, ((far, side), piece) in enumerate(zip(keys, pieces)):
        where = aligned(place(far, eig // rows) * rows, rows)
        for part in range(2):
            columns = pl.ds(part * depth + side * width, width)
            copies.append(pltpu.make_async_copy(piece.at[part], flat.at[where, columns], sem.at[2 * n + part]))
    for copy in copies:
        copy.start()
    for copy in copies:
        copy.wait()

    def step(n, carry):
        top, side = choose(n, [b[0] for b in blocks]), choose(n, [b[1] for b in blocks])
        out[n, 0], out[n, 1] = gram_block(flat[aligned(top * eig, eig), :], flat[aligned(side * eig, eig), :])
        return carry

    lax.fori_loop(0, len(blocks), step, 0)
    diagonal = [out.at[n] for n, block in enumerate(blocks) if block[0] == block[1]]
    direct_sums(diagonal, own, traces)


def early_gram(keys, pieces, own_elems, spins, eig, rb_count):
    blocks = early_blocks(spins)
    depth = 2 * rb_count * pieces[0].shape[2]
    return pl.pallas_call(
        functools.partial(early_kernel, eig, keys, rb_count, blocks),
        out_shape=(
            jax.ShapeDtypeStruct(((spins - 1) * eig, depth), BF16),
            jax.ShapeDtypeStruct((len(blocks), 2, eig, eig), BF16),
            sums_shape(2 * own_elems.shape[0]),
        ),
        in_specs=[ANY] * len(pieces) + [VMEM],
        out_specs=(VMEM, VMEM, VMEM),
        scratch_shapes=[pltpu.SemaphoreType.DMA((2 * len(pieces),))],
        compiler_params=params(32),
        cost_estimate=LONG,
        name="early_gram",
    )(*pieces, own_elems)


def side_columns(ref, rows, side, width, rb_count):
    return [ref[rows, (part * rb_count + side) * width : (part * rb_count + side + 1) * width] for part in range(2)]


def half_products(left, right):
    real = dot_nt(left[0], right[0]) + dot_nt(left[1], right[1])
    imag = dot_nt(left[0], right[1]) - dot_nt(left[1], right[0])
    return real, imag


def gather_last(eig, keys, others, pieces, last):
    rows, width = pieces[0].shape[1:]
    for (far, _), piece in zip(keys, pieces):
        where = aligned((place(far, eig // rows) - others * (eig // rows)) * rows, rows)
        for part in range(2):
            last[where, part * width : (part + 1) * width] = piece[part]


def late_begin_kernel(eig, keys, rb_count, flat, begun, *refs):
    pieces, (out, last) = refs[:-2], refs[-2:]
    side, width, others = keys[0][1], pieces[0].shape[2], flat.shape[0] // eig
    gather_last(eig, keys, others, pieces, last)
    right = [last[:, :width], last[:, width:]]
    for n in range(others):
        left = side_columns(flat, slice(n * eig, (n + 1) * eig), side, width, rb_count)
        out[n, 0], out[n, 1] = half_products(left, right)
    out[others, 0], out[others, 1] = half_products(right, right)


def late_begin(keys, flat, begun, pieces, spins, eig, rb_count):
    return pl.pallas_call(
        functools.partial(late_begin_kernel, eig, keys, rb_count),
        out_shape=jax.ShapeDtypeStruct((spins, 2, eig, eig), F32),
        in_specs=[VMEM, ANY] + [VMEM] * len(pieces),
        out_specs=VMEM,
        scratch_shapes=[pltpu.VMEM((eig, 2 * pieces[0].shape[2]), BF16)],
        compiler_params=params(32),
        cost_estimate=LITTLE,
        name="late_begin",
    )(flat, begun, *pieces)


def late_rows_kernel(eig, keys, rb_count, flat, partial, *refs):
    pieces, (out, last) = refs[:-2], refs[-2:]
    side, width = keys[0][1], pieces[0].shape[2]
    gather_last(eig, keys, flat.shape[0] // eig, pieces, last)
    right = [last[:, :width], last[:, width:]]
    for n in range(out.shape[0]):
        left = side_columns(flat, slice(n * eig, (n + 1) * eig), side, width, rb_count)
        real, imag = half_products(left, right)
        out[n, 0], out[n, 1] = (partial[n, 0] + real).astype(BF16), (partial[n, 1] + imag).astype(BF16)


def late_rest_kernel(eig, side, rb_count, flat, partial, last, own, carried, out, traces):
    count, width = out.shape[0] - 1, last.shape[1] // 2
    others = flat.shape[0] // eig
    right = [last[:, :width], last[:, width:]]
    for n in range(count + 1):
        spin = others - count + n
        left = right
        if n < count:
            left = side_columns(flat, slice(spin * eig, (spin + 1) * eig), side, width, rb_count)
        real, imag = half_products(left, right)
        out[n, 0], out[n, 1] = (partial[spin, 0] + real).astype(BF16), (partial[spin, 1] + imag).astype(BF16)
    direct_sums([out.at[count]], own, traces, carried)


def late_rows(keys, flat, partial, pieces, spins, eig, rb_count):
    return pl.pallas_call(
        functools.partial(late_rows_kernel, eig, keys, rb_count),
        out_shape=(
            jax.ShapeDtypeStruct((spins // 2, 2, eig, eig), BF16),
            jax.ShapeDtypeStruct((eig, 2 * pieces[0].shape[2]), BF16),
        ),
        in_specs=[VMEM] * (2 + len(pieces)),
        out_specs=(VMEM, VMEM),
        compiler_params=params(32),
        cost_estimate=LONG,
        name="late_rows",
    )(flat, partial, *pieces)


def late_rest(side, flat, partial, last, own, carried, spins, eig, rb_count):
    return pl.pallas_call(
        functools.partial(late_rest_kernel, eig, side, rb_count),
        out_shape=(
            jax.ShapeDtypeStruct((spins - spins // 2, 2, eig, eig), BF16),
            sums_shape(carried.shape[0]),
        ),
        in_specs=[VMEM] * 5,
        out_specs=(VMEM, VMEM),
        compiler_params=params(32),
        cost_estimate=LITTLE,
        name="late_rest",
    )(flat, partial, last, own, carried)


def factors_kernel(diag_mom, elems, right_ref, left_ref, own_ref, held, sem):
    rank = lax.axis_index("rb")
    eig = held.shape[-1]
    copies = []
    for time in range(2):
        which = diag_mom[0, rank, lax.bitwise_xor(rank, time)]
        copies.append(pltpu.make_async_copy(elems.at[which], held.at[time], sem.at[time]))
    for slot in range(own_ref.shape[0]):
        copies.append(pltpu.make_async_copy(elems.at[diag_mom[0, slot, rank]], own_ref.at[slot], sem.at[2 + slot]))
    for copy in copies:
        copy.start()
    for copy in copies:
        copy.wait()
    for time in range(2):
        re, im = held[time, 0], held[time, 1]
        right_ref[time, :eig, :eig] = re
        right_ref[time, :eig, eig:] = im
        right_ref[time, eig:, :eig] = -im
        right_ref[time, eig:, eig:] = re
        re_t = re.astype(F32).T.astype(BF16)
        im_t = im.astype(F32).T.astype(BF16)
        left_ref[time, :eig, :eig] = re_t
        left_ref[time, :eig, eig:] = im_t
        left_ref[time, eig:, :eig] = im_t
        left_ref[time, eig:, eig:] = -re_t


def factors(diag_mom, src_elems):
    slots, eig = diag_mom.shape[1], src_elems.shape[-1]
    form = jax.ShapeDtypeStruct((2, 2 * eig, 2 * eig), BF16)
    return pl.pallas_call(
        factors_kernel,
        out_shape=(form, form, jax.ShapeDtypeStruct((slots, 2, eig, eig), BF16)),
        in_specs=[SMEM, ANY],
        out_specs=(VMEM, VMEM, VMEM),
        scratch_shapes=[pltpu.VMEM((2, 2, eig, eig), BF16), pltpu.SemaphoreType.DMA((2 + slots,))],
        compiler_params=params(32),
        cost_estimate=LITTLE,
        name="factors",
    )(diag_mom, src_elems)


def right_products(x, count, from_right):
    rows = [jnp.concatenate([x[n, 0], x[n, 1]], axis=1) for n in range(count)]
    return dot(jnp.concatenate(rows, axis=0), from_right)


def left_product(y, n, from_left):
    eig = y.shape[-1]
    return dot(from_left, y[n].reshape(2 * eig, eig))


def paired(product, partner):
    eig = partner.shape[1]
    p_re, p_im = product[:, :eig], product[:, eig:]
    w_re, w_im = partner[:eig], partner[eig:]
    return fold(p_re * w_re - p_im * w_im), fold(p_re * w_im + p_im * w_re)


def own_products_kernel(own, right, left, products, partners):
    count = own.shape[0]
    products[...] = right_products(own, count, right[0])
    for n in range(count):
        partners[n] = left_product(own, n, left[0])


def own_products(own, right, left):
    count, eig = own.shape[0], own.shape[-1]
    return pl.pallas_call(
        own_products_kernel,
        out_shape=(
            jax.ShapeDtypeStruct((count * eig, 2 * eig), F32),
            jax.ShapeDtypeStruct((count, 2 * eig, eig), F32),
        ),
        in_specs=[VMEM] * 3,
        out_specs=(VMEM, VMEM),
        compiler_params=params(32),
        cost_estimate=LITTLE,
        name="own_products",
    )(own, right, left)


def joined_kernel(other, right, left, products, partners, carried, out):
    count, eig = other.shape[0], other.shape[-1]
    theirs = right_products(other, count, right[1])
    real, imag = [carried[0]], [carried[1]]
    for n in range(count):
        rows = slice(n * eig, (n + 1) * eig)
        sums = [paired(theirs[rows], partners[n]), paired(products[rows, :], left_product(other, n, left[1]))]
        real += [pair[0] for pair in sums]
        imag += [pair[1] for pair in sums]
    out[0] = functools.reduce(jnp.add, real)
    out[1] = functools.reduce(jnp.add, imag)


def joined_traces(other, right, left, products, partners, carried):
    return pl.pallas_call(
        joined_kernel,
        out_shape=sums_shape(2),
        in_specs=[VMEM] * 6,
        out_specs=VMEM,
        compiler_params=params(32),
        cost_estimate=LITTLE,
        name="late_cross",
    )(other, right, left, products, partners, carried)


def cross_kernel(offs, own, other, right, left, *refs):
    carried, out = refs[:-1], refs[-1]
    eig = own.shape[-1]
    if len(other.shape) > len(own.shape):
        other = other.at[1 - lax.axis_index("rb")]
    real, imag = [], []

    def add(x, y, count, from_right, from_left):
        product = right_products(x, count, from_right)
        for n in range(count):
            pair = paired(product[n * eig : (n + 1) * eig], left_product(y, n, from_left))
            real.append(pair[0])
            imag.append(pair[1])

    add(other, own, own.shape[0], right[1], left[0])
    add(own, other, offs, right[0], left[1])
    out[0] = functools.reduce(jnp.add, real + [ref[0] for ref in carried])
    out[1] = functools.reduce(jnp.add, imag + [ref[1] for ref in carried])


def cross_traces(offs, own, other, right, left, carried, name):
    return pl.pallas_call(
        functools.partial(cross_kernel, offs),
        out_shape=sums_shape(2),
        in_specs=[VMEM] * (4 + len(carried)),
        out_specs=VMEM,
        compiler_params=params(32),
        cost_estimate=LITTLE,
        name=name,
    )(own, other, right, left, *carried)


def last_cross_kernel(offs, own, other, right, left, direct, carried, out):
    count = direct.shape[0]
    for n in range(count):
        out[n] = direct[n]
    cross_kernel(offs, own, other, right, left, carried, out.at[pl.ds(count, 2)])


def last_cross(offs, own, other, right, left, direct, carried):
    return pl.pallas_call(
        functools.partial(last_cross_kernel, offs),
        out_shape=sums_shape(direct.shape[0] + 2),
        in_specs=[VMEM] * 6,
        out_specs=VMEM,
        compiler_params=params(32),
        cost_estimate=LITTLE,
        name="last_cross",
    )(own, other, right, left, direct, carried)


def final_kernel(slots, mine, theirs, count, out):
    rank = lax.axis_index("rb")
    lane = lax.broadcasted_iota(jnp.int32, (1, LANES), 1)

    def totals(ref):
        rows = jnp.concatenate([jnp.sum(ref[n], axis=0, keepdims=True) for n in range(ref.shape[0])], axis=0)
        sums = jnp.broadcast_to(jnp.sum(rows, axis=1, keepdims=True), rows.shape)
        return [sums[n : n + 1] for n in range(ref.shape[0])]

    def put(slot, kind, re, im):
        value = jnp.where(lane == 0, re, im) * 0.25
        out[0, slot, kind : kind + 1, :] = jnp.where(slot < count[0], value, 0.0)[:, :2]

    m, t = totals(mine), totals(theirs)
    for slot in range(slots):
        m_re, m_im, t_re, t_im = m[2 * slot], m[2 * slot + 1], t[2 * slot], t[2 * slot + 1]
        put(slot, 0, m_re * t_re - m_im * t_im, m_re * t_im + m_im * t_re)
        here = rank == slot
        put(slot, 1, jnp.where(here, m[2 * slots], t[2 * slots]), jnp.where(here, m[2 * slots + 1], t[2 * slots + 1]))


def final(mine, theirs, diag_count, slots):
    return pl.pallas_call(
        functools.partial(final_kernel, slots),
        out_shape=jax.ShapeDtypeStruct((1, slots, 2, 2), F32),
        in_specs=[VMEM, VMEM, SMEM],
        out_specs=VMEM,
        compiler_params=params(32),
        name="final",
    )(mine, theirs, diag_count)


def shards(peram, src_elems, owner_times, diag_mom, diag_count):
    tp_count, rb_count = lax.axis_size("tp"), lax.axis_size("rb")
    eig = src_elems.shape[-1]
    spins = tp_count * peram.shape[0] // eig
    slots = diag_mom.shape[1]

    head, tail, late, own = travel_order(tp_count, rb_count)
    early_keys = head + tail
    picked = pick(owner_times, peram, head, "pick_head", [jax.ShapeDtypeStruct((4, *peram.shape), BF16)])
    picked.update(pick(owner_times, peram, tail + late + own, "pick_tail", []))

    def send(key):
        far, side = key
        swapped = tp_count // 4 if far >= tp_count // 2 else 0
        pairs = [
            (tp * rb_count + rb, (tp ^ far ^ (swapped if tp < tp_count // 2 else 0)) * rb_count + (rb ^ side))
            for tp in range(tp_count)
            for rb in range(rb_count)
        ]
        return lax.ppermute(picked[key], ("tp", "rb"), pairs)

    swap = [(rb, rb ^ 1) for rb in range(rb_count)]
    right, left, own_elems = factors(diag_mom, src_elems)
    arrived = [send(key) for key in early_keys] + [picked[key] for key in own]
    flat, early, direct = early_gram(early_keys + own, arrived, own_elems, spins, eig, rb_count)
    early_both = lax.all_to_all(jnp.stack([early] * rb_count), "rb", 0, 0)
    offs = early.shape[0] - (spins - 1)
    begun = cross_traces(offs, early, early_both, right, left, [], "early_cross")

    halves = [[key for key in late if key[1] == side] for side in range(rb_count)]
    sent = [[send(key) for key in keys] for keys in halves]
    half = late_begin(halves[0], flat, begun, sent[0], spins, eig, rb_count)
    blocks, last = late_rows(halves[1], flat, half, sent[1], spins, eig, rb_count)
    swapped = lax.ppermute(blocks, "rb", swap)
    rest, traces = late_rest(1, flat, half, last, own_elems, direct, spins, eig, rb_count)
    rest_swapped = lax.ppermute(rest, "rb", swap)
    products, partners = own_products(blocks, right, left)
    partial = joined_traces(swapped, right, left, products, partners, begun)
    mine = last_cross(rest.shape[0] - 1, rest, rest_swapped, right, left, traces, partial)
    theirs = lax.ppermute(mine, "rb", swap)
    return final(mine, theirs, diag_count, slots)


def solution(mesh):
    in_specs = (
        P(("grp", "tp"), None, None, "rb"),
        P("grp", None, None, None),
        P("grp", None),
        P(("grp", "tp"), None, None),
        P(("grp", "tp")),
    )
    out_specs = P(("grp", "tp"), None, None, None)
    return jax.shard_map(shards, mesh=mesh, in_specs=in_specs, out_specs=out_specs, check_vma=False)
```

```python
import functools

import jax
import jax.numpy as jnp
from jax import lax
from jax.experimental import pallas as pl
from jax.experimental.pallas import tpu as pltpu
from jax.sharding import PartitionSpec as P

F32 = jnp.float32
BF16 = jnp.bfloat16
ANY = pl.BlockSpec(memory_space=pl.ANY)
SMEM = pl.BlockSpec(memory_space=pltpu.SMEM)
VMEM = pl.BlockSpec(memory_space=pltpu.VMEM)
SUBLANES = 8
LANES = 128
STEP = 16
MIB = 1 << 20
LITTLE = pl.CostEstimate(flops=1000, bytes_accessed=1000, transcendentals=0)
LONG = pl.CostEstimate(flops=5 * 10**10, bytes_accessed=1000, transcendentals=0)


def in_hbm(array):
    return pltpu.with_memory_space_constraint(array, pltpu.HBM)


def params(mib):
    return pltpu.CompilerParams(vmem_limit_bytes=mib * MIB)


def dot(left, right):
    return jnp.dot(left, right, preferred_element_type=F32)


def dot_nt(left, right):
    return lax.dot_general(left, right, (((1,), (1,)), ((), ())), preferred_element_type=F32)


def choose(index, values):
    out = jnp.int32(values[0])
    for n in range(1, len(values)):
        out = jnp.where(index == n, jnp.int32(values[n]), out)
    return out


def aligned(start, size):
    return pl.ds(pl.multiple_of(start, size), size)


def travel_order(tp_count, rb_count):
    half, quarter = tp_count // 2, tp_count // 4

    def both(distances):
        return [(far, side) for far in distances for side in range(rb_count)]

    long, late = both(range(half, half + quarter)), both(reversed(range(half + quarter, tp_count)))
    near, rest = both(reversed(range(quarter, half))), both(range(1, quarter))
    own, other = (0, 0), [(0, side) for side in range(1, rb_count)]
    step, part = len(long) // 4, len(rest) // 2
    head = long[: 2 * step] + near[: 2 * step] + long[2 * step : 3 * step]
    tail = rest[:part] + other + near[2 * step : 3 * step] + long[3 * step :] + rest[part:] + near[3 * step :]
    return head, tail, late, [own]


def distance(far, tp_rank, tp_count):
    if far < tp_count // 2:
        return far
    return lax.bitwise_xor(jnp.int32(far), jnp.where(tp_rank < tp_count // 2, jnp.int32(tp_count // 4), jnp.int32(0)))


def pick_kernel(keys, times, table, *refs):
    outs, (held, wide, taken_times, sem, times_sem) = refs[:-5], refs[-5:]
    tp_rank, rb_rank = lax.axis_index("tp"), lax.axis_index("rb")
    rows, _, packed, _ = table.shape

    def fetch(chunk):
        where = aligned(chunk * STEP, STEP)
        return pltpu.make_async_copy(table.at[where], held.at[where], sem.at[chunk])

    copy = pltpu.make_async_copy(times, taken_times, times_sem)
    copy.start()
    for chunk in range(rows // STEP):
        fetch(chunk).start()
    copy.wait()

    def step(chunk, carry):
        fetch(chunk).wait()
        where = aligned(chunk * STEP, STEP)
        for n, (far, side) in enumerate(keys):
            owner = lax.bitwise_xor(tp_rank, distance(far, tp_rank, taken_times.shape[1]))
            time = taken_times[lax.bitwise_xor(rb_rank, side), owner]
            slot = n % wide.shape[0]
            wide[slot] = held[where, time].astype(F32).reshape(STEP * packed, LANES)
            for tile in range(packed // 2):
                for part in range(2):
                    taken = wide[slot, pl.ds(2 * tile + part, STEP, stride=packed), :]
                    outs[n][part, where, tile * LANES : (tile + 1) * LANES] = taken.astype(BF16)
        return carry

    lax.fori_loop(0, rows // STEP, step, 0)


def pick(owner_times, peram, keys, name, spare):
    rows, times, parts, width = peram.shape
    tiles = width // LANES
    table = peram.reshape(rows, times, parts, tiles, LANES).swapaxes(2, 3)
    table = table.reshape(rows, times, tiles * parts, LANES)
    picked = pl.pallas_call(
        functools.partial(pick_kernel, keys),
        out_shape=[jax.ShapeDtypeStruct((parts, rows, width), BF16)] * len(keys) + spare,
        in_specs=[ANY, ANY],
        out_specs=[VMEM] * len(keys) + [ANY] * len(spare),
        scratch_shapes=[
            pltpu.VMEM(table.shape, BF16),
            pltpu.VMEM((4, STEP * tiles * parts, LANES), F32),
            pltpu.SMEM(owner_times.shape[::-1], jnp.int32),
            pltpu.SemaphoreType.DMA((rows // STEP,)),
            pltpu.SemaphoreType.DMA,
        ],
        compiler_params=params(32),
        cost_estimate=LITTLE,
        name=name,
    )(in_hbm(owner_times.T), in_hbm(table))
    return dict(zip(keys, picked))


def place(far, per_spin):
    low = lax.axis_index("tp") % per_spin
    return (far // per_spin) * per_spin + lax.bitwise_xor(jnp.int32(far % per_spin), low)


def gram_block(left, right):
    depth = left.shape[1] // 2
    real = dot_nt(left, right)
    imag = dot_nt(left[:, :depth], right[:, depth:]) - dot_nt(left[:, depth:], right[:, :depth])
    return real.astype(BF16), imag.astype(BF16)


def fold(values):
    rows, columns = values.shape
    folded = jnp.sum(values.reshape(rows // SUBLANES, SUBLANES, columns), axis=0)
    return functools.reduce(jnp.add, [folded[:, n : n + LANES] for n in range(0, columns, LANES)])


def direct_sums(diagonal, own, out, carried=None):
    real = functools.reduce(jnp.add, [block[0].astype(F32) for block in diagonal])
    imag = functools.reduce(jnp.add, [block[1].astype(F32) for block in diagonal])
    for slot in range(own.shape[0]):
        elem_re, elem_im = own[slot, 0].astype(F32), own[slot, 1].astype(F32)
        sums = [fold(elem_re * real + elem_im * imag), fold(elem_im * real - elem_re * imag)]
        for part in range(2):
            n = 2 * slot + part
            out[n] = sums[part] if carried is None else sums[part] + carried[n]


def sums_shape(count):
    return jax.ShapeDtypeStruct((count, SUBLANES, LANES), F32)


def early_blocks(spins):
    off = [(s, t) for s in range(spins - 1) for t in range(s + 1, spins - 1)]
    return off + [(s, s) for s in range(spins - 1)]


def early_kernel(eig, keys, rb_count, blocks, *refs):
    pieces, (own, flat, out, traces, sem) = refs[:-5], refs[-5:]
    rows, width = pieces[0].shape[1:]
    depth = rb_count * width
    copies = []
    for n, ((far, side), piece) in enumerate(zip(keys, pieces)):
        where = aligned(place(far, eig // rows) * rows, rows)
        for part in range(2):
            columns = pl.ds(part * depth + side * width, width)
            copies.append(pltpu.make_async_copy(piece.at[part], flat.at[where, columns], sem.at[2 * n + part]))
    for copy in copies:
        copy.start()
    for copy in copies:
        copy.wait()

    def step(n, carry):
        top, side = choose(n, [b[0] for b in blocks]), choose(n, [b[1] for b in blocks])
        out[n, 0], out[n, 1] = gram_block(flat[aligned(top * eig, eig), :], flat[aligned(side * eig, eig), :])
        return carry

    lax.fori_loop(0, len(blocks), step, 0)
    diagonal = [out.at[n] for n, block in enumerate(blocks) if block[0] == block[1]]
    direct_sums(diagonal, own, traces)


def early_gram(keys, pieces, own_elems, spins, eig, rb_count):
    blocks = early_blocks(spins)
    depth = 2 * rb_count * pieces[0].shape[2]
    return pl.pallas_call(
        functools.partial(early_kernel, eig, keys, rb_count, blocks),
        out_shape=(
            jax.ShapeDtypeStruct(((spins - 1) * eig, depth), BF16),
            jax.ShapeDtypeStruct((len(blocks), 2, eig, eig), BF16),
            sums_shape(2 * own_elems.shape[0]),
        ),
        in_specs=[ANY] * len(pieces) + [VMEM],
        out_specs=(VMEM, VMEM, VMEM),
        scratch_shapes=[pltpu.SemaphoreType.DMA((2 * len(pieces),))],
        compiler_params=params(32),
        cost_estimate=LONG,
        name="early_gram",
    )(*pieces, own_elems)


def side_columns(ref, rows, side, width, rb_count):
    return [ref[rows, (part * rb_count + side) * width : (part * rb_count + side + 1) * width] for part in range(2)]


def half_products(left, right):
    real = dot_nt(left[0], right[0]) + dot_nt(left[1], right[1])
    imag = dot_nt(left[0], right[1]) - dot_nt(left[1], right[0])
    return real, imag


def gather_last(eig, keys, others, pieces, last):
    rows, width = pieces[0].shape[1:]
    for (far, _), piece in zip(keys, pieces):
        where = aligned((place(far, eig // rows) - others * (eig // rows)) * rows, rows)
        for part in range(2):
            last[where, part * width : (part + 1) * width] = piece[part]


def late_begin_kernel(eig, keys, rb_count, flat, begun, *refs):
    pieces, (out, last) = refs[:-2], refs[-2:]
    side, width, others = keys[0][1], pieces[0].shape[2], flat.shape[0] // eig
    gather_last(eig, keys, others, pieces, last)
    right = [last[:, :width], last[:, width:]]
    for n in range(others):
        left = side_columns(flat, slice(n * eig, (n + 1) * eig), side, width, rb_count)
        out[n, 0], out[n, 1] = half_products(left, right)
    out[others, 0], out[others, 1] = half_products(right, right)


def late_begin(keys, flat, begun, pieces, spins, eig, rb_count):
    return pl.pallas_call(
        functools.partial(late_begin_kernel, eig, keys, rb_count),
        out_shape=jax.ShapeDtypeStruct((spins, 2, eig, eig), F32),
        in_specs=[VMEM, ANY] + [VMEM] * len(pieces),
        out_specs=VMEM,
        scratch_shapes=[pltpu.VMEM((eig, 2 * pieces[0].shape[2]), BF16)],
        compiler_params=params(32),
        cost_estimate=LITTLE,
        name="late_begin",
    )(flat, begun, *pieces)


def late_rows_kernel(eig, keys, rb_count, flat, partial, *refs):
    pieces, (out, last) = refs[:-2], refs[-2:]
    side, width = keys[0][1], pieces[0].shape[2]
    gather_last(eig, keys, flat.shape[0] // eig, pieces, last)
    right = [last[:, :width], last[:, width:]]
    for n in range(out.shape[0]):
        left = side_columns(flat, slice(n * eig, (n + 1) * eig), side, width, rb_count)
        real, imag = half_products(left, right)
        out[n, 0], out[n, 1] = (partial[n, 0] + real).astype(BF16), (partial[n, 1] + imag).astype(BF16)


def late_rest_kernel(eig, side, rb_count, flat, partial, last, own, carried, out, traces):
    count, width = out.shape[0] - 1, last.shape[1] // 2
    others = flat.shape[0] // eig
    right = [last[:, :width], last[:, width:]]
    for n in range(count + 1):
        spin = others - count + n
        left = right
        if n < count:
            left = side_columns(flat, slice(spin * eig, (spin + 1) * eig), side, width, rb_count)
        real, imag = half_products(left, right)
        out[n, 0], out[n, 1] = (partial[spin, 0] + real).astype(BF16), (partial[spin, 1] + imag).astype(BF16)
    direct_sums([out.at[count]], own, traces, carried)


def late_rows(keys, flat, partial, pieces, spins, eig, rb_count):
    return pl.pallas_call(
        functools.partial(late_rows_kernel, eig, keys, rb_count),
        out_shape=(
            jax.ShapeDtypeStruct((spins // 2, 2, eig, eig), BF16),
            jax.ShapeDtypeStruct((eig, 2 * pieces[0].shape[2]), BF16),
        ),
        in_specs=[VMEM] * (2 + len(pieces)),
        out_specs=(VMEM, VMEM),
        compiler_params=params(32),
        cost_estimate=LONG,
        name="late_rows",
    )(flat, partial, *pieces)


def late_rest(side, flat, partial, last, own, carried, spins, eig, rb_count):
    return pl.pallas_call(
        functools.partial(late_rest_kernel, eig, side, rb_count),
        out_shape=(
            jax.ShapeDtypeStruct((spins - spins // 2, 2, eig, eig), BF16),
            sums_shape(carried.shape[0]),
        ),
        in_specs=[VMEM] * 5,
        out_specs=(VMEM, VMEM),
        compiler_params=params(32),
        cost_estimate=LITTLE,
        name="late_rest",
    )(flat, partial, last, own, carried)


def factors_kernel(diag_mom, elems, right_ref, left_ref, own_ref, held, sem):
    rank = lax.axis_index("rb")
    eig = held.shape[-1]
    copies = []
    for time in range(2):
        which = diag_mom[0, rank, lax.bitwise_xor(rank, time)]
        copies.append(pltpu.make_async_copy(elems.at[which], held.at[time], sem.at[time]))
    for slot in range(own_ref.shape[0]):
        copies.append(pltpu.make_async_copy(elems.at[diag_mom[0, slot, rank]], own_ref.at[slot], sem.at[2 + slot]))
    for copy in copies:
        copy.start()
    for copy in copies:
        copy.wait()
    for time in range(2):
        re, im = held[time, 0], held[time, 1]
        right_ref[time, :eig, :eig] = re
        right_ref[time, :eig, eig:] = im
        right_ref[time, eig:, :eig] = -im
        right_ref[time, eig:, eig:] = re
        re_t = re.astype(F32).T.astype(BF16)
        im_t = im.astype(F32).T.astype(BF16)
        left_ref[time, :eig, :eig] = re_t
        left_ref[time, :eig, eig:] = im_t
        left_ref[time, eig:, :eig] = im_t
        left_ref[time, eig:, eig:] = -re_t


def factors(diag_mom, src_elems):
    slots, eig = diag_mom.shape[1], src_elems.shape[-1]
    form = jax.ShapeDtypeStruct((2, 2 * eig, 2 * eig), BF16)
    return pl.pallas_call(
        factors_kernel,
        out_shape=(form, form, jax.ShapeDtypeStruct((slots, 2, eig, eig), BF16)),
        in_specs=[SMEM, ANY],
        out_specs=(VMEM, VMEM, VMEM),
        scratch_shapes=[pltpu.VMEM((2, 2, eig, eig), BF16), pltpu.SemaphoreType.DMA((2 + slots,))],
        compiler_params=params(32),
        cost_estimate=LITTLE,
        name="factors",
    )(diag_mom, src_elems)


def right_products(x, count, from_right):
    rows = [jnp.concatenate([x[n, 0], x[n, 1]], axis=1) for n in range(count)]
    return dot(jnp.concatenate(rows, axis=0), from_right)


def left_product(y, n, from_left):
    eig = y.shape[-1]
    return dot(from_left, y[n].reshape(2 * eig, eig))


def paired(product, partner):
    eig = partner.shape[1]
    p_re, p_im = product[:, :eig], product[:, eig:]
    w_re, w_im = partner[:eig], partner[eig:]
    return fold(p_re * w_re - p_im * w_im), fold(p_re * w_im + p_im * w_re)


def own_products_kernel(own, right, left, products, partners):
    count = own.shape[0]
    products[...] = right_products(own, count, right[0])
    for n in range(count):
        partners[n] = left_product(own, n, left[0])


def own_products(own, right, left):
    count, eig = own.shape[0], own.shape[-1]
    return pl.pallas_call(
        own_products_kernel,
        out_shape=(
            jax.ShapeDtypeStruct((count * eig, 2 * eig), F32),
            jax.ShapeDtypeStruct((count, 2 * eig, eig), F32),
        ),
        in_specs=[VMEM] * 3,
        out_specs=(VMEM, VMEM),
        compiler_params=params(32),
        cost_estimate=LITTLE,
        name="own_products",
    )(own, right, left)


def joined_kernel(other, right, left, products, partners, carried, out):
    count, eig = other.shape[0], other.shape[-1]
    theirs = right_products(other, count, right[1])
    real, imag = [carried[0]], [carried[1]]
    for n in range(count):
        rows = slice(n * eig, (n + 1) * eig)
        sums = [paired(theirs[rows], partners[n]), paired(products[rows, :], left_product(other, n, left[1]))]
        real += [pair[0] for pair in sums]
        imag += [pair[1] for pair in sums]
    out[0] = functools.reduce(jnp.add, real)
    out[1] = functools.reduce(jnp.add, imag)


def joined_traces(other, right, left, products, partners, carried):
    return pl.pallas_call(
        joined_kernel,
        out_shape=sums_shape(2),
        in_specs=[VMEM] * 6,
        out_specs=VMEM,
        compiler_params=params(32),
        cost_estimate=LITTLE,
        name="late_cross",
    )(other, right, left, products, partners, carried)


def cross_kernel(offs, own, other, right, left, *refs):
    carried, out = refs[:-1], refs[-1]
    eig = own.shape[-1]
    if len(other.shape) > len(own.shape):
        other = other.at[1 - lax.axis_index("rb")]
    real, imag = [], []

    def add(x, y, count, from_right, from_left):
        product = right_products(x, count, from_right)
        for n in range(count):
            pair = paired(product[n * eig : (n + 1) * eig], left_product(y, n, from_left))
            real.append(pair[0])
            imag.append(pair[1])

    add(other, own, own.shape[0], right[1], left[0])
    add(own, other, offs, right[0], left[1])
    out[0] = functools.reduce(jnp.add, real + [ref[0] for ref in carried])
    out[1] = functools.reduce(jnp.add, imag + [ref[1] for ref in carried])


def cross_traces(offs, own, other, right, left, carried, name):
    return pl.pallas_call(
        functools.partial(cross_kernel, offs),
        out_shape=sums_shape(2),
        in_specs=[VMEM] * (4 + len(carried)),
        out_specs=VMEM,
        compiler_params=params(32),
        cost_estimate=LITTLE,
        name=name,
    )(own, other, right, left, *carried)


def last_cross_kernel(offs, own, other, right, left, direct, carried, out):
    count = direct.shape[0]
    for n in range(count):
        out[n] = direct[n]
    cross_kernel(offs, own, other, right, left, carried, out.at[pl.ds(count, 2)])


def last_cross(offs, own, other, right, left, direct, carried):
    return pl.pallas_call(
        functools.partial(last_cross_kernel, offs),
        out_shape=sums_shape(direct.shape[0] + 2),
        in_specs=[VMEM] * 6,
        out_specs=VMEM,
        compiler_params=params(32),
        cost_estimate=LITTLE,
        name="last_cross",
    )(own, other, right, left, direct, carried)


def final_kernel(slots, mine, theirs, count, out):
    rank = lax.axis_index("rb")
    lane = lax.broadcasted_iota(jnp.int32, (1, LANES), 1)

    def totals(ref):
        rows = jnp.concatenate([jnp.sum(ref[n], axis=0, keepdims=True) for n in range(ref.shape[0])], axis=0)
        sums = jnp.broadcast_to(jnp.sum(rows, axis=1, keepdims=True), rows.shape)
        return [sums[n : n + 1] for n in range(ref.shape[0])]

    def put(slot, kind, re, im):
        value = jnp.where(lane == 0, re, im) * 0.25
        out[0, slot, kind : kind + 1, :] = jnp.where(slot < count[0], value, 0.0)[:, :2]

    m, t = totals(mine), totals(theirs)
    for slot in range(slots):
        m_re, m_im, t_re, t_im = m[2 * slot], m[2 * slot + 1], t[2 * slot], t[2 * slot + 1]
        put(slot, 0, m_re * t_re - m_im * t_im, m_re * t_im + m_im * t_re)
        here = rank == slot
        put(slot, 1, jnp.where(here, m[2 * slots], t[2 * slots]), jnp.where(here, m[2 * slots + 1], t[2 * slots + 1]))


def final(mine, theirs, diag_count, slots):
    return pl.pallas_call(
        functools.partial(final_kernel, slots),
        out_shape=jax.ShapeDtypeStruct((1, slots, 2, 2), F32),
        in_specs=[VMEM, VMEM, SMEM],
        out_specs=VMEM,
        compiler_params=params(32),
        name="final",
    )(mine, theirs, diag_count)


def shards(peram, src_elems, owner_times, diag_mom, diag_count):
    tp_count, rb_count = lax.axis_size("tp"), lax.axis_size("rb")
    eig = src_elems.shape[-1]
    spins = tp_count * peram.shape[0] // eig
    slots = diag_mom.shape[1]

    head, tail, late, own = travel_order(tp_count, rb_count)
    early_keys = head + tail
    picked = pick(owner_times, peram, head, "pick_head", [jax.ShapeDtypeStruct((4, *peram.shape), BF16)])
    picked.update(pick(owner_times, peram, tail + late + own, "pick_tail", []))

    def send(key):
        far, side = key
        swapped = tp_count // 4 if far >= tp_count // 2 else 0
        pairs = [
            (tp * rb_count + rb, (tp ^ far ^ (swapped if tp < tp_count // 2 else 0)) * rb_count + (rb ^ side))
            for tp in range(tp_count)
            for rb in range(rb_count)
        ]
        return lax.ppermute(picked[key], ("tp", "rb"), pairs)

    swap = [(rb, rb ^ 1) for rb in range(rb_count)]
    right, left, own_elems = factors(diag_mom, src_elems)
    arrived = [send(key) for key in early_keys] + [picked[key] for key in own]
    flat, early, direct = early_gram(early_keys + own, arrived, own_elems, spins, eig, rb_count)
    early_both = lax.all_to_all(jnp.stack([early] * rb_count), "rb", 0, 0)
    offs = early.shape[0] - (spins - 1)
    begun = cross_traces(offs, early, early_both, right, left, [], "early_cross")

    halves = [[key for key in late if key[1] == side] for side in range(rb_count)]
    halves[0].reverse()
    sent = [[send(key) for key in keys] for keys in halves]
    half = late_begin(halves[0], flat, begun, sent[0], spins, eig, rb_count)
    blocks, last = late_rows(halves[1], flat, half, sent[1], spins, eig, rb_count)
    swapped = lax.ppermute(blocks, "rb", swap)
    rest, traces = late_rest(1, flat, half, last, own_elems, direct, spins, eig, rb_count)
    rest_swapped = lax.ppermute(rest, "rb", swap)
    products, partners = own_products(blocks, right, left)
    partial = joined_traces(swapped, right, left, products, partners, begun)
    mine = last_cross(rest.shape[0] - 1, rest, rest_swapped, right, left, traces, partial)
    theirs = lax.ppermute(mine, "rb", swap)
    return final(mine, theirs, diag_count, slots)


def solution(mesh):
    in_specs = (
        P(("grp", "tp"), None, None, "rb"),
        P("grp", None, None, None),
        P("grp", None),
        P(("grp", "tp"), None, None),
        P(("grp", "tp")),
    )
    out_specs = P(("grp", "tp"), None, None, None)
    return jax.shard_map(shards, mesh=mesh, in_specs=in_specs, out_specs=out_specs, check_vma=False)
```

```python
import functools

import jax
import jax.numpy as jnp
from jax import lax
from jax.experimental import pallas as pl
from jax.experimental.pallas import tpu as pltpu
from jax.sharding import PartitionSpec as P

F32 = jnp.float32
BF16 = jnp.bfloat16
ANY = pl.BlockSpec(memory_space=pl.ANY)
SMEM = pl.BlockSpec(memory_space=pltpu.SMEM)
VMEM = pl.BlockSpec(memory_space=pltpu.VMEM)
SUBLANES = 8
LANES = 128
STEP = 16
MIB = 1 << 20
LITTLE = pl.CostEstimate(flops=1000, bytes_accessed=1000, transcendentals=0)
LONG = pl.CostEstimate(flops=5 * 10**10, bytes_accessed=1000, transcendentals=0)


def in_hbm(array):
    return pltpu.with_memory_space_constraint(array, pltpu.HBM)


def params(mib):
    return pltpu.CompilerParams(vmem_limit_bytes=mib * MIB)


def dot(left, right):
    return jnp.dot(left, right, preferred_element_type=F32)


def dot_nt(left, right):
    return lax.dot_general(left, right, (((1,), (1,)), ((), ())), preferred_element_type=F32)


def choose(index, values):
    out = jnp.int32(values[0])
    for n in range(1, len(values)):
        out = jnp.where(index == n, jnp.int32(values[n]), out)
    return out


def aligned(start, size):
    return pl.ds(pl.multiple_of(start, size), size)


def travel_order(tp_count, rb_count):
    half, quarter = tp_count // 2, tp_count // 4

    def both(distances):
        return [(far, side) for far in distances for side in range(rb_count)]

    long, late = both(range(half, half + quarter)), both(reversed(range(half + quarter, tp_count)))
    near, rest = both(reversed(range(quarter, half))), both(range(1, quarter))
    own, other = (0, 0), [(0, side) for side in range(1, rb_count)]
    step, part = len(long) // 4, len(rest) // 2
    head = long[: 2 * step] + near[: 2 * step] + long[2 * step : 3 * step]
    tail = other + rest[:part] + near[2 * step : 3 * step] + long[3 * step :] + rest[part:] + near[3 * step :]
    return head, tail, late, [own]


def distance(far, tp_rank, tp_count):
    if far < tp_count // 2:
        return far
    return lax.bitwise_xor(jnp.int32(far), jnp.where(tp_rank < tp_count // 2, jnp.int32(tp_count // 4), jnp.int32(0)))


def pick_kernel(keys, times, table, *refs):
    outs, (held, wide, taken_times, sem, times_sem) = refs[:-5], refs[-5:]
    tp_rank, rb_rank = lax.axis_index("tp"), lax.axis_index("rb")
    rows, _, packed, _ = table.shape

    def fetch(chunk):
        where = aligned(chunk * STEP, STEP)
        return pltpu.make_async_copy(table.at[where], held.at[where], sem.at[chunk])

    copy = pltpu.make_async_copy(times, taken_times, times_sem)
    copy.start()
    for chunk in range(rows // STEP):
        fetch(chunk).start()
    copy.wait()

    def step(chunk, carry):
        fetch(chunk).wait()
        where = aligned(chunk * STEP, STEP)
        for n, (far, side) in enumerate(keys):
            owner = lax.bitwise_xor(tp_rank, distance(far, tp_rank, taken_times.shape[1]))
            time = taken_times[lax.bitwise_xor(rb_rank, side), owner]
            slot = n % wide.shape[0]
            wide[slot] = held[where, time].astype(F32).reshape(STEP * packed, LANES)
            for tile in range(packed // 2):
                for part in range(2):
                    taken = wide[slot, pl.ds(2 * tile + part, STEP, stride=packed), :]
                    outs[n][part, where, tile * LANES : (tile + 1) * LANES] = taken.astype(BF16)
        return carry

    lax.fori_loop(0, rows // STEP, step, 0)


def pick(owner_times, peram, keys, name, spare):
    rows, times, parts, width = peram.shape
    tiles = width // LANES
    table = peram.reshape(rows, times, parts, tiles, LANES).swapaxes(2, 3)
    table = table.reshape(rows, times, tiles * parts, LANES)
    picked = pl.pallas_call(
        functools.partial(pick_kernel, keys),
        out_shape=[jax.ShapeDtypeStruct((parts, rows, width), BF16)] * len(keys) + spare,
        in_specs=[ANY, ANY],
        out_specs=[VMEM] * len(keys) + [ANY] * len(spare),
        scratch_shapes=[
            pltpu.VMEM(table.shape, BF16),
            pltpu.VMEM((4, STEP * tiles * parts, LANES), F32),
            pltpu.SMEM(owner_times.shape[::-1], jnp.int32),
            pltpu.SemaphoreType.DMA((rows // STEP,)),
            pltpu.SemaphoreType.DMA,
        ],
        compiler_params=params(32),
        cost_estimate=LITTLE,
        name=name,
    )(in_hbm(owner_times.T), in_hbm(table))
    return dict(zip(keys, picked))


def place(far, per_spin):
    low = lax.axis_index("tp") % per_spin
    return (far // per_spin) * per_spin + lax.bitwise_xor(jnp.int32(far % per_spin), low)


def gram_block(left, right):
    depth = left.shape[1] // 2
    real = dot_nt(left, right)
    imag = dot_nt(left[:, :depth], right[:, depth:]) - dot_nt(left[:, depth:], right[:, :depth])
    return real.astype(BF16), imag.astype(BF16)


def fold(values):
    rows, columns = values.shape
    folded = jnp.sum(values.reshape(rows // SUBLANES, SUBLANES, columns), axis=0)
    return functools.reduce(jnp.add, [folded[:, n : n + LANES] for n in range(0, columns, LANES)])


def direct_sums(diagonal, own, out, carried=None):
    real = functools.reduce(jnp.add, [block[0].astype(F32) for block in diagonal])
    imag = functools.reduce(jnp.add, [block[1].astype(F32) for block in diagonal])
    for slot in range(own.shape[0]):
        elem_re, elem_im = own[slot, 0].astype(F32), own[slot, 1].astype(F32)
        sums = [fold(elem_re * real + elem_im * imag), fold(elem_im * real - elem_re * imag)]
        for part in range(2):
            n = 2 * slot + part
            out[n] = sums[part] if carried is None else sums[part] + carried[n]


def sums_shape(count):
    return jax.ShapeDtypeStruct((count, SUBLANES, LANES), F32)


def early_blocks(spins):
    off = [(s, t) for s in range(spins - 1) for t in range(s + 1, spins - 1)]
    return off + [(s, s) for s in range(spins - 1)]


def early_kernel(eig, keys, rb_count, blocks, *refs):
    pieces, (own, flat, out, traces, sem) = refs[:-5], refs[-5:]
    rows, width = pieces[0].shape[1:]
    depth = rb_count * width
    copies = []
    for n, ((far, side), piece) in enumerate(zip(keys, pieces)):
        where = aligned(place(far, eig // rows) * rows, rows)
        for part in range(2):
            columns = pl.ds(part * depth + side * width, width)
            copies.append(pltpu.make_async_copy(piece.at[part], flat.at[where, columns], sem.at[2 * n + part]))
    for copy in copies:
        copy.start()
    for copy in copies:
        copy.wait()

    def step(n, carry):
        top, side = choose(n, [b[0] for b in blocks]), choose(n, [b[1] for b in blocks])
        out[n, 0], out[n, 1] = gram_block(flat[aligned(top * eig, eig), :], flat[aligned(side * eig, eig), :])
        return carry

    lax.fori_loop(0, len(blocks), step, 0)
    diagonal = [out.at[n] for n, block in enumerate(blocks) if block[0] == block[1]]
    direct_sums(diagonal, own, traces)


def early_gram(keys, pieces, own_elems, spins, eig, rb_count):
    blocks = early_blocks(spins)
    depth = 2 * rb_count * pieces[0].shape[2]
    return pl.pallas_call(
        functools.partial(early_kernel, eig, keys, rb_count, blocks),
        out_shape=(
            jax.ShapeDtypeStruct(((spins - 1) * eig, depth), BF16),
            jax.ShapeDtypeStruct((len(blocks), 2, eig, eig), BF16),
            sums_shape(2 * own_elems.shape[0]),
        ),
        in_specs=[ANY] * len(pieces) + [VMEM],
        out_specs=(VMEM, VMEM, VMEM),
        scratch_shapes=[pltpu.SemaphoreType.DMA((2 * len(pieces),))],
        compiler_params=params(32),
        cost_estimate=LONG,
        name="early_gram",
    )(*pieces, own_elems)


def side_columns(ref, rows, side, width, rb_count):
    return [ref[rows, (part * rb_count + side) * width : (part * rb_count + side + 1) * width] for part in range(2)]


def half_products(left, right):
    real = dot_nt(left[0], right[0]) + dot_nt(left[1], right[1])
    imag = dot_nt(left[0], right[1]) - dot_nt(left[1], right[0])
    return real, imag


def gather_last(eig, keys, others, pieces, last):
    rows, width = pieces[0].shape[1:]
    for (far, _), piece in zip(keys, pieces):
        where = aligned((place(far, eig // rows) - others * (eig // rows)) * rows, rows)
        for part in range(2):
            last[where, part * width : (part + 1) * width] = piece[part]


def late_begin_kernel(eig, keys, rb_count, flat, begun, *refs):
    pieces, (out, last) = refs[:-2], refs[-2:]
    side, width, others = keys[0][1], pieces[0].shape[2], flat.shape[0] // eig
    gather_last(eig, keys, others, pieces, last)
    right = [last[:, :width], last[:, width:]]
    for n in range(others):
        left = side_columns(flat, slice(n * eig, (n + 1) * eig), side, width, rb_count)
        out[n, 0], out[n, 1] = half_products(left, right)
    out[others, 0], out[others, 1] = half_products(right, right)


def late_begin(keys, flat, begun, pieces, spins, eig, rb_count):
    return pl.pallas_call(
        functools.partial(late_begin_kernel, eig, keys, rb_count),
        out_shape=jax.ShapeDtypeStruct((spins, 2, eig, eig), F32),
        in_specs=[VMEM, ANY] + [VMEM] * len(pieces),
        out_specs=VMEM,
        scratch_shapes=[pltpu.VMEM((eig, 2 * pieces[0].shape[2]), BF16)],
        compiler_params=params(32),
        cost_estimate=LITTLE,
        name="late_begin",
    )(flat, begun, *pieces)


def late_rows_kernel(eig, keys, rb_count, flat, partial, *refs):
    pieces, (out, last) = refs[:-2], refs[-2:]
    side, width = keys[0][1], pieces[0].shape[2]
    gather_last(eig, keys, flat.shape[0] // eig, pieces, last)
    right = [last[:, :width], last[:, width:]]
    for n in range(out.shape[0]):
        left = side_columns(flat, slice(n * eig, (n + 1) * eig), side, width, rb_count)
        real, imag = half_products(left, right)
        out[n, 0], out[n, 1] = (partial[n, 0] + real).astype(BF16), (partial[n, 1] + imag).astype(BF16)


def late_rest_kernel(eig, side, rb_count, flat, partial, last, own, carried, out, traces):
    count, width = out.shape[0] - 1, last.shape[1] // 2
    others = flat.shape[0] // eig
    right = [last[:, :width], last[:, width:]]
    for n in range(count + 1):
        spin = others - count + n
        left = right
        if n < count:
            left = side_columns(flat, slice(spin * eig, (spin + 1) * eig), side, width, rb_count)
        real, imag = half_products(left, right)
        out[n, 0], out[n, 1] = (partial[spin, 0] + real).astype(BF16), (partial[spin, 1] + imag).astype(BF16)
    direct_sums([out.at[count]], own, traces, carried)


def late_rows(keys, flat, partial, pieces, spins, eig, rb_count):
    return pl.pallas_call(
        functools.partial(late_rows_kernel, eig, keys, rb_count),
        out_shape=(
            jax.ShapeDtypeStruct((spins // 2, 2, eig, eig), BF16),
            jax.ShapeDtypeStruct((eig, 2 * pieces[0].shape[2]), BF16),
        ),
        in_specs=[VMEM] * (2 + len(pieces)),
        out_specs=(VMEM, VMEM),
        compiler_params=params(32),
        cost_estimate=LONG,
        name="late_rows",
    )(flat, partial, *pieces)


def late_rest(side, flat, partial, last, own, carried, spins, eig, rb_count):
    return pl.pallas_call(
        functools.partial(late_rest_kernel, eig, side, rb_count),
        out_shape=(
            jax.ShapeDtypeStruct((spins - spins // 2, 2, eig, eig), BF16),
            sums_shape(carried.shape[0]),
        ),
        in_specs=[VMEM] * 5,
        out_specs=(VMEM, VMEM),
        compiler_params=params(32),
        cost_estimate=LITTLE,
        name="late_rest",
    )(flat, partial, last, own, carried)


def factors_kernel(diag_mom, elems, right_ref, left_ref, own_ref, held, sem):
    rank = lax.axis_index("rb")
    eig = held.shape[-1]
    copies = []
    for time in range(2):
        which = diag_mom[0, rank, lax.bitwise_xor(rank, time)]
        copies.append(pltpu.make_async_copy(elems.at[which], held.at[time], sem.at[time]))
    for slot in range(own_ref.shape[0]):
        copies.append(pltpu.make_async_copy(elems.at[diag_mom[0, slot, rank]], own_ref.at[slot], sem.at[2 + slot]))
    for copy in copies:
        copy.start()
    for copy in copies:
        copy.wait()
    for time in range(2):
        re, im = held[time, 0], held[time, 1]
        right_ref[time, :eig, :eig] = re
        right_ref[time, :eig, eig:] = im
        right_ref[time, eig:, :eig] = -im
        right_ref[time, eig:, eig:] = re
        re_t = re.astype(F32).T.astype(BF16)
        im_t = im.astype(F32).T.astype(BF16)
        left_ref[time, :eig, :eig] = re_t
        left_ref[time, :eig, eig:] = im_t
        left_ref[time, eig:, :eig] = im_t
        left_ref[time, eig:, eig:] = -re_t


def factors(diag_mom, src_elems):
    slots, eig = diag_mom.shape[1], src_elems.shape[-1]
    form = jax.ShapeDtypeStruct((2, 2 * eig, 2 * eig), BF16)
    return pl.pallas_call(
        factors_kernel,
        out_shape=(form, form, jax.ShapeDtypeStruct((slots, 2, eig, eig), BF16)),
        in_specs=[SMEM, ANY],
        out_specs=(VMEM, VMEM, VMEM),
        scratch_shapes=[pltpu.VMEM((2, 2, eig, eig), BF16), pltpu.SemaphoreType.DMA((2 + slots,))],
        compiler_params=params(32),
        cost_estimate=LITTLE,
        name="factors",
    )(diag_mom, src_elems)


def right_products(x, count, from_right):
    rows = [jnp.concatenate([x[n, 0], x[n, 1]], axis=1) for n in range(count)]
    return dot(jnp.concatenate(rows, axis=0), from_right)


def left_product(y, n, from_left):
    eig = y.shape[-1]
    return dot(from_left, y[n].reshape(2 * eig, eig))


def paired(product, partner):
    eig = partner.shape[1]
    p_re, p_im = product[:, :eig], product[:, eig:]
    w_re, w_im = partner[:eig], partner[eig:]
    return fold(p_re * w_re - p_im * w_im), fold(p_re * w_im + p_im * w_re)


def own_products_kernel(own, right, left, products, partners):
    count = own.shape[0]
    products[...] = right_products(own, count, right[0])
    for n in range(count):
        partners[n] = left_product(own, n, left[0])


def own_products(own, right, left):
    count, eig = own.shape[0], own.shape[-1]
    return pl.pallas_call(
        own_products_kernel,
        out_shape=(
            jax.ShapeDtypeStruct((count * eig, 2 * eig), F32),
            jax.ShapeDtypeStruct((count, 2 * eig, eig), F32),
        ),
        in_specs=[VMEM] * 3,
        out_specs=(VMEM, VMEM),
        compiler_params=params(32),
        cost_estimate=LITTLE,
        name="own_products",
    )(own, right, left)


def joined_kernel(other, right, left, products, partners, carried, out):
    count, eig = other.shape[0], other.shape[-1]
    theirs = right_products(other, count, right[1])
    real, imag = [carried[0]], [carried[1]]
    for n in range(count):
        rows = slice(n * eig, (n + 1) * eig)
        sums = [paired(theirs[rows], partners[n]), paired(products[rows, :], left_product(other, n, left[1]))]
        real += [pair[0] for pair in sums]
        imag += [pair[1] for pair in sums]
    out[0] = functools.reduce(jnp.add, real)
    out[1] = functools.reduce(jnp.add, imag)


def joined_traces(other, right, left, products, partners, carried):
    return pl.pallas_call(
        joined_kernel,
        out_shape=sums_shape(2),
        in_specs=[VMEM] * 6,
        out_specs=VMEM,
        compiler_params=params(32),
        cost_estimate=LITTLE,
        name="late_cross",
    )(other, right, left, products, partners, carried)


def cross_kernel(offs, own, other, right, left, *refs):
    carried, out = refs[:-1], refs[-1]
    eig = own.shape[-1]
    if len(other.shape) > len(own.shape):
        other = other.at[1 - lax.axis_index("rb")]
    real, imag = [], []

    def add(x, y, count, from_right, from_left):
        product = right_products(x, count, from_right)
        for n in range(count):
            pair = paired(product[n * eig : (n + 1) * eig], left_product(y, n, from_left))
            real.append(pair[0])
            imag.append(pair[1])

    add(other, own, own.shape[0], right[1], left[0])
    add(own, other, offs, right[0], left[1])
    out[0] = functools.reduce(jnp.add, real + [ref[0] for ref in carried])
    out[1] = functools.reduce(jnp.add, imag + [ref[1] for ref in carried])


def cross_traces(offs, own, other, right, left, carried, name):
    return pl.pallas_call(
        functools.partial(cross_kernel, offs),
        out_shape=sums_shape(2),
        in_specs=[VMEM] * (4 + len(carried)),
        out_specs=VMEM,
        compiler_params=params(32),
        cost_estimate=LITTLE,
        name=name,
    )(own, other, right, left, *carried)


def last_cross_kernel(offs, own, other, right, left, direct, carried, out):
    count = direct.shape[0]
    for n in range(count):
        out[n] = direct[n]
    cross_kernel(offs, own, other, right, left, carried, out.at[pl.ds(count, 2)])


def last_cross(offs, own, other, right, left, direct, carried):
    return pl.pallas_call(
        functools.partial(last_cross_kernel, offs),
        out_shape=sums_shape(direct.shape[0] + 2),
        in_specs=[VMEM] * 6,
        out_specs=VMEM,
        compiler_params=params(32),
        cost_estimate=LITTLE,
        name="last_cross",
    )(own, other, right, left, direct, carried)


def final_kernel(slots, mine, theirs, count, out):
    rank = lax.axis_index("rb")
    lane = lax.broadcasted_iota(jnp.int32, (1, LANES), 1)

    def totals(ref):
        rows = jnp.concatenate([jnp.sum(ref[n], axis=0, keepdims=True) for n in range(ref.shape[0])], axis=0)
        sums = jnp.broadcast_to(jnp.sum(rows, axis=1, keepdims=True), rows.shape)
        return [sums[n : n + 1] for n in range(ref.shape[0])]

    def put(slot, kind, re, im):
        value = jnp.where(lane == 0, re, im) * 0.25
        out[0, slot, kind : kind + 1, :] = jnp.where(slot < count[0], value, 0.0)[:, :2]

    m, t = totals(mine), totals(theirs)
    for slot in range(slots):
        m_re, m_im, t_re, t_im = m[2 * slot], m[2 * slot + 1], t[2 * slot], t[2 * slot + 1]
        put(slot, 0, m_re * t_re - m_im * t_im, m_re * t_im + m_im * t_re)
        here = rank == slot
        put(slot, 1, jnp.where(here, m[2 * slots], t[2 * slots]), jnp.where(here, m[2 * slots + 1], t[2 * slots + 1]))


def final(mine, theirs, diag_count, slots):
    return pl.pallas_call(
        functools.partial(final_kernel, slots),
        out_shape=jax.ShapeDtypeStruct((1, slots, 2, 2), F32),
        in_specs=[VMEM, VMEM, SMEM],
        out_specs=VMEM,
        compiler_params=params(32),
        name="final",
    )(mine, theirs, diag_count)


def shards(peram, src_elems, owner_times, diag_mom, diag_count):
    tp_count, rb_count = lax.axis_size("tp"), lax.axis_size("rb")
    eig = src_elems.shape[-1]
    spins = tp_count * peram.shape[0] // eig
    slots = diag_mom.shape[1]

    head, tail, late, own = travel_order(tp_count, rb_count)
    early_keys = head + tail
    picked = pick(owner_times, peram, head, "pick_head", [jax.ShapeDtypeStruct((4, *peram.shape), BF16)])
    picked.update(pick(owner_times, peram, tail + late + own, "pick_tail", []))

    def send(key):
        far, side = key
        swapped = tp_count // 4 if far >= tp_count // 2 else 0
        pairs = [
            (tp * rb_count + rb, (tp ^ far ^ (swapped if tp < tp_count // 2 else 0)) * rb_count + (rb ^ side))
            for tp in range(tp_count)
            for rb in range(rb_count)
        ]
        return lax.ppermute(picked[key], ("tp", "rb"), pairs)

    swap = [(rb, rb ^ 1) for rb in range(rb_count)]
    right, left, own_elems = factors(diag_mom, src_elems)
    arrived = [send(key) for key in early_keys] + [picked[key] for key in own]
    flat, early, direct = early_gram(early_keys + own, arrived, own_elems, spins, eig, rb_count)
    early_both = lax.all_to_all(jnp.stack([early] * rb_count), "rb", 0, 0)
    offs = early.shape[0] - (spins - 1)
    begun = cross_traces(offs, early, early_both, right, left, [], "early_cross")

    halves = [[key for key in late if key[1] == side] for side in range(rb_count)]
    halves[0].reverse()
    sent = [[send(key) for key in keys] for keys in halves]
    half = late_begin(halves[0], flat, begun, sent[0], spins, eig, rb_count)
    blocks, last = late_rows(halves[1], flat, half, sent[1], spins, eig, rb_count)
    swapped = lax.ppermute(blocks, "rb", swap)
    rest, traces = late_rest(1, flat, half, last, own_elems, direct, spins, eig, rb_count)
    rest_swapped = lax.ppermute(rest, "rb", swap)
    products, partners = own_products(blocks, right, left)
    partial = joined_traces(swapped, right, left, products, partners, begun)
    mine = last_cross(rest.shape[0] - 1, rest, rest_swapped, right, left, traces, partial)
    theirs = lax.ppermute(mine, "rb", swap)
    return final(mine, theirs, diag_count, slots)


def solution(mesh):
    in_specs = (
        P(("grp", "tp"), None, None, "rb"),
        P("grp", None, None, None),
        P("grp", None),
        P(("grp", "tp"), None, None),
        P(("grp", "tp")),
    )
    out_specs = P(("grp", "tp"), None, None, None)
    return jax.shard_map(shards, mesh=mesh, in_specs=in_specs, out_specs=out_specs, check_vma=False)
```
